32 devices in a mesh: page: 4 (over z), row: 8 (over y, x, core).
Axes of the slice: x: 2, y: 2, z: 4, core: 2. Of those that a mesh axis runs over, the one named last changes fastest.
Arguments:
- qkv_rows: bfloat16 [4, 512, 3840], P('page', 'row'), may hold values from -12 to 12
- residual: bfloat16 [4, 512, 1280], P('page', 'row'), may hold values from -40 to 40
- out_weight: bfloat16 [1280, 1280], P('page'), may hold values from -0.15625 to 0.15625
- norm_gain: float32 [1280], replicated, may hold values from 0.1 to 1.9
- merge_weight: bfloat16 [5120, 5120], P('row'), may hold values from -0.078125 to 0.078125
- merge_bias: float32 [5120], P('row'), may hold values from -3 to 3
- page_grid: int32 [4, 2], P('page'), may hold values from 2 to 64, as said below
Outputs:
- merged: bfloat16 [4, 5120, 128], P('page', 'row')
The draws below stay inside these ranges and needn't reach their ends.
Inputs may be any that keep to these rules, and one draw needn't show every extreme that they name: `page_grid`: rows and columns are even; rows times columns is at most 512, and one page of every draw has exactly 512 live patches in 64 rows of 8 columns; columns are at least 8.
All inputs are finite; a program needn't handle non-finite values.
Results may differ from the reference program's by a relative error of at most 0.0049.
Values may be sent and summed in bfloat16 or wider, within the bound.
No kernel may reach another device: no remote copies, remote signals or barrier semaphores. Data moves between devices by JAX's collectives and lax.ppermute only.
A program may use at most 64 MiB of HBM per device.

```python
import math
import jax
import jax.numpy as jnp
from jax import lax

D = 1280
HEADS = 16
MHID = 5120
HDIM = 80
PAGES = 4
PATCHES = 512
GROUPS = 128


def draw_qkv_rows(key, part):
    keys_all = jax.random.split(key, 1)
    shape = (PAGES, PATCHES, 3 * D)
    column = jnp.arange(3 * D)[None, None, :]
    col_scale = jnp.where(column < 2 * D, 1.5, 2.0)
    base = jnp.clip(jax.random.normal(keys_all[0], shape, jnp.float32), -6.0, 6.0) * col_scale
    return base.astype(jnp.bfloat16)


def draw_residual(key, part):
    keys_all = jax.random.split(key, 3)
    shape = (PAGES, PATCHES, D)
    col_scale = jnp.exp(jax.random.uniform(keys_all[1], (1, 1, D), jnp.float32, math.log(0.3), math.log(3.0)))
    base = jnp.clip(jax.random.normal(keys_all[0], shape, jnp.float32), -6.0, 6.0)
    row_scale = jnp.exp(jax.random.uniform(keys_all[2], (PAGES, PATCHES, 1), jnp.float32, math.log(0.5), math.log(2.0)))
    base = base * col_scale * row_scale
    return base.astype(jnp.bfloat16)


def draw_page_grid(key, part):
    keys_all = jax.random.split(key, 3)
    col_cap = min(64, PATCHES // 16)
    half_cols = jax.random.randint(keys_all[0], (PAGES,), 4, col_cap + 1)
    cols_n = 2 * half_cols
    row_cap = PATCHES // (2 * cols_n)
    spread = jax.random.randint(keys_all[1], (PAGES,), 0, 1 << 20)
    half_rows = row_cap // 2 + spread % (row_cap - row_cap // 2 + 1)
    rows_n = 2 * jnp.maximum(half_rows, 1)
    forced = jax.random.randint(keys_all[2], (), 0, PAGES)
    page_ids = jnp.arange(PAGES)
    rows_n = jnp.where(page_ids == forced, PATCHES // 8, rows_n)
    cols_n = jnp.where(page_ids == forced, 8, cols_n)
    return jnp.stack([rows_n, cols_n], axis=1).astype(jnp.int32)


def block_levels(stream_key, shape, cuts, least, top_value):
    level = 1.0
    for position, shards_of in cuts:
        heights = jax.random.uniform(jax.random.fold_in(jax.random.fold_in(stream_key, 6), position), (shards_of,), jnp.float32, least / len(cuts), top_value / len(cuts))
        level = level * jnp.repeat(jnp.exp(heights), shape[position] // shards_of).reshape((-1,) + (1,) * (len(shape) - 1 - position))
    return level


def centred(rng, dims, scale, limit, cuts=(), kind=jnp.bfloat16):
    gain = block_levels(rng, dims, cuts, -0.22, 0.18) if cuts else 1.0
    entries = jax.random.normal(rng, dims, jnp.float32) * scale * gain
    return jnp.minimum(jnp.maximum(entries, -limit), limit).astype(kind)


def setup_inputs(seed: int = 0) -> dict:
    key_list = jax.random.split(jax.random.key(seed), 8)
    return {
        "qkv_rows": draw_qkv_rows(jax.random.fold_in(key_list[7], 71), 0),
        "residual": draw_residual(jax.random.fold_in(key_list[7], 71), 0),
        "out_weight": centred(key_list[2], (D, D), D ** -0.5, 0.15625, ((0, 4),)),
        "norm_gain": jnp.clip(1.0 + 0.18 * jax.random.normal(key_list[3], (D,), jnp.float32), 0.1, 1.9),
        "merge_weight": centred(key_list[4], (MHID, 4 * D), (4 * D) ** -0.5, 0.078125, ((0, 8),)),
        "merge_bias": centred(key_list[5], (MHID,), 0.5, 3.0, ((0, 8),), jnp.float32),
        "page_grid": draw_page_grid(jax.random.fold_in(key_list[7], 71), 0),
    }


def head_attention(operands, key_valid):
    queries, key_rows, value_rows = operands
    scores = jnp.dot(queries, key_rows.T, preferred_element_type=jnp.float32) / math.sqrt(HDIM)
    scores = jnp.where(key_valid[None, :], scores, -1e+30)
    peak = lax.optimization_barrier(jnp.max(scores, axis=1, keepdims=True))
    weights = jnp.exp(scores - peak)
    total = lax.optimization_barrier(jnp.sum(weights, axis=1, keepdims=True))
    probs = weights.astype(jnp.bfloat16)
    mixed = jnp.dot(probs, value_rows, preferred_element_type=jnp.float32) / total
    return mixed.astype(jnp.bfloat16)

def group_index(grid_row):
    rows_n = grid_row[0]
    cols_n = grid_row[1]
    slots = jnp.arange(GROUPS, dtype=jnp.int32)
    half_cols = cols_n // 2
    live = slots < rows_n // 2 * half_cols
    first = jnp.where(live, 2 * (slots // half_cols) * cols_n + 2 * (slots % half_cols), 0).astype(jnp.int32)
    return (live, [first, first + 1, first + cols_n, first + cols_n + 1])

def reference(qkv_rows, residual, out_weight, norm_gain, merge_weight, merge_bias, page_grid):

    def page_layer(operands):
        page_qkv, page_resid, grid_row = operands
        valid_len = grid_row[0] * grid_row[1]
        key_valid = jnp.arange(PATCHES, dtype=jnp.int32) < valid_len
        queries = page_qkv[:, :D].reshape(PATCHES, HEADS, HDIM).transpose(1, 0, 2)
        key_rows = page_qkv[:, D:2 * D].reshape(PATCHES, HEADS, HDIM).transpose(1, 0, 2)
        value_rows = page_qkv[:, 2 * D:].reshape(PATCHES, HEADS, HDIM).transpose(1, 0, 2)
        heads_out = lax.map(lambda ops: head_attention(ops, key_valid), (queries, key_rows, value_rows))
        attn = heads_out.transpose(1, 0, 2).reshape(PATCHES, D)
        hidden = page_resid.astype(jnp.float32) + jnp.dot(attn, out_weight, preferred_element_type=jnp.float32)
        normed = (hidden * lax.rsqrt(lax.optimization_barrier(jnp.mean(hidden * hidden, axis=1, keepdims=True)) + 1e-06) * norm_gain).astype(jnp.bfloat16)
        live, corners = group_index(grid_row)
        grouped = jnp.concatenate([jnp.take(normed, corner, axis=0) for corner in corners], axis=1)
        merged = jnp.dot(merge_weight, grouped.T, preferred_element_type=jnp.float32) + merge_bias[:, None]
        merged = jax.nn.gelu(merged, approximate=False)
        return jnp.where(live[None, :], merged, 0.0).astype(jnp.bfloat16)
    return lax.map(page_layer, (qkv_rows, residual, page_grid))
```

```python
import functools
import math

import jax
import jax.numpy as jnp
from jax import lax
from jax.experimental import pallas as pl
from jax.experimental.pallas import tpu as pltpu
from jax.sharding import PartitionSpec as P

D = 1280
HEADS = 16
HDIM = 80


def local_any(qkv_rows, residual, out_weight, norm_gain, merge_weight, merge_bias, page_grid):
    row_count = lax.axis_size("row")
    q_split = max(1, row_count // HEADS)
    head_groups = row_count // q_split
    width = D // head_groups
    heads_per = width // HDIM
    band_len = qkv_rows.shape[1]
    part_len = band_len // q_split
    local_qkv = qkv_rows[0]
    queries = local_qkv[:, :D]
    key_vals = jnp.concatenate(
        [
            local_qkv[:, D : 2 * D].reshape(band_len, head_groups, width),
            local_qkv[:, 2 * D :].reshape(band_len, head_groups, width),
        ],
        axis=2,
    )
    q_send = (
        queries.reshape(q_split, part_len, head_groups, width)
        .transpose(2, 0, 1, 3)
        .reshape(row_count, part_len, width)
    )
    kv_send = jnp.broadcast_to(
        key_vals.transpose(1, 0, 2)[:, None], (head_groups, q_split, band_len, 2 * width)
    )
    kv_send = kv_send.reshape(row_count, band_len, 2 * width)
    q_recv, kv_recv = (
        lax.all_to_all(q_send, "row", split_axis=0, concat_axis=1, tiled=True),
        lax.all_to_all(kv_send, "row", split_axis=0, concat_axis=1, tiled=True),
    )
    kv_local = kv_recv[0]
    positions = jnp.arange(row_count * band_len, dtype=jnp.int32)
    valid_len = page_grid[0, 0] * page_grid[0, 1]
    key_valid = positions < valid_len
    key_total = kv_local.shape[0]
    key_heads = kv_local[:, :width].reshape(key_total, heads_per, HDIM)
    value_heads = kv_local[:, width:].reshape(key_total, heads_per, HDIM)
    query_total = row_count * part_len
    q_block = math.gcd(query_total, 512)
    q_blocks = q_recv[0].reshape(query_total // q_block, q_block, heads_per, HDIM)
    root_dim = math.sqrt(HDIM)

    def attend(q_span):
        scores = (
            jnp.einsum("qhd,khd->hqk", q_span, key_heads, preferred_element_type=jnp.float32)
            / root_dim
        )
        scores = jnp.where(key_valid[None, None, :], scores, -1e30)
        peak = jnp.max(scores, axis=2, keepdims=True)
        weights = jnp.exp(scores - peak)
        total = jnp.sum(weights, axis=2, keepdims=True)
        mixed = (
            jnp.einsum(
                "hqk,khd->hqd",
                weights.astype(jnp.bfloat16),
                value_heads,
                preferred_element_type=jnp.float32,
            )
            / total
        )
        return mixed.transpose(1, 0, 2).reshape(q_span.shape[0], width).astype(jnp.bfloat16)

    attn_heads = lax.map(attend, q_blocks).reshape(row_count, part_len, width)
    returned = lax.all_to_all(attn_heads, "row", split_axis=0, concat_axis=0, tiled=True)
    attn = (
        returned.reshape(head_groups, q_split, part_len, width)
        .transpose(1, 2, 0, 3)
        .reshape(band_len, D)
    )
    projected = jnp.dot(
        attn,
        lax.all_gather(out_weight, "page", axis=0, tiled=True),
        preferred_element_type=jnp.float32,
    )
    hidden = residual[0].astype(jnp.float32) + projected
    normed = (
        hidden * lax.rsqrt(jnp.mean(hidden * hidden, axis=1, keepdims=True) + 1e-06) * norm_gain
    ).astype(jnp.bfloat16)
    rows_n = page_grid[0, 0]
    cols_n = page_grid[0, 1]
    group_total = band_len * row_count // 4
    slots = jnp.arange(group_total, dtype=jnp.int32)
    half_cols = cols_n // 2
    live = slots < rows_n // 2 * half_cols
    first = jnp.where(live, 2 * (slots // half_cols) * cols_n + 2 * (slots % half_cols), 0)
    corners = [first, first + 1, first + cols_n, first + cols_n + 1]
    local_units = merge_weight.shape[0]
    page_all = lax.all_gather(normed, "row", axis=0, tiled=True)
    merged_sum = jnp.zeros((local_units, group_total), jnp.float32)
    for corner in range(4):
        picked = jnp.take(page_all, corners[corner], axis=0)
        merged_sum = merged_sum + jnp.einsum(
            "md,gd->mg",
            merge_weight[:, corner * D : (corner + 1) * D],
            picked,
            preferred_element_type=jnp.float32,
        )
    merged = jax.nn.gelu(merged_sum + merge_bias[:, None], approximate=False)
    merged = jnp.where(live[None, :], merged, 0.0).astype(jnp.bfloat16)
    return merged[None]


ROWS = 8
PAGES = 4
HPAIR = 2 * HDIM
KEEP = 128
REST = HPAIR - KEEP


def vmem(count):
    return [pl.BlockSpec(memory_space=pltpu.VMEM)] * count


def row_index():
    return lax.axis_index("row")


def spread_kernel(qkv_ref, *rest):
    outs, held = rest[:ROWS], rest[ROWS]
    me = row_index()
    for dest in range(ROWS):
        for part in range(3):
            at = part * D + dest * HPAIR
            held[dest, :, part * HPAIR : (part + 1) * HPAIR] = qkv_ref[0, :, at : at + HPAIR]
    for step in range(ROWS):
        outs[step][...] = held[me ^ step]


def corner_rows(grid_ref, groups, corner):
    rows_n, cols_n = grid_ref[0, 0], grid_ref[0, 1]
    half = cols_n // 2
    slots = lax.broadcasted_iota(jnp.int32, (groups, 1), 0)
    line = jnp.floor((slots.astype(jnp.float32) + 0.5) / half.astype(jnp.float32)).astype(jnp.int32)
    first = 2 * line * cols_n + 2 * (slots - line * half)
    picked = first + (corner // 2) * cols_n + corner % 2
    return jnp.where(slots < (rows_n // 2) * half, picked, -1)


def select_rows(grid_ref, patches):
    groups = patches // 4
    wanted = jnp.concatenate([corner_rows(grid_ref, groups, corner) for corner in range(4)], axis=0)
    at = lax.broadcasted_iota(jnp.int32, (patches, patches), 1)
    return jnp.where(at == wanted, 1.0, 0.0).astype(jnp.bfloat16)


def attend_kernel(grid_ref, *rest):
    blocks = rest[:ROWS]
    out_ref, q_all, k_all, v_all = rest[ROWS:]
    me = row_index()
    band = blocks[0].shape[0]
    patches = band * ROWS
    for step in range(ROWS):
        at = pl.ds(pl.multiple_of((me ^ step) * band, band), band)
        q_all[at, :] = blocks[step][:, :HPAIR]
        k_all[at, :] = blocks[step][:, HPAIR : 2 * HPAIR]
        v_all[at, :] = blocks[step][:, 2 * HPAIR :]
    select = select_rows(grid_ref, patches)
    queries = jnp.dot(select, q_all[...], preferred_element_type=jnp.float32).astype(jnp.bfloat16)
    lane = lax.broadcasted_iota(jnp.int32, (1, HPAIR), 1)
    live = lax.broadcasted_iota(jnp.int32, (1, patches), 1) < grid_ref[0, 0] * grid_ref[0, 1]
    keys, values = k_all[...], v_all[...]
    mixed = []
    for head in range(2):
        mine = (lane >= head * HDIM) & (lane < (head + 1) * HDIM)
        asked = jnp.where(mine, queries, jnp.zeros_like(queries))
        scores = lax.dot_general(asked, keys, (((1,), (1,)), ((), ())), preferred_element_type=jnp.float32)
        scores = jnp.where(live, scores * (1.0 / math.sqrt(HDIM)), -1e30)
        weights = jnp.exp(scores - jnp.max(scores, axis=1, keepdims=True))
        total = jnp.sum(weights, axis=1, keepdims=True)
        mixed.append(
            jnp.dot(weights.astype(jnp.bfloat16), values, preferred_element_type=jnp.float32) / total
        )
    attn = jnp.where(lane < HDIM, mixed[0], mixed[1])
    out_ref[:patches, :] = attn[:, :KEEP].astype(jnp.bfloat16)
    groups = patches // 4
    tail = [attn[corner * groups : (corner + 1) * groups, KEEP:] for corner in range(4)]
    out_ref[patches:, :] = jnp.concatenate(tail, axis=1).astype(jnp.bfloat16)


def residual_kernel(grid_ref, *rest):
    blocks = rest[:ROWS]
    out_ref, held = rest[ROWS:]
    me = row_index()
    band = blocks[0].shape[0]
    for step in range(ROWS):
        held[pl.ds(pl.multiple_of((me ^ step) * band, band), band), :] = blocks[step][...]
    select = select_rows(grid_ref, band * ROWS)
    out_ref[...] = jnp.dot(select, held[...], preferred_element_type=jnp.float32).astype(jnp.bfloat16)


def weight_kernel(own_ref, *rest):
    mine, theirs = rest[: PAGES - 1], rest[PAGES - 1 : 2 * PAGES - 2]
    out_ref = rest[-1]
    page, core = lax.axis_index("page"), row_index() % 2

    def place(pair, block):
        out_ref[pl.ds(pl.multiple_of(pair * KEEP, KEEP), KEEP), :] = block[:KEEP]
        out_ref[pl.ds(pl.multiple_of(ROWS * KEEP + pair * REST, REST), REST), :] = block[KEEP:]

    place(2 * page, own_ref[:HPAIR])
    place(2 * page + 1, own_ref[HPAIR:])
    for step in range(1, PAGES):
        source = lax.rem(page + PAGES - step, PAGES)
        place(2 * source + core, mine[step - 1][...])
        place(2 * source + 1 - core, theirs[step - 1][...])


def merge_kernel(grid_ref, *rest):
    pieces = rest[:ROWS]
    resid_ref, proj_ref, gain_ref, weight_hbm, bias_ref, out_ref, attn, hidden, weight, sem = rest[ROWS:]
    fetch = pltpu.make_async_copy(weight_hbm, weight, sem)
    fetch.start()
    me = row_index()
    patches = attn.shape[0]
    groups = patches // 4
    for step in range(ROWS):
        pair = me ^ step
        attn[:, pl.ds(pl.multiple_of(pair * KEEP, KEEP), KEEP)] = pieces[step][:patches]
    lane = lax.broadcasted_iota(jnp.int32, (1, KEEP), 1) // REST
    for half in range(2):
        tails = []
        for corner in range(4):
            total = jnp.zeros((groups, KEEP), jnp.float32)
            for step in range(ROWS):
                pair = me ^ step
                tail = pieces[step][patches:].astype(jnp.float32)
                shift = lax.rem((pair + 4 - corner) * REST, KEEP)
                turned = pltpu.roll(tail, shift, axis=1)
                total = jnp.where((lane == lax.rem(pair, 4)) & (pair // 4 == half), turned, total)
            tails.append(total.astype(jnp.bfloat16))
        attn[:, ROWS * KEEP + half * KEEP : ROWS * KEEP + (half + 1) * KEEP] = jnp.concatenate(tails, axis=0)
    squares = jnp.zeros((patches, 1), jnp.float32)
    cols = 256
    for at in range(0, D, cols):
        part = jnp.dot(attn[...], proj_ref[:, at : at + cols], preferred_element_type=jnp.float32)
        part = part + resid_ref[:, at : at + cols].astype(jnp.float32)
        hidden[:, at : at + cols] = part
        squares = squares + jnp.sum(part * part, axis=1, keepdims=True)
    scale = lax.rsqrt(squares * (1.0 / D) + 1e-06)
    fetch.wait()
    total = jnp.zeros((weight.shape[0], groups), jnp.float32)
    for corner in range(4):
        span = slice(corner * groups, (corner + 1) * groups)
        normed = (hidden[span, :] * scale[span] * gain_ref[...]).astype(jnp.bfloat16)
        total = total + lax.dot_general(
            weight[:, corner * D : (corner + 1) * D], normed, (((1,), (1,)), ((), ())), preferred_element_type=jnp.float32
        )
    total = total + bias_ref[...]
    merged = 0.5 * total * (1.0 + lax.erf(total * math.sqrt(0.5)))
    live = lax.broadcasted_iota(jnp.int32, (1, groups), 1) < (grid_ref[0, 0] // 2) * (grid_ref[0, 1] // 2)
    out_ref[0] = jnp.where(live, merged, 0.0).astype(jnp.bfloat16)


def params():
    return pltpu.CompilerParams(vmem_limit_bytes=40 * 1024 * 1024)


def cost(flops, moved):
    return pl.CostEstimate(flops=flops, bytes_accessed=moved, transcendentals=0)


def swap(value, step):
    return lax.ppermute(value, "row", [(row, row ^ step) for row in range(ROWS)])


def gather_rows(value):
    far = [swap(value, step) for step in (2, 4, 6)]
    near = [swap(piece, 1) for piece in [value] + far]
    return [value, near[0], far[0], near[1], far[1], near[2], far[2], near[3]]


def local_eight(qkv_rows, residual, out_weight, norm_gain, merge_weight, merge_bias, page_grid):
    band = qkv_rows.shape[1]
    patches = band * ROWS
    units = merge_weight.shape[0]
    smem = pl.BlockSpec(memory_space=pltpu.SMEM)
    bf16, f32 = jnp.bfloat16, jnp.float32

    core = row_index() % 2
    moving = lax.dynamic_slice_in_dim(out_weight, core * HPAIR, HPAIR, 0)
    mine = []
    for _ in range(PAGES - 1):
        moving = lax.ppermute(moving, "page", [(page, (page + 1) % PAGES) for page in range(PAGES)])
        mine.append(moving)
    theirs = [swap(piece, 1) for piece in mine]

    sends = pl.pallas_call(
        spread_kernel,
        out_shape=[jax.ShapeDtypeStruct((band, 3 * HPAIR), bf16)] * ROWS,
        in_specs=vmem(1),
        out_specs=vmem(ROWS),
        scratch_shapes=[pltpu.VMEM((ROWS, band, 3 * HPAIR), bf16)],
        compiler_params=params(),
        name="spread",
    )(qkv_rows)
    blocks = [sends[0]] + [swap(sends[step], step) for step in range(1, ROWS)]
    attn = pl.pallas_call(
        attend_kernel,
        out_shape=jax.ShapeDtypeStruct((patches + patches // 4, KEEP), bf16),
        in_specs=[smem] + vmem(ROWS),
        out_specs=pl.BlockSpec(memory_space=pltpu.VMEM),
        scratch_shapes=[pltpu.VMEM((patches, HPAIR), bf16)] * 3,
        compiler_params=params(),
        cost_estimate=cost(6 * patches * patches * 256, 1 << 20),
        name="attend",
    )(page_grid, *blocks)
    resid = pl.pallas_call(
        residual_kernel,
        out_shape=jax.ShapeDtypeStruct((patches, D), bf16),
        in_specs=[smem] + vmem(ROWS),
        out_specs=pl.BlockSpec(memory_space=pltpu.VMEM),
        scratch_shapes=[pltpu.VMEM((patches, D), bf16)],
        compiler_params=params(),
        cost_estimate=cost(2 * patches * patches * D, 4 * patches * D),
        name="residual_rows",
    )(page_grid, *gather_rows(residual[0]))
    proj = pl.pallas_call(
        weight_kernel,
        out_shape=jax.ShapeDtypeStruct((D, D), bf16),
        in_specs=vmem(2 * PAGES - 1),
        out_specs=pl.BlockSpec(memory_space=pltpu.VMEM),
        compiler_params=params(),
        cost_estimate=cost(0, 4 * D * D),
        name="projection_rows",
    )(out_weight, *mine, *theirs)
    pieces = gather_rows(attn)
    merged = pl.pallas_call(
        merge_kernel,
        out_shape=jax.ShapeDtypeStruct((1, units, patches // 4), bf16),
        in_specs=[smem] + vmem(ROWS + 3) + [pl.BlockSpec(memory_space=pl.ANY)] + vmem(1),
        out_specs=pl.BlockSpec(memory_space=pltpu.VMEM),
        scratch_shapes=[
            pltpu.VMEM((patches, D), bf16),
            pltpu.VMEM((patches, D), f32),
            pltpu.VMEM((units, 4 * D), bf16),
            pltpu.SemaphoreType.DMA,
        ],
        compiler_params=params(),
        cost_estimate=cost(2 * patches * D * (D + units), 16 << 20),
        name="merge",
    )(page_grid, *pieces, resid, proj, norm_gain.reshape(1, D), merge_weight, merge_bias.reshape(units, 1))
    return merged


def solution(mesh):
    in_specs = (
        P("page", "row", None),
        P("page", "row", None),
        P("page", None),
        P(),
        P("row", None),
        P("row"),
        P("page", None),
    )
    out_specs = P("page", "row", None)
    local = local_eight if mesh.shape["row"] == 8 and mesh.shape["page"] == 4 else local_any
    return jax.shard_map(local, mesh=mesh, in_specs=in_specs, out_specs=out_specs, check_vma=False)
```

```python
import functools
import math

import jax
import jax.numpy as jnp
from jax import lax
from jax.experimental import pallas as pl
from jax.experimental.pallas import tpu as pltpu
from jax.sharding import PartitionSpec as P

D = 1280
HEADS = 16
HDIM = 80


def local_any(qkv_rows, residual, out_weight, norm_gain, merge_weight, merge_bias, page_grid):
    row_count = lax.axis_size("row")
    q_split = max(1, row_count // HEADS)
    head_groups = row_count // q_split
    width = D // head_groups
    heads_per = width // HDIM
    band_len = qkv_rows.shape[1]
    part_len = band_len // q_split
    local_qkv = qkv_rows[0]
    queries = local_qkv[:, :D]
    key_vals = jnp.concatenate(
        [
            local_qkv[:, D : 2 * D].reshape(band_len, head_groups, width),
            local_qkv[:, 2 * D :].reshape(band_len, head_groups, width),
        ],
        axis=2,
    )
    q_send = (
        queries.reshape(q_split, part_len, head_groups, width)
        .transpose(2, 0, 1, 3)
        .reshape(row_count, part_len, width)
    )
    kv_send = jnp.broadcast_to(
        key_vals.transpose(1, 0, 2)[:, None], (head_groups, q_split, band_len, 2 * width)
    )
    kv_send = kv_send.reshape(row_count, band_len, 2 * width)
    q_recv, kv_recv = (
        lax.all_to_all(q_send, "row", split_axis=0, concat_axis=1, tiled=True),
        lax.all_to_all(kv_send, "row", split_axis=0, concat_axis=1, tiled=True),
    )
    kv_local = kv_recv[0]
    positions = jnp.arange(row_count * band_len, dtype=jnp.int32)
    valid_len = page_grid[0, 0] * page_grid[0, 1]
    key_valid = positions < valid_len
    key_total = kv_local.shape[0]
    key_heads = kv_local[:, :width].reshape(key_total, heads_per, HDIM)
    value_heads = kv_local[:, width:].reshape(key_total, heads_per, HDIM)
    query_total = row_count * part_len
    q_block = math.gcd(query_total, 512)
    q_blocks = q_recv[0].reshape(query_total // q_block, q_block, heads_per, HDIM)
    root_dim = math.sqrt(HDIM)

    def attend(q_span):
        scores = (
            jnp.einsum("qhd,khd->hqk", q_span, key_heads, preferred_element_type=jnp.float32)
            / root_dim
        )
        scores = jnp.where(key_valid[None, None, :], scores, -1e30)
        peak = jnp.max(scores, axis=2, keepdims=True)
        weights = jnp.exp(scores - peak)
        total = jnp.sum(weights, axis=2, keepdims=True)
        mixed = (
            jnp.einsum(
                "hqk,khd->hqd",
                weights.astype(jnp.bfloat16),
                value_heads,
                preferred_element_type=jnp.float32,
            )
            / total
        )
        return mixed.transpose(1, 0, 2).reshape(q_span.shape[0], width).astype(jnp.bfloat16)

    attn_heads = lax.map(attend, q_blocks).reshape(row_count, part_len, width)
    returned = lax.all_to_all(attn_heads, "row", split_axis=0, concat_axis=0, tiled=True)
    attn = (
        returned.reshape(head_groups, q_split, part_len, width)
        .transpose(1, 2, 0, 3)
        .reshape(band_len, D)
    )
    projected = jnp.dot(
        attn,
        lax.all_gather(out_weight, "page", axis=0, tiled=True),
        preferred_element_type=jnp.float32,
    )
    hidden = residual[0].astype(jnp.float32) + projected
    normed = (
        hidden * lax.rsqrt(jnp.mean(hidden * hidden, axis=1, keepdims=True) + 1e-06) * norm_gain
    ).astype(jnp.bfloat16)
    rows_n = page_grid[0, 0]
    cols_n = page_grid[0, 1]
    group_total = band_len * row_count // 4
    slots = jnp.arange(group_total, dtype=jnp.int32)
    half_cols = cols_n // 2
    live = slots < rows_n // 2 * half_cols
    first = jnp.where(live, 2 * (slots // half_cols) * cols_n + 2 * (slots % half_cols), 0)
    corners = [first, first + 1, first + cols_n, first + cols_n + 1]
    local_units = merge_weight.shape[0]
    page_all = lax.all_gather(normed, "row", axis=0, tiled=True)
    merged_sum = jnp.zeros((local_units, group_total), jnp.float32)
    for corner in range(4):
        picked = jnp.take(page_all, corners[corner], axis=0)
        merged_sum = merged_sum + jnp.einsum(
            "md,gd->mg",
            merge_weight[:, corner * D : (corner + 1) * D],
            picked,
            preferred_element_type=jnp.float32,
        )
    merged = jax.nn.gelu(merged_sum + merge_bias[:, None], approximate=False)
    merged = jnp.where(live[None, :], merged, 0.0).astype(jnp.bfloat16)
    return merged[None]


ROWS = 8
PAGES = 4
HPAIR = 2 * HDIM
WIDE = 128
REST = HPAIR - WIDE
MAIN = ROWS * WIDE
ROOT = math.log2(math.e) / math.sqrt(HDIM)
BF16 = jnp.bfloat16
F32 = jnp.float32


def row_index():
    return lax.axis_index("row")


def pack_tail(wide):
    groups = wide.shape[0] // 4
    return jnp.concatenate([wide[at * groups : (at + 1) * groups] for at in range(4)], axis=1)


def spread_kernel(qkv_ref, resid_ref, *rest):
    outs, held = rest[:ROWS], rest[ROWS]
    me = row_index()
    for dest in range(ROWS):
        at = dest * HPAIR
        resid = [resid_ref[0, :, dest * WIDE : (dest + 1) * WIDE]]
        resid.append(resid_ref[0, :, MAIN + dest * REST : MAIN + (dest + 1) * REST])
        parts = [qkv_ref[0, :, part * D + at : part * D + at + HPAIR] for part in range(3)]
        held[dest] = jnp.concatenate(parts + resid, axis=1)
    for step in range(ROWS):
        outs[step][...] = held[me ^ step]


def slice_kernel(weight_ref, token_ref, out_ref):
    del token_ref
    me = row_index()
    depth = weight_ref.shape[0]
    out_ref[:depth, :] = weight_ref[:, pl.ds(pl.multiple_of(me * WIDE, WIDE), WIDE)]
    tile = weight_ref[:, pl.ds(pl.multiple_of(MAIN + me // 4 * WIDE, WIDE), WIDE)]
    tail = tile[:, :REST]
    for at in range(1, 4):
        tail = jnp.where(lax.rem(me, 4) == at, tile[:, at * REST : (at + 1) * REST], tail)
    out_ref[depth:, :] = pack_tail(tail)


def layout_kernel(grid_ref, gain_ref, bias_ref, token_ref, select_ref, keys_ref, live_ref, gain_out, bias_out):
    del token_ref
    rows_n, cols_n = grid_ref[0, 0], grid_ref[0, 1]
    patches = select_ref.shape[0]
    groups = patches // 4
    half = cols_n // 2
    count = (rows_n // 2) * half
    slots = lax.broadcasted_iota(jnp.int32, (groups, 1), 0)
    line = jnp.floor((slots.astype(F32) + 0.5) / half.astype(F32)).astype(jnp.int32)
    first = 2 * line * cols_n + 2 * (slots - line * half)
    at = lax.broadcasted_iota(jnp.int32, (groups, patches), 1)
    for corner in range(4):
        wanted = jnp.where(slots < count, first + (corner // 2) * cols_n + corner % 2, -1)
        select_ref[corner * groups : (corner + 1) * groups, :] = jnp.where(at == wanted, 1.0, 0.0).astype(BF16)
    key = lax.broadcasted_iota(jnp.int32, keys_ref.shape, 1)
    keys_ref[...] = jnp.where(key < rows_n * cols_n, 0.0, -1e30)
    slot = lax.broadcasted_iota(jnp.int32, live_ref.shape, 1)
    live_ref[...] = jnp.where(slot < count, 1.0, 0.0)
    gain_out[...] = gain_ref[...]
    bias_out[...] = bias_ref[...]


def attend_kernel(select_ref, dead_ref, *rest):
    blocks = rest[:ROWS]
    out_ref, q_all, k_all, v_all = rest[ROWS:]
    me = row_index()
    band = blocks[0].shape[0]
    patches = band * ROWS
    for step in range(ROWS):
        at = pl.ds(pl.multiple_of((me ^ step) * band, band), band)
        q_all[at, :] = blocks[step][:, :HPAIR]
        k_all[at, :] = blocks[step][:, HPAIR : 2 * HPAIR]
        v_all[at, :] = blocks[step][:, 2 * HPAIR : 3 * HPAIR]
    queries = jnp.dot(select_ref[...], q_all[...], preferred_element_type=F32).astype(BF16)
    lane = lax.broadcasted_iota(jnp.int32, (1, HPAIR), 1)
    keys, values, dead = k_all[...], v_all[...], dead_ref[...]
    mixed = []
    for head in range(2):
        mine = (lane >= head * HDIM) & (lane < (head + 1) * HDIM)
        asked = jnp.where(mine, queries, jnp.zeros_like(queries))
        scores = lax.dot_general(asked, keys, (((1,), (1,)), ((), ())), preferred_element_type=F32) + dead
        weights = jnp.exp2((scores - jnp.max(scores, axis=1, keepdims=True)) * ROOT)
        total = jnp.sum(weights, axis=1, keepdims=True)
        mixed.append(jnp.dot(weights.astype(BF16), values, preferred_element_type=F32) / total)
    attn = jnp.where(lane < HDIM, mixed[0], mixed[1])
    out_ref[:patches, :] = attn[:, :WIDE].astype(BF16)
    out_ref[patches:, :] = pack_tail(attn[:, WIDE:]).astype(BF16)


def ready_kernel(select_ref, token_ref, *rest):
    del token_ref
    blocks, slices = rest[:ROWS], rest[ROWS : ROWS + PAGES]
    resid_ref, main_ref, tail_ref, held = rest[ROWS + PAGES :]
    me = row_index()
    page = lax.axis_index("page")
    band = blocks[0].shape[0]
    for step in range(ROWS):
        at = pl.ds(pl.multiple_of((me ^ step) * band, band), band)
        held[at, :] = blocks[step][:, 3 * HPAIR :]
    resid_ref[...] = jnp.dot(select_ref[...], held[...], preferred_element_type=F32)
    tail_ref[...] = jnp.zeros_like(tail_ref)
    depth = 2 * HPAIR
    for step in range(PAGES):
        source = lax.rem(page + PAGES - step, PAGES)
        packed = slices[step][depth:]
        tail = jnp.concatenate([packed[:, at * REST : (at + 1) * REST] for at in range(4)], axis=0)
        whole = jnp.concatenate([slices[step][:depth], tail], axis=1)
        for core in range(2):
            pair = 2 * source + core
            rows = whole[core * HPAIR : (core + 1) * HPAIR]
            main_ref[pl.ds(pl.multiple_of(pair * WIDE, WIDE), WIDE), :] = rows[:WIDE]
            for corner in range(4):
                spot = pl.multiple_of(pair * WIDE + corner * REST, REST)
                tail_ref[corner, pl.ds(spot, REST), :] = rows[WIDE:]


def collect(pieces, full):
    me = row_index()
    for step in range(ROWS):
        full[:, pl.ds(pl.multiple_of((me ^ step) * WIDE, WIDE), WIDE)] = pieces[step][...]


def project_kernel(*rest):
    pieces = rest[:ROWS]
    main_ref, tail_ref, resid_ref, out_ref, full = rest[ROWS:]
    collect(pieces, full)
    patches = resid_ref.shape[0]
    groups = patches // 4
    hidden = jnp.dot(full[:patches], main_ref[...], preferred_element_type=F32) + resid_ref[...]
    ends = []
    for corner in range(4):
        span = slice(corner * groups, (corner + 1) * groups)
        part = hidden[span] + jnp.dot(full[patches:], tail_ref[corner], preferred_element_type=F32)
        out_ref[span, :] = part[:, :WIDE].astype(BF16)
        ends.append(part[:, WIDE:])
    out_ref[patches:, :] = jnp.concatenate(ends, axis=1).astype(BF16)


def tail_kernel(weight_ref, token_ref, out_ref):
    del token_ref
    for pair in range(ROWS):
        cut = [corner * D + MAIN + pair * REST for corner in range(4)]
        out_ref[:, pair * WIDE : (pair + 1) * WIDE] = jnp.concatenate(
            [weight_ref[:, at : at + REST] for at in cut], axis=1
        )


def merge_kernel(*rest):
    pieces = rest[:ROWS]
    weight_ref, tail_ref, gain_ref, bias_ref, live_ref, out_ref, full = rest[ROWS:]
    collect(pieces, full)
    groups = live_ref.shape[1]
    patches = 4 * groups
    gain = gain_ref[...]
    ends = full[patches:].astype(F32)
    squares = ends * ends
    folded = squares[:, :WIDE]
    for pair in range(1, ROWS):
        folded = folded + squares[:, pair * WIDE : (pair + 1) * WIDE]
    lane = lax.broadcasted_iota(jnp.int32, (1, WIDE), 1)
    contract = (((1,), (1,)), ((), ()))
    total = jnp.zeros((weight_ref.shape[0], groups), F32)
    spread = jnp.zeros((groups, WIDE), F32)
    for corner in range(4):
        mine = (lane >= corner * REST) & (lane < (corner + 1) * REST)
        rows = full[corner * groups : (corner + 1) * groups].astype(F32)
        square = jnp.sum(rows * rows, axis=1, keepdims=True)
        square = square + jnp.sum(jnp.where(mine, folded, 0.0), axis=1, keepdims=True)
        scale = lax.rsqrt(square * (1.0 / D) + 1e-06)
        spread = jnp.where(mine, scale, spread)
        normed = (rows * scale * gain[:, :MAIN]).astype(BF16)
        total = total + lax.dot_general(
            weight_ref[:, corner * D : corner * D + MAIN], normed, contract, preferred_element_type=F32
        )
    normed = []
    for pair in range(ROWS):
        piece = gain[:, MAIN + pair * REST : MAIN + (pair + 1) * REST]
        piece = jnp.concatenate([piece] * 4, axis=1)
        normed.append((ends[:, pair * WIDE : (pair + 1) * WIDE] * spread * piece).astype(BF16))
    total = total + lax.dot_general(
        tail_ref[...], jnp.concatenate(normed, axis=1), contract, preferred_element_type=F32
    )
    total = total + bias_ref[...]
    merged = 0.5 * total * (1.0 + lax.erf(total * math.sqrt(0.5)))
    out_ref[0] = jnp.where(live_ref[...] > 0.0, merged, 0.0).astype(BF16)


def kernel(body, name, out_shape, scratch=(), first="vmem", tokens=(), count=0, limit=24, flops=0, moved=0):
    spaces = {"vmem": pltpu.VMEM, "smem": pltpu.SMEM, "any": pl.ANY}
    specs = [pl.BlockSpec(memory_space=pltpu.VMEM) for _ in range(count)]
    specs[0] = pl.BlockSpec(memory_space=spaces[first])
    for at in tokens:
        specs[at] = pl.BlockSpec(memory_space=pl.ANY)
    return pl.pallas_call(
        body,
        out_shape=out_shape,
        in_specs=specs,
        out_specs=jax.tree.map(lambda _: pl.BlockSpec(memory_space=pltpu.VMEM), out_shape),
        scratch_shapes=list(scratch),
        compiler_params=pltpu.CompilerParams(vmem_limit_bytes=limit * 1024 * 1024),
        cost_estimate=pl.CostEstimate(flops=flops, bytes_accessed=moved, transcendentals=0),
        name=name,
    )


def shape(*dims, dtype=BF16):
    return jax.ShapeDtypeStruct(dims, dtype)


def swap(value, step):
    return lax.ppermute(value, "row", [(row, row ^ step) for row in range(ROWS)])


def gather_rows(value):
    far = [swap(value, step) for step in (6, 2, 4)]
    near = [swap(piece, 1) for piece in [value] + far]
    return [value, near[0], far[1], near[2], far[2], near[3], far[0], near[1]]


def local_eight(qkv_rows, residual, out_weight, norm_gain, merge_weight, merge_bias, page_grid):
    band = qkv_rows.shape[1]
    patches = band * ROWS
    groups = patches // 4
    units = merge_weight.shape[0]
    depth = out_weight.shape[0]
    piece = shape(patches + groups, WIDE)
    assembled = pltpu.VMEM((patches + groups, MAIN), BF16)

    sends = kernel(
        spread_kernel,
        "spread",
        [shape(band, 4 * HPAIR)] * ROWS,
        [pltpu.VMEM((ROWS, band, 4 * HPAIR), BF16)],
        count=2,
        moved=1 << 20,
    )(qkv_rows, residual)
    blocks = [None] * ROWS
    blocks[0] = sends[0]
    for step in (6, 7, 2, 4, 3, 5, 1):
        blocks[step] = swap(sends[step], step)
    own = kernel(slice_kernel, "weight_slice", shape(depth + depth // 4, WIDE), tokens=(1,), count=2, moved=1 << 20)(
        out_weight, sends[0]
    )
    slices = [own]
    for _ in range(PAGES - 1):
        slices.append(lax.ppermute(slices[-1], "page", [(page, (page + 1) % PAGES) for page in range(PAGES)]))
    select, dead, live, gain, bias = kernel(
        layout_kernel,
        "layout",
        [
            shape(patches, patches),
            shape(1, patches, dtype=F32),
            shape(1, groups, dtype=F32),
            shape(1, D, dtype=F32),
            shape(units, 1, dtype=F32),
        ],
        first="smem",
        tokens=(3,),
        count=4,
        moved=1 << 20,
    )(page_grid, norm_gain.reshape(1, D), merge_bias.reshape(units, 1), sends[0])
    attn = kernel(
        attend_kernel,
        "attend",
        piece,
        [pltpu.VMEM((patches, HPAIR), BF16)] * 3,
        count=2 + ROWS,
        flops=6 * patches * patches * 256,
        moved=1 << 20,
    )(select, dead, *blocks)
    resid, main, tail = kernel(
        ready_kernel,
        "ready",
        [shape(patches, HPAIR, dtype=F32), shape(MAIN, HPAIR), shape(4, MAIN, HPAIR)],
        [pltpu.VMEM((patches, HPAIR), BF16)],
        tokens=(1,),
        count=2 + ROWS + PAGES,
        flops=2 * patches * patches * 256,
        moved=4 << 20,
    )(select, attn, *blocks, *slices)
    hidden = kernel(
        project_kernel,
        "project",
        piece,
        [assembled],
        count=ROWS + 3,
        flops=4 * patches * MAIN * 256,
        moved=4 << 20,
    )(*gather_rows(attn), main, tail, resid)
    ends = kernel(tail_kernel, "merge_tail", shape(units, MAIN), tokens=(1,), count=2, moved=4 << 20)(merge_weight, hidden)
    return kernel(
        merge_kernel,
        "merge",
        shape(1, units, groups),
        [assembled],
        count=ROWS + 5,
        flops=10 * units * groups * MAIN,
        moved=8 << 20,
    )(*gather_rows(hidden), merge_weight, ends, gain, bias, live)


def solution(mesh):
    in_specs = (
        P("page", "row", None),
        P("page", "row", None),
        P("page", None),
        P(),
        P("row", None),
        P("row"),
        P("page", None),
    )
    out_specs = P("page", "row", None)
    local = local_eight if mesh.shape["row"] == 8 and mesh.shape["page"] == 4 else local_any
    return jax.shard_map(local, mesh=mesh, in_specs=in_specs, out_specs=out_specs, check_vma=False)
```

```python
import functools
import math

import jax
import jax.numpy as jnp
from jax import lax
from jax.experimental import pallas as pl
from jax.experimental.pallas import tpu as pltpu
from jax.sharding import PartitionSpec as P

D = 1280
HEADS = 16
HDIM = 80


def local_any(qkv_rows, residual, out_weight, norm_gain, merge_weight, merge_bias, page_grid):
    row_count = lax.axis_size("row")
    q_split = max(1, row_count // HEADS)
    head_groups = row_count // q_split
    width = D // head_groups
    heads_per = width // HDIM
    band_len = qkv_rows.shape[1]
    part_len = band_len // q_split
    local_qkv = qkv_rows[0]
    queries = local_qkv[:, :D]
    key_vals = jnp.concatenate(
        [
            local_qkv[:, D : 2 * D].reshape(band_len, head_groups, width),
            local_qkv[:, 2 * D :].reshape(band_len, head_groups, width),
        ],
        axis=2,
    )
    q_send = (
        queries.reshape(q_split, part_len, head_groups, width)
        .transpose(2, 0, 1, 3)
        .reshape(row_count, part_len, width)
    )
    kv_send = jnp.broadcast_to(
        key_vals.transpose(1, 0, 2)[:, None], (head_groups, q_split, band_len, 2 * width)
    )
    kv_send = kv_send.reshape(row_count, band_len, 2 * width)
    q_recv, kv_recv = (
        lax.all_to_all(q_send, "row", split_axis=0, concat_axis=1, tiled=True),
        lax.all_to_all(kv_send, "row", split_axis=0, concat_axis=1, tiled=True),
    )
    kv_local = kv_recv[0]
    positions = jnp.arange(row_count * band_len, dtype=jnp.int32)
    valid_len = page_grid[0, 0] * page_grid[0, 1]
    key_valid = positions < valid_len
    key_total = kv_local.shape[0]
    key_heads = kv_local[:, :width].reshape(key_total, heads_per, HDIM)
    value_heads = kv_local[:, width:].reshape(key_total, heads_per, HDIM)
    query_total = row_count * part_len
    q_block = math.gcd(query_total, 512)
    q_blocks = q_recv[0].reshape(query_total // q_block, q_block, heads_per, HDIM)
    root_dim = math.sqrt(HDIM)

    def attend(q_span):
        scores = (
            jnp.einsum("qhd,khd->hqk", q_span, key_heads, preferred_element_type=jnp.float32)
            / root_dim
        )
        scores = jnp.where(key_valid[None, None, :], scores, -1e30)
        peak = jnp.max(scores, axis=2, keepdims=True)
        weights = jnp.exp(scores - peak)
        total = jnp.sum(weights, axis=2, keepdims=True)
        mixed = (
            jnp.einsum(
                "hqk,khd->hqd",
                weights.astype(jnp.bfloat16),
                value_heads,
                preferred_element_type=jnp.float32,
            )
            / total
        )
        return mixed.transpose(1, 0, 2).reshape(q_span.shape[0], width).astype(jnp.bfloat16)

    attn_heads = lax.map(attend, q_blocks).reshape(row_count, part_len, width)
    returned = lax.all_to_all(attn_heads, "row", split_axis=0, concat_axis=0, tiled=True)
    attn = (
        returned.reshape(head_groups, q_split, part_len, width)
        .transpose(1, 2, 0, 3)
        .reshape(band_len, D)
    )
    projected = jnp.dot(
        attn,
        lax.all_gather(out_weight, "page", axis=0, tiled=True),
        preferred_element_type=jnp.float32,
    )
    hidden = residual[0].astype(jnp.float32) + projected
    normed = (
        hidden * lax.rsqrt(jnp.mean(hidden * hidden, axis=1, keepdims=True) + 1e-06) * norm_gain
    ).astype(jnp.bfloat16)
    rows_n = page_grid[0, 0]
    cols_n = page_grid[0, 1]
    group_total = band_len * row_count // 4
    slots = jnp.arange(group_total, dtype=jnp.int32)
    half_cols = cols_n // 2
    live = slots < rows_n // 2 * half_cols
    first = jnp.where(live, 2 * (slots // half_cols) * cols_n + 2 * (slots % half_cols), 0)
    corners = [first, first + 1, first + cols_n, first + cols_n + 1]
    local_units = merge_weight.shape[0]
    page_all = lax.all_gather(normed, "row", axis=0, tiled=True)
    merged_sum = jnp.zeros((local_units, group_total), jnp.float32)
    for corner in range(4):
        picked = jnp.take(page_all, corners[corner], axis=0)
        merged_sum = merged_sum + jnp.einsum(
            "md,gd->mg",
            merge_weight[:, corner * D : (corner + 1) * D],
            picked,
            preferred_element_type=jnp.float32,
        )
    merged = jax.nn.gelu(merged_sum + merge_bias[:, None], approximate=False)
    merged = jnp.where(live[None, :], merged, 0.0).astype(jnp.bfloat16)
    return merged[None]


ROWS = 8
PAGES = 4
HPAIR = 2 * HDIM
WIDE = 128
REST = HPAIR - WIDE
MAIN = ROWS * WIDE
NOTES = 16
ROOT = math.log2(math.e) / math.sqrt(HDIM)
BF16 = jnp.bfloat16
F32 = jnp.float32


def row_index():
    return lax.axis_index("row")


def pack_tail(wide):
    groups = wide.shape[0] // 4
    return jnp.concatenate([wide[at * groups : (at + 1) * groups] for at in range(4)], axis=1)


def spread_kernel(qkv_hbm, resid_hbm, weight_hbm, grid_hbm, *rest):
    outs = rest[:ROWS]
    slice_ref, grid_out, qkv, resid, tile, held, grid, sems = rest[ROWS:]
    me = row_index()
    depth = weight_hbm.shape[0]
    main = pl.ds(pl.multiple_of(me * WIDE, WIDE), WIDE)
    ends = pl.ds(pl.multiple_of(MAIN + me // 4 * WIDE, WIDE), WIDE)
    copies = [
        pltpu.make_async_copy(qkv_hbm.at[0], qkv, sems.at[0]),
        pltpu.make_async_copy(resid_hbm.at[0], resid, sems.at[1]),
        pltpu.make_async_copy(weight_hbm.at[:, main], slice_ref.at[:depth], sems.at[2]),
        pltpu.make_async_copy(weight_hbm.at[:, ends], tile, sems.at[3]),
        pltpu.make_async_copy(grid_hbm, grid, sems.at[4]),
    ]
    for copy in copies:
        copy.start()
    for copy in copies:
        copy.wait()
    for dest in range(ROWS):
        at = dest * HPAIR
        parts = [qkv[:, part * D + at : part * D + at + HPAIR] for part in range(3)]
        parts.append(resid[:, dest * WIDE : (dest + 1) * WIDE])
        parts.append(resid[:, MAIN + dest * REST : MAIN + (dest + 1) * REST])
        held[dest] = jnp.concatenate(parts, axis=1)
    for step in range(ROWS):
        outs[step][...] = held[me ^ step]
    tail = tile[:, :REST]
    for at in range(1, 4):
        tail = jnp.where(lax.rem(me, 4) == at, tile[:, at * REST : (at + 1) * REST], tail)
    slice_ref[depth:, :] = pack_tail(tail)
    row = lax.broadcasted_iota(jnp.int32, grid_out.shape, 0)
    grid_out[...] = jnp.where(row == 0, grid[0, 0], grid[0, 1])


def layout_kernel(grid_ref, gain_ref, bias_ref, early_ref, select_ref, keys_ref, live_ref, gain_out, bias_out):
    del early_ref
    rows_n, cols_n = grid_ref[:1, :1], grid_ref[1:2, :1]
    patches = select_ref.shape[0]
    groups = patches // 4
    half = cols_n >> 1
    count = (rows_n >> 1) * half
    slots = lax.broadcasted_iota(jnp.int32, (groups, 1), 0)
    line = jnp.floor((slots.astype(F32) + 0.5) / half.astype(F32)).astype(jnp.int32)
    first = 2 * line * cols_n + 2 * (slots - line * half)
    at = lax.broadcasted_iota(jnp.int32, (groups, patches), 1)
    for corner in range(4):
        wanted = jnp.where(slots < count, first + (corner // 2) * cols_n + corner % 2, -1)
        select_ref[corner * groups : (corner + 1) * groups, :] = jnp.where(at == wanted, 1.0, 0.0).astype(BF16)
    key = lax.broadcasted_iota(jnp.int32, keys_ref.shape, 1)
    keys_ref[...] = jnp.where(key < rows_n * cols_n, 0.0, -1e30)
    slot = lax.broadcasted_iota(jnp.int32, live_ref.shape, 1)
    live_ref[...] = jnp.where(slot < count, 1.0, 0.0)
    gain_out[...] = gain_ref[...].reshape(gain_out.shape)
    bias = jnp.broadcast_to(bias_ref[...].reshape(1, bias_out.shape[0]), (8, bias_out.shape[0]))
    bias_out[...] = bias.T[:, :1]


def attend_kernel(select_ref, dead_ref, *rest):
    blocks = rest[:ROWS]
    out_ref, q_all, k_all, v_all = rest[ROWS:]
    me = row_index()
    band = blocks[0].shape[0]
    patches = band * ROWS
    for step in range(ROWS):
        at = pl.ds(pl.multiple_of((me ^ step) * band, band), band)
        q_all[at, :] = blocks[step][:, :HPAIR]
        k_all[at, :] = blocks[step][:, HPAIR : 2 * HPAIR]
        v_all[at, :] = blocks[step][:, 2 * HPAIR : 3 * HPAIR]
    queries = jnp.dot(select_ref[...], q_all[...], preferred_element_type=F32).astype(BF16)
    lane = lax.broadcasted_iota(jnp.int32, (1, HPAIR), 1)
    keys, values, dead = k_all[...], v_all[...], dead_ref[...]
    mixed = []
    for head in range(2):
        mine = (lane >= head * HDIM) & (lane < (head + 1) * HDIM)
        asked = jnp.where(mine, queries, jnp.zeros_like(queries))
        scores = lax.dot_general(asked, keys, (((1,), (1,)), ((), ())), preferred_element_type=F32) + dead
        weights = jnp.exp2((scores - jnp.max(scores, axis=1, keepdims=True)) * ROOT)
        total = jnp.sum(weights, axis=1, keepdims=True)
        mixed.append(jnp.dot(weights.astype(BF16), values, preferred_element_type=F32) / total)
    attn = jnp.where(lane < HDIM, mixed[0], mixed[1])
    out_ref[:patches, :] = attn[:, :WIDE].astype(BF16)
    out_ref[patches:, :] = pack_tail(attn[:, WIDE:]).astype(BF16)


def ready_kernel(select_ref, gain_ref, token_ref, *rest):
    del token_ref
    blocks, slices = rest[:ROWS], rest[ROWS : ROWS + PAGES]
    resid_ref, gain_out, main_ref, tail_ref, held = rest[ROWS + PAGES :]
    me = row_index()
    page = lax.axis_index("page")
    band = blocks[0].shape[0]
    for step in range(ROWS):
        at = pl.ds(pl.multiple_of((me ^ step) * band, band), band)
        held[at, :] = blocks[step][:, 3 * HPAIR :]
    resid_ref[...] = jnp.dot(select_ref[...], held[...], preferred_element_type=F32)
    gain = jnp.zeros(gain_out.shape, F32)
    for pair in range(ROWS):
        parts = [gain_ref[:, pair * WIDE : (pair + 1) * WIDE]]
        parts.append(gain_ref[:, MAIN + pair * REST : MAIN + (pair + 1) * REST])
        gain = jnp.where(me == pair, jnp.concatenate(parts, axis=1), gain)
    gain_out[...] = gain
    tail_ref[...] = jnp.zeros_like(tail_ref)
    depth = 2 * HPAIR
    for step in range(PAGES):
        source = lax.rem(page + PAGES - step, PAGES)
        packed = slices[step][depth:]
        tail = jnp.concatenate([packed[:, at * REST : (at + 1) * REST] for at in range(4)], axis=0)
        whole = jnp.concatenate([slices[step][:depth], tail], axis=1)
        for core in range(2):
            pair = 2 * source + core
            rows = whole[core * HPAIR : (core + 1) * HPAIR]
            main_ref[pl.ds(pl.multiple_of(pair * WIDE, WIDE), WIDE), :] = rows[:WIDE]
            for corner in range(4):
                spot = pl.multiple_of(pair * WIDE + corner * REST, REST)
                tail_ref[corner, pl.ds(spot, REST), :] = rows[WIDE:]


def collect(pieces, full):
    me = row_index()
    for step in range(ROWS):
        full[:, pl.ds(pl.multiple_of((me ^ step) * WIDE, WIDE), WIDE)] = pieces[step][...]


def project_kernel(*rest):
    pieces = rest[:ROWS]
    main_ref, tail_ref, resid_ref, gain_ref, out_ref, full = rest[ROWS:]
    collect(pieces, full)
    patches = resid_ref.shape[0]
    groups = patches // 4
    base = jnp.dot(full[:patches], main_ref[...], preferred_element_type=F32) + resid_ref[...]
    ones = jnp.ones((NOTES, HPAIR), BF16)
    contract = (((1,), (1,)), ((), ()))
    row = lax.broadcasted_iota(jnp.int32, (NOTES, groups), 0)
    notes = jnp.zeros((NOTES, groups), F32)
    ends = []
    for corner in range(4):
        span = slice(corner * groups, (corner + 1) * groups)
        hidden = base[span] + jnp.dot(full[patches:], tail_ref[corner], preferred_element_type=F32)
        square = hidden * hidden
        high = square.astype(BF16)
        low = (square - high.astype(F32)).astype(BF16)
        total = lax.dot_general(ones, high, contract, preferred_element_type=F32)
        total = total + lax.dot_general(ones, low, contract, preferred_element_type=F32)
        coarse = total.astype(BF16).astype(F32)
        notes = jnp.where(row == corner, coarse, jnp.where(row == 4 + corner, total - coarse, notes))
        sent = hidden * gain_ref[...]
        out_ref[span, :] = sent[:, :WIDE].astype(BF16)
        ends.append(sent[:, WIDE:])
    out_ref[patches : patches + groups, :] = jnp.concatenate(ends, axis=1).astype(BF16)
    out_ref[patches + groups :, :] = notes.astype(BF16)


def tail_kernel(weight_ref, token_ref, out_ref):
    del token_ref
    for pair in range(ROWS):
        cut = [corner * D + MAIN + pair * REST for corner in range(4)]
        out_ref[:, pair * WIDE : (pair + 1) * WIDE] = jnp.concatenate(
            [weight_ref[:, at : at + REST] for at in cut], axis=1
        )


def merge_kernel(*rest):
    pieces = rest[:ROWS]
    weight_ref, tail_ref, bias_ref, live_ref, out_ref, full = rest[ROWS:]
    collect(pieces, full)
    groups = live_ref.shape[1]
    patches = 4 * groups
    notes = jnp.zeros((NOTES, groups), F32)
    for step in range(ROWS):
        notes = notes + pieces[step][patches + groups :].astype(F32)
    scale = lax.rsqrt((notes[:4] + notes[4:8]) * (1.0 / D) + 1e-06)
    contract = (((1,), (1,)), ((), ()))
    total = jnp.zeros((weight_ref.shape[0], groups), F32)
    for corner in range(4):
        total = total + scale[corner : corner + 1] * lax.dot_general(
            weight_ref[:, corner * D : corner * D + MAIN],
            full[corner * groups : (corner + 1) * groups],
            contract,
            preferred_element_type=F32,
        )
    spread = jnp.concatenate([jnp.broadcast_to(scale[at : at + 1], (REST, groups)) for at in range(4)], axis=0).T
    ends = full[patches : patches + groups].astype(F32) * jnp.concatenate([spread] * ROWS, axis=1)
    total = total + lax.dot_general(tail_ref[...], ends.astype(BF16), contract, preferred_element_type=F32)
    total = total + bias_ref[...]
    merged = 0.5 * total * (1.0 + lax.erf(total * math.sqrt(0.5)))
    out_ref[0] = jnp.where(live_ref[...] > 0.0, merged, 0.0).astype(BF16)


def kernel(body, name, out_shape, scratch=(), fetched=(), count=0, limit=24, flops=0, moved=0):
    specs = [pl.BlockSpec(memory_space=pltpu.VMEM) for _ in range(count)]
    for at in fetched:
        specs[at] = pl.BlockSpec(memory_space=pl.ANY)
    return pl.pallas_call(
        body,
        out_shape=out_shape,
        in_specs=specs,
        out_specs=jax.tree.map(lambda _: pl.BlockSpec(memory_space=pltpu.VMEM), out_shape),
        scratch_shapes=list(scratch),
        compiler_params=pltpu.CompilerParams(vmem_limit_bytes=limit * 1024 * 1024),
        cost_estimate=pl.CostEstimate(flops=flops, bytes_accessed=moved, transcendentals=0),
        name=name,
    )


def shape(*dims, dtype=BF16):
    return jax.ShapeDtypeStruct(dims, dtype)


def swap(value, step):
    return lax.ppermute(value, "row", [(row, row ^ step) for row in range(ROWS)])


def turn(value, step):
    return lax.ppermute(value, "page", [(page, (page + step) % PAGES) for page in range(PAGES)])


def gather_rows(value):
    far = [swap(value, step) for step in (6, 2, 4)]
    near = [swap(piece, 1) for piece in [value] + far]
    return [value, near[0], far[1], near[2], far[2], near[3], far[0], near[1]]


def local_eight(qkv_rows, residual, out_weight, norm_gain, merge_weight, merge_bias, page_grid):
    band = qkv_rows.shape[1]
    patches = band * ROWS
    groups = patches // 4
    units = merge_weight.shape[0]
    depth = out_weight.shape[0]
    piece = patches + groups

    *sends, own, grid = kernel(
        spread_kernel,
        "spread",
        [shape(band, 4 * HPAIR)] * ROWS + [shape(depth + depth // 4, WIDE), shape(8, WIDE, dtype=jnp.int32)],
        [
            pltpu.VMEM((band, 3 * D), BF16),
            pltpu.VMEM((band, D), BF16),
            pltpu.VMEM((depth, WIDE), BF16),
            pltpu.VMEM((ROWS, band, 4 * HPAIR), BF16),
            pltpu.SMEM(page_grid.shape, jnp.int32),
            pltpu.SemaphoreType.DMA((5,)),
        ],
        fetched=range(4),
        count=4,
        limit=24,
        moved=1 << 20,
    )(*[pltpu.with_memory_space_constraint(value, pltpu.HBM) for value in (qkv_rows, residual, out_weight, page_grid)])
    blocks = [sends[0]] + [swap(sends[step], step) for step in range(1, ROWS)]
    slices = [own] + [turn(own, step) for step in range(1, PAGES)]
    select, dead, live, gain, bias = kernel(
        layout_kernel,
        "layout",
        [
            shape(patches, patches),
            shape(1, patches, dtype=F32),
            shape(1, groups, dtype=F32),
            shape(1, D, dtype=F32),
            shape(units, 1, dtype=F32),
        ],
        fetched=(3,),
        count=4,
        moved=1 << 20,
    )(grid, norm_gain, merge_bias, blocks[4])
    attn = kernel(
        attend_kernel,
        "attend",
        shape(piece, WIDE),
        [pltpu.VMEM((patches, HPAIR), BF16)] * 3,
        count=2 + ROWS,
        flops=20 * patches * patches * 4096,
        moved=1 << 20,
    )(select, dead, *blocks)
    resid, own_gain, main, tail = kernel(
        ready_kernel,
        "ready",
        [shape(patches, HPAIR, dtype=F32), shape(1, HPAIR, dtype=F32), shape(MAIN, HPAIR), shape(4, MAIN, HPAIR)],
        [pltpu.VMEM((patches, HPAIR), BF16)],
        fetched=(2,),
        count=3 + ROWS + PAGES,
        flops=10 * patches * patches * 4096,
        moved=4 << 20,
    )(select, gain, attn, *blocks, *slices)
    hidden = kernel(
        project_kernel,
        "project",
        shape(piece + NOTES, WIDE),
        [pltpu.VMEM((piece, MAIN), BF16)],
        count=ROWS + 4,
        flops=4 * patches * MAIN * 256,
        moved=4 << 20,
    )(*gather_rows(attn), main, tail, resid, own_gain)
    ends = kernel(tail_kernel, "merge_tail", shape(units, MAIN), fetched=(1,), count=2, moved=4 << 20)(
        merge_weight, hidden
    )
    return kernel(
        merge_kernel,
        "merge",
        shape(1, units, groups),
        [pltpu.VMEM((piece + NOTES, MAIN), BF16)],
        count=ROWS + 4,
        flops=10 * units * groups * MAIN,
        moved=8 << 20,
    )(*gather_rows(hidden), merge_weight, ends, bias, live)


def solution(mesh):
    in_specs = (
        P("page", "row", None),
        P("page", "row", None),
        P("page", None),
        P(),
        P("row", None),
        P("row"),
        P("page", None),
    )
    out_specs = P("page", "row", None)
    local = local_eight if mesh.shape["row"] == 8 and mesh.shape["page"] == 4 else local_any
    return jax.shard_map(local, mesh=mesh, in_specs=in_specs, out_specs=out_specs, check_vma=False)
```

```python
import functools
import math

import jax
import jax.numpy as jnp
from jax import lax
from jax.experimental import pallas as pl
from jax.experimental.pallas import tpu as pltpu
from jax.sharding import PartitionSpec as P

D = 1280
HEADS = 16
HDIM = 80


def local_any(qkv_rows, residual, out_weight, norm_gain, merge_weight, merge_bias, page_grid):
    row_count = lax.axis_size("row")
    q_split = max(1, row_count // HEADS)
    head_groups = row_count // q_split
    width = D // head_groups
    heads_per = width // HDIM
    band_len = qkv_rows.shape[1]
    part_len = band_len // q_split
    local_qkv = qkv_rows[0]
    queries = local_qkv[:, :D]
    key_vals = jnp.concatenate(
        [
            local_qkv[:, D : 2 * D].reshape(band_len, head_groups, width),
            local_qkv[:, 2 * D :].reshape(band_len, head_groups, width),
        ],
        axis=2,
    )
    q_send = (
        queries.reshape(q_split, part_len, head_groups, width)
        .transpose(2, 0, 1, 3)
        .reshape(row_count, part_len, width)
    )
    kv_send = jnp.broadcast_to(
        key_vals.transpose(1, 0, 2)[:, None], (head_groups, q_split, band_len, 2 * width)
    )
    kv_send = kv_send.reshape(row_count, band_len, 2 * width)
    q_recv, kv_recv = (
        lax.all_to_all(q_send, "row", split_axis=0, concat_axis=1, tiled=True),
        lax.all_to_all(kv_send, "row", split_axis=0, concat_axis=1, tiled=True),
    )
    kv_local = kv_recv[0]
    positions = jnp.arange(row_count * band_len, dtype=jnp.int32)
    valid_len = page_grid[0, 0] * page_grid[0, 1]
    key_valid = positions < valid_len
    key_total = kv_local.shape[0]
    key_heads = kv_local[:, :width].reshape(key_total, heads_per, HDIM)
    value_heads = kv_local[:, width:].reshape(key_total, heads_per, HDIM)
    query_total = row_count * part_len
    q_block = math.gcd(query_total, 512)
    q_blocks = q_recv[0].reshape(query_total // q_block, q_block, heads_per, HDIM)
    root_dim = math.sqrt(HDIM)

    def attend(q_span):
        scores = (
            jnp.einsum("qhd,khd->hqk", q_span, key_heads, preferred_element_type=jnp.float32)
            / root_dim
        )
        scores = jnp.where(key_valid[None, None, :], scores, -1e30)
        peak = jnp.max(scores, axis=2, keepdims=True)
        weights = jnp.exp(scores - peak)
        total = jnp.sum(weights, axis=2, keepdims=True)
        mixed = (
            jnp.einsum(
                "hqk,khd->hqd",
                weights.astype(jnp.bfloat16),
                value_heads,
                preferred_element_type=jnp.float32,
            )
            / total
        )
        return mixed.transpose(1, 0, 2).reshape(q_span.shape[0], width).astype(jnp.bfloat16)

    attn_heads = lax.map(attend, q_blocks).reshape(row_count, part_len, width)
    returned = lax.all_to_all(attn_heads, "row", split_axis=0, concat_axis=0, tiled=True)
    attn = (
        returned.reshape(head_groups, q_split, part_len, width)
        .transpose(1, 2, 0, 3)
        .reshape(band_len, D)
    )
    projected = jnp.dot(
        attn,
        lax.all_gather(out_weight, "page", axis=0, tiled=True),
        preferred_element_type=jnp.float32,
    )
    hidden = residual[0].astype(jnp.float32) + projected
    normed = (
        hidden * lax.rsqrt(jnp.mean(hidden * hidden, axis=1, keepdims=True) + 1e-06) * norm_gain
    ).astype(jnp.bfloat16)
    rows_n = page_grid[0, 0]
    cols_n = page_grid[0, 1]
    group_total = band_len * row_count // 4
    slots = jnp.arange(group_total, dtype=jnp.int32)
    half_cols = cols_n // 2
    live = slots < rows_n // 2 * half_cols
    first = jnp.where(live, 2 * (slots // half_cols) * cols_n + 2 * (slots % half_cols), 0)
    corners = [first, first + 1, first + cols_n, first + cols_n + 1]
    local_units = merge_weight.shape[0]
    page_all = lax.all_gather(normed, "row", axis=0, tiled=True)
    merged_sum = jnp.zeros((local_units, group_total), jnp.float32)
    for corner in range(4):
        picked = jnp.take(page_all, corners[corner], axis=0)
        merged_sum = merged_sum + jnp.einsum(
            "md,gd->mg",
            merge_weight[:, corner * D : (corner + 1) * D],
            picked,
            preferred_element_type=jnp.float32,
        )
    merged = jax.nn.gelu(merged_sum + merge_bias[:, None], approximate=False)
    merged = jnp.where(live[None, :], merged, 0.0).astype(jnp.bfloat16)
    return merged[None]


ROWS = 8
PAGES = 4
HPAIR = 2 * HDIM
WIDE = 128
REST = HPAIR - WIDE
MAIN = ROWS * WIDE
NOTES = 16
ROOT = math.log2(math.e) / math.sqrt(HDIM)
BF16 = jnp.bfloat16
F32 = jnp.float32


def row_index():
    return lax.axis_index("row")


def pack_tail(wide):
    groups = wide.shape[0] // 4
    return jnp.concatenate([wide[at * groups : (at + 1) * groups] for at in range(4)], axis=1)


def spread_kernel(qkv_hbm, resid_hbm, weight_hbm, grid_hbm, *rest):
    outs = rest[:ROWS]
    slice_ref, grid_out, qkv, resid, tile, held, grid, sems = rest[ROWS:]
    me = row_index()
    depth = weight_hbm.shape[0]
    main = pl.ds(pl.multiple_of(me * WIDE, WIDE), WIDE)
    ends = pl.ds(pl.multiple_of(MAIN + me // 4 * WIDE, WIDE), WIDE)
    copies = [
        pltpu.make_async_copy(qkv_hbm.at[0], qkv, sems.at[0]),
        pltpu.make_async_copy(resid_hbm.at[0], resid, sems.at[1]),
        pltpu.make_async_copy(weight_hbm.at[:, main], slice_ref.at[:depth], sems.at[2]),
        pltpu.make_async_copy(weight_hbm.at[:, ends], tile, sems.at[3]),
        pltpu.make_async_copy(grid_hbm, grid, sems.at[4]),
    ]
    for copy in copies:
        copy.start()
    for copy in copies:
        copy.wait()
    for dest in range(ROWS):
        at = dest * HPAIR
        parts = [qkv[:, part * D + at : part * D + at + HPAIR] for part in range(3)]
        parts.append(resid[:, dest * WIDE : (dest + 1) * WIDE])
        parts.append(resid[:, MAIN + dest * REST : MAIN + (dest + 1) * REST])
        held[dest] = jnp.concatenate(parts, axis=1)
    for step in range(ROWS):
        outs[step][...] = held[me ^ step]
    tail = tile[:, :REST]
    for at in range(1, 4):
        tail = jnp.where(lax.rem(me, 4) == at, tile[:, at * REST : (at + 1) * REST], tail)
    slice_ref[depth:, :] = pack_tail(tail)
    row = lax.broadcasted_iota(jnp.int32, grid_out.shape, 0)
    grid_out[...] = jnp.where(row == 0, grid[0, 0], grid[0, 1])


def layout_kernel(grid_ref, gain_hbm, bias_hbm, *rest):
    select_ref, keys_ref, live_ref, gain_out, bias_out, gain_ref, bias_ref, sems = rest[-8:]
    fetch_gain = pltpu.make_async_copy(gain_hbm, gain_ref, sems.at[0])
    fetch_bias = pltpu.make_async_copy(bias_hbm, bias_ref, sems.at[1])
    fetch_gain.start()
    fetch_bias.start()
    rows_n, cols_n = grid_ref[:1, :1], grid_ref[1:2, :1]
    patches = select_ref.shape[0]
    groups = patches // 4
    half = cols_n >> 1
    count = (rows_n >> 1) * half
    slots = lax.broadcasted_iota(jnp.int32, (groups, 1), 0)
    line = jnp.floor((slots.astype(F32) + 0.5) / half.astype(F32)).astype(jnp.int32)
    first = 2 * line * cols_n + 2 * (slots - line * half)
    at = lax.broadcasted_iota(jnp.int32, (groups, patches), 1)
    for corner in range(4):
        wanted = jnp.where(slots < count, first + (corner // 2) * cols_n + corner % 2, -1)
        select_ref[corner * groups : (corner + 1) * groups, :] = jnp.where(at == wanted, 1.0, 0.0).astype(BF16)
    key = lax.broadcasted_iota(jnp.int32, keys_ref.shape, 1)
    keys_ref[...] = jnp.where(key < rows_n * cols_n, 0.0, -1e30)
    slot = lax.broadcasted_iota(jnp.int32, live_ref.shape, 1)
    live_ref[...] = jnp.where(slot < count, 1.0, 0.0)
    fetch_gain.wait()
    fetch_bias.wait()
    gain_out[...] = gain_ref[...].reshape(gain_out.shape)
    bias = jnp.broadcast_to(bias_ref[...].reshape(1, bias_out.shape[0]), (8, bias_out.shape[0]))
    bias_out[...] = bias.T[:, :1]


def attend_kernel(select_ref, dead_ref, *rest):
    blocks = rest[:ROWS]
    out_ref, q_all, k_all, v_all = rest[-4:]
    me = row_index()
    band = blocks[0].shape[0]
    patches = band * ROWS
    for step in range(ROWS):
        at = pl.ds(pl.multiple_of((me ^ step) * band, band), band)
        q_all[at, :] = blocks[step][:, :HPAIR]
        k_all[at, :] = blocks[step][:, HPAIR : 2 * HPAIR]
        v_all[at, :] = blocks[step][:, 2 * HPAIR : 3 * HPAIR]
    queries = jnp.dot(select_ref[...], q_all[...], preferred_element_type=F32).astype(BF16)
    lane = lax.broadcasted_iota(jnp.int32, (1, HPAIR), 1)
    keys, values, dead = k_all[...], v_all[...], dead_ref[...]
    mixed = []
    for head in range(2):
        mine = (lane >= head * HDIM) & (lane < (head + 1) * HDIM)
        asked = jnp.where(mine, queries, jnp.zeros_like(queries))
        scores = lax.dot_general(asked, keys, (((1,), (1,)), ((), ())), preferred_element_type=F32) + dead
        weights = jnp.exp2((scores - jnp.max(scores, axis=1, keepdims=True)) * ROOT)
        total = jnp.sum(weights, axis=1, keepdims=True)
        mixed.append(jnp.dot(weights.astype(BF16), values, preferred_element_type=F32) / total)
    attn = jnp.where(lane < HDIM, mixed[0], mixed[1])
    out_ref[:patches, :] = attn[:, :WIDE].astype(BF16)
    out_ref[patches:, :] = pack_tail(attn[:, WIDE:]).astype(BF16)


def ready_kernel(select_ref, gain_ref, token_ref, *rest):
    del token_ref
    blocks, slices = rest[:ROWS], rest[ROWS : ROWS + PAGES]
    resid_ref, gain_out, main_ref, tail_ref, held = rest[ROWS + PAGES :]
    me = row_index()
    page = lax.axis_index("page")
    band = blocks[0].shape[0]
    for step in range(ROWS):
        at = pl.ds(pl.multiple_of((me ^ step) * band, band), band)
        held[at, :] = blocks[step][:, 3 * HPAIR :]
    resid_ref[...] = jnp.dot(select_ref[...], held[...], preferred_element_type=F32)
    gain = jnp.zeros(gain_out.shape, F32)
    for pair in range(ROWS):
        parts = [gain_ref[:, pair * WIDE : (pair + 1) * WIDE]]
        parts.append(gain_ref[:, MAIN + pair * REST : MAIN + (pair + 1) * REST])
        gain = jnp.where(me == pair, jnp.concatenate(parts, axis=1), gain)
    gain_out[...] = gain
    tail_ref[...] = jnp.zeros_like(tail_ref)
    depth = 2 * HPAIR
    for step in range(PAGES):
        source = lax.rem(page + PAGES - step, PAGES)
        packed = slices[step][depth:]
        tail = jnp.concatenate([packed[:, at * REST : (at + 1) * REST] for at in range(4)], axis=0)
        whole = jnp.concatenate([slices[step][:depth], tail], axis=1)
        for core in range(2):
            pair = 2 * source + core
            rows = whole[core * HPAIR : (core + 1) * HPAIR]
            main_ref[pl.ds(pl.multiple_of(pair * WIDE, WIDE), WIDE), :] = rows[:WIDE]
            for corner in range(4):
                spot = pl.multiple_of(pair * WIDE + corner * REST, REST)
                tail_ref[corner, pl.ds(spot, REST), :] = rows[WIDE:]


def collect(pieces, full):
    me = row_index()
    for step in range(ROWS):
        full[:, pl.ds(pl.multiple_of((me ^ step) * WIDE, WIDE), WIDE)] = pieces[step][...]


def project_kernel(*rest):
    pieces = rest[:ROWS]
    main_ref, tail_ref, resid_ref, gain_ref, out_ref, full = rest[ROWS:]
    collect(pieces, full)
    patches = resid_ref.shape[0]
    groups = patches // 4
    base = jnp.dot(full[:patches], main_ref[...], preferred_element_type=F32) + resid_ref[...]
    ones = jnp.ones((NOTES, HPAIR), BF16)
    contract = (((1,), (1,)), ((), ()))
    row = lax.broadcasted_iota(jnp.int32, (NOTES, groups), 0)
    notes = jnp.zeros((NOTES, groups), F32)
    ends = []
    for corner in range(4):
        span = slice(corner * groups, (corner + 1) * groups)
        hidden = base[span] + jnp.dot(full[patches:], tail_ref[corner], preferred_element_type=F32)
        square = hidden * hidden
        high = square.astype(BF16)
        low = (square - high.astype(F32)).astype(BF16)
        total = lax.dot_general(ones, high, contract, preferred_element_type=F32)
        total = total + lax.dot_general(ones, low, contract, preferred_element_type=F32)
        coarse = total.astype(BF16).astype(F32)
        notes = jnp.where(row == corner, coarse, jnp.where(row == 4 + corner, total - coarse, notes))
        sent = hidden * gain_ref[...]
        out_ref[span, :] = sent[:, :WIDE].astype(BF16)
        ends.append(sent[:, WIDE:])
    out_ref[patches : patches + groups, :] = jnp.concatenate(ends, axis=1).astype(BF16)
    out_ref[patches + groups :, :] = notes.astype(BF16)


def tail_kernel(weight_ref, token_ref, out_ref):
    del token_ref
    for pair in range(ROWS):
        cut = [corner * D + MAIN + pair * REST for corner in range(4)]
        out_ref[:, pair * WIDE : (pair + 1) * WIDE] = jnp.concatenate(
            [weight_ref[:, at : at + REST] for at in cut], axis=1
        )


def merge_kernel(*rest):
    pieces = rest[:ROWS]
    weight_ref, tail_ref, bias_ref, live_ref, out_ref, full = rest[ROWS:]
    collect(pieces, full)
    groups = live_ref.shape[1]
    patches = 4 * groups
    notes = jnp.zeros((NOTES, groups), F32)
    for step in range(ROWS):
        notes = notes + pieces[step][patches + groups :].astype(F32)
    scale = lax.rsqrt((notes[:4] + notes[4:8]) * (1.0 / D) + 1e-06)
    contract = (((1,), (1,)), ((), ()))
    total = jnp.zeros((weight_ref.shape[0], groups), F32)
    for corner in range(4):
        total = total + scale[corner : corner + 1] * lax.dot_general(
            weight_ref[:, corner * D : corner * D + MAIN],
            full[corner * groups : (corner + 1) * groups],
            contract,
            preferred_element_type=F32,
        )
    spread = jnp.concatenate([jnp.broadcast_to(scale[at : at + 1], (REST, groups)) for at in range(4)], axis=0).T
    ends = full[patches : patches + groups].astype(F32) * jnp.concatenate([spread] * ROWS, axis=1)
    total = total + lax.dot_general(tail_ref[...], ends.astype(BF16), contract, preferred_element_type=F32)
    total = total + bias_ref[...]
    merged = 0.5 * total * (1.0 + lax.erf(total * math.sqrt(0.5)))
    out_ref[0] = jnp.where(live_ref[...] > 0.0, merged, 0.0).astype(BF16)


def kernel(body, name, out_shape, scratch=(), fetched=(), count=0, limit=24, flops=0, moved=0):
    specs = [pl.BlockSpec(memory_space=pltpu.VMEM) for _ in range(count)]
    for at in fetched:
        specs[at] = pl.BlockSpec(memory_space=pl.ANY)
    return pl.pallas_call(
        body,
        out_shape=out_shape,
        in_specs=specs,
        out_specs=jax.tree.map(lambda _: pl.BlockSpec(memory_space=pltpu.VMEM), out_shape),
        scratch_shapes=list(scratch),
        compiler_params=pltpu.CompilerParams(vmem_limit_bytes=limit * 1024 * 1024),
        cost_estimate=pl.CostEstimate(flops=flops, bytes_accessed=moved, transcendentals=0),
        name=name,
    )


def in_hbm(value):
    return pltpu.with_memory_space_constraint(value, pltpu.HBM)


def shape(*dims, dtype=BF16):
    return jax.ShapeDtypeStruct(dims, dtype)


def swap(value, step):
    return lax.ppermute(value, "row", [(row, row ^ step) for row in range(ROWS)])


def turn(value, step):
    return lax.ppermute(value, "page", [(page, (page + step) % PAGES) for page in range(PAGES)])


def gather_rows(value):
    far = [swap(value, step) for step in (6, 2, 4)]
    near = [swap(piece, 1) for piece in [value] + far]
    return [value, near[0], far[1], near[2], far[2], near[3], far[0], near[1]]


def local_eight(qkv_rows, residual, out_weight, norm_gain, merge_weight, merge_bias, page_grid):
    band = qkv_rows.shape[1]
    patches = band * ROWS
    groups = patches // 4
    units = merge_weight.shape[0]
    depth = out_weight.shape[0]
    piece = patches + groups

    *sends, own, grid = kernel(
        spread_kernel,
        "spread",
        [shape(band, 4 * HPAIR)] * ROWS + [shape(depth + depth // 4, WIDE), shape(8, WIDE, dtype=jnp.int32)],
        [
            pltpu.VMEM((band, 3 * D), BF16),
            pltpu.VMEM((band, D), BF16),
            pltpu.VMEM((depth, WIDE), BF16),
            pltpu.VMEM((ROWS, band, 4 * HPAIR), BF16),
            pltpu.SMEM(page_grid.shape, jnp.int32),
            pltpu.SemaphoreType.DMA((5,)),
        ],
        fetched=range(4),
        count=4,
        limit=24,
        moved=1 << 20,
    )(in_hbm(qkv_rows), in_hbm(residual), in_hbm(out_weight), in_hbm(page_grid))
    blocks = [sends[0]] + [swap(sends[step], step) for step in range(1, ROWS)]
    slices = [own] + [turn(own, step) for step in range(1, PAGES)]
    select, dead, live, gain, bias = kernel(
        layout_kernel,
        "layout",
        [
            shape(patches, patches),
            shape(1, patches, dtype=F32),
            shape(1, groups, dtype=F32),
            shape(1, D, dtype=F32),
            shape(units, 1, dtype=F32),
        ],
        [pltpu.VMEM((D,), F32), pltpu.VMEM((units,), F32), pltpu.SemaphoreType.DMA((2,))],
        fetched=range(1, 3 + 5),
        count=3 + 5,
        moved=1 << 20,
    )(grid, in_hbm(norm_gain), in_hbm(merge_bias), *blocks[1:6])
    early = [slices[1], slices[2]]
    attn = kernel(
        attend_kernel,
        "attend",
        shape(piece, WIDE),
        [pltpu.VMEM((patches, HPAIR), BF16)] * 3,
        fetched=range(2 + ROWS, 2 + ROWS + len(early)),
        count=2 + ROWS + len(early),
        flops=20 * patches * patches * 4096,
        moved=1 << 20,
    )(select, dead, *blocks, *early)
    resid, own_gain, main, tail = kernel(
        ready_kernel,
        "ready",
        [shape(patches, HPAIR, dtype=F32), shape(1, HPAIR, dtype=F32), shape(MAIN, HPAIR), shape(4, MAIN, HPAIR)],
        [pltpu.VMEM((patches, HPAIR), BF16)],
        fetched=(2,),
        count=3 + ROWS + PAGES,
        flops=10 * patches * patches * 4096,
        moved=4 << 20,
    )(select, gain, attn, *blocks, *slices)
    hidden = kernel(
        project_kernel,
        "project",
        shape(piece + NOTES, WIDE),
        [pltpu.VMEM((piece, MAIN), BF16)],
        count=ROWS + 4,
        flops=4 * patches * MAIN * 256,
        moved=4 << 20,
    )(*gather_rows(attn), main, tail, resid, own_gain)
    ends = kernel(tail_kernel, "merge_tail", shape(units, MAIN), fetched=(1,), count=2, moved=4 << 20)(
        merge_weight, hidden
    )
    return kernel(
        merge_kernel,
        "merge",
        shape(1, units, groups),
        [pltpu.VMEM((piece + NOTES, MAIN), BF16)],
        count=ROWS + 4,
        flops=10 * units * groups * MAIN,
        moved=8 << 20,
    )(*gather_rows(hidden), merge_weight, ends, bias, live)


def solution(mesh):
    in_specs = (
        P("page", "row", None),
        P("page", "row", None),
        P("page", None),
        P(),
        P("row", None),
        P("row"),
        P("page", None),
    )
    out_specs = P("page", "row", None)
    local = local_eight if mesh.shape["row"] == 8 and mesh.shape["page"] == 4 else local_any
    return jax.shard_map(local, mesh=mesh, in_specs=in_specs, out_specs=out_specs, check_vma=False)
```

```python
import functools
import math

import jax
import jax.numpy as jnp
from jax import lax
from jax.experimental import pallas as pl
from jax.experimental.pallas import tpu as pltpu
from jax.sharding import PartitionSpec as P

D = 1280
HEADS = 16
HDIM = 80


def local_any(qkv_rows, residual, out_weight, norm_gain, merge_weight, merge_bias, page_grid):
    row_count = lax.axis_size("row")
    q_split = max(1, row_count // HEADS)
    head_groups = row_count // q_split
    width = D // head_groups
    heads_per = width // HDIM
    band_len = qkv_rows.shape[1]
    part_len = band_len // q_split
    local_qkv = qkv_rows[0]
    queries = local_qkv[:, :D]
    key_vals = jnp.concatenate(
        [
            local_qkv[:, D : 2 * D].reshape(band_len, head_groups, width),
            local_qkv[:, 2 * D :].reshape(band_len, head_groups, width),
        ],
        axis=2,
    )
    q_send = (
        queries.reshape(q_split, part_len, head_groups, width)
        .transpose(2, 0, 1, 3)
        .reshape(row_count, part_len, width)
    )
    kv_send = jnp.broadcast_to(
        key_vals.transpose(1, 0, 2)[:, None], (head_groups, q_split, band_len, 2 * width)
    )
    kv_send = kv_send.reshape(row_count, band_len, 2 * width)
    q_recv, kv_recv = (
        lax.all_to_all(q_send, "row", split_axis=0, concat_axis=1, tiled=True),
        lax.all_to_all(kv_send, "row", split_axis=0, concat_axis=1, tiled=True),
    )
    kv_local = kv_recv[0]
    positions = jnp.arange(row_count * band_len, dtype=jnp.int32)
    valid_len = page_grid[0, 0] * page_grid[0, 1]
    key_valid = positions < valid_len
    key_total = kv_local.shape[0]
    key_heads = kv_local[:, :width].reshape(key_total, heads_per, HDIM)
    value_heads = kv_local[:, width:].reshape(key_total, heads_per, HDIM)
    query_total = row_count * part_len
    q_block = math.gcd(query_total, 512)
    q_blocks = q_recv[0].reshape(query_total // q_block, q_block, heads_per, HDIM)
    root_dim = math.sqrt(HDIM)

    def attend(q_span):
        scores = (
            jnp.einsum("qhd,khd->hqk", q_span, key_heads, preferred_element_type=jnp.float32)
            / root_dim
        )
        scores = jnp.where(key_valid[None, None, :], scores, -1e30)
        peak = jnp.max(scores, axis=2, keepdims=True)
        weights = jnp.exp(scores - peak)
        total = jnp.sum(weights, axis=2, keepdims=True)
        mixed = (
            jnp.einsum(
                "hqk,khd->hqd",
                weights.astype(jnp.bfloat16),
                value_heads,
                preferred_element_type=jnp.float32,
            )
            / total
        )
        return mixed.transpose(1, 0, 2).reshape(q_span.shape[0], width).astype(jnp.bfloat16)

    attn_heads = lax.map(attend, q_blocks).reshape(row_count, part_len, width)
    returned = lax.all_to_all(attn_heads, "row", split_axis=0, concat_axis=0, tiled=True)
    attn = (
        returned.reshape(head_groups, q_split, part_len, width)
        .transpose(1, 2, 0, 3)
        .reshape(band_len, D)
    )
    projected = jnp.dot(
        attn,
        lax.all_gather(out_weight, "page", axis=0, tiled=True),
        preferred_element_type=jnp.float32,
    )
    hidden = residual[0].astype(jnp.float32) + projected
    normed = (
        hidden * lax.rsqrt(jnp.mean(hidden * hidden, axis=1, keepdims=True) + 1e-06) * norm_gain
    ).astype(jnp.bfloat16)
    rows_n = page_grid[0, 0]
    cols_n = page_grid[0, 1]
    group_total = band_len * row_count // 4
    slots = jnp.arange(group_total, dtype=jnp.int32)
    half_cols = cols_n // 2
    live = slots < rows_n // 2 * half_cols
    first = jnp.where(live, 2 * (slots // half_cols) * cols_n + 2 * (slots % half_cols), 0)
    corners = [first, first + 1, first + cols_n, first + cols_n + 1]
    local_units = merge_weight.shape[0]
    page_all = lax.all_gather(normed, "row", axis=0, tiled=True)
    merged_sum = jnp.zeros((local_units, group_total), jnp.float32)
    for corner in range(4):
        picked = jnp.take(page_all, corners[corner], axis=0)
        merged_sum = merged_sum + jnp.einsum(
            "md,gd->mg",
            merge_weight[:, corner * D : (corner + 1) * D],
            picked,
            preferred_element_type=jnp.float32,
        )
    merged = jax.nn.gelu(merged_sum + merge_bias[:, None], approximate=False)
    merged = jnp.where(live[None, :], merged, 0.0).astype(jnp.bfloat16)
    return merged[None]


ROWS = 8
PAGES = 4
HPAIR = 2 * HDIM
WIDE = 128
REST = HPAIR - WIDE
MAIN = ROWS * WIDE
NOTES = 16
BLOCK_ORDER = (0, 6, 7, 2, 4, 3, 5, 1)
PIECE_ORDER = (0, 6, 2, 4, 1, 7, 3, 5)
ROOT = math.log2(math.e) / math.sqrt(HDIM)
BF16 = jnp.bfloat16
F32 = jnp.float32


def row_index():
    return lax.axis_index("row")


def pack_tail(wide):
    groups = wide.shape[0] // 4
    return jnp.concatenate([wide[at * groups : (at + 1) * groups] for at in range(4)], axis=1)


def spread_kernel(qkv_hbm, resid_hbm, weight_hbm, grid_hbm, *rest):
    outs = rest[:ROWS]
    slice_ref, grid_out, qkv, resid, tile, held, grid, sems = rest[ROWS:]
    me = row_index()
    depth = weight_hbm.shape[0]
    main = pl.ds(pl.multiple_of(me * WIDE, WIDE), WIDE)
    ends = pl.ds(pl.multiple_of(MAIN + me // 4 * WIDE, WIDE), WIDE)
    copies = [
        pltpu.make_async_copy(qkv_hbm.at[0], qkv, sems.at[0]),
        pltpu.make_async_copy(resid_hbm.at[0], resid, sems.at[1]),
        pltpu.make_async_copy(weight_hbm.at[:, main], slice_ref.at[:depth], sems.at[2]),
        pltpu.make_async_copy(weight_hbm.at[:, ends], tile, sems.at[3]),
        pltpu.make_async_copy(grid_hbm, grid, sems.at[4]),
    ]
    for copy in copies:
        copy.start()
    for copy in copies:
        copy.wait()
    for dest in range(ROWS):
        at = dest * HPAIR
        parts = [qkv[:, part * D + at : part * D + at + HPAIR] for part in range(3)]
        parts.append(resid[:, dest * WIDE : (dest + 1) * WIDE])
        parts.append(resid[:, MAIN + dest * REST : MAIN + (dest + 1) * REST])
        held[dest] = jnp.concatenate(parts, axis=1)
    for step in range(ROWS):
        outs[step][...] = held[me ^ step]
    tail = tile[:, :REST]
    for at in range(1, 4):
        tail = jnp.where(lax.rem(me, 4) == at, tile[:, at * REST : (at + 1) * REST], tail)
    slice_ref[depth:, :] = pack_tail(tail)
    row = lax.broadcasted_iota(jnp.int32, grid_out.shape, 0)
    grid_out[...] = jnp.where(row == 0, grid[0, 0], grid[0, 1])


def layout_kernel(grid_ref, gain_hbm, bias_hbm, *rest):
    select_ref, keys_ref, live_ref, gain_out, bias_out, gain_ref, bias_ref, sems = rest[-8:]
    fetch_gain = pltpu.make_async_copy(gain_hbm, gain_ref, sems.at[0])
    fetch_bias = pltpu.make_async_copy(bias_hbm, bias_ref, sems.at[1])
    fetch_gain.start()
    fetch_bias.start()
    rows_n, cols_n = grid_ref[:1, :1], grid_ref[1:2, :1]
    patches = select_ref.shape[0]
    groups = patches // 4
    half = cols_n >> 1
    count = (rows_n >> 1) * half
    slots = lax.broadcasted_iota(jnp.int32, (groups, 1), 0)
    line = jnp.floor((slots.astype(F32) + 0.5) / half.astype(F32)).astype(jnp.int32)
    first = 2 * line * cols_n + 2 * (slots - line * half)
    at = lax.broadcasted_iota(jnp.int32, (groups, patches), 1)
    for corner in range(4):
        wanted = jnp.where(slots < count, first + (corner // 2) * cols_n + corner % 2, -1)
        select_ref[corner * groups : (corner + 1) * groups, :] = jnp.where(at == wanted, 1.0, 0.0).astype(BF16)
    key = lax.broadcasted_iota(jnp.int32, keys_ref.shape, 1)
    keys_ref[...] = jnp.where(key < rows_n * cols_n, 0.0, -1e30)
    slot = lax.broadcasted_iota(jnp.int32, live_ref.shape, 1)
    live_ref[...] = jnp.where(slot < count, 1.0, 0.0)
    fetch_gain.wait()
    fetch_bias.wait()
    gain_out[...] = gain_ref[...].reshape(gain_out.shape)
    bias = jnp.broadcast_to(bias_ref[...].reshape(1, bias_out.shape[0]), (8, bias_out.shape[0]))
    bias_out[...] = bias.T[:, :1]


def attend_kernel(select_ref, dead_ref, *rest):
    blocks = rest[:ROWS]
    out_ref, q_all, k_all, v_all = rest[-4:]
    me = row_index()
    band = blocks[0].shape[0]
    patches = band * ROWS
    for step, block in zip(BLOCK_ORDER, blocks):
        at = pl.ds(pl.multiple_of((me ^ step) * band, band), band)
        q_all[at, :] = block[:, :HPAIR]
        k_all[at, :] = block[:, HPAIR : 2 * HPAIR]
        v_all[at, :] = block[:, 2 * HPAIR : 3 * HPAIR]
    queries = jnp.dot(select_ref[...], q_all[...], preferred_element_type=F32).astype(BF16)
    lane = lax.broadcasted_iota(jnp.int32, (1, HPAIR), 1)
    keys, values, dead = k_all[...], v_all[...], dead_ref[...]
    mixed = []
    for head in range(2):
        mine = (lane >= head * HDIM) & (lane < (head + 1) * HDIM)
        asked = jnp.where(mine, queries, jnp.zeros_like(queries))
        scores = lax.dot_general(asked, keys, (((1,), (1,)), ((), ())), preferred_element_type=F32) + dead
        weights = jnp.exp2((scores - jnp.max(scores, axis=1, keepdims=True)) * ROOT)
        total = jnp.sum(weights, axis=1, keepdims=True)
        mixed.append(jnp.dot(weights.astype(BF16), values, preferred_element_type=F32) / total)
    attn = jnp.where(lane < HDIM, mixed[0], mixed[1])
    out_ref[:patches, :] = attn[:, :WIDE].astype(BF16)
    out_ref[patches:, :] = pack_tail(attn[:, WIDE:]).astype(BF16)


def ready_kernel(select_ref, gain_ref, token_ref, *rest):
    del token_ref
    blocks, slices = rest[:ROWS], rest[ROWS : ROWS + PAGES]
    resid_ref, gain_out, main_ref, tail_ref, held = rest[ROWS + PAGES :]
    me = row_index()
    page = lax.axis_index("page")
    band = blocks[0].shape[0]
    for step, block in zip(BLOCK_ORDER, blocks):
        at = pl.ds(pl.multiple_of((me ^ step) * band, band), band)
        held[at, :] = block[:, 3 * HPAIR :]
    resid_ref[...] = jnp.dot(select_ref[...], held[...], preferred_element_type=F32)
    gain = jnp.zeros(gain_out.shape, F32)
    for pair in range(ROWS):
        parts = [gain_ref[:, pair * WIDE : (pair + 1) * WIDE]]
        parts.append(gain_ref[:, MAIN + pair * REST : MAIN + (pair + 1) * REST])
        gain = jnp.where(me == pair, jnp.concatenate(parts, axis=1), gain)
    gain_out[...] = gain
    tail_ref[...] = jnp.zeros_like(tail_ref)
    depth = 2 * HPAIR
    for step in range(PAGES):
        source = lax.rem(page + PAGES - step, PAGES)
        packed = slices[step][depth:]
        tail = jnp.concatenate([packed[:, at * REST : (at + 1) * REST] for at in range(4)], axis=0)
        whole = jnp.concatenate([slices[step][:depth], tail], axis=1)
        for core in range(2):
            pair = 2 * source + core
            rows = whole[core * HPAIR : (core + 1) * HPAIR]
            main_ref[pl.ds(pl.multiple_of(pair * WIDE, WIDE), WIDE), :] = rows[:WIDE]
            for corner in range(4):
                spot = pl.multiple_of(pair * WIDE + corner * REST, REST)
                tail_ref[corner, pl.ds(spot, REST), :] = rows[WIDE:]


def collect(pieces, full):
    me = row_index()
    for step, piece in zip(PIECE_ORDER, pieces):
        full[:, pl.ds(pl.multiple_of((me ^ step) * WIDE, WIDE), WIDE)] = piece[...]


def project_kernel(*rest):
    pieces = rest[:ROWS]
    main_ref, tail_ref, resid_ref, gain_ref, out_ref, full = rest[ROWS:]
    collect(pieces, full)
    patches = resid_ref.shape[0]
    groups = patches // 4
    base = jnp.dot(full[:patches], main_ref[...], preferred_element_type=F32) + resid_ref[...]
    ones = jnp.ones((NOTES, HPAIR), BF16)
    contract = (((1,), (1,)), ((), ()))
    row = lax.broadcasted_iota(jnp.int32, (NOTES, groups), 0)
    notes = jnp.zeros((NOTES, groups), F32)
    ends = []
    for corner in range(4):
        span = slice(corner * groups, (corner + 1) * groups)
        hidden = base[span] + jnp.dot(full[patches:], tail_ref[corner], preferred_element_type=F32)
        square = hidden * hidden
        high = square.astype(BF16)
        low = (square - high.astype(F32)).astype(BF16)
        total = lax.dot_general(ones, high, contract, preferred_element_type=F32)
        total = total + lax.dot_general(ones, low, contract, preferred_element_type=F32)
        coarse = total.astype(BF16).astype(F32)
        notes = jnp.where(row == corner, coarse, jnp.where(row == 4 + corner, total - coarse, notes))
        sent = hidden * gain_ref[...]
        out_ref[span, :] = sent[:, :WIDE].astype(BF16)
        ends.append(sent[:, WIDE:])
    out_ref[patches : patches + groups, :] = jnp.concatenate(ends, axis=1).astype(BF16)
    out_ref[patches + groups :, :] = notes.astype(BF16)


def tail_kernel(weight_ref, token_ref, out_ref):
    del token_ref
    for pair in range(ROWS):
        cut = [corner * D + MAIN + pair * REST for corner in range(4)]
        out_ref[:, pair * WIDE : (pair + 1) * WIDE] = jnp.concatenate(
            [weight_ref[:, at : at + REST] for at in cut], axis=1
        )


def merge_kernel(*rest):
    pieces = rest[:ROWS]
    weight_ref, tail_ref, bias_ref, live_ref, out_ref, full = rest[ROWS:]
    collect(pieces, full)
    groups = live_ref.shape[1]
    patches = 4 * groups
    notes = jnp.zeros((NOTES, groups), F32)
    for step in range(ROWS):
        notes = notes + pieces[step][patches + groups :].astype(F32)
    scale = lax.rsqrt((notes[:4] + notes[4:8]) * (1.0 / D) + 1e-06)
    contract = (((1,), (1,)), ((), ()))
    total = jnp.zeros((weight_ref.shape[0], groups), F32)
    for corner in range(4):
        total = total + scale[corner : corner + 1] * lax.dot_general(
            weight_ref[:, corner * D : corner * D + MAIN],
            full[corner * groups : (corner + 1) * groups],
            contract,
            preferred_element_type=F32,
        )
    spread = jnp.concatenate([jnp.broadcast_to(scale[at : at + 1], (REST, groups)) for at in range(4)], axis=0).T
    ends = full[patches : patches + groups].astype(F32) * jnp.concatenate([spread] * ROWS, axis=1)
    total = total + lax.dot_general(tail_ref[...], ends.astype(BF16), contract, preferred_element_type=F32)
    total = total + bias_ref[...]
    merged = 0.5 * total * (1.0 + lax.erf(total * math.sqrt(0.5)))
    out_ref[0] = jnp.where(live_ref[...] > 0.0, merged, 0.0).astype(BF16)


def kernel(body, name, out_shape, scratch=(), fetched=(), count=0, limit=24, flops=0, moved=0):
    specs = [pl.BlockSpec(memory_space=pltpu.VMEM) for _ in range(count)]
    for at in fetched:
        specs[at] = pl.BlockSpec(memory_space=pl.ANY)
    return pl.pallas_call(
        body,
        out_shape=out_shape,
        in_specs=specs,
        out_specs=jax.tree.map(lambda _: pl.BlockSpec(memory_space=pltpu.VMEM), out_shape),
        scratch_shapes=list(scratch),
        compiler_params=pltpu.CompilerParams(vmem_limit_bytes=limit * 1024 * 1024),
        cost_estimate=pl.CostEstimate(flops=flops, bytes_accessed=moved, transcendentals=0),
        name=name,
    )


def in_hbm(value):
    return pltpu.with_memory_space_constraint(value, pltpu.HBM)


def shape(*dims, dtype=BF16):
    return jax.ShapeDtypeStruct(dims, dtype)


def swap(value, step):
    return lax.ppermute(value, "row", [(row, row ^ step) for row in range(ROWS)])


def turn(value, step):
    return lax.ppermute(value, "page", [(page, (page + step) % PAGES) for page in range(PAGES)])


def gather_rows(value):
    far = [swap(value, step) for step in (6, 2, 4)]
    return [value] + far + [swap(piece, 1) for piece in [value] + far]


def local_eight(qkv_rows, residual, out_weight, norm_gain, merge_weight, merge_bias, page_grid):
    band = qkv_rows.shape[1]
    patches = band * ROWS
    groups = patches // 4
    units = merge_weight.shape[0]
    depth = out_weight.shape[0]
    piece = patches + groups

    *sends, own, grid = kernel(
        spread_kernel,
        "spread",
        [shape(band, 4 * HPAIR)] * ROWS + [shape(depth + depth // 4, WIDE), shape(8, WIDE, dtype=jnp.int32)],
        [
            pltpu.VMEM((band, 3 * D), BF16),
            pltpu.VMEM((band, D), BF16),
            pltpu.VMEM((depth, WIDE), BF16),
            pltpu.VMEM((ROWS, band, 4 * HPAIR), BF16),
            pltpu.SMEM(page_grid.shape, jnp.int32),
            pltpu.SemaphoreType.DMA((5,)),
        ],
        fetched=range(4),
        count=4,
        limit=24,
        moved=1 << 20,
    )(in_hbm(qkv_rows), in_hbm(residual), in_hbm(out_weight), in_hbm(page_grid))
    blocks = [sends[0]] + [swap(sends[step], step) for step in BLOCK_ORDER[1:]]
    slices = [own] + [turn(own, step) for step in range(1, PAGES)]
    select, dead, live, gain, bias = kernel(
        layout_kernel,
        "layout",
        [
            shape(patches, patches),
            shape(1, patches, dtype=F32),
            shape(1, groups, dtype=F32),
            shape(1, D, dtype=F32),
            shape(units, 1, dtype=F32),
        ],
        [pltpu.VMEM((D,), F32), pltpu.VMEM((units,), F32), pltpu.SemaphoreType.DMA((2,))],
        fetched=range(1, 3 + 5),
        count=3 + 5,
        moved=1 << 20,
    )(grid, in_hbm(norm_gain), in_hbm(merge_bias), *blocks[1:6])
    early = [slices[1], slices[2]]
    attn = kernel(
        attend_kernel,
        "attend",
        shape(piece, WIDE),
        [pltpu.VMEM((patches, HPAIR), BF16)] * 3,
        fetched=range(2 + ROWS, 2 + ROWS + len(early)),
        count=2 + ROWS + len(early),
        flops=20 * patches * patches * 4096,
        moved=1 << 20,
    )(select, dead, *blocks, *early)
    resid, own_gain, main, tail = kernel(
        ready_kernel,
        "ready",
        [shape(patches, HPAIR, dtype=F32), shape(1, HPAIR, dtype=F32), shape(MAIN, HPAIR), shape(4, MAIN, HPAIR)],
        [pltpu.VMEM((patches, HPAIR), BF16)],
        fetched=(2,),
        count=3 + ROWS + PAGES,
        flops=10 * patches * patches * 4096,
        moved=4 << 20,
    )(select, gain, attn, *blocks, *slices)
    hidden = kernel(
        project_kernel,
        "project",
        shape(piece + NOTES, WIDE),
        [pltpu.VMEM((piece, MAIN), BF16)],
        count=ROWS + 4,
        flops=4 * patches * MAIN * 256,
        moved=4 << 20,
    )(*gather_rows(attn), main, tail, resid, own_gain)
    ends = kernel(tail_kernel, "merge_tail", shape(units, MAIN), fetched=(1,), count=2, moved=4 << 20)(
        merge_weight, hidden
    )
    return kernel(
        merge_kernel,
        "merge",
        shape(1, units, groups),
        [pltpu.VMEM((piece + NOTES, MAIN), BF16)],
        count=ROWS + 4,
        flops=10 * units * groups * MAIN,
        moved=8 << 20,
    )(*gather_rows(hidden), merge_weight, ends, bias, live)


def solution(mesh):
    in_specs = (
        P("page", "row", None),
        P("page", "row", None),
        P("page", None),
        P(),
        P("row", None),
        P("row"),
        P("page", None),
    )
    out_specs = P("page", "row", None)
    local = local_eight if mesh.shape["row"] == 8 and mesh.shape["page"] == 4 else local_any
    return jax.shard_map(local, mesh=mesh, in_specs=in_specs, out_specs=out_specs, check_vma=False)
```

```python
import functools
import math

import jax
import jax.numpy as jnp
from jax import lax
from jax.experimental import pallas as pl
from jax.experimental.pallas import tpu as pltpu
from jax.sharding import PartitionSpec as P

D = 1280
HEADS = 16
HDIM = 80


def local_any(qkv_rows, residual, out_weight, norm_gain, merge_weight, merge_bias, page_grid):
    row_count = lax.axis_size("row")
    q_split = max(1, row_count // HEADS)
    head_groups = row_count // q_split
    width = D // head_groups
    heads_per = width // HDIM
    band_len = qkv_rows.shape[1]
    part_len = band_len // q_split
    local_qkv = qkv_rows[0]
    queries = local_qkv[:, :D]
    key_vals = jnp.concatenate(
        [
            local_qkv[:, D : 2 * D].reshape(band_len, head_groups, width),
            local_qkv[:, 2 * D :].reshape(band_len, head_groups, width),
        ],
        axis=2,
    )
    q_send = (
        queries.reshape(q_split, part_len, head_groups, width)
        .transpose(2, 0, 1, 3)
        .reshape(row_count, part_len, width)
    )
    kv_send = jnp.broadcast_to(
        key_vals.transpose(1, 0, 2)[:, None], (head_groups, q_split, band_len, 2 * width)
    )
    kv_send = kv_send.reshape(row_count, band_len, 2 * width)
    q_recv, kv_recv = (
        lax.all_to_all(q_send, "row", split_axis=0, concat_axis=1, tiled=True),
        lax.all_to_all(kv_send, "row", split_axis=0, concat_axis=1, tiled=True),
    )
    kv_local = kv_recv[0]
    positions = jnp.arange(row_count * band_len, dtype=jnp.int32)
    valid_len = page_grid[0, 0] * page_grid[0, 1]
    key_valid = positions < valid_len
    key_total = kv_local.shape[0]
    key_heads = kv_local[:, :width].reshape(key_total, heads_per, HDIM)
    value_heads = kv_local[:, width:].reshape(key_total, heads_per, HDIM)
    query_total = row_count * part_len
    q_block = math.gcd(query_total, 512)
    q_blocks = q_recv[0].reshape(query_total // q_block, q_block, heads_per, HDIM)
    root_dim = math.sqrt(HDIM)

    def attend(q_span):
        scores = (
            jnp.einsum("qhd,khd->hqk", q_span, key_heads, preferred_element_type=jnp.float32)
            / root_dim
        )
        scores = jnp.where(key_valid[None, None, :], scores, -1e30)
        peak = jnp.max(scores, axis=2, keepdims=True)
        weights = jnp.exp(scores - peak)
        total = jnp.sum(weights, axis=2, keepdims=True)
        mixed = (
            jnp.einsum(
                "hqk,khd->hqd",
                weights.astype(jnp.bfloat16),
                value_heads,
                preferred_element_type=jnp.float32,
            )
            / total
        )
        return mixed.transpose(1, 0, 2).reshape(q_span.shape[0], width).astype(jnp.bfloat16)

    attn_heads = lax.map(attend, q_blocks).reshape(row_count, part_len, width)
    returned = lax.all_to_all(attn_heads, "row", split_axis=0, concat_axis=0, tiled=True)
    attn = (
        returned.reshape(head_groups, q_split, part_len, width)
        .transpose(1, 2, 0, 3)
        .reshape(band_len, D)
    )
    projected = jnp.dot(
        attn,
        lax.all_gather(out_weight, "page", axis=0, tiled=True),
        preferred_element_type=jnp.float32,
    )
    hidden = residual[0].astype(jnp.float32) + projected
    normed = (
        hidden * lax.rsqrt(jnp.mean(hidden * hidden, axis=1, keepdims=True) + 1e-06) * norm_gain
    ).astype(jnp.bfloat16)
    rows_n = page_grid[0, 0]
    cols_n = page_grid[0, 1]
    group_total = band_len * row_count // 4
    slots = jnp.arange(group_total, dtype=jnp.int32)
    half_cols = cols_n // 2
    live = slots < rows_n // 2 * half_cols
    first = jnp.where(live, 2 * (slots // half_cols) * cols_n + 2 * (slots % half_cols), 0)
    corners = [first, first + 1, first + cols_n, first + cols_n + 1]
    local_units = merge_weight.shape[0]
    page_all = lax.all_gather(normed, "row", axis=0, tiled=True)
    merged_sum = jnp.zeros((local_units, group_total), jnp.float32)
    for corner in range(4):
        picked = jnp.take(page_all, corners[corner], axis=0)
        merged_sum = merged_sum + jnp.einsum(
            "md,gd->mg",
            merge_weight[:, corner * D : (corner + 1) * D],
            picked,
            preferred_element_type=jnp.float32,
        )
    merged = jax.nn.gelu(merged_sum + merge_bias[:, None], approximate=False)
    merged = jnp.where(live[None, :], merged, 0.0).astype(jnp.bfloat16)
    return merged[None]


ROWS = 8
PAGES = 4
HPAIR = 2 * HDIM
WIDE = 128
REST = HPAIR - WIDE
MAIN = ROWS * WIDE
NOTES = 16
BLOCK_ORDER = (0, 6, 7, 2, 4, 3, 5, 1)
SHIFTS = (0, 2, 1, 3)
ROOT = math.log2(math.e) / math.sqrt(HDIM)
BF16 = jnp.bfloat16
F32 = jnp.float32


def row_index():
    return lax.axis_index("row")


def pack_tail(wide):
    groups = wide.shape[0] // 4
    return jnp.concatenate([wide[at * groups : (at + 1) * groups] for at in range(4)], axis=1)


def spread_kernel(qkv_hbm, resid_hbm, weight_hbm, grid_hbm, *rest):
    outs = rest[:ROWS]
    slice_ref, grid_out, qkv, resid, tile, held, grid, sems = rest[ROWS:]
    me = row_index()
    depth = weight_hbm.shape[0]
    main = pl.ds(pl.multiple_of(me * WIDE, WIDE), WIDE)
    ends = pl.ds(pl.multiple_of(MAIN + me // 4 * WIDE, WIDE), WIDE)
    copies = [
        pltpu.make_async_copy(qkv_hbm.at[0], qkv, sems.at[0]),
        pltpu.make_async_copy(resid_hbm.at[0], resid, sems.at[1]),
        pltpu.make_async_copy(weight_hbm.at[:, main], slice_ref.at[:depth], sems.at[2]),
        pltpu.make_async_copy(weight_hbm.at[:, ends], tile, sems.at[3]),
        pltpu.make_async_copy(grid_hbm, grid, sems.at[4]),
    ]
    for copy in copies:
        copy.start()
    for copy in copies:
        copy.wait()
    for dest in range(ROWS):
        at = dest * HPAIR
        parts = [qkv[:, part * D + at : part * D + at + HPAIR] for part in range(3)]
        parts.append(resid[:, dest * WIDE : (dest + 1) * WIDE])
        parts.append(resid[:, MAIN + dest * REST : MAIN + (dest + 1) * REST])
        held[dest] = jnp.concatenate(parts, axis=1)
    for step in range(ROWS):
        outs[step][...] = held[me ^ step]
    tail = tile[:, :REST]
    for at in range(1, 4):
        tail = jnp.where(lax.rem(me, 4) == at, tile[:, at * REST : (at + 1) * REST], tail)
    slice_ref[depth:, :] = pack_tail(tail)
    row = lax.broadcasted_iota(jnp.int32, grid_out.shape, 0)
    grid_out[...] = jnp.where(row == 0, grid[0, 0], grid[0, 1])


def layout_kernel(grid_ref, gain_hbm, bias_hbm, *rest):
    select_ref, keys_ref, live_ref, gain_out, bias_out, gain_ref, bias_ref, sems = rest[-8:]
    fetch_gain = pltpu.make_async_copy(gain_hbm, gain_ref, sems.at[0])
    fetch_bias = pltpu.make_async_copy(bias_hbm, bias_ref, sems.at[1])
    fetch_gain.start()
    fetch_bias.start()
    rows_n, cols_n = grid_ref[:1, :1], grid_ref[1:2, :1]
    patches = select_ref.shape[0]
    groups = patches // 4
    half = cols_n >> 1
    count = (rows_n >> 1) * half
    slots = lax.broadcasted_iota(jnp.int32, (groups, 1), 0)
    line = jnp.floor((slots.astype(F32) + 0.5) / half.astype(F32)).astype(jnp.int32)
    first = 2 * line * cols_n + 2 * (slots - line * half)
    at = lax.broadcasted_iota(jnp.int32, (groups, patches), 1)
    for corner in range(4):
        wanted = jnp.where(slots < count, first + (corner // 2) * cols_n + corner % 2, -1)
        select_ref[corner * groups : (corner + 1) * groups, :] = jnp.where(at == wanted, 1.0, 0.0).astype(BF16)
    key = lax.broadcasted_iota(jnp.int32, keys_ref.shape, 1)
    keys_ref[...] = jnp.where(key < rows_n * cols_n, 0.0, -1e30)
    slot = lax.broadcasted_iota(jnp.int32, live_ref.shape, 1)
    live_ref[...] = jnp.where(slot < count, 1.0, 0.0)
    fetch_gain.wait()
    fetch_bias.wait()
    gain_out[...] = gain_ref[...].reshape(gain_out.shape)
    bias = jnp.broadcast_to(bias_ref[...].reshape(1, bias_out.shape[0]), (8, bias_out.shape[0]))
    bias_out[...] = bias.T[:, :1]


def attend_kernel(select_ref, dead_ref, *rest):
    blocks = rest[:ROWS]
    out_ref, q_all, k_all, v_all = rest[-4:]
    me = row_index()
    band = blocks[0].shape[0]
    patches = band * ROWS
    for step, block in zip(BLOCK_ORDER, blocks):
        at = pl.ds(pl.multiple_of((me ^ step) * band, band), band)
        q_all[at, :] = block[:, :HPAIR]
        k_all[at, :] = block[:, HPAIR : 2 * HPAIR]
        v_all[at, :] = block[:, 2 * HPAIR : 3 * HPAIR]
    queries = jnp.dot(select_ref[...], q_all[...], preferred_element_type=F32).astype(BF16)
    lane = lax.broadcasted_iota(jnp.int32, (1, HPAIR), 1)
    keys, values, dead = k_all[...], v_all[...], dead_ref[...]
    mixed = []
    for head in range(2):
        mine = (lane >= head * HDIM) & (lane < (head + 1) * HDIM)
        asked = jnp.where(mine, queries, jnp.zeros_like(queries))
        scores = lax.dot_general(asked, keys, (((1,), (1,)), ((), ())), preferred_element_type=F32) + dead
        weights = jnp.exp2((scores - jnp.max(scores, axis=1, keepdims=True)) * ROOT)
        total = jnp.sum(weights, axis=1, keepdims=True)
        mixed.append(jnp.dot(weights.astype(BF16), values, preferred_element_type=F32) / total)
    attn = jnp.where(lane < HDIM, mixed[0], mixed[1])
    out_ref[:patches, :] = attn[:, :WIDE].astype(BF16)
    out_ref[patches:, :] = pack_tail(attn[:, WIDE:]).astype(BF16)


def weight_rows(cut):
    depth = 2 * HPAIR
    packed = cut[depth:]
    tail = jnp.concatenate([packed[:, at * REST : (at + 1) * REST] for at in range(4)], axis=0)
    whole = jnp.concatenate([cut[:depth], tail], axis=1)
    return [whole[core * HPAIR : (core + 1) * HPAIR] for core in range(2)]


def place_rows(rows, base, main_ref, tail_ref):
    for core in range(2):
        pair = base + core
        main_ref[pl.ds(pl.multiple_of(pair * WIDE, WIDE), WIDE), :] = rows[core][:WIDE]
        for corner in range(4):
            spot = pl.multiple_of(pair * WIDE + corner * REST, REST)
            tail_ref[corner, pl.ds(spot, REST), :] = rows[core][WIDE:]


def ready_kernel(select_ref, gain_ref, token_ref, *rest):
    del token_ref
    blocks, slices = rest[:ROWS], rest[ROWS : ROWS + PAGES - 1]
    resid_ref, gain_out, main_ref, tail_ref, held = rest[-5:]
    me = row_index()
    page = lax.axis_index("page")
    band = blocks[0].shape[0]
    for step, block in zip(BLOCK_ORDER, blocks):
        at = pl.ds(pl.multiple_of((me ^ step) * band, band), band)
        held[at, :] = block[:, 3 * HPAIR :]
    resid_ref[...] = jnp.dot(select_ref[...], held[...], preferred_element_type=F32)
    gain = jnp.zeros(gain_out.shape, F32)
    for pair in range(ROWS):
        parts = [gain_ref[:, pair * WIDE : (pair + 1) * WIDE]]
        parts.append(gain_ref[:, MAIN + pair * REST : MAIN + (pair + 1) * REST])
        gain = jnp.where(me == pair, jnp.concatenate(parts, axis=1), gain)
    gain_out[...] = gain
    main_ref[...] = jnp.zeros_like(main_ref)
    tail_ref[...] = jnp.zeros_like(tail_ref)
    for step, cut in zip(SHIFTS, slices):
        source = lax.rem(page + PAGES - step, PAGES)
        place_rows(weight_rows(cut), 2 * source, main_ref, tail_ref)


def last_kernel(cut_ref, token_ref, main_ref, tail_ref):
    del token_ref
    tail_ref[...] = jnp.zeros_like(tail_ref)
    place_rows(weight_rows(cut_ref), 0, main_ref, tail_ref)


def collect(pieces, full):
    me = row_index()
    core = me % 2
    first, second = 2 + 2 * core, 4 - 2 * core
    near = [0, first, second, 6]
    far = [1, 1 ^ second, 1 ^ first, 7]
    for step, piece in zip(near + far, pieces):
        full[:, pl.ds(pl.multiple_of((me ^ step) * WIDE, WIDE), WIDE)] = piece[...]


def project_kernel(*rest):
    pieces = rest[:ROWS]
    main_ref, tail_ref, last_main_ref, last_tail_ref, resid_ref, gain_ref, out_ref, full = rest[ROWS:]
    collect(pieces, full)
    patches = resid_ref.shape[0]
    groups = patches // 4
    source = lax.rem(lax.axis_index("page") + PAGES - SHIFTS[-1], PAGES)
    late = pl.ds(pl.multiple_of(source * 2 * WIDE, 2 * WIDE), 2 * WIDE)
    base = jnp.dot(full[:patches], main_ref[...], preferred_element_type=F32) + resid_ref[...]
    base = base + jnp.dot(full[:patches, late], last_main_ref[...], preferred_element_type=F32)
    ones = jnp.ones((NOTES, HPAIR), BF16)
    contract = (((1,), (1,)), ((), ()))
    row = lax.broadcasted_iota(jnp.int32, (NOTES, groups), 0)
    notes = jnp.zeros((NOTES, groups), F32)
    ends = []
    for corner in range(4):
        span = slice(corner * groups, (corner + 1) * groups)
        hidden = base[span] + jnp.dot(full[patches:], tail_ref[corner], preferred_element_type=F32)
        hidden = hidden + jnp.dot(full[patches:, late], last_tail_ref[corner], preferred_element_type=F32)
        square = hidden * hidden
        high = square.astype(BF16)
        low = (square - high.astype(F32)).astype(BF16)
        total = lax.dot_general(ones, high, contract, preferred_element_type=F32)
        total = total + lax.dot_general(ones, low, contract, preferred_element_type=F32)
        coarse = total.astype(BF16).astype(F32)
        notes = jnp.where(row == corner, coarse, jnp.where(row == 4 + corner, total - coarse, notes))
        sent = hidden * gain_ref[...]
        out_ref[span, :] = sent[:, :WIDE].astype(BF16)
        ends.append(sent[:, WIDE:])
    out_ref[patches : patches + groups, :] = jnp.concatenate(ends, axis=1).astype(BF16)
    out_ref[patches + groups :, :] = notes.astype(BF16)


def tail_kernel(weight_ref, token_ref, out_ref):
    del token_ref
    for pair in range(ROWS):
        cut = [corner * D + MAIN + pair * REST for corner in range(4)]
        out_ref[:, pair * WIDE : (pair + 1) * WIDE] = jnp.concatenate(
            [weight_ref[:, at : at + REST] for at in cut], axis=1
        )


def merge_kernel(*rest):
    pieces = rest[:ROWS]
    weight_ref, tail_ref, bias_ref, live_ref, out_ref, full = rest[ROWS:]
    collect(pieces, full)
    groups = live_ref.shape[1]
    patches = 4 * groups
    notes = jnp.zeros((NOTES, groups), F32)
    for step in range(ROWS):
        notes = notes + pieces[step][patches + groups :].astype(F32)
    scale = lax.rsqrt((notes[:4] + notes[4:8]) * (1.0 / D) + 1e-06)
    contract = (((1,), (1,)), ((), ()))
    total = jnp.zeros((weight_ref.shape[0], groups), F32)
    for corner in range(4):
        total = total + scale[corner : corner + 1] * lax.dot_general(
            weight_ref[:, corner * D : corner * D + MAIN],
            full[corner * groups : (corner + 1) * groups],
            contract,
            preferred_element_type=F32,
        )
    spread = jnp.concatenate([jnp.broadcast_to(scale[at : at + 1], (REST, groups)) for at in range(4)], axis=0).T
    ends = full[patches : patches + groups].astype(F32) * jnp.concatenate([spread] * ROWS, axis=1)
    total = total + lax.dot_general(tail_ref[...], ends.astype(BF16), contract, preferred_element_type=F32)
    total = total + bias_ref[...]
    merged = 0.5 * total * (1.0 + lax.erf(total * math.sqrt(0.5)))
    out_ref[0] = jnp.where(live_ref[...] > 0.0, merged, 0.0).astype(BF16)


def kernel(body, name, out_shape, scratch=(), fetched=(), count=0, limit=24, flops=0, moved=0):
    specs = [pl.BlockSpec(memory_space=pltpu.VMEM) for _ in range(count)]
    for at in fetched:
        specs[at] = pl.BlockSpec(memory_space=pl.ANY)
    return pl.pallas_call(
        body,
        out_shape=out_shape,
        in_specs=specs,
        out_specs=jax.tree.map(lambda _: pl.BlockSpec(memory_space=pltpu.VMEM), out_shape),
        scratch_shapes=list(scratch),
        compiler_params=pltpu.CompilerParams(vmem_limit_bytes=limit * 1024 * 1024),
        cost_estimate=pl.CostEstimate(flops=flops, bytes_accessed=moved, transcendentals=0),
        name=name,
    )


def in_hbm(value):
    return pltpu.with_memory_space_constraint(value, pltpu.HBM)


def shape(*dims, dtype=BF16):
    return jax.ShapeDtypeStruct(dims, dtype)


def swap(value, step):
    return lax.ppermute(value, "row", [(row, row ^ step) for row in range(ROWS)])


def turn(value, step):
    return lax.ppermute(value, "page", [(page, (page + step) % PAGES) for page in range(PAGES)])


def gather_rows(value, early=None, late=None):
    first = [(row, row ^ (2 + 2 * (row % 2))) for row in range(ROWS)]
    second = [(row, row ^ (4 - 2 * (row % 2))) for row in range(ROWS)]
    head = lax.ppermute(value, "row", first)
    side = lax.ppermute(value, "row", second)
    if early is not None:
        head = lax.optimization_barrier((head, early))[0]
    diagonal = lax.ppermute(head, "row", second)
    if late is not None:
        head = lax.optimization_barrier((head, late))[0]
    mine = [value, head, side, diagonal]
    return mine + [swap(piece, 1) for piece in mine]


def local_eight(qkv_rows, residual, out_weight, norm_gain, merge_weight, merge_bias, page_grid):
    band = qkv_rows.shape[1]
    patches = band * ROWS
    groups = patches // 4
    units = merge_weight.shape[0]
    depth = out_weight.shape[0]
    piece = patches + groups

    *sends, own, grid = kernel(
        spread_kernel,
        "spread",
        [shape(band, 4 * HPAIR)] * ROWS + [shape(depth + depth // 4, WIDE), shape(8, WIDE, dtype=jnp.int32)],
        [
            pltpu.VMEM((band, 3 * D), BF16),
            pltpu.VMEM((band, D), BF16),
            pltpu.VMEM((depth, WIDE), BF16),
            pltpu.VMEM((ROWS, band, 4 * HPAIR), BF16),
            pltpu.SMEM(page_grid.shape, jnp.int32),
            pltpu.SemaphoreType.DMA((5,)),
        ],
        fetched=range(4),
        count=4,
        limit=24,
        moved=1 << 20,
    )(in_hbm(qkv_rows), in_hbm(residual), in_hbm(out_weight), in_hbm(page_grid))
    blocks = [sends[0]] + [swap(sends[step], step) for step in BLOCK_ORDER[1:]]
    slices = [own] + [turn(own, step) for step in SHIFTS[1:]]
    select, dead, live, gain, bias = kernel(
        layout_kernel,
        "layout",
        [
            shape(patches, patches),
            shape(1, patches, dtype=F32),
            shape(1, groups, dtype=F32),
            shape(1, D, dtype=F32),
            shape(units, 1, dtype=F32),
        ],
        [pltpu.VMEM((D,), F32), pltpu.VMEM((units,), F32), pltpu.SemaphoreType.DMA((2,))],
        fetched=range(1, 3 + 3),
        count=3 + 3,
        moved=1 << 20,
    )(grid, in_hbm(norm_gain), in_hbm(merge_bias), *blocks[1:4])
    attn = kernel(
        attend_kernel,
        "attend",
        shape(piece, WIDE),
        [pltpu.VMEM((patches, HPAIR), BF16)] * 3,
        count=2 + ROWS,
        flops=20 * patches * patches * 4096,
        moved=1 << 20,
    )(select, dead, *blocks)
    resid, own_gain, main, tail = kernel(
        ready_kernel,
        "ready",
        [shape(patches, HPAIR, dtype=F32), shape(1, HPAIR, dtype=F32), shape(MAIN, HPAIR), shape(4, MAIN, HPAIR)],
        [pltpu.VMEM((patches, HPAIR), BF16)],
        fetched=(2,),
        count=2 + ROWS + PAGES,
        flops=10 * patches * patches * 4096,
        moved=4 << 20,
    )(select, gain, attn, *blocks, *slices[:-1])
    last = kernel(
        last_kernel,
        "ready_last",
        [shape(2 * WIDE, HPAIR), shape(4, 2 * WIDE, HPAIR)],
        fetched=(1,),
        count=2,
        moved=4 << 20,
    )(slices[-1], main)
    pieces = gather_rows(attn, main, last[0])
    hidden = kernel(
        project_kernel,
        "project",
        shape(piece + NOTES, WIDE),
        [pltpu.VMEM((piece, MAIN), BF16)],
        count=ROWS + 6,
        flops=4 * patches * MAIN * 256,
        moved=4 << 20,
    )(*pieces, main, tail, *last, resid, own_gain)
    ends = kernel(tail_kernel, "merge_tail", shape(units, MAIN), fetched=(1,), count=2, moved=4 << 20)(
        merge_weight, hidden
    )
    return kernel(
        merge_kernel,
        "merge",
        shape(1, units, groups),
        [pltpu.VMEM((piece + NOTES, MAIN), BF16)],
        count=ROWS + 4,
        flops=10 * units * groups * MAIN,
        moved=8 << 20,
    )(*gather_rows(hidden), merge_weight, ends, bias, live)


def solution(mesh):
    in_specs = (
        P("page", "row", None),
        P("page", "row", None),
        P("page", None),
        P(),
        P("row", None),
        P("row"),
        P("page", None),
    )
    out_specs = P("page", "row", None)
    local = local_eight if mesh.shape["row"] == 8 and mesh.shape["page"] == 4 else local_any
    return jax.shard_map(local, mesh=mesh, in_specs=in_specs, out_specs=out_specs, check_vma=False)
```

```python
import functools
import math

import jax
import jax.numpy as jnp
from jax import lax
from jax.experimental import pallas as pl
from jax.experimental.pallas import tpu as pltpu
from jax.sharding import PartitionSpec as P

D = 1280
HEADS = 16
HDIM = 80


def local_any(qkv_rows, residual, out_weight, norm_gain, merge_weight, merge_bias, page_grid):
    row_count = lax.axis_size("row")
    q_split = max(1, row_count // HEADS)
    head_groups = row_count // q_split
    width = D // head_groups
    heads_per = width // HDIM
    band_len = qkv_rows.shape[1]
    part_len = band_len // q_split
    local_qkv = qkv_rows[0]
    queries = local_qkv[:, :D]
    key_vals = jnp.concatenate(
        [
            local_qkv[:, D : 2 * D].reshape(band_len, head_groups, width),
            local_qkv[:, 2 * D :].reshape(band_len, head_groups, width),
        ],
        axis=2,
    )
    q_send = (
        queries.reshape(q_split, part_len, head_groups, width)
        .transpose(2, 0, 1, 3)
        .reshape(row_count, part_len, width)
    )
    kv_send = jnp.broadcast_to(
        key_vals.transpose(1, 0, 2)[:, None], (head_groups, q_split, band_len, 2 * width)
    )
    kv_send = kv_send.reshape(row_count, band_len, 2 * width)
    q_recv, kv_recv = (
        lax.all_to_all(q_send, "row", split_axis=0, concat_axis=1, tiled=True),
        lax.all_to_all(kv_send, "row", split_axis=0, concat_axis=1, tiled=True),
    )
    kv_local = kv_recv[0]
    positions = jnp.arange(row_count * band_len, dtype=jnp.int32)
    valid_len = page_grid[0, 0] * page_grid[0, 1]
    key_valid = positions < valid_len
    key_total = kv_local.shape[0]
    key_heads = kv_local[:, :width].reshape(key_total, heads_per, HDIM)
    value_heads = kv_local[:, width:].reshape(key_total, heads_per, HDIM)
    query_total = row_count * part_len
    q_block = math.gcd(query_total, 512)
    q_blocks = q_recv[0].reshape(query_total // q_block, q_block, heads_per, HDIM)
    root_dim = math.sqrt(HDIM)

    def attend(q_span):
        scores = (
            jnp.einsum("qhd,khd->hqk", q_span, key_heads, preferred_element_type=jnp.float32)
            / root_dim
        )
        scores = jnp.where(key_valid[None, None, :], scores, -1e30)
        peak = jnp.max(scores, axis=2, keepdims=True)
        weights = jnp.exp(scores - peak)
        total = jnp.sum(weights, axis=2, keepdims=True)
        mixed = (
            jnp.einsum(
                "hqk,khd->hqd",
                weights.astype(jnp.bfloat16),
                value_heads,
                preferred_element_type=jnp.float32,
            )
            / total
        )
        return mixed.transpose(1, 0, 2).reshape(q_span.shape[0], width).astype(jnp.bfloat16)

    attn_heads = lax.map(attend, q_blocks).reshape(row_count, part_len, width)
    returned = lax.all_to_all(attn_heads, "row", split_axis=0, concat_axis=0, tiled=True)
    attn = (
        returned.reshape(head_groups, q_split, part_len, width)
        .transpose(1, 2, 0, 3)
        .reshape(band_len, D)
    )
    projected = jnp.dot(
        attn,
        lax.all_gather(out_weight, "page", axis=0, tiled=True),
        preferred_element_type=jnp.float32,
    )
    hidden = residual[0].astype(jnp.float32) + projected
    normed = (
        hidden * lax.rsqrt(jnp.mean(hidden * hidden, axis=1, keepdims=True) + 1e-06) * norm_gain
    ).astype(jnp.bfloat16)
    rows_n = page_grid[0, 0]
    cols_n = page_grid[0, 1]
    group_total = band_len * row_count // 4
    slots = jnp.arange(group_total, dtype=jnp.int32)
    half_cols = cols_n // 2
    live = slots < rows_n // 2 * half_cols
    first = jnp.where(live, 2 * (slots // half_cols) * cols_n + 2 * (slots % half_cols), 0)
    corners = [first, first + 1, first + cols_n, first + cols_n + 1]
    local_units = merge_weight.shape[0]
    page_all = lax.all_gather(normed, "row", axis=0, tiled=True)
    merged_sum = jnp.zeros((local_units, group_total), jnp.float32)
    for corner in range(4):
        picked = jnp.take(page_all, corners[corner], axis=0)
        merged_sum = merged_sum + jnp.einsum(
            "md,gd->mg",
            merge_weight[:, corner * D : (corner + 1) * D],
            picked,
            preferred_element_type=jnp.float32,
        )
    merged = jax.nn.gelu(merged_sum + merge_bias[:, None], approximate=False)
    merged = jnp.where(live[None, :], merged, 0.0).astype(jnp.bfloat16)
    return merged[None]


ROWS = 8
PAGES = 4
HPAIR = 2 * HDIM
WIDE = 128
REST = HPAIR - WIDE
MAIN = ROWS * WIDE
NOTES = 16
BLOCK_ORDER = (0, 2, 4, 6, 7, 3, 5, 1)
PIECE_ORDER = (0, 2, 4, 1, 3, 5, 6, 7)
EARLY = 6
SHIFTS = (0, 2, 1, 3)
ROOT = math.log2(math.e) / math.sqrt(HDIM)
BF16 = jnp.bfloat16
F32 = jnp.float32


def row_index():
    return lax.axis_index("row")


def pack_tail(wide):
    groups = wide.shape[0] // 4
    return jnp.concatenate([wide[at * groups : (at + 1) * groups] for at in range(4)], axis=1)


def spread_kernel(qkv_hbm, resid_hbm, weight_hbm, grid_hbm, *rest):
    outs = rest[:ROWS]
    slice_ref, grid_out, qkv, resid, tile, held, grid, sems = rest[ROWS:]
    me = row_index()
    depth = weight_hbm.shape[0]
    main = pl.ds(pl.multiple_of(me * WIDE, WIDE), WIDE)
    ends = pl.ds(pl.multiple_of(MAIN + me // 4 * WIDE, WIDE), WIDE)
    copies = [
        pltpu.make_async_copy(qkv_hbm.at[0], qkv, sems.at[0]),
        pltpu.make_async_copy(resid_hbm.at[0], resid, sems.at[1]),
        pltpu.make_async_copy(weight_hbm.at[:, main], slice_ref.at[:depth], sems.at[2]),
        pltpu.make_async_copy(weight_hbm.at[:, ends], tile, sems.at[3]),
        pltpu.make_async_copy(grid_hbm, grid, sems.at[4]),
    ]
    for copy in copies:
        copy.start()
    for copy in copies:
        copy.wait()
    for dest in range(ROWS):
        at = dest * HPAIR
        parts = [qkv[:, part * D + at : part * D + at + HPAIR] for part in range(3)]
        parts.append(resid[:, dest * WIDE : (dest + 1) * WIDE])
        parts.append(resid[:, MAIN + dest * REST : MAIN + (dest + 1) * REST])
        held[dest] = jnp.concatenate(parts, axis=1)
    for step in range(ROWS):
        outs[step][...] = held[me ^ step]
    tail = tile[:, :REST]
    for at in range(1, 4):
        tail = jnp.where(lax.rem(me, 4) == at, tile[:, at * REST : (at + 1) * REST], tail)
    slice_ref[depth:, :] = pack_tail(tail)
    row = lax.broadcasted_iota(jnp.int32, grid_out.shape, 0)
    grid_out[...] = jnp.where(row == 0, grid[0, 0], grid[0, 1])


def layout_kernel(grid_ref, *rest):
    select_ref, keys_ref, live_ref = rest[-3:]
    rows_n, cols_n = grid_ref[:1, :1], grid_ref[1:2, :1]
    patches = select_ref.shape[0]
    groups = patches // 4
    half = cols_n >> 1
    count = (rows_n >> 1) * half
    slots = lax.broadcasted_iota(jnp.int32, (groups, 1), 0)
    line = jnp.floor((slots.astype(F32) + 0.5) / half.astype(F32)).astype(jnp.int32)
    first = 2 * line * cols_n + 2 * (slots - line * half)
    at = lax.broadcasted_iota(jnp.int32, (groups, patches), 1)
    for corner in range(4):
        wanted = jnp.where(slots < count, first + (corner // 2) * cols_n + corner % 2, -1)
        select_ref[corner * groups : (corner + 1) * groups, :] = jnp.where(at == wanted, 1.0, 0.0).astype(BF16)
    key = lax.broadcasted_iota(jnp.int32, keys_ref.shape, 1)
    keys_ref[...] = jnp.where(key < rows_n * cols_n, 0.0, -1e30)
    slot = lax.broadcasted_iota(jnp.int32, live_ref.shape, 1)
    live_ref[...] = jnp.where(slot < count, 1.0, 0.0)


def attend_kernel(select_ref, dead_ref, *rest):
    blocks = rest[:ROWS]
    out_ref, q_all, k_all, v_all = rest[-4:]
    me = row_index()
    band = blocks[0].shape[0]
    patches = band * ROWS
    for step, block in zip(BLOCK_ORDER, blocks):
        at = pl.ds(pl.multiple_of((me ^ step) * band, band), band)
        q_all[at, :] = block[:, :HPAIR]
        k_all[at, :] = block[:, HPAIR : 2 * HPAIR]
        v_all[at, :] = block[:, 2 * HPAIR : 3 * HPAIR]
    queries = jnp.dot(select_ref[...], q_all[...], preferred_element_type=F32).astype(BF16)
    lane = lax.broadcasted_iota(jnp.int32, (1, HPAIR), 1)
    keys, values, dead = k_all[...], v_all[...], dead_ref[...]
    mixed = []
    for head in range(2):
        mine = (lane >= head * HDIM) & (lane < (head + 1) * HDIM)
        asked = jnp.where(mine, queries, jnp.zeros_like(queries))
        scores = lax.dot_general(asked, keys, (((1,), (1,)), ((), ())), preferred_element_type=F32) + dead
        weights = jnp.exp2((scores - jnp.max(scores, axis=1, keepdims=True)) * ROOT)
        total = jnp.sum(weights, axis=1, keepdims=True)
        mixed.append(jnp.dot(weights.astype(BF16), values, preferred_element_type=F32) / total)
    attn = jnp.where(lane < HDIM, mixed[0], mixed[1])
    out_ref[:patches, :] = attn[:, :WIDE].astype(BF16)
    out_ref[patches:, :] = pack_tail(attn[:, WIDE:]).astype(BF16)


def weight_rows(cut):
    depth = 2 * HPAIR
    packed = cut[depth:]
    tail = jnp.concatenate([packed[:, at * REST : (at + 1) * REST] for at in range(4)], axis=0)
    whole = jnp.concatenate([cut[:depth], tail], axis=1)
    return [whole[core * HPAIR : (core + 1) * HPAIR] for core in range(2)]


def place_rows(rows, base, main_ref, tail_ref):
    for core in range(2):
        pair = base + core
        main_ref[pl.ds(pl.multiple_of(pair * WIDE, WIDE), WIDE), :] = rows[core][:WIDE]
        for corner in range(4):
            spot = pl.multiple_of(pair * WIDE + corner * REST, REST)
            tail_ref[corner, pl.ds(spot, REST), :] = rows[core][WIDE:]


def ready_kernel(select_ref, gain_hbm, token_ref, *rest):
    del token_ref
    blocks, slices = rest[:ROWS], rest[ROWS : ROWS + PAGES - 1]
    resid_ref, gain_out, main_ref, tail_ref, held, line, sem = rest[-7:]
    fetch = pltpu.make_async_copy(gain_hbm, line, sem)
    fetch.start()
    me = row_index()
    page = lax.axis_index("page")
    band = blocks[0].shape[0]
    for step, block in zip(BLOCK_ORDER, blocks):
        at = pl.ds(pl.multiple_of((me ^ step) * band, band), band)
        held[at, :] = block[:, 3 * HPAIR :]
    resid_ref[...] = jnp.dot(select_ref[...], held[...], preferred_element_type=F32)
    main_ref[...] = jnp.zeros_like(main_ref)
    tail_ref[...] = jnp.zeros_like(tail_ref)
    for step, cut in zip(SHIFTS, slices):
        source = lax.rem(page + PAGES - step, PAGES)
        place_rows(weight_rows(cut), 2 * source, main_ref, tail_ref)
    fetch.wait()
    whole = line[...].reshape(1, D)
    gain = jnp.zeros(gain_out.shape, F32)
    for pair in range(ROWS):
        parts = [whole[:, pair * WIDE : (pair + 1) * WIDE]]
        parts.append(whole[:, MAIN + pair * REST : MAIN + (pair + 1) * REST])
        gain = jnp.where(me == pair, jnp.concatenate(parts, axis=1), gain)
    gain_out[...] = gain


def last_kernel(cut_ref, token_ref, main_ref, tail_ref):
    del token_ref
    tail_ref[...] = jnp.zeros_like(tail_ref)
    place_rows(weight_rows(cut_ref), 0, main_ref, tail_ref)


def far_block():
    me = row_index()
    return pl.ds(pl.multiple_of((me // 2 ^ 3) * 2 * WIDE, 2 * WIDE), 2 * WIDE)


def collect_early(pieces, full):
    me = row_index()
    full[:, far_block()] = jnp.zeros((full.shape[0], 2 * WIDE), BF16)
    for step, piece in zip(PIECE_ORDER[:EARLY], pieces):
        full[:, pl.ds(pl.multiple_of((me ^ step) * WIDE, WIDE), WIDE)] = piece[...]


def collect_late(same, other):
    core = row_index() % 2
    left = jnp.where(core == 0, same[...], other[...])
    right = jnp.where(core == 0, other[...], same[...])
    return jnp.concatenate([left, right], axis=1)


def late_source():
    return lax.rem(lax.axis_index("page") + PAGES - SHIFTS[-1], PAGES)


def project_early_kernel(*rest):
    pieces = rest[:EARLY]
    main_ref, tail_ref, last_main_ref, last_tail_ref, resid_ref, out_ref, full = rest[EARLY:]
    collect_early(pieces, full)
    patches = resid_ref.shape[0]
    groups = patches // 4
    late = pl.ds(pl.multiple_of(late_source() * 2 * WIDE, 2 * WIDE), 2 * WIDE)
    base = jnp.dot(full[:patches], main_ref[...], preferred_element_type=F32) + resid_ref[...]
    base = base + jnp.dot(full[:patches, late], last_main_ref[...], preferred_element_type=F32)
    for corner in range(4):
        span = slice(corner * groups, (corner + 1) * groups)
        part = jnp.dot(full[patches:], tail_ref[corner], preferred_element_type=F32)
        part = part + jnp.dot(full[patches:, late], last_tail_ref[corner], preferred_element_type=F32)
        out_ref[span, :] = base[span] + part


def project_kernel(*rest):
    same, other, base_ref, main_ref, tail_ref, last_main_ref, last_tail_ref, gain_ref, out_ref = rest
    patches = base_ref.shape[0]
    groups = patches // 4
    block = far_block()
    is_last = late_source() == (row_index() // 2 ^ 3)
    full = collect_late(same, other)
    main = jnp.where(is_last, last_main_ref[...], main_ref[block, :])
    base = base_ref[...] + jnp.dot(full[:patches], main, preferred_element_type=F32)
    ones = jnp.ones((NOTES, HPAIR), BF16)
    contract = (((1,), (1,)), ((), ()))
    row = lax.broadcasted_iota(jnp.int32, (NOTES, groups), 0)
    notes = jnp.zeros((NOTES, groups), F32)
    ends = []
    for corner in range(4):
        span = slice(corner * groups, (corner + 1) * groups)
        tail = jnp.where(is_last, last_tail_ref[corner], tail_ref[corner, block, :])
        hidden = base[span] + jnp.dot(full[patches:], tail, preferred_element_type=F32)
        square = hidden * hidden
        high = square.astype(BF16)
        low = (square - high.astype(F32)).astype(BF16)
        total = lax.dot_general(ones, high, contract, preferred_element_type=F32)
        total = total + lax.dot_general(ones, low, contract, preferred_element_type=F32)
        coarse = total.astype(BF16).astype(F32)
        notes = jnp.where(row == corner, coarse, jnp.where(row == 4 + corner, total - coarse, notes))
        sent = hidden * gain_ref[...]
        out_ref[span, :] = sent[:, :WIDE].astype(BF16)
        ends.append(sent[:, WIDE:])
    out_ref[patches : patches + groups, :] = jnp.concatenate(ends, axis=1).astype(BF16)
    out_ref[patches + groups :, :] = notes.astype(BF16)


def tail_kernel(weight_ref, bias_hbm, token_ref, out_ref, bias_out, line, sem):
    del token_ref
    fetch = pltpu.make_async_copy(bias_hbm, line, sem)
    fetch.start()
    for pair in range(ROWS):
        cut = [corner * D + MAIN + pair * REST for corner in range(4)]
        out_ref[:, pair * WIDE : (pair + 1) * WIDE] = jnp.concatenate(
            [weight_ref[:, at : at + REST] for at in cut], axis=1
        )
    fetch.wait()
    units = bias_out.shape[0]
    bias_out[...] = jnp.broadcast_to(line[...].reshape(1, units), (8, units)).T[:, :1]


def merge_early_kernel(*rest):
    pieces = rest[:EARLY]
    weight_ref, out_ref, full = rest[EARLY:]
    collect_early(pieces, full)
    groups = out_ref.shape[2]
    for corner in range(4):
        out_ref[corner] = lax.dot_general(
            weight_ref[:, corner * D : corner * D + MAIN],
            full[corner * groups : (corner + 1) * groups],
            (((1,), (1,)), ((), ())),
            preferred_element_type=F32,
        )


def merge_kernel(*rest):
    pieces = rest[:ROWS]
    early_ref, weight_ref, tail_ref, bias_ref, live_ref, out_ref, ends_ref = rest[ROWS:]
    me = row_index()
    groups = live_ref.shape[1]
    patches = 4 * groups
    notes = jnp.zeros((NOTES, groups), F32)
    for step, piece in zip(PIECE_ORDER, pieces):
        ends_ref[:, pl.ds(pl.multiple_of((me ^ step) * WIDE, WIDE), WIDE)] = piece[patches : patches + groups]
        notes = notes + piece[patches + groups :].astype(F32)
    scale = lax.rsqrt((notes[:4] + notes[4:8]) * (1.0 / D) + 1e-06)
    contract = (((1,), (1,)), ((), ()))
    full = collect_late(pieces[EARLY], pieces[EARLY + 1])
    total = jnp.zeros(bias_ref.shape[:1] + (groups,), F32)
    for corner in range(4):
        at = pl.multiple_of(corner * D + (me // 2 ^ 3) * 2 * WIDE, 2 * WIDE)
        part = lax.dot_general(
            weight_ref[:, pl.ds(at, 2 * WIDE)],
            full[corner * groups : (corner + 1) * groups],
            contract,
            preferred_element_type=F32,
        )
        total = total + scale[corner : corner + 1] * (early_ref[corner] + part)
    spread = jnp.concatenate([jnp.broadcast_to(scale[at : at + 1], (REST, groups)) for at in range(4)], axis=0).T
    ends = ends_ref[...].astype(F32) * jnp.concatenate([spread] * ROWS, axis=1)
    total = total + lax.dot_general(tail_ref[...], ends.astype(BF16), contract, preferred_element_type=F32)
    total = total + bias_ref[...]
    merged = 0.5 * total * (1.0 + lax.erf(total * math.sqrt(0.5)))
    out_ref[0] = jnp.where(live_ref[...] > 0.0, merged, 0.0).astype(BF16)


def kernel(body, name, out_shape, scratch=(), fetched=(), count=0, limit=24, flops=0, moved=0):
    specs = [pl.BlockSpec(memory_space=pltpu.VMEM) for _ in range(count)]
    for at in fetched:
        specs[at] = pl.BlockSpec(memory_space=pl.ANY)
    return pl.pallas_call(
        body,
        out_shape=out_shape,
        in_specs=specs,
        out_specs=jax.tree.map(lambda _: pl.BlockSpec(memory_space=pltpu.VMEM), out_shape),
        scratch_shapes=list(scratch),
        compiler_params=pltpu.CompilerParams(vmem_limit_bytes=limit * 1024 * 1024),
        cost_estimate=pl.CostEstimate(flops=flops, bytes_accessed=moved, transcendentals=0),
        name=name,
    )


def in_hbm(value):
    return pltpu.with_memory_space_constraint(value, pltpu.HBM)


def shape(*dims, dtype=BF16):
    return jax.ShapeDtypeStruct(dims, dtype)


def swap(value, step):
    return lax.ppermute(value, "row", [(row, row ^ step) for row in range(ROWS)])


def turn(value, step):
    return lax.ppermute(value, "page", [(page, (page + step) % PAGES) for page in range(PAGES)])


def gather_rows(value, *early):
    far = [swap(value, step) for step in (2, 4, 6)]
    passed = [value] + far
    for at, array in enumerate(early):
        if array is not None:
            passed[at] = lax.optimization_barrier((passed[at], array))[0]
    near = [swap(piece, 1) for piece in passed]
    return [value, far[0], far[1], near[0], near[1], near[2], far[2], near[3]]


def local_eight(qkv_rows, residual, out_weight, norm_gain, merge_weight, merge_bias, page_grid):
    band = qkv_rows.shape[1]
    patches = band * ROWS
    groups = patches // 4
    units = merge_weight.shape[0]
    depth = out_weight.shape[0]
    piece = patches + groups

    *sends, own, grid = kernel(
        spread_kernel,
        "spread",
        [shape(band, 4 * HPAIR)] * ROWS + [shape(depth + depth // 4, WIDE), shape(8, WIDE, dtype=jnp.int32)],
        [
            pltpu.VMEM((band, 3 * D), BF16),
            pltpu.VMEM((band, D), BF16),
            pltpu.VMEM((depth, WIDE), BF16),
            pltpu.VMEM((ROWS, band, 4 * HPAIR), BF16),
            pltpu.SMEM(page_grid.shape, jnp.int32),
            pltpu.SemaphoreType.DMA((5,)),
        ],
        fetched=range(4),
        count=4,
        limit=24,
        moved=1 << 20,
    )(in_hbm(qkv_rows), in_hbm(residual), in_hbm(out_weight), in_hbm(page_grid))
    blocks = [sends[0]] + [swap(sends[step], step) for step in BLOCK_ORDER[1:]]
    slices = [own] + [turn(own, step) for step in SHIFTS[1:]]
    select, dead, live = kernel(
        layout_kernel,
        "layout",
        [shape(patches, patches), shape(1, patches, dtype=F32), shape(1, groups, dtype=F32)],
        fetched=range(1, 1 + 3),
        count=1 + 3,
        moved=1 << 20,
    )(grid, *blocks[1:4])
    attn = kernel(
        attend_kernel,
        "attend",
        shape(piece, WIDE),
        [pltpu.VMEM((patches, HPAIR), BF16)] * 3,
        count=2 + ROWS,
        flops=20 * patches * patches * 4096,
        moved=1 << 20,
    )(select, dead, *blocks)
    resid, own_gain, main, tail = kernel(
        ready_kernel,
        "ready",
        [shape(patches, HPAIR, dtype=F32), shape(1, HPAIR, dtype=F32), shape(MAIN, HPAIR), shape(4, MAIN, HPAIR)],
        [pltpu.VMEM((patches, HPAIR), BF16), pltpu.VMEM((D,), F32), pltpu.SemaphoreType.DMA],
        fetched=(1, 2),
        count=2 + ROWS + PAGES,
        flops=10 * patches * patches * 4096,
        moved=4 << 20,
    )(select, in_hbm(norm_gain), attn, *blocks, *slices[:-1])
    last = kernel(
        last_kernel,
        "ready_last",
        [shape(2 * WIDE, HPAIR), shape(4, 2 * WIDE, HPAIR)],
        fetched=(1,),
        count=2,
        moved=4 << 20,
    )(slices[-1], main)
    pieces = gather_rows(attn, main, None, last[0])
    base = kernel(
        project_early_kernel,
        "project_early",
        shape(patches, HPAIR, dtype=F32),
        [pltpu.VMEM((piece, MAIN), BF16)],
        count=EARLY + 5,
        flops=4 * patches * MAIN * 4096,
        moved=4 << 20,
    )(*pieces[:EARLY], main, tail, *last, resid)
    hidden = kernel(
        project_kernel,
        "project",
        shape(piece + NOTES, WIDE),
        count=2 + 6,
        flops=patches * MAIN * 256,
        moved=4 << 20,
    )(*pieces[EARLY:], base, main, tail, *last, own_gain)
    ends, bias = kernel(
        tail_kernel,
        "merge_tail",
        [shape(units, MAIN), shape(units, 1, dtype=F32)],
        [pltpu.VMEM((units,), F32), pltpu.SemaphoreType.DMA],
        fetched=(1, 2),
        count=3,
        moved=4 << 20,
    )(merge_weight, in_hbm(merge_bias), hidden)
    pieces = gather_rows(hidden)
    early = kernel(
        merge_early_kernel,
        "merge_early",
        shape(4, units, groups, dtype=F32),
        [pltpu.VMEM((piece + NOTES, MAIN), BF16)],
        count=EARLY + 1,
        flops=8 * units * groups * MAIN * 16,
        moved=8 << 20,
    )(*pieces[:EARLY], merge_weight)
    return kernel(
        merge_kernel,
        "merge",
        shape(1, units, groups),
        [pltpu.VMEM((groups, MAIN), BF16)],
        count=ROWS + 5,
        flops=4 * units * groups * MAIN,
        moved=8 << 20,
    )(*pieces, early, merge_weight, ends, bias, live)


def solution(mesh):
    in_specs = (
        P("page", "row", None),
        P("page", "row", None),
        P("page", None),
        P(),
        P("row", None),
        P("row"),
        P("page", None),
    )
    out_specs = P("page", "row", None)
    local = local_eight if mesh.shape["row"] == 8 and mesh.shape["page"] == 4 else local_any
    return jax.shard_map(local, mesh=mesh, in_specs=in_specs, out_specs=out_specs, check_vma=False)
```

```python
import functools
import math

import jax
import jax.numpy as jnp
from jax import lax
from jax.experimental import pallas as pl
from jax.experimental.pallas import tpu as pltpu
from jax.sharding import PartitionSpec as P

D = 1280
HEADS = 16
HDIM = 80


def local_any(qkv_rows, residual, out_weight, norm_gain, merge_weight, merge_bias, page_grid):
    row_count = lax.axis_size("row")
    q_split = max(1, row_count // HEADS)
    head_groups = row_count // q_split
    width = D // head_groups
    heads_per = width // HDIM
    band_len = qkv_rows.shape[1]
    part_len = band_len // q_split
    local_qkv = qkv_rows[0]
    queries = local_qkv[:, :D]
    key_vals = jnp.concatenate(
        [
            local_qkv[:, D : 2 * D].reshape(band_len, head_groups, width),
            local_qkv[:, 2 * D :].reshape(band_len, head_groups, width),
        ],
        axis=2,
    )
    q_send = (
        queries.reshape(q_split, part_len, head_groups, width)
        .transpose(2, 0, 1, 3)
        .reshape(row_count, part_len, width)
    )
    kv_send = jnp.broadcast_to(
        key_vals.transpose(1, 0, 2)[:, None], (head_groups, q_split, band_len, 2 * width)
    )
    kv_send = kv_send.reshape(row_count, band_len, 2 * width)
    q_recv, kv_recv = (
        lax.all_to_all(q_send, "row", split_axis=0, concat_axis=1, tiled=True),
        lax.all_to_all(kv_send, "row", split_axis=0, concat_axis=1, tiled=True),
    )
    kv_local = kv_recv[0]
    positions = jnp.arange(row_count * band_len, dtype=jnp.int32)
    valid_len = page_grid[0, 0] * page_grid[0, 1]
    key_valid = positions < valid_len
    key_total = kv_local.shape[0]
    key_heads = kv_local[:, :width].reshape(key_total, heads_per, HDIM)
    value_heads = kv_local[:, width:].reshape(key_total, heads_per, HDIM)
    query_total = row_count * part_len
    q_block = math.gcd(query_total, 512)
    q_blocks = q_recv[0].reshape(query_total // q_block, q_block, heads_per, HDIM)
    root_dim = math.sqrt(HDIM)

    def attend(q_span):
        scores = (
            jnp.einsum("qhd,khd->hqk", q_span, key_heads, preferred_element_type=jnp.float32)
            / root_dim
        )
        scores = jnp.where(key_valid[None, None, :], scores, -1e30)
        peak = jnp.max(scores, axis=2, keepdims=True)
        weights = jnp.exp(scores - peak)
        total = jnp.sum(weights, axis=2, keepdims=True)
        mixed = (
            jnp.einsum(
                "hqk,khd->hqd",
                weights.astype(jnp.bfloat16),
                value_heads,
                preferred_element_type=jnp.float32,
            )
            / total
        )
        return mixed.transpose(1, 0, 2).reshape(q_span.shape[0], width).astype(jnp.bfloat16)

    attn_heads = lax.map(attend, q_blocks).reshape(row_count, part_len, width)
    returned = lax.all_to_all(attn_heads, "row", split_axis=0, concat_axis=0, tiled=True)
    attn = (
        returned.reshape(head_groups, q_split, part_len, width)
        .transpose(1, 2, 0, 3)
        .reshape(band_len, D)
    )
    projected = jnp.dot(
        attn,
        lax.all_gather(out_weight, "page", axis=0, tiled=True),
        preferred_element_type=jnp.float32,
    )
    hidden = residual[0].astype(jnp.float32) + projected
    normed = (
        hidden * lax.rsqrt(jnp.mean(hidden * hidden, axis=1, keepdims=True) + 1e-06) * norm_gain
    ).astype(jnp.bfloat16)
    rows_n = page_grid[0, 0]
    cols_n = page_grid[0, 1]
    group_total = band_len * row_count // 4
    slots = jnp.arange(group_total, dtype=jnp.int32)
    half_cols = cols_n // 2
    live = slots < rows_n // 2 * half_cols
    first = jnp.where(live, 2 * (slots // half_cols) * cols_n + 2 * (slots % half_cols), 0)
    corners = [first, first + 1, first + cols_n, first + cols_n + 1]
    local_units = merge_weight.shape[0]
    page_all = lax.all_gather(normed, "row", axis=0, tiled=True)
    merged_sum = jnp.zeros((local_units, group_total), jnp.float32)
    for corner in range(4):
        picked = jnp.take(page_all, corners[corner], axis=0)
        merged_sum = merged_sum + jnp.einsum(
            "md,gd->mg",
            merge_weight[:, corner * D : (corner + 1) * D],
            picked,
            preferred_element_type=jnp.float32,
        )
    merged = jax.nn.gelu(merged_sum + merge_bias[:, None], approximate=False)
    merged = jnp.where(live[None, :], merged, 0.0).astype(jnp.bfloat16)
    return merged[None]


ROWS = 8
PAGES = 4
HPAIR = 2 * HDIM
WIDE = 128
REST = HPAIR - WIDE
MAIN = ROWS * WIDE
NOTES = 16
BLOCK_ORDER = (0, 2, 4, 6, 7, 3, 5, 1)
PIECE_ORDER = (0, 2, 4, 1, 3, 5, 6, 7)
EARLY = 6
SHIFTS = (0, 2, 1, 3)
ROOT = math.log2(math.e) / math.sqrt(HDIM)
BF16 = jnp.bfloat16
F32 = jnp.float32


def row_index():
    return lax.axis_index("row")


def pack_tail(wide):
    groups = wide.shape[0] // 4
    return jnp.concatenate([wide[at * groups : (at + 1) * groups] for at in range(4)], axis=1)


def spread_kernel(qkv_hbm, resid_hbm, weight_hbm, grid_hbm, *rest):
    outs = rest[:ROWS]
    slice_ref, grid_out, qkv, resid, tile, held, grid, sems = rest[ROWS:]
    me = row_index()
    depth = weight_hbm.shape[0]
    main = pl.ds(pl.multiple_of(me * WIDE, WIDE), WIDE)
    ends = pl.ds(pl.multiple_of(MAIN + me // 4 * WIDE, WIDE), WIDE)
    copies = [
        pltpu.make_async_copy(qkv_hbm.at[0], qkv, sems.at[0]),
        pltpu.make_async_copy(resid_hbm.at[0], resid, sems.at[1]),
        pltpu.make_async_copy(weight_hbm.at[:, main], slice_ref.at[:depth], sems.at[2]),
        pltpu.make_async_copy(weight_hbm.at[:, ends], tile, sems.at[3]),
        pltpu.make_async_copy(grid_hbm, grid, sems.at[4]),
    ]
    for copy in copies:
        copy.start()
    for copy in copies:
        copy.wait()
    for dest in range(ROWS):
        at = dest * HPAIR
        parts = [qkv[:, part * D + at : part * D + at + HPAIR] for part in range(3)]
        parts.append(resid[:, dest * WIDE : (dest + 1) * WIDE])
        parts.append(resid[:, MAIN + dest * REST : MAIN + (dest + 1) * REST])
        held[dest] = jnp.concatenate(parts, axis=1)
    for step in range(ROWS):
        outs[step][...] = held[me ^ step]
    tail = tile[:, :REST]
    for at in range(1, 4):
        tail = jnp.where(lax.rem(me, 4) == at, tile[:, at * REST : (at + 1) * REST], tail)
    slice_ref[depth:, :] = pack_tail(tail)
    row = lax.broadcasted_iota(jnp.int32, grid_out.shape, 0)
    grid_out[...] = jnp.where(row == 0, grid[0, 0], grid[0, 1])


def layout_kernel(grid_ref, *rest):
    select_ref, keys_ref, live_ref = rest[-3:]
    rows_n, cols_n = grid_ref[:1, :1], grid_ref[1:2, :1]
    patches = select_ref.shape[0]
    groups = patches // 4
    half = cols_n >> 1
    count = (rows_n >> 1) * half
    slots = lax.broadcasted_iota(jnp.int32, (groups, 1), 0)
    line = jnp.floor((slots.astype(F32) + 0.5) / half.astype(F32)).astype(jnp.int32)
    first = 2 * line * cols_n + 2 * (slots - line * half)
    at = lax.broadcasted_iota(jnp.int32, (groups, patches), 1)
    for corner in range(4):
        wanted = jnp.where(slots < count, first + (corner // 2) * cols_n + corner % 2, -1)
        select_ref[corner * groups : (corner + 1) * groups, :] = jnp.where(at == wanted, 1.0, 0.0).astype(BF16)
    key = lax.broadcasted_iota(jnp.int32, keys_ref.shape, 1)
    keys_ref[...] = jnp.where(key < rows_n * cols_n, 0.0, -1e30)
    slot = lax.broadcasted_iota(jnp.int32, live_ref.shape, 1)
    live_ref[...] = jnp.where(slot < count, 1.0, 0.0)


def attend_kernel(select_ref, dead_ref, *rest):
    blocks = rest[:ROWS]
    out_ref, q_all, k_all, v_all = rest[-4:]
    me = row_index()
    band = blocks[0].shape[0]
    patches = band * ROWS
    for step, block in zip(BLOCK_ORDER, blocks):
        at = pl.ds(pl.multiple_of((me ^ step) * band, band), band)
        q_all[at, :] = block[:, :HPAIR]
        k_all[at, :] = block[:, HPAIR : 2 * HPAIR]
        v_all[at, :] = block[:, 2 * HPAIR : 3 * HPAIR]
    queries = jnp.dot(select_ref[...], q_all[...], preferred_element_type=F32).astype(BF16)
    lane = lax.broadcasted_iota(jnp.int32, (1, HPAIR), 1)
    keys, values, dead = k_all[...], v_all[...], dead_ref[...]
    mixed = []
    for head in range(2):
        mine = (lane >= head * HDIM) & (lane < (head + 1) * HDIM)
        asked = jnp.where(mine, queries, jnp.zeros_like(queries))
        scores = lax.dot_general(asked, keys, (((1,), (1,)), ((), ())), preferred_element_type=F32) + dead
        weights = jnp.exp2((scores - jnp.max(scores, axis=1, keepdims=True)) * ROOT)
        total = jnp.sum(weights, axis=1, keepdims=True)
        mixed.append(jnp.dot(weights.astype(BF16), values, preferred_element_type=F32) / total)
    attn = jnp.where(lane < HDIM, mixed[0], mixed[1])
    out_ref[:patches, :] = attn[:, :WIDE].astype(BF16)
    out_ref[patches:, :] = pack_tail(attn[:, WIDE:]).astype(BF16)


def weight_rows(cut):
    depth = 2 * HPAIR
    packed = cut[depth:]
    tail = jnp.concatenate([packed[:, at * REST : (at + 1) * REST] for at in range(4)], axis=0)
    whole = jnp.concatenate([cut[:depth], tail], axis=1)
    return [whole[core * HPAIR : (core + 1) * HPAIR] for core in range(2)]


def place_rows(rows, base, main_ref, tail_ref):
    for core in range(2):
        pair = base + core
        main_ref[pl.ds(pl.multiple_of(pair * WIDE, WIDE), WIDE), :] = rows[core][:WIDE]
        for corner in range(4):
            spot = pl.multiple_of(pair * WIDE + corner * REST, REST)
            tail_ref[corner, pl.ds(spot, REST), :] = rows[core][WIDE:]


def ready_kernel(select_ref, gain_hbm, token_ref, *rest):
    del token_ref
    blocks, slices = rest[:ROWS], rest[ROWS : ROWS + PAGES - 1]
    resid_ref, gain_out, main_ref, tail_ref, held, line, sem = rest[-7:]
    fetch = pltpu.make_async_copy(gain_hbm, line, sem)
    fetch.start()
    me = row_index()
    page = lax.axis_index("page")
    band = blocks[0].shape[0]
    for step, block in zip(BLOCK_ORDER, blocks):
        at = pl.ds(pl.multiple_of((me ^ step) * band, band), band)
        held[at, :] = block[:, 3 * HPAIR :]
    resid_ref[...] = jnp.dot(select_ref[...], held[...], preferred_element_type=F32)
    main_ref[...] = jnp.zeros_like(main_ref)
    tail_ref[...] = jnp.zeros_like(tail_ref)
    for step, cut in zip(SHIFTS, slices):
        source = lax.rem(page + PAGES - step, PAGES)
        place_rows(weight_rows(cut), 2 * source, main_ref, tail_ref)
    fetch.wait()
    whole = line[...].reshape(1, D)
    gain = jnp.zeros(gain_out.shape, F32)
    for pair in range(ROWS):
        parts = [whole[:, pair * WIDE : (pair + 1) * WIDE]]
        parts.append(whole[:, MAIN + pair * REST : MAIN + (pair + 1) * REST])
        gain = jnp.where(me == pair, jnp.concatenate(parts, axis=1), gain)
    gain_out[...] = gain


def last_kernel(cut_ref, token_ref, main_ref, tail_ref):
    del token_ref
    tail_ref[...] = jnp.zeros_like(tail_ref)
    place_rows(weight_rows(cut_ref), 0, main_ref, tail_ref)


def far_block():
    me = row_index()
    return pl.ds(pl.multiple_of((me // 2 ^ 3) * 2 * WIDE, 2 * WIDE), 2 * WIDE)


def collect_early(pieces, full):
    me = row_index()
    full[:, far_block()] = jnp.zeros((full.shape[0], 2 * WIDE), BF16)
    for step, piece in zip(PIECE_ORDER[:EARLY], pieces):
        full[:, pl.ds(pl.multiple_of((me ^ step) * WIDE, WIDE), WIDE)] = piece[...]


def collect_late(same, other):
    core = row_index() % 2
    left = jnp.where(core == 0, same[...], other[...])
    right = jnp.where(core == 0, other[...], same[...])
    return jnp.concatenate([left, right], axis=1)


def late_source():
    return lax.rem(lax.axis_index("page") + PAGES - SHIFTS[-1], PAGES)


def project_early_kernel(*rest):
    pieces = rest[:EARLY]
    main_ref, tail_ref, last_main_ref, last_tail_ref, resid_ref, out_ref, full = rest[EARLY:]
    collect_early(pieces, full)
    patches = resid_ref.shape[0]
    groups = patches // 4
    late = pl.ds(pl.multiple_of(late_source() * 2 * WIDE, 2 * WIDE), 2 * WIDE)
    base = jnp.dot(full[:patches], main_ref[...], preferred_element_type=F32) + resid_ref[...]
    base = base + jnp.dot(full[:patches, late], last_main_ref[...], preferred_element_type=F32)
    for corner in range(4):
        span = slice(corner * groups, (corner + 1) * groups)
        part = jnp.dot(full[patches:], tail_ref[corner], preferred_element_type=F32)
        part = part + jnp.dot(full[patches:, late], last_tail_ref[corner], preferred_element_type=F32)
        out_ref[span, :] = base[span] + part


def project_kernel(*rest):
    same, other, base_ref, main_ref, tail_ref, last_main_ref, last_tail_ref, gain_ref, out_ref = rest
    patches = base_ref.shape[0]
    groups = patches // 4
    block = far_block()
    is_last = late_source() == (row_index() // 2 ^ 3)
    full = collect_late(same, other)
    main = jnp.where(is_last, last_main_ref[...], main_ref[block, :])
    base = base_ref[...] + jnp.dot(full[:patches], main, preferred_element_type=F32)
    ones = jnp.ones((NOTES, HPAIR), BF16)
    contract = (((1,), (1,)), ((), ()))
    row = lax.broadcasted_iota(jnp.int32, (NOTES, groups), 0)
    notes = jnp.zeros((NOTES, groups), F32)
    ends = []
    for corner in range(4):
        span = slice(corner * groups, (corner + 1) * groups)
        tail = jnp.where(is_last, last_tail_ref[corner], tail_ref[corner, block, :])
        hidden = base[span] + jnp.dot(full[patches:], tail, preferred_element_type=F32)
        square = hidden * hidden
        high = square.astype(BF16)
        low = (square - high.astype(F32)).astype(BF16)
        total = lax.dot_general(ones, high, contract, preferred_element_type=F32)
        total = total + lax.dot_general(ones, low, contract, preferred_element_type=F32)
        coarse = total.astype(BF16).astype(F32)
        notes = jnp.where(row == corner, coarse, jnp.where(row == 4 + corner, total - coarse, notes))
        sent = hidden * gain_ref[...]
        out_ref[span, :] = sent[:, :WIDE].astype(BF16)
        ends.append(sent[:, WIDE:])
    out_ref[patches : patches + groups, :] = jnp.concatenate(ends, axis=1).astype(BF16)
    out_ref[patches + groups :, :] = notes.astype(BF16)


def tail_kernel(weight_ref, bias_hbm, token_ref, out_ref, bias_out, line, sem):
    del token_ref
    fetch = pltpu.make_async_copy(bias_hbm, line, sem)
    fetch.start()
    for pair in range(ROWS):
        cut = [corner * D + MAIN + pair * REST for corner in range(4)]
        out_ref[:, pair * WIDE : (pair + 1) * WIDE] = jnp.concatenate(
            [weight_ref[:, at : at + REST] for at in cut], axis=1
        )
    fetch.wait()
    units = bias_out.shape[0]
    bias_out[...] = jnp.broadcast_to(line[...].reshape(1, units), (8, units)).T[:, :1]


def piece_steps():
    core = row_index() % 2
    first, second = 2 + 2 * core, 4 - 2 * core
    return [0, first, second, 6, 1, 1 ^ second, 1 ^ first, 7]


def merge_product(weight_ref, corner, pieces):
    me = row_index()
    groups = pieces[0][1].shape[0] // 4
    at = [pl.multiple_of(corner * D + (me ^ step) * WIDE, WIDE) for step, _ in pieces]
    return lax.dot_general(
        jnp.concatenate([weight_ref[:, pl.ds(spot, WIDE)] for spot in at], axis=1),
        jnp.concatenate([piece[corner * groups : (corner + 1) * groups] for _, piece in pieces], axis=1),
        (((1,), (1,)), ((), ())),
        preferred_element_type=F32,
    )


def merge_early_kernel(*rest):
    pieces, (weight_ref, out_ref) = rest[:4], rest[4:]
    steps = piece_steps()
    patches = 4 * out_ref.shape[2]
    own, one, near_own, near_one = [
        (steps[at], piece[:patches]) for at, piece in zip((0, 1, 4, 5), pieces)
    ]
    for corner in range(4):
        out_ref[corner] = merge_product(weight_ref, corner, (own, near_own)) + merge_product(
            weight_ref, corner, (one, near_one)
        )


def merge_kernel(*rest):
    pieces = rest[:ROWS]
    early_ref, weight_ref, tail_ref, bias_ref, live_ref, out_ref, ends_ref = rest[ROWS:]
    me = row_index()
    groups = live_ref.shape[1]
    patches = 4 * groups
    notes = jnp.zeros((NOTES, groups), F32)
    steps = piece_steps()
    for step, piece in zip(steps, pieces):
        ends_ref[:, pl.ds(pl.multiple_of((me ^ step) * WIDE, WIDE), WIDE)] = piece[patches : patches + groups]
        notes = notes + piece[patches + groups :].astype(F32)
    late = [[(steps[at], pieces[at][:patches]) for at in couple] for couple in ((2, 6), (3, 7))]
    scale = lax.rsqrt((notes[:4] + notes[4:8]) * (1.0 / D) + 1e-06)
    total = jnp.zeros(bias_ref.shape[:1] + (groups,), F32)
    for corner in range(4):
        part = early_ref[corner]
        for couple in late:
            part = part + merge_product(weight_ref, corner, couple)
        total = total + scale[corner : corner + 1] * part
    spread = jnp.concatenate([jnp.broadcast_to(scale[at : at + 1], (REST, groups)) for at in range(4)], axis=0).T
    ends = ends_ref[...].astype(F32) * jnp.concatenate([spread] * ROWS, axis=1)
    total = total + lax.dot_general(
        tail_ref[...], ends.astype(BF16), (((1,), (1,)), ((), ())), preferred_element_type=F32
    )
    total = total + bias_ref[...]
    merged = 0.5 * total * (1.0 + lax.erf(total * math.sqrt(0.5)))
    out_ref[0] = jnp.where(live_ref[...] > 0.0, merged, 0.0).astype(BF16)


def kernel(body, name, out_shape, scratch=(), fetched=(), count=0, limit=24, flops=0, moved=0):
    specs = [pl.BlockSpec(memory_space=pltpu.VMEM) for _ in range(count)]
    for at in fetched:
        specs[at] = pl.BlockSpec(memory_space=pl.ANY)
    return pl.pallas_call(
        body,
        out_shape=out_shape,
        in_specs=specs,
        out_specs=jax.tree.map(lambda _: pl.BlockSpec(memory_space=pltpu.VMEM), out_shape),
        scratch_shapes=list(scratch),
        compiler_params=pltpu.CompilerParams(vmem_limit_bytes=limit * 1024 * 1024),
        cost_estimate=pl.CostEstimate(flops=flops, bytes_accessed=moved, transcendentals=0),
        name=name,
    )


def in_hbm(value):
    return pltpu.with_memory_space_constraint(value, pltpu.HBM)


def shape(*dims, dtype=BF16):
    return jax.ShapeDtypeStruct(dims, dtype)


def swap(value, step):
    return lax.ppermute(value, "row", [(row, row ^ step) for row in range(ROWS)])


def turn(value, step):
    return lax.ppermute(value, "page", [(page, (page + step) % PAGES) for page in range(PAGES)])


def gather_rows(value, *early):
    far = [swap(value, step) for step in (2, 4, 6)]
    passed = [value] + far
    for at, array in enumerate(early):
        if array is not None:
            passed[at] = lax.optimization_barrier((passed[at], array))[0]
    near = [swap(piece, 1) for piece in passed]
    return [value, far[0], far[1], near[0], near[1], near[2], far[2], near[3]]


def after(value, array):
    return lax.optimization_barrier((value, array))[0]


def local_eight(qkv_rows, residual, out_weight, norm_gain, merge_weight, merge_bias, page_grid):
    band = qkv_rows.shape[1]
    patches = band * ROWS
    groups = patches // 4
    units = merge_weight.shape[0]
    depth = out_weight.shape[0]
    piece = patches + groups

    *sends, own, grid = kernel(
        spread_kernel,
        "spread",
        [shape(band, 4 * HPAIR)] * ROWS + [shape(depth + depth // 4, WIDE), shape(8, WIDE, dtype=jnp.int32)],
        [
            pltpu.VMEM((band, 3 * D), BF16),
            pltpu.VMEM((band, D), BF16),
            pltpu.VMEM((depth, WIDE), BF16),
            pltpu.VMEM((ROWS, band, 4 * HPAIR), BF16),
            pltpu.SMEM(page_grid.shape, jnp.int32),
            pltpu.SemaphoreType.DMA((5,)),
        ],
        fetched=range(4),
        count=4,
        limit=24,
        moved=1 << 20,
    )(in_hbm(qkv_rows), in_hbm(residual), in_hbm(out_weight), in_hbm(page_grid))
    blocks = [sends[0]] + [swap(sends[step], step) for step in BLOCK_ORDER[1:]]
    slices = [own] + [turn(own, step) for step in SHIFTS[1:]]
    select, dead, live = kernel(
        layout_kernel,
        "layout",
        [shape(patches, patches), shape(1, patches, dtype=F32), shape(1, groups, dtype=F32)],
        fetched=range(1, 1 + 3),
        count=1 + 3,
        moved=1 << 20,
    )(grid, *blocks[1:4])
    attn = kernel(
        attend_kernel,
        "attend",
        shape(piece, WIDE),
        [pltpu.VMEM((patches, HPAIR), BF16)] * 3,
        count=2 + ROWS,
        flops=20 * patches * patches * 4096,
        moved=1 << 20,
    )(select, dead, *blocks)
    resid, own_gain, main, tail = kernel(
        ready_kernel,
        "ready",
        [shape(patches, HPAIR, dtype=F32), shape(1, HPAIR, dtype=F32), shape(MAIN, HPAIR), shape(4, MAIN, HPAIR)],
        [pltpu.VMEM((patches, HPAIR), BF16), pltpu.VMEM((D,), F32), pltpu.SemaphoreType.DMA],
        fetched=(1, 2),
        count=2 + ROWS + PAGES,
        flops=10 * patches * patches * 4096,
        moved=4 << 20,
    )(select, in_hbm(norm_gain), attn, *blocks, *slices[:-1])
    last = kernel(
        last_kernel,
        "ready_last",
        [shape(2 * WIDE, HPAIR), shape(4, 2 * WIDE, HPAIR)],
        fetched=(1,),
        count=2,
        moved=4 << 20,
    )(slices[-1], main)
    pieces = gather_rows(attn, main, None, last[0])
    base = kernel(
        project_early_kernel,
        "project_early",
        shape(patches, HPAIR, dtype=F32),
        [pltpu.VMEM((piece, MAIN), BF16)],
        count=EARLY + 5,
        flops=4 * patches * MAIN * 4096,
        moved=4 << 20,
    )(*pieces[:EARLY], main, tail, *last, resid)
    hidden = kernel(
        project_kernel,
        "project",
        shape(piece + NOTES, WIDE),
        count=2 + 6,
        flops=patches * MAIN * 256,
        moved=4 << 20,
    )(*pieces[EARLY:], base, main, tail, *last, own_gain)
    ends, bias = kernel(
        tail_kernel,
        "merge_tail",
        [shape(units, MAIN), shape(units, 1, dtype=F32)],
        [pltpu.VMEM((units,), F32), pltpu.SemaphoreType.DMA],
        fetched=(1, 2),
        count=3,
        moved=4 << 20,
    )(merge_weight, in_hbm(merge_bias), hidden)
    first = [(row, row ^ (2 + 2 * (row % 2))) for row in range(ROWS)]
    second = [(row, row ^ (4 - 2 * (row % 2))) for row in range(ROWS)]
    one = lax.ppermute(hidden, "row", first)
    two = lax.ppermute(after(hidden, ends), "row", second)
    three = lax.ppermute(one, "row", second)
    near = [swap(hidden, 1), swap(one, 1), swap(two, 1)]
    early = kernel(
        merge_early_kernel,
        "merge_early",
        shape(4, units, groups, dtype=F32),
        count=5,
        flops=4 * units * groups * MAIN * 16,
        moved=8 << 20,
    )(hidden, one, near[0], near[1], merge_weight)
    near.append(swap(after(three, early), 1))
    return kernel(
        merge_kernel,
        "merge",
        shape(1, units, groups),
        [pltpu.VMEM((groups, MAIN), BF16)],
        count=ROWS + 5,
        flops=4 * units * groups * MAIN,
        moved=8 << 20,
    )(hidden, one, two, three, *near, early, merge_weight, ends, bias, live)


def solution(mesh):
    in_specs = (
        P("page", "row", None),
        P("page", "row", None),
        P("page", None),
        P(),
        P("row", None),
        P("row"),
        P("page", None),
    )
    out_specs = P("page", "row", None)
    local = local_eight if mesh.shape["row"] == 8 and mesh.shape["page"] == 4 else local_any
    return jax.shard_map(local, mesh=mesh, in_specs=in_specs, out_specs=out_specs, check_vma=False)
```

```python
import functools
import math

import jax
import jax.numpy as jnp
from jax import lax
from jax.experimental import pallas as pl
from jax.experimental.pallas import tpu as pltpu
from jax.sharding import PartitionSpec as P

D = 1280
HEADS = 16
HDIM = 80


def local_any(qkv_rows, residual, out_weight, norm_gain, merge_weight, merge_bias, page_grid):
    row_count = lax.axis_size("row")
    q_split = max(1, row_count // HEADS)
    head_groups = row_count // q_split
    width = D // head_groups
    heads_per = width // HDIM
    band_len = qkv_rows.shape[1]
    part_len = band_len // q_split
    local_qkv = qkv_rows[0]
    queries = local_qkv[:, :D]
    key_vals = jnp.concatenate(
        [
            local_qkv[:, D : 2 * D].reshape(band_len, head_groups, width),
            local_qkv[:, 2 * D :].reshape(band_len, head_groups, width),
        ],
        axis=2,
    )
    q_send = (
        queries.reshape(q_split, part_len, head_groups, width)
        .transpose(2, 0, 1, 3)
        .reshape(row_count, part_len, width)
    )
    kv_send = jnp.broadcast_to(
        key_vals.transpose(1, 0, 2)[:, None], (head_groups, q_split, band_len, 2 * width)
    )
    kv_send = kv_send.reshape(row_count, band_len, 2 * width)
    q_recv, kv_recv = (
        lax.all_to_all(q_send, "row", split_axis=0, concat_axis=1, tiled=True),
        lax.all_to_all(kv_send, "row", split_axis=0, concat_axis=1, tiled=True),
    )
    kv_local = kv_recv[0]
    positions = jnp.arange(row_count * band_len, dtype=jnp.int32)
    valid_len = page_grid[0, 0] * page_grid[0, 1]
    key_valid = positions < valid_len
    key_total = kv_local.shape[0]
    key_heads = kv_local[:, :width].reshape(key_total, heads_per, HDIM)
    value_heads = kv_local[:, width:].reshape(key_total, heads_per, HDIM)
    query_total = row_count * part_len
    q_block = math.gcd(query_total, 512)
    q_blocks = q_recv[0].reshape(query_total // q_block, q_block, heads_per, HDIM)
    root_dim = math.sqrt(HDIM)

    def attend(q_span):
        scores = (
            jnp.einsum("qhd,khd->hqk", q_span, key_heads, preferred_element_type=jnp.float32)
            / root_dim
        )
        scores = jnp.where(key_valid[None, None, :], scores, -1e30)
        peak = jnp.max(scores, axis=2, keepdims=True)
        weights = jnp.exp(scores - peak)
        total = jnp.sum(weights, axis=2, keepdims=True)
        mixed = (
            jnp.einsum(
                "hqk,khd->hqd",
                weights.astype(jnp.bfloat16),
                value_heads,
                preferred_element_type=jnp.float32,
            )
            / total
        )
        return mixed.transpose(1, 0, 2).reshape(q_span.shape[0], width).astype(jnp.bfloat16)

    attn_heads = lax.map(attend, q_blocks).reshape(row_count, part_len, width)
    returned = lax.all_to_all(attn_heads, "row", split_axis=0, concat_axis=0, tiled=True)
    attn = (
        returned.reshape(head_groups, q_split, part_len, width)
        .transpose(1, 2, 0, 3)
        .reshape(band_len, D)
    )
    projected = jnp.dot(
        attn,
        lax.all_gather(out_weight, "page", axis=0, tiled=True),
        preferred_element_type=jnp.float32,
    )
    hidden = residual[0].astype(jnp.float32) + projected
    normed = (
        hidden * lax.rsqrt(jnp.mean(hidden * hidden, axis=1, keepdims=True) + 1e-06) * norm_gain
    ).astype(jnp.bfloat16)
    rows_n = page_grid[0, 0]
    cols_n = page_grid[0, 1]
    group_total = band_len * row_count // 4
    slots = jnp.arange(group_total, dtype=jnp.int32)
    half_cols = cols_n // 2
    live = slots < rows_n // 2 * half_cols
    first = jnp.where(live, 2 * (slots // half_cols) * cols_n + 2 * (slots % half_cols), 0)
    corners = [first, first + 1, first + cols_n, first + cols_n + 1]
    local_units = merge_weight.shape[0]
    page_all = lax.all_gather(normed, "row", axis=0, tiled=True)
    merged_sum = jnp.zeros((local_units, group_total), jnp.float32)
    for corner in range(4):
        picked = jnp.take(page_all, corners[corner], axis=0)
        merged_sum = merged_sum + jnp.einsum(
            "md,gd->mg",
            merge_weight[:, corner * D : (corner + 1) * D],
            picked,
            preferred_element_type=jnp.float32,
        )
    merged = jax.nn.gelu(merged_sum + merge_bias[:, None], approximate=False)
    merged = jnp.where(live[None, :], merged, 0.0).astype(jnp.bfloat16)
    return merged[None]


ROWS = 8
PAGES = 4
HPAIR = 2 * HDIM
WIDE = 128
REST = HPAIR - WIDE
MAIN = ROWS * WIDE
NOTES = 16
BLOCK_ORDER = (0, 2, 4, 6, 7, 3, 5, 1)
PIECE_ORDER = (0, 2, 4, 1, 3, 5, 6, 7)
EARLY = 6
SHIFTS = (0, 2, 1, 3)
ROOT = math.log2(math.e) / math.sqrt(HDIM)
BF16 = jnp.bfloat16
F32 = jnp.float32


def row_index():
    return lax.axis_index("row")


def pack_tail(wide):
    groups = wide.shape[0] // 4
    return jnp.concatenate([wide[at * groups : (at + 1) * groups] for at in range(4)], axis=1)


def spread_kernel(qkv_hbm, resid_hbm, weight_hbm, grid_hbm, *rest):
    outs = rest[:ROWS]
    slice_ref, grid_out, qkv, resid, tile, held, grid, sems = rest[ROWS:]
    me = row_index()
    depth = weight_hbm.shape[0]
    main = pl.ds(pl.multiple_of(me * WIDE, WIDE), WIDE)
    ends = pl.ds(pl.multiple_of(MAIN + me // 4 * WIDE, WIDE), WIDE)
    copies = [
        pltpu.make_async_copy(qkv_hbm.at[0], qkv, sems.at[0]),
        pltpu.make_async_copy(resid_hbm.at[0], resid, sems.at[1]),
        pltpu.make_async_copy(weight_hbm.at[:, main], slice_ref.at[:depth], sems.at[2]),
        pltpu.make_async_copy(weight_hbm.at[:, ends], tile, sems.at[3]),
        pltpu.make_async_copy(grid_hbm, grid, sems.at[4]),
    ]
    for copy in copies:
        copy.start()
    for copy in copies:
        copy.wait()
    for dest in range(ROWS):
        at = dest * HPAIR
        parts = [qkv[:, part * D + at : part * D + at + HPAIR] for part in range(3)]
        parts.append(resid[:, dest * WIDE : (dest + 1) * WIDE])
        parts.append(resid[:, MAIN + dest * REST : MAIN + (dest + 1) * REST])
        held[dest] = jnp.concatenate(parts, axis=1)
    for step in range(ROWS):
        outs[step][...] = held[me ^ step]
    tail = tile[:, :REST]
    for at in range(1, 4):
        tail = jnp.where(lax.rem(me, 4) == at, tile[:, at * REST : (at + 1) * REST], tail)
    slice_ref[depth:, :] = pack_tail(tail)
    row = lax.broadcasted_iota(jnp.int32, grid_out.shape, 0)
    grid_out[...] = jnp.where(row == 0, grid[0, 0], grid[0, 1])


def layout_kernel(grid_ref, *rest):
    select_ref, keys_ref, live_ref = rest[-3:]
    rows_n, cols_n = grid_ref[:1, :1], grid_ref[1:2, :1]
    patches = select_ref.shape[0]
    groups = patches // 4
    half = cols_n >> 1
    count = (rows_n >> 1) * half
    slots = lax.broadcasted_iota(jnp.int32, (groups, 1), 0)
    line = jnp.floor((slots.astype(F32) + 0.5) / half.astype(F32)).astype(jnp.int32)
    first = 2 * line * cols_n + 2 * (slots - line * half)
    at = lax.broadcasted_iota(jnp.int32, (groups, patches), 1)
    for corner in range(4):
        wanted = jnp.where(slots < count, first + (corner // 2) * cols_n + corner % 2, -1)
        select_ref[corner * groups : (corner + 1) * groups, :] = jnp.where(at == wanted, 1.0, 0.0).astype(BF16)
    key = lax.broadcasted_iota(jnp.int32, keys_ref.shape, 1)
    keys_ref[...] = jnp.where(key < rows_n * cols_n, 0.0, -1e30)
    slot = lax.broadcasted_iota(jnp.int32, live_ref.shape, 1)
    live_ref[...] = jnp.where(slot < count, 1.0, 0.0)


def attend_kernel(select_ref, dead_ref, *rest):
    blocks = rest[:ROWS]
    out_ref, q_all, k_all, v_all = rest[-4:]
    me = row_index()
    band = blocks[0].shape[0]
    patches = band * ROWS
    for step, block in zip(BLOCK_ORDER, blocks):
        at = pl.ds(pl.multiple_of((me ^ step) * band, band), band)
        q_all[at, :] = block[:, :HPAIR]
        k_all[at, :] = block[:, HPAIR : 2 * HPAIR]
        v_all[at, :] = block[:, 2 * HPAIR : 3 * HPAIR]
    queries = jnp.dot(select_ref[...], q_all[...], preferred_element_type=F32).astype(BF16)
    lane = lax.broadcasted_iota(jnp.int32, (1, HPAIR), 1)
    keys, values, dead = k_all[...], v_all[...], dead_ref[...]
    mixed = []
    for head in range(2):
        mine = (lane >= head * HDIM) & (lane < (head + 1) * HDIM)
        asked = jnp.where(mine, queries, jnp.zeros_like(queries))
        scores = lax.dot_general(asked, keys, (((1,), (1,)), ((), ())), preferred_element_type=F32) + dead
        weights = jnp.exp2((scores - jnp.max(scores, axis=1, keepdims=True)) * ROOT)
        total = jnp.sum(weights, axis=1, keepdims=True)
        mixed.append(jnp.dot(weights.astype(BF16), values, preferred_element_type=F32) / total)
    attn = jnp.where(lane < HDIM, mixed[0], mixed[1])
    out_ref[:patches, :] = attn[:, :WIDE].astype(BF16)
    out_ref[patches:, :] = pack_tail(attn[:, WIDE:]).astype(BF16)


def weight_rows(cut):
    depth = 2 * HPAIR
    packed = cut[depth:]
    tail = jnp.concatenate([packed[:, at * REST : (at + 1) * REST] for at in range(4)], axis=0)
    whole = jnp.concatenate([cut[:depth], tail], axis=1)
    return [whole[core * HPAIR : (core + 1) * HPAIR] for core in range(2)]


def place_rows(rows, base, main_ref, tail_ref):
    for core in range(2):
        pair = base + core
        main_ref[pl.ds(pl.multiple_of(pair * WIDE, WIDE), WIDE), :] = rows[core][:WIDE]
        for corner in range(4):
            spot = pl.multiple_of(pair * WIDE + corner * REST, REST)
            tail_ref[corner, pl.ds(spot, REST), :] = rows[core][WIDE:]


def ready_kernel(select_ref, gain_hbm, token_ref, *rest):
    del token_ref
    blocks, slices = rest[:ROWS], rest[ROWS : ROWS + PAGES - 1]
    resid_ref, gain_out, main_ref, tail_ref, held, line, sem = rest[-7:]
    fetch = pltpu.make_async_copy(gain_hbm, line, sem)
    fetch.start()
    me = row_index()
    page = lax.axis_index("page")
    band = blocks[0].shape[0]
    for step, block in zip(BLOCK_ORDER, blocks):
        at = pl.ds(pl.multiple_of((me ^ step) * band, band), band)
        held[at, :] = block[:, 3 * HPAIR :]
    resid_ref[...] = jnp.dot(select_ref[...], held[...], preferred_element_type=F32)
    main_ref[...] = jnp.zeros_like(main_ref)
    tail_ref[...] = jnp.zeros_like(tail_ref)
    for step, cut in zip(SHIFTS, slices):
        source = lax.rem(page + PAGES - step, PAGES)
        place_rows(weight_rows(cut), 2 * source, main_ref, tail_ref)
    fetch.wait()
    whole = line[...].reshape(1, D)
    gain = jnp.zeros(gain_out.shape, F32)
    for pair in range(ROWS):
        parts = [whole[:, pair * WIDE : (pair + 1) * WIDE]]
        parts.append(whole[:, MAIN + pair * REST : MAIN + (pair + 1) * REST])
        gain = jnp.where(me == pair, jnp.concatenate(parts, axis=1), gain)
    gain_out[...] = gain


def last_kernel(cut_ref, token_ref, main_ref, tail_ref):
    del token_ref
    tail_ref[...] = jnp.zeros_like(tail_ref)
    place_rows(weight_rows(cut_ref), 0, main_ref, tail_ref)


def far_block():
    me = row_index()
    return pl.ds(pl.multiple_of((me // 2 ^ 3) * 2 * WIDE, 2 * WIDE), 2 * WIDE)


def collect_early(pieces, full):
    me = row_index()
    full[:, far_block()] = jnp.zeros((full.shape[0], 2 * WIDE), BF16)
    for step, piece in zip(PIECE_ORDER[:EARLY], pieces):
        full[:, pl.ds(pl.multiple_of((me ^ step) * WIDE, WIDE), WIDE)] = piece[...]


def collect_late(same, other):
    core = row_index() % 2
    left = jnp.where(core == 0, same[...], other[...])
    right = jnp.where(core == 0, other[...], same[...])
    return jnp.concatenate([left, right], axis=1)


def late_source():
    return lax.rem(lax.axis_index("page") + PAGES - SHIFTS[-1], PAGES)


def project_early_kernel(*rest):
    pieces = rest[:EARLY]
    main_ref, tail_ref, last_main_ref, last_tail_ref, resid_ref, out_ref, full = rest[EARLY:]
    collect_early(pieces, full)
    patches = resid_ref.shape[0]
    groups = patches // 4
    late = pl.ds(pl.multiple_of(late_source() * 2 * WIDE, 2 * WIDE), 2 * WIDE)
    base = jnp.dot(full[:patches], main_ref[...], preferred_element_type=F32) + resid_ref[...]
    base = base + jnp.dot(full[:patches, late], last_main_ref[...], preferred_element_type=F32)
    for corner in range(4):
        span = slice(corner * groups, (corner + 1) * groups)
        part = jnp.dot(full[patches:], tail_ref[corner], preferred_element_type=F32)
        part = part + jnp.dot(full[patches:, late], last_tail_ref[corner], preferred_element_type=F32)
        out_ref[span, :] = base[span] + part


def piece_rows(refs, what, groups):
    order = (0, 1, "ends", 2, 3, "notes")
    at = order.index(what) * groups
    size = NOTES if what == "notes" else groups
    if len(refs) == 2 and at >= 3 * groups:
        return refs[1], slice(at - 3 * groups, at - 3 * groups + size)
    return refs[0], slice(at, at + size)


def piece_part(refs, what, groups):
    ref, span = piece_rows(refs, what, groups)
    return ref[span, :]


def project_kernel(*rest):
    same, other, base_ref, main_ref, tail_ref, last_main_ref, last_tail_ref, gain_ref, out_ref, *halves = rest
    patches = base_ref.shape[0]
    groups = patches // 4

    def put(what, rows):
        for refs in ([out_ref], halves):
            ref, span = piece_rows(refs, what, groups)
            ref[span, :] = rows.astype(BF16)

    block = far_block()
    is_last = late_source() == (row_index() // 2 ^ 3)
    full = collect_late(same, other)
    main = jnp.where(is_last, last_main_ref[...], main_ref[block, :])
    base = base_ref[...] + jnp.dot(full[:patches], main, preferred_element_type=F32)
    ones = jnp.ones((NOTES, HPAIR), BF16)
    contract = (((1,), (1,)), ((), ()))
    row = lax.broadcasted_iota(jnp.int32, (NOTES, groups), 0)
    notes = jnp.zeros((NOTES, groups), F32)
    ends = []
    for corner in range(4):
        span = slice(corner * groups, (corner + 1) * groups)
        tail = jnp.where(is_last, last_tail_ref[corner], tail_ref[corner, block, :])
        hidden = base[span] + jnp.dot(full[patches:], tail, preferred_element_type=F32)
        square = hidden * hidden
        high = square.astype(BF16)
        low = (square - high.astype(F32)).astype(BF16)
        total = lax.dot_general(ones, high, contract, preferred_element_type=F32)
        total = total + lax.dot_general(ones, low, contract, preferred_element_type=F32)
        coarse = total.astype(BF16).astype(F32)
        notes = jnp.where(row == corner, coarse, jnp.where(row == 4 + corner, total - coarse, notes))
        sent = hidden * gain_ref[...]
        put(corner, sent[:, :WIDE])
        ends.append(sent[:, WIDE:])
    put("ends", jnp.concatenate(ends, axis=1))
    put("notes", notes)


def tail_kernel(weight_ref, bias_hbm, token_ref, out_ref, bias_out, line, sem):
    del token_ref
    fetch = pltpu.make_async_copy(bias_hbm, line, sem)
    fetch.start()
    for pair in range(ROWS):
        cut = [corner * D + MAIN + pair * REST for corner in range(4)]
        out_ref[:, pair * WIDE : (pair + 1) * WIDE] = jnp.concatenate(
            [weight_ref[:, at : at + REST] for at in cut], axis=1
        )
    fetch.wait()
    units = bias_out.shape[0]
    bias_out[...] = jnp.broadcast_to(line[...].reshape(1, units), (8, units)).T[:, :1]


def piece_steps():
    core = row_index() % 2
    first, second = 2 + 2 * core, 4 - 2 * core
    return [0, first, second, 6, 1, 1 ^ second, 1 ^ first, 7]


def merge_product(weight_ref, corner, groups, pieces):
    me = row_index()
    at = [pl.multiple_of(corner * D + (me ^ step) * WIDE, WIDE) for step, _ in pieces]
    return lax.dot_general(
        jnp.concatenate([weight_ref[:, pl.ds(spot, WIDE)] for spot in at], axis=1),
        jnp.concatenate([piece_part(refs, corner, groups) for _, refs in pieces], axis=1),
        (((1,), (1,)), ((), ())),
        preferred_element_type=F32,
    )


def merge_early_kernel(*rest):
    own, near_own, one, near_one = rest[:1], rest[1:2], rest[2:4], rest[4:6]
    weight_ref, out_ref = rest[6:]
    steps = piece_steps()
    groups = out_ref.shape[2]
    for corner in range(4):
        out_ref[corner] = merge_product(
            weight_ref, corner, groups, [(steps[0], own), (steps[4], near_own)]
        ) + merge_product(weight_ref, corner, groups, [(steps[1], one), (steps[5], near_one)])


def merge_kernel(*rest):
    pieces, rest = [], list(rest)
    for count in (1, 2, 1, 2, 1, 2, 1, 2):
        pieces.append(rest[:count])
        del rest[:count]
    early_ref, weight_ref, tail_ref, bias_ref, live_ref, out_ref, ends_ref = rest
    me = row_index()
    groups = live_ref.shape[1]
    notes = jnp.zeros((NOTES, groups), F32)
    steps = piece_steps()
    for step, refs in zip(steps, pieces):
        ends_ref[:, pl.ds(pl.multiple_of((me ^ step) * WIDE, WIDE), WIDE)] = piece_part(refs, "ends", groups)
        notes = notes + piece_part(refs, "notes", groups).astype(F32)
    late = [[(steps[at], pieces[at]) for at in couple] for couple in ((2, 6), (3, 7))]
    scale = lax.rsqrt((notes[:4] + notes[4:8]) * (1.0 / D) + 1e-06)
    total = jnp.zeros(bias_ref.shape[:1] + (groups,), F32)
    for corner in range(4):
        part = early_ref[corner]
        for couple in late:
            part = part + merge_product(weight_ref, corner, groups, couple)
        total = total + scale[corner : corner + 1] * part
    spread = jnp.concatenate([jnp.broadcast_to(scale[at : at + 1], (REST, groups)) for at in range(4)], axis=0).T
    ends = ends_ref[...].astype(F32) * jnp.concatenate([spread] * ROWS, axis=1)
    total = total + lax.dot_general(
        tail_ref[...], ends.astype(BF16), (((1,), (1,)), ((), ())), preferred_element_type=F32
    )
    total = total + bias_ref[...]
    merged = 0.5 * total * (1.0 + lax.erf(total * math.sqrt(0.5)))
    out_ref[0] = jnp.where(live_ref[...] > 0.0, merged, 0.0).astype(BF16)


def kernel(body, name, out_shape, scratch=(), fetched=(), count=0, limit=24, flops=0, moved=0):
    specs = [pl.BlockSpec(memory_space=pltpu.VMEM) for _ in range(count)]
    for at in fetched:
        specs[at] = pl.BlockSpec(memory_space=pl.ANY)
    return pl.pallas_call(
        body,
        out_shape=out_shape,
        in_specs=specs,
        out_specs=jax.tree.map(lambda _: pl.BlockSpec(memory_space=pltpu.VMEM), out_shape),
        scratch_shapes=list(scratch),
        compiler_params=pltpu.CompilerParams(vmem_limit_bytes=limit * 1024 * 1024),
        cost_estimate=pl.CostEstimate(flops=flops, bytes_accessed=moved, transcendentals=0),
        name=name,
    )


def in_hbm(value):
    return pltpu.with_memory_space_constraint(value, pltpu.HBM)


def shape(*dims, dtype=BF16):
    return jax.ShapeDtypeStruct(dims, dtype)


def swap(value, step):
    return lax.ppermute(value, "row", [(row, row ^ step) for row in range(ROWS)])


def turn(value, step):
    return lax.ppermute(value, "page", [(page, (page + step) % PAGES) for page in range(PAGES)])


def gather_rows(value, *early):
    far = [swap(value, step) for step in (2, 4, 6)]
    passed = [value] + far
    for at, array in enumerate(early):
        if array is not None:
            passed[at] = lax.optimization_barrier((passed[at], array))[0]
    near = [swap(piece, 1) for piece in passed]
    return [value, far[0], far[1], near[0], near[1], near[2], far[2], near[3]]


def after(value, *arrays):
    return lax.optimization_barrier((value, *arrays))[0]


def local_eight(qkv_rows, residual, out_weight, norm_gain, merge_weight, merge_bias, page_grid):
    band = qkv_rows.shape[1]
    patches = band * ROWS
    groups = patches // 4
    units = merge_weight.shape[0]
    depth = out_weight.shape[0]
    piece = patches + groups

    *sends, own, grid = kernel(
        spread_kernel,
        "spread",
        [shape(band, 4 * HPAIR)] * ROWS + [shape(depth + depth // 4, WIDE), shape(8, WIDE, dtype=jnp.int32)],
        [
            pltpu.VMEM((band, 3 * D), BF16),
            pltpu.VMEM((band, D), BF16),
            pltpu.VMEM((depth, WIDE), BF16),
            pltpu.VMEM((ROWS, band, 4 * HPAIR), BF16),
            pltpu.SMEM(page_grid.shape, jnp.int32),
            pltpu.SemaphoreType.DMA((5,)),
        ],
        fetched=range(4),
        count=4,
        limit=24,
        moved=1 << 20,
    )(in_hbm(qkv_rows), in_hbm(residual), in_hbm(out_weight), in_hbm(page_grid))
    blocks = [sends[0]] + [swap(sends[step], step) for step in BLOCK_ORDER[1:]]
    slices = [own] + [turn(own, step) for step in SHIFTS[1:]]
    select, dead, live = kernel(
        layout_kernel,
        "layout",
        [shape(patches, patches), shape(1, patches, dtype=F32), shape(1, groups, dtype=F32)],
        fetched=range(1, 1 + 3),
        count=1 + 3,
        moved=1 << 20,
    )(grid, *blocks[1:4])
    attn = kernel(
        attend_kernel,
        "attend",
        shape(piece, WIDE),
        [pltpu.VMEM((patches, HPAIR), BF16)] * 3,
        count=2 + ROWS,
        flops=20 * patches * patches * 4096,
        moved=1 << 20,
    )(select, dead, *blocks)
    resid, own_gain, main, tail = kernel(
        ready_kernel,
        "ready",
        [shape(patches, HPAIR, dtype=F32), shape(1, HPAIR, dtype=F32), shape(MAIN, HPAIR), shape(4, MAIN, HPAIR)],
        [pltpu.VMEM((patches, HPAIR), BF16), pltpu.VMEM((D,), F32), pltpu.SemaphoreType.DMA],
        fetched=(1, 2),
        count=2 + ROWS + PAGES,
        flops=10 * patches * patches * 4096,
        moved=4 << 20,
    )(select, in_hbm(norm_gain), attn, *blocks, *slices[:-1])
    last = kernel(
        last_kernel,
        "ready_last",
        [shape(2 * WIDE, HPAIR), shape(4, 2 * WIDE, HPAIR)],
        fetched=(1,),
        count=2,
        moved=4 << 20,
    )(slices[-1], main)
    pieces = gather_rows(attn, main, None, last[0])
    base = kernel(
        project_early_kernel,
        "project_early",
        shape(patches, HPAIR, dtype=F32),
        [pltpu.VMEM((piece, MAIN), BF16)],
        count=EARLY + 5,
        flops=4 * patches * MAIN * 4096,
        moved=4 << 20,
    )(*pieces[:EARLY], main, tail, *last, resid)
    hidden, *halves = kernel(
        project_kernel,
        "project",
        [shape(piece + NOTES, WIDE), shape(3 * groups, WIDE), shape(2 * groups + NOTES, WIDE)],
        count=2 + 6,
        flops=patches * MAIN * 256,
        moved=4 << 20,
    )(*pieces[EARLY:], base, main, tail, *last, own_gain)
    ends, bias = kernel(
        tail_kernel,
        "merge_tail",
        [shape(units, MAIN), shape(units, 1, dtype=F32)],
        [pltpu.VMEM((units,), F32), pltpu.SemaphoreType.DMA],
        fetched=(1, 2),
        count=3,
        moved=4 << 20,
    )(merge_weight, in_hbm(merge_bias), hidden)
    first = [(row, row ^ (2 + 2 * (row % 2))) for row in range(ROWS)]
    second = [(row, row ^ (4 - 2 * (row % 2))) for row in range(ROWS)]
    one = [lax.ppermute(half, "row", first) for half in halves]
    two = lax.ppermute(hidden, "row", second)
    three = [lax.ppermute(half, "row", second) for half in one]
    near = [[swap(after(hidden, one[1], ends), 1)], [swap(after(half, three[1]), 1) for half in one], [swap(after(two, three[1]), 1)]]
    early = kernel(
        merge_early_kernel,
        "merge_early",
        shape(4, units, groups, dtype=F32),
        count=7,
        flops=1000,
        moved=8 << 20,
    )(hidden, *near[0], *one, *near[1], merge_weight)
    near.append([swap(half, 1) for half in three])
    return kernel(
        merge_kernel,
        "merge",
        shape(1, units, groups),
        [pltpu.VMEM((groups, MAIN), BF16)],
        count=12 + 5,
        flops=4 * units * groups * MAIN,
        moved=8 << 20,
    )(hidden, *one, two, *three, *sum(near, []), early, merge_weight, ends, bias, live)


def solution(mesh):
    in_specs = (
        P("page", "row", None),
        P("page", "row", None),
        P("page", None),
        P(),
        P("row", None),
        P("row"),
        P("page", None),
    )
    out_specs = P("page", "row", None)
    local = local_eight if mesh.shape["row"] == 8 and mesh.shape["page"] == 4 else local_any
    return jax.shard_map(local, mesh=mesh, in_specs=in_specs, out_specs=out_specs, check_vma=False)
```

```python
import functools
import math

import jax
import jax.numpy as jnp
from jax import lax
from jax.experimental import pallas as pl
from jax.experimental.pallas import tpu as pltpu
from jax.sharding import PartitionSpec as P

D = 1280
HEADS = 16
HDIM = 80


def local_any(qkv_rows, residual, out_weight, norm_gain, merge_weight, merge_bias, page_grid):
    row_count = lax.axis_size("row")
    q_split = max(1, row_count // HEADS)
    head_groups = row_count // q_split
    width = D // head_groups
    heads_per = width // HDIM
    band_len = qkv_rows.shape[1]
    part_len = band_len // q_split
    local_qkv = qkv_rows[0]
    queries = local_qkv[:, :D]
    key_vals = jnp.concatenate(
        [
            local_qkv[:, D : 2 * D].reshape(band_len, head_groups, width),
            local_qkv[:, 2 * D :].reshape(band_len, head_groups, width),
        ],
        axis=2,
    )
    q_send = (
        queries.reshape(q_split, part_len, head_groups, width)
        .transpose(2, 0, 1, 3)
        .reshape(row_count, part_len, width)
    )
    kv_send = jnp.broadcast_to(
        key_vals.transpose(1, 0, 2)[:, None], (head_groups, q_split, band_len, 2 * width)
    )
    kv_send = kv_send.reshape(row_count, band_len, 2 * width)
    q_recv, kv_recv = (
        lax.all_to_all(q_send, "row", split_axis=0, concat_axis=1, tiled=True),
        lax.all_to_all(kv_send, "row", split_axis=0, concat_axis=1, tiled=True),
    )
    kv_local = kv_recv[0]
    positions = jnp.arange(row_count * band_len, dtype=jnp.int32)
    valid_len = page_grid[0, 0] * page_grid[0, 1]
    key_valid = positions < valid_len
    key_total = kv_local.shape[0]
    key_heads = kv_local[:, :width].reshape(key_total, heads_per, HDIM)
    value_heads = kv_local[:, width:].reshape(key_total, heads_per, HDIM)
    query_total = row_count * part_len
    q_block = math.gcd(query_total, 512)
    q_blocks = q_recv[0].reshape(query_total // q_block, q_block, heads_per, HDIM)
    root_dim = math.sqrt(HDIM)

    def attend(q_span):
        scores = (
            jnp.einsum("qhd,khd->hqk", q_span, key_heads, preferred_element_type=jnp.float32)
            / root_dim
        )
        scores = jnp.where(key_valid[None, None, :], scores, -1e30)
        peak = jnp.max(scores, axis=2, keepdims=True)
        weights = jnp.exp(scores - peak)
        total = jnp.sum(weights, axis=2, keepdims=True)
        mixed = (
            jnp.einsum(
                "hqk,khd->hqd",
                weights.astype(jnp.bfloat16),
                value_heads,
                preferred_element_type=jnp.float32,
            )
            / total
        )
        return mixed.transpose(1, 0, 2).reshape(q_span.shape[0], width).astype(jnp.bfloat16)

    attn_heads = lax.map(attend, q_blocks).reshape(row_count, part_len, width)
    returned = lax.all_to_all(attn_heads, "row", split_axis=0, concat_axis=0, tiled=True)
    attn = (
        returned.reshape(head_groups, q_split, part_len, width)
        .transpose(1, 2, 0, 3)
        .reshape(band_len, D)
    )
    projected = jnp.dot(
        attn,
        lax.all_gather(out_weight, "page", axis=0, tiled=True),
        preferred_element_type=jnp.float32,
    )
    hidden = residual[0].astype(jnp.float32) + projected
    normed = (
        hidden * lax.rsqrt(jnp.mean(hidden * hidden, axis=1, keepdims=True) + 1e-06) * norm_gain
    ).astype(jnp.bfloat16)
    rows_n = page_grid[0, 0]
    cols_n = page_grid[0, 1]
    group_total = band_len * row_count // 4
    slots = jnp.arange(group_total, dtype=jnp.int32)
    half_cols = cols_n // 2
    live = slots < rows_n // 2 * half_cols
    first = jnp.where(live, 2 * (slots // half_cols) * cols_n + 2 * (slots % half_cols), 0)
    corners = [first, first + 1, first + cols_n, first + cols_n + 1]
    local_units = merge_weight.shape[0]
    page_all = lax.all_gather(normed, "row", axis=0, tiled=True)
    merged_sum = jnp.zeros((local_units, group_total), jnp.float32)
    for corner in range(4):
        picked = jnp.take(page_all, corners[corner], axis=0)
        merged_sum = merged_sum + jnp.einsum(
            "md,gd->mg",
            merge_weight[:, corner * D : (corner + 1) * D],
            picked,
            preferred_element_type=jnp.float32,
        )
    merged = jax.nn.gelu(merged_sum + merge_bias[:, None], approximate=False)
    merged = jnp.where(live[None, :], merged, 0.0).astype(jnp.bfloat16)
    return merged[None]


ROWS = 8
PAGES = 4
HPAIR = 2 * HDIM
WIDE = 128
REST = HPAIR - WIDE
MAIN = ROWS * WIDE
NOTES = 16
BLOCK_ORDER = (0, 2, 4, 6, 7, 3, 5, 1)
PIECE_ORDER = (0, 2, 4, 1, 3, 5, 6, 7)
EARLY = 6
ROOT = math.log2(math.e) / math.sqrt(HDIM)
BF16 = jnp.bfloat16
F32 = jnp.float32


def row_index():
    return lax.axis_index("row")


def pack_tail(wide):
    groups = wide.shape[0] // 4
    return jnp.concatenate([wide[at * groups : (at + 1) * groups] for at in range(4)], axis=1)


def spread_kernel(qkv_hbm, resid_hbm, weight_hbm, grid_hbm, *rest):
    outs = rest[:ROWS]
    chip_ref, slice_ref, grid_out, qkv, resid, main, tile, held, grid, sems = rest[ROWS:]
    me = row_index()
    depth = weight_hbm.shape[0]
    chip = pl.ds(pl.multiple_of(me // 2 * 2 * WIDE, 2 * WIDE), 2 * WIDE)
    ends = pl.ds(pl.multiple_of(MAIN + me // 4 * WIDE, WIDE), WIDE)
    copies = [
        pltpu.make_async_copy(qkv_hbm.at[0], qkv, sems.at[0]),
        pltpu.make_async_copy(resid_hbm.at[0], resid, sems.at[1]),
        pltpu.make_async_copy(weight_hbm.at[:, chip], main, sems.at[2]),
        pltpu.make_async_copy(weight_hbm.at[:, ends], tile, sems.at[3]),
        pltpu.make_async_copy(grid_hbm, grid, sems.at[4]),
    ]
    for copy in copies:
        copy.start()
    for copy in copies:
        copy.wait()
    for dest in range(ROWS):
        at = dest * HPAIR
        parts = [qkv[:, part * D + at : part * D + at + HPAIR] for part in range(3)]
        parts.append(resid[:, dest * WIDE : (dest + 1) * WIDE])
        parts.append(resid[:, MAIN + dest * REST : MAIN + (dest + 1) * REST])
        held[dest] = jnp.concatenate(parts, axis=1)
    for step in range(ROWS):
        outs[step][...] = held[me ^ step]
    low = me // 2 % 2 == 0
    size = depth + depth // 4
    for core in range(2):
        tail = jnp.where(low, tile[:, core * REST : (core + 1) * REST], tile[:, (core + 2) * REST : (core + 3) * REST])
        chip_ref[core * size : core * size + depth, :] = main[:, core * WIDE : (core + 1) * WIDE]
        chip_ref[core * size + depth : (core + 1) * size, :] = pack_tail(tail)
    slice_ref[...] = chip_ref[pl.ds(pl.multiple_of(me % 2 * size, 16), size), :]
    row = lax.broadcasted_iota(jnp.int32, grid_out.shape, 0)
    grid_out[...] = jnp.where(row == 0, grid[0, 0], grid[0, 1])


def layout_kernel(grid_ref, *rest):
    select_ref, keys_ref, live_ref = rest[-3:]
    rows_n, cols_n = grid_ref[:1, :1], grid_ref[1:2, :1]
    patches = select_ref.shape[0]
    groups = patches // 4
    half = cols_n >> 1
    count = (rows_n >> 1) * half
    slots = lax.broadcasted_iota(jnp.int32, (groups, 1), 0)
    line = jnp.floor((slots.astype(F32) + 0.5) / half.astype(F32)).astype(jnp.int32)
    first = 2 * line * cols_n + 2 * (slots - line * half)
    at = lax.broadcasted_iota(jnp.int32, (groups, patches), 1)
    for corner in range(4):
        wanted = jnp.where(slots < count, first + (corner // 2) * cols_n + corner % 2, -1)
        select_ref[corner * groups : (corner + 1) * groups, :] = jnp.where(at == wanted, 1.0, 0.0).astype(BF16)
    key = lax.broadcasted_iota(jnp.int32, keys_ref.shape, 1)
    keys_ref[...] = jnp.where(key < rows_n * cols_n, 0.0, -1e30)
    slot = lax.broadcasted_iota(jnp.int32, live_ref.shape, 1)
    live_ref[...] = jnp.where(slot < count, 1.0, 0.0)


def attend_kernel(select_ref, dead_ref, *rest):
    blocks = rest[:ROWS]
    out_ref, q_all, k_all, v_all = rest[-4:]
    me = row_index()
    band = blocks[0].shape[0]
    patches = band * ROWS
    for step, block in zip(BLOCK_ORDER, blocks):
        at = pl.ds(pl.multiple_of((me ^ step) * band, band), band)
        q_all[at, :] = block[:, :HPAIR]
        k_all[at, :] = block[:, HPAIR : 2 * HPAIR]
        v_all[at, :] = block[:, 2 * HPAIR : 3 * HPAIR]
    queries = jnp.dot(select_ref[...], q_all[...], preferred_element_type=F32).astype(BF16)
    lane = lax.broadcasted_iota(jnp.int32, (1, HPAIR), 1)
    keys, values, dead = k_all[...], v_all[...], dead_ref[...]
    mixed = []
    for head in range(2):
        mine = (lane >= head * HDIM) & (lane < (head + 1) * HDIM)
        asked = jnp.where(mine, queries, jnp.zeros_like(queries))
        scores = lax.dot_general(asked, keys, (((1,), (1,)), ((), ())), preferred_element_type=F32) + dead
        weights = jnp.exp2((scores - jnp.max(scores, axis=1, keepdims=True)) * ROOT)
        total = jnp.sum(weights, axis=1, keepdims=True)
        mixed.append(jnp.dot(weights.astype(BF16), values, preferred_element_type=F32) / total)
    attn = jnp.where(lane < HDIM, mixed[0], mixed[1])
    out_ref[:patches, :] = attn[:, :WIDE].astype(BF16)
    out_ref[patches:, :] = pack_tail(attn[:, WIDE:]).astype(BF16)


def weight_rows(cut):
    depth = 2 * HPAIR
    packed = cut[depth:]
    tail = jnp.concatenate([packed[:, at * REST : (at + 1) * REST] for at in range(4)], axis=0)
    whole = jnp.concatenate([cut[:depth], tail], axis=1)
    return [whole[core * HPAIR : (core + 1) * HPAIR] for core in range(2)]


def place_rows(rows, base, main_ref, tail_ref):
    for core in range(2):
        pair = base + core
        main_ref[pl.ds(pl.multiple_of(pair * WIDE, WIDE), WIDE), :] = rows[core][:WIDE]
        for corner in range(4):
            spot = pl.multiple_of(pair * WIDE + corner * REST, REST)
            tail_ref[corner, pl.ds(spot, REST), :] = rows[core][WIDE:]


def ready_kernel(select_ref, gain_hbm, token_ref, *rest):
    del token_ref
    blocks = rest[:ROWS]
    own_ref, across_ref, near_ref = rest[ROWS : ROWS + 3]
    resid_ref, gain_out, main_ref, tail_ref, held, line, sem = rest[-7:]
    fetch = pltpu.make_async_copy(gain_hbm, line, sem)
    fetch.start()
    me = row_index()
    page = lax.axis_index("page")
    band = blocks[0].shape[0]
    for step, block in zip(BLOCK_ORDER, blocks):
        at = pl.ds(pl.multiple_of((me ^ step) * band, band), band)
        held[at, :] = block[:, 3 * HPAIR :]
    resid_ref[...] = jnp.dot(select_ref[...], held[...], preferred_element_type=F32)
    main_ref[...] = jnp.zeros_like(main_ref)
    tail_ref[...] = jnp.zeros_like(tail_ref)
    core = me % 2
    size = own_ref.shape[0]
    half = pl.ds(pl.multiple_of(core * size, 16), size)
    cuts = ((0, own_ref[...]), (2, across_ref[...]), (3 - 2 * core, near_ref[half, :]))
    for step, cut in cuts:
        place_rows(weight_rows(cut), 2 * lax.rem(page + step, PAGES), main_ref, tail_ref)
    fetch.wait()
    whole = line[...].reshape(1, D)
    gain = jnp.zeros(gain_out.shape, F32)
    for pair in range(ROWS):
        parts = [whole[:, pair * WIDE : (pair + 1) * WIDE]]
        parts.append(whole[:, MAIN + pair * REST : MAIN + (pair + 1) * REST])
        gain = jnp.where(me == pair, jnp.concatenate(parts, axis=1), gain)
    gain_out[...] = gain


def last_kernel(swapped_ref, token_ref, main_ref, tail_ref):
    del token_ref
    size = swapped_ref.shape[0] // 2
    cut = swapped_ref[pl.ds(pl.multiple_of(row_index() % 2 * size, 16), size), :]
    tail_ref[...] = jnp.zeros_like(tail_ref)
    place_rows(weight_rows(cut), 0, main_ref, tail_ref)


def far_block():
    me = row_index()
    return pl.ds(pl.multiple_of((me // 2 ^ 3) * 2 * WIDE, 2 * WIDE), 2 * WIDE)


def collect_early(pieces, full):
    me = row_index()
    full[:, far_block()] = jnp.zeros((full.shape[0], 2 * WIDE), BF16)
    for step, piece in zip(PIECE_ORDER[:EARLY], pieces):
        full[:, pl.ds(pl.multiple_of((me ^ step) * WIDE, WIDE), WIDE)] = piece[...]


def collect_late(same, other):
    core = row_index() % 2
    left = jnp.where(core == 0, same[...], other[...])
    right = jnp.where(core == 0, other[...], same[...])
    return jnp.concatenate([left, right], axis=1)


def late_source():
    return lax.rem(lax.axis_index("page") + 1 + 2 * (row_index() % 2), PAGES)


def project_early_kernel(*rest):
    pieces = rest[:EARLY]
    main_ref, tail_ref, last_main_ref, last_tail_ref, resid_ref, out_ref, full = rest[EARLY:]
    collect_early(pieces, full)
    patches = resid_ref.shape[0]
    groups = patches // 4
    late = pl.ds(pl.multiple_of(late_source() * 2 * WIDE, 2 * WIDE), 2 * WIDE)
    base = jnp.dot(full[:patches], main_ref[...], preferred_element_type=F32) + resid_ref[...]
    base = base + jnp.dot(full[:patches, late], last_main_ref[...], preferred_element_type=F32)
    for corner in range(4):
        span = slice(corner * groups, (corner + 1) * groups)
        part = jnp.dot(full[patches:], tail_ref[corner], preferred_element_type=F32)
        part = part + jnp.dot(full[patches:, late], last_tail_ref[corner], preferred_element_type=F32)
        out_ref[span, :] = base[span] + part


def project_kernel(*rest):
    same, other, base_ref, main_ref, tail_ref, last_main_ref, last_tail_ref, gain_ref, out_ref = rest
    patches = base_ref.shape[0]
    groups = patches // 4
    block = far_block()
    is_last = late_source() == (row_index() // 2 ^ 3)
    full = collect_late(same, other)
    main = jnp.where(is_last, last_main_ref[...], main_ref[block, :])
    base = base_ref[...] + jnp.dot(full[:patches], main, preferred_element_type=F32)
    ones = jnp.ones((NOTES, HPAIR), BF16)
    contract = (((1,), (1,)), ((), ()))
    row = lax.broadcasted_iota(jnp.int32, (NOTES, groups), 0)
    notes = jnp.zeros((NOTES, groups), F32)
    ends = []
    for corner in range(4):
        span = slice(corner * groups, (corner + 1) * groups)
        tail = jnp.where(is_last, last_tail_ref[corner], tail_ref[corner, block, :])
        hidden = base[span] + jnp.dot(full[patches:], tail, preferred_element_type=F32)
        square = hidden * hidden
        high = square.astype(BF16)
        low = (square - high.astype(F32)).astype(BF16)
        total = lax.dot_general(ones, high, contract, preferred_element_type=F32)
        total = total + lax.dot_general(ones, low, contract, preferred_element_type=F32)
        coarse = total.astype(BF16).astype(F32)
        notes = jnp.where(row == corner, coarse, jnp.where(row == 4 + corner, total - coarse, notes))
        sent = hidden * gain_ref[...]
        out_ref[span, :] = sent[:, :WIDE].astype(BF16)
        ends.append(sent[:, WIDE:])
    out_ref[patches : patches + groups, :] = jnp.concatenate(ends, axis=1).astype(BF16)
    out_ref[patches + groups :, :] = notes.astype(BF16)


def tail_kernel(weight_ref, bias_hbm, token_ref, out_ref, bias_out, line, sem):
    del token_ref
    fetch = pltpu.make_async_copy(bias_hbm, line, sem)
    fetch.start()
    for pair in range(ROWS):
        cut = [corner * D + MAIN + pair * REST for corner in range(4)]
        out_ref[:, pair * WIDE : (pair + 1) * WIDE] = jnp.concatenate(
            [weight_ref[:, at : at + REST] for at in cut], axis=1
        )
    fetch.wait()
    units = bias_out.shape[0]
    bias_out[...] = jnp.broadcast_to(line[...].reshape(1, units), (8, units)).T[:, :1]


def chip_product(weight_ref, corner, groups, other, rows):
    at = pl.multiple_of(corner * D + (row_index() // 2 ^ other) * 2 * WIDE, 2 * WIDE)
    return lax.dot_general(
        weight_ref[:, pl.ds(at, 2 * WIDE)],
        rows[corner * groups : (corner + 1) * groups],
        (((1,), (1,)), ((), ())),
        preferred_element_type=F32,
    )


def merge_first_kernel(own, near_own, one, near_one, weight_ref, out_ref):
    groups = out_ref.shape[2]
    rows = [collect_late(own, near_own), collect_late(one, near_one)]
    for corner in range(4):
        out_ref[corner] = chip_product(weight_ref, corner, groups, 0, rows[0]) + chip_product(
            weight_ref, corner, groups, 1, rows[1]
        )


def merge_second_kernel(two, near_two, sum_ref, weight_ref, out_ref):
    groups = out_ref.shape[2]
    rows = collect_late(two, near_two)
    for corner in range(4):
        out_ref[corner] = sum_ref[corner] + chip_product(weight_ref, corner, groups, 2, rows)


def merge_kernel(*rest):
    pieces = rest[:ROWS]
    early_ref, weight_ref, tail_ref, bias_ref, live_ref, out_ref, ends_ref = rest[ROWS:]
    me = row_index()
    groups = live_ref.shape[1]
    patches = 4 * groups
    notes = jnp.zeros((NOTES, groups), F32)
    for step, piece in zip(PIECE_ORDER, pieces):
        ends_ref[:, pl.ds(pl.multiple_of((me ^ step) * WIDE, WIDE), WIDE)] = piece[patches : patches + groups]
        notes = notes + piece[patches + groups :].astype(F32)
    scale = lax.rsqrt((notes[:4] + notes[4:8]) * (1.0 / D) + 1e-06)
    contract = (((1,), (1,)), ((), ()))
    rows = collect_late(pieces[EARLY], pieces[EARLY + 1])
    total = jnp.zeros(bias_ref.shape[:1] + (groups,), F32)
    for corner in range(4):
        part = early_ref[corner] + chip_product(weight_ref, corner, groups, 3, rows)
        total = total + scale[corner : corner + 1] * part
    spread = jnp.concatenate([jnp.broadcast_to(scale[at : at + 1], (REST, groups)) for at in range(4)], axis=0).T
    ends = ends_ref[...].astype(F32) * jnp.concatenate([spread] * ROWS, axis=1)
    total = total + lax.dot_general(tail_ref[...], ends.astype(BF16), contract, preferred_element_type=F32)
    total = total + bias_ref[...]
    merged = 0.5 * total * (1.0 + lax.erf(total * math.sqrt(0.5)))
    out_ref[0] = jnp.where(live_ref[...] > 0.0, merged, 0.0).astype(BF16)


def kernel(body, name, out_shape, scratch=(), fetched=(), count=0, limit=24, flops=0, moved=0):
    specs = [pl.BlockSpec(memory_space=pltpu.VMEM) for _ in range(count)]
    for at in fetched:
        specs[at] = pl.BlockSpec(memory_space=pl.ANY)
    return pl.pallas_call(
        body,
        out_shape=out_shape,
        in_specs=specs,
        out_specs=jax.tree.map(lambda _: pl.BlockSpec(memory_space=pltpu.VMEM), out_shape),
        scratch_shapes=list(scratch),
        compiler_params=pltpu.CompilerParams(vmem_limit_bytes=limit * 1024 * 1024),
        cost_estimate=pl.CostEstimate(flops=flops, bytes_accessed=moved, transcendentals=0),
        name=name,
    )


def in_hbm(value):
    return pltpu.with_memory_space_constraint(value, pltpu.HBM)


def shape(*dims, dtype=BF16):
    return jax.ShapeDtypeStruct(dims, dtype)


def swap(value, step):
    return lax.ppermute(value, "row", [(row, row ^ step) for row in range(ROWS)])


def turn(value, low, high):
    pairs = [
        (page * ROWS + row, (page + (high if row % 2 else low)) % PAGES * ROWS + row)
        for page in range(PAGES)
        for row in range(ROWS)
    ]
    return lax.ppermute(value, ("page", "row"), pairs)


def after(value, *arrays):
    return lax.optimization_barrier((value, *arrays))[0]


def local_eight(qkv_rows, residual, out_weight, norm_gain, merge_weight, merge_bias, page_grid):
    band = qkv_rows.shape[1]
    patches = band * ROWS
    groups = patches // 4
    units = merge_weight.shape[0]
    depth = out_weight.shape[0]
    piece = patches + groups
    size = depth + depth // 4

    *sends, chip, own, grid = kernel(
        spread_kernel,
        "spread",
        [shape(band, 4 * HPAIR)] * ROWS
        + [shape(2 * size, WIDE), shape(size, WIDE), shape(8, WIDE, dtype=jnp.int32)],
        [
            pltpu.VMEM((band, 3 * D), BF16),
            pltpu.VMEM((band, D), BF16),
            pltpu.VMEM((depth, 2 * WIDE), BF16),
            pltpu.VMEM((depth, WIDE), BF16),
            pltpu.VMEM((ROWS, band, 4 * HPAIR), BF16),
            pltpu.SMEM(page_grid.shape, jnp.int32),
            pltpu.SemaphoreType.DMA((5,)),
        ],
        fetched=range(4),
        count=4,
        limit=24,
        moved=1 << 20,
    )(in_hbm(qkv_rows), in_hbm(residual), in_hbm(out_weight), in_hbm(page_grid))
    blocks = [sends[0]] + [swap(sends[step], step) for step in BLOCK_ORDER[1:]]
    select, dead, live = kernel(
        layout_kernel,
        "layout",
        [shape(patches, patches), shape(1, patches, dtype=F32), shape(1, groups, dtype=F32)],
        fetched=range(1, 1 + 3),
        count=1 + 3,
        moved=1 << 20,
    )(grid, *blocks[1:4])
    across = turn(after(own, *()), 2, 2)
    near = turn(after(chip, *()), 1, PAGES - 1)
    swapped = swap(near, 1)
    attn = kernel(
        attend_kernel,
        "attend",
        shape(piece, WIDE),
        [pltpu.VMEM((patches, HPAIR), BF16)] * 3,
        count=2 + ROWS,
        flops=20 * patches * patches * 4096,
        moved=1 << 20,
    )(select, dead, *blocks)
    resid, own_gain, main, tail = kernel(
        ready_kernel,
        "ready",
        [shape(patches, HPAIR, dtype=F32), shape(1, HPAIR, dtype=F32), shape(MAIN, HPAIR), shape(4, MAIN, HPAIR)],
        [pltpu.VMEM((patches, HPAIR), BF16), pltpu.VMEM((D,), F32), pltpu.SemaphoreType.DMA],
        fetched=(1, 2),
        count=3 + ROWS + 3,
        flops=10 * patches * patches * 4096,
        moved=4 << 20,
    )(select, in_hbm(norm_gain), attn, *blocks, own, across, near)
    last = kernel(
        last_kernel,
        "ready_last",
        [shape(2 * WIDE, HPAIR), shape(4, 2 * WIDE, HPAIR)],
        fetched=(1,),
        count=2,
        moved=4 << 20,
    )(swapped, main)
    x, y, far = [swap(attn, step) for step in (2, 4, 6)]
    pieces = [attn, x, y, swap(after(attn, main), 1), swap(x, 1), swap(after(y, last[0]), 1), far, swap(far, 1)]
    base = kernel(
        project_early_kernel,
        "project_early",
        shape(patches, HPAIR, dtype=F32),
        [pltpu.VMEM((piece, MAIN), BF16)],
        count=EARLY + 5,
        flops=4 * patches * MAIN * 4096,
        moved=4 << 20,
    )(*pieces[:EARLY], main, tail, *last, resid)
    hidden = kernel(
        project_kernel,
        "project",
        shape(piece + NOTES, WIDE),
        count=2 + 6,
        flops=patches * MAIN * 256,
        moved=4 << 20,
    )(*pieces[EARLY:], base, main, tail, *last, own_gain)
    ends, bias = kernel(
        tail_kernel,
        "merge_tail",
        [shape(units, MAIN), shape(units, 1, dtype=F32)],
        [pltpu.VMEM((units,), F32), pltpu.SemaphoreType.DMA],
        fetched=(1, 2),
        count=3,
        moved=4 << 20,
    )(merge_weight, in_hbm(merge_bias), hidden)
    sums = shape(4, units, groups, dtype=F32)
    x, y, far = [swap(hidden, step) for step in (2, 4, 6)]
    near_own, near_x = swap(after(hidden, ends), 1), swap(x, 1)
    first = kernel(
        merge_first_kernel, "merge_first", sums, count=5, flops=4 * units * groups * MAIN * 1, moved=4 << 20
    )(hidden, near_own, x, near_x, merge_weight)
    near_y = swap(y, 1)
    second = kernel(
        merge_second_kernel, "merge_second", sums, count=4, flops=2 * units * groups * MAIN * 1, moved=4 << 20
    )(y, near_y, first, merge_weight)
    pieces = [hidden, x, y, near_own, near_x, near_y, far, swap(far, 1)]
    return kernel(
        merge_kernel,
        "merge",
        shape(1, units, groups),
        [pltpu.VMEM((groups, MAIN), BF16)],
        count=ROWS + 5,
        flops=4 * units * groups * MAIN,
        moved=8 << 20,
    )(*pieces, second, merge_weight, ends, bias, live)


def solution(mesh):
    in_specs = (
        P("page", "row", None),
        P("page", "row", None),
        P("page", None),
        P(),
        P("row", None),
        P("row"),
        P("page", None),
    )
    out_specs = P("page", "row", None)
    local = local_eight if mesh.shape["row"] == 8 and mesh.shape["page"] == 4 else local_any
    return jax.shard_map(local, mesh=mesh, in_specs=in_specs, out_specs=out_specs, check_vma=False)
```

```python
import functools
import math

import jax
import jax.numpy as jnp
from jax import lax
from jax.experimental import pallas as pl
from jax.experimental.pallas import tpu as pltpu
from jax.sharding import PartitionSpec as P

D = 1280
HEADS = 16
HDIM = 80


def local_any(qkv_rows, residual, out_weight, norm_gain, merge_weight, merge_bias, page_grid):
    row_count = lax.axis_size("row")
    q_split = max(1, row_count // HEADS)
    head_groups = row_count // q_split
    width = D // head_groups
    heads_per = width // HDIM
    band_len = qkv_rows.shape[1]
    part_len = band_len // q_split
    local_qkv = qkv_rows[0]
    queries = local_qkv[:, :D]
    key_vals = jnp.concatenate(
        [
            local_qkv[:, D : 2 * D].reshape(band_len, head_groups, width),
            local_qkv[:, 2 * D :].reshape(band_len, head_groups, width),
        ],
        axis=2,
    )
    q_send = (
        queries.reshape(q_split, part_len, head_groups, width)
        .transpose(2, 0, 1, 3)
        .reshape(row_count, part_len, width)
    )
    kv_send = jnp.broadcast_to(
        key_vals.transpose(1, 0, 2)[:, None], (head_groups, q_split, band_len, 2 * width)
    )
    kv_send = kv_send.reshape(row_count, band_len, 2 * width)
    q_recv, kv_recv = (
        lax.all_to_all(q_send, "row", split_axis=0, concat_axis=1, tiled=True),
        lax.all_to_all(kv_send, "row", split_axis=0, concat_axis=1, tiled=True),
    )
    kv_local = kv_recv[0]
    positions = jnp.arange(row_count * band_len, dtype=jnp.int32)
    valid_len = page_grid[0, 0] * page_grid[0, 1]
    key_valid = positions < valid_len
    key_total = kv_local.shape[0]
    key_heads = kv_local[:, :width].reshape(key_total, heads_per, HDIM)
    value_heads = kv_local[:, width:].reshape(key_total, heads_per, HDIM)
    query_total = row_count * part_len
    q_block = math.gcd(query_total, 512)
    q_blocks = q_recv[0].reshape(query_total // q_block, q_block, heads_per, HDIM)
    root_dim = math.sqrt(HDIM)

    def attend(q_span):
        scores = (
            jnp.einsum("qhd,khd->hqk", q_span, key_heads, preferred_element_type=jnp.float32)
            / root_dim
        )
        scores = jnp.where(key_valid[None, None, :], scores, -1e30)
        peak = jnp.max(scores, axis=2, keepdims=True)
        weights = jnp.exp(scores - peak)
        total = jnp.sum(weights, axis=2, keepdims=True)
        mixed = (
            jnp.einsum(
                "hqk,khd->hqd",
                weights.astype(jnp.bfloat16),
                value_heads,
                preferred_element_type=jnp.float32,
            )
            / total
        )
        return mixed.transpose(1, 0, 2).reshape(q_span.shape[0], width).astype(jnp.bfloat16)

    attn_heads = lax.map(attend, q_blocks).reshape(row_count, part_len, width)
    returned = lax.all_to_all(attn_heads, "row", split_axis=0, concat_axis=0, tiled=True)
    attn = (
        returned.reshape(head_groups, q_split, part_len, width)
        .transpose(1, 2, 0, 3)
        .reshape(band_len, D)
    )
    projected = jnp.dot(
        attn,
        lax.all_gather(out_weight, "page", axis=0, tiled=True),
        preferred_element_type=jnp.float32,
    )
    hidden = residual[0].astype(jnp.float32) + projected
    normed = (
        hidden * lax.rsqrt(jnp.mean(hidden * hidden, axis=1, keepdims=True) + 1e-06) * norm_gain
    ).astype(jnp.bfloat16)
    rows_n = page_grid[0, 0]
    cols_n = page_grid[0, 1]
    group_total = band_len * row_count // 4
    slots = jnp.arange(group_total, dtype=jnp.int32)
    half_cols = cols_n // 2
    live = slots < rows_n // 2 * half_cols
    first = jnp.where(live, 2 * (slots // half_cols) * cols_n + 2 * (slots % half_cols), 0)
    corners = [first, first + 1, first + cols_n, first + cols_n + 1]
    local_units = merge_weight.shape[0]
    page_all = lax.all_gather(normed, "row", axis=0, tiled=True)
    merged_sum = jnp.zeros((local_units, group_total), jnp.float32)
    for corner in range(4):
        picked = jnp.take(page_all, corners[corner], axis=0)
        merged_sum = merged_sum + jnp.einsum(
            "md,gd->mg",
            merge_weight[:, corner * D : (corner + 1) * D],
            picked,
            preferred_element_type=jnp.float32,
        )
    merged = jax.nn.gelu(merged_sum + merge_bias[:, None], approximate=False)
    merged = jnp.where(live[None, :], merged, 0.0).astype(jnp.bfloat16)
    return merged[None]


ROWS = 8
PAGES = 4
HPAIR = 2 * HDIM
WIDE = 128
REST = HPAIR - WIDE
MAIN = ROWS * WIDE
NOTES = 16
BLOCK_ORDER = (0, 4, 2, 6, 7, 3, 5, 1)
PIECE_ORDER = (0, 2, 4, 1, 3, 5, 6, 7)
EARLY = 6
ROOT = math.log2(math.e) / math.sqrt(HDIM)
BF16 = jnp.bfloat16
F32 = jnp.float32


def row_index():
    return lax.axis_index("row")


def pack_tail(wide):
    groups = wide.shape[0] // 4
    return jnp.concatenate([wide[at * groups : (at + 1) * groups] for at in range(4)], axis=1)


def spread_kernel(qkv_hbm, resid_hbm, weight_hbm, grid_hbm, *rest):
    outs = rest[:ROWS]
    chip_ref, slice_ref, grid_out, qkv, resid, main, tile, held, grid, sems = rest[ROWS:]
    me = row_index()
    depth = weight_hbm.shape[0]
    chip = pl.ds(pl.multiple_of(me // 2 * 2 * WIDE, 2 * WIDE), 2 * WIDE)
    ends = pl.ds(pl.multiple_of(MAIN + me // 4 * WIDE, WIDE), WIDE)
    copies = [
        pltpu.make_async_copy(qkv_hbm.at[0], qkv, sems.at[0]),
        pltpu.make_async_copy(resid_hbm.at[0], resid, sems.at[1]),
        pltpu.make_async_copy(weight_hbm.at[:, chip], main, sems.at[2]),
        pltpu.make_async_copy(weight_hbm.at[:, ends], tile, sems.at[3]),
        pltpu.make_async_copy(grid_hbm, grid, sems.at[4]),
    ]
    for copy in copies:
        copy.start()
    for copy in copies:
        copy.wait()
    for dest in range(ROWS):
        at = dest * HPAIR
        parts = [qkv[:, part * D + at : part * D + at + HPAIR] for part in range(3)]
        parts.append(resid[:, dest * WIDE : (dest + 1) * WIDE])
        parts.append(resid[:, MAIN + dest * REST : MAIN + (dest + 1) * REST])
        held[dest] = jnp.concatenate(parts, axis=1)
    for step in range(ROWS):
        outs[step][...] = held[me ^ step]
    low = me // 2 % 2 == 0
    size = depth + depth // 4
    for core in range(2):
        tail = jnp.where(low, tile[:, core * REST : (core + 1) * REST], tile[:, (core + 2) * REST : (core + 3) * REST])
        chip_ref[core * size : core * size + depth, :] = main[:, core * WIDE : (core + 1) * WIDE]
        chip_ref[core * size + depth : (core + 1) * size, :] = pack_tail(tail)
    slice_ref[...] = chip_ref[pl.ds(pl.multiple_of(me % 2 * size, 16), size), :]
    row = lax.broadcasted_iota(jnp.int32, grid_out.shape, 0)
    grid_out[...] = jnp.where(row == 0, grid[0, 0], grid[0, 1])


def layout_kernel(grid_ref, *rest):
    select_ref, keys_ref, live_ref = rest[-3:]
    rows_n, cols_n = grid_ref[:1, :1], grid_ref[1:2, :1]
    patches = select_ref.shape[0]
    groups = patches // 4
    half = cols_n >> 1
    count = (rows_n >> 1) * half
    slots = lax.broadcasted_iota(jnp.int32, (groups, 1), 0)
    line = jnp.floor((slots.astype(F32) + 0.5) / half.astype(F32)).astype(jnp.int32)
    first = 2 * line * cols_n + 2 * (slots - line * half)
    at = lax.broadcasted_iota(jnp.int32, (groups, patches), 1)
    for corner in range(4):
        wanted = jnp.where(slots < count, first + (corner // 2) * cols_n + corner % 2, -1)
        select_ref[corner * groups : (corner + 1) * groups, :] = jnp.where(at == wanted, 1.0, 0.0).astype(BF16)
    key = lax.broadcasted_iota(jnp.int32, keys_ref.shape, 1)
    keys_ref[...] = jnp.where(key < rows_n * cols_n, 0.0, -1e30)
    slot = lax.broadcasted_iota(jnp.int32, live_ref.shape, 1)
    live_ref[...] = jnp.where(slot < count, 1.0, 0.0)


def attend_kernel(select_ref, dead_ref, *rest):
    blocks = rest[:ROWS]
    out_ref, q_all, k_all, v_all = rest[-4:]
    me = row_index()
    band = blocks[0].shape[0]
    patches = band * ROWS
    for step, block in zip(BLOCK_ORDER, blocks):
        at = pl.ds(pl.multiple_of((me ^ step) * band, band), band)
        q_all[at, :] = block[:, :HPAIR]
        k_all[at, :] = block[:, HPAIR : 2 * HPAIR]
        v_all[at, :] = block[:, 2 * HPAIR : 3 * HPAIR]
    queries = jnp.dot(select_ref[...], q_all[...], preferred_element_type=F32).astype(BF16)
    lane = lax.broadcasted_iota(jnp.int32, (1, HPAIR), 1)
    keys, values, dead = k_all[...], v_all[...], dead_ref[...]
    mixed = []
    for head in range(2):
        mine = (lane >= head * HDIM) & (lane < (head + 1) * HDIM)
        asked = jnp.where(mine, queries, jnp.zeros_like(queries))
        scores = lax.dot_general(asked, keys, (((1,), (1,)), ((), ())), preferred_element_type=F32) + dead
        weights = jnp.exp2((scores - jnp.max(scores, axis=1, keepdims=True)) * ROOT)
        total = jnp.sum(weights, axis=1, keepdims=True)
        mixed.append(jnp.dot(weights.astype(BF16), values, preferred_element_type=F32) / total)
    attn = jnp.where(lane < HDIM, mixed[0], mixed[1])
    out_ref[:patches, :] = attn[:, :WIDE].astype(BF16)
    out_ref[patches:, :] = pack_tail(attn[:, WIDE:]).astype(BF16)


def weight_rows(cut):
    depth = 2 * HPAIR
    packed = cut[depth:]
    tail = jnp.concatenate([packed[:, at * REST : (at + 1) * REST] for at in range(4)], axis=0)
    whole = jnp.concatenate([cut[:depth], tail], axis=1)
    return [whole[core * HPAIR : (core + 1) * HPAIR] for core in range(2)]


def place_rows(rows, base, main_ref, tail_ref):
    for core in range(2):
        pair = base + core
        main_ref[pl.ds(pl.multiple_of(pair * WIDE, WIDE), WIDE), :] = rows[core][:WIDE]
        for corner in range(4):
            spot = pl.multiple_of(pair * WIDE + corner * REST, REST)
            tail_ref[corner, pl.ds(spot, REST), :] = rows[core][WIDE:]


def ready_kernel(select_ref, gain_hbm, token_ref, *rest):
    del token_ref
    blocks = rest[:ROWS]
    own_ref, across_ref, near_ref = rest[ROWS : ROWS + 3]
    resid_ref, gain_out, main_ref, tail_ref, held, line, sem = rest[-7:]
    fetch = pltpu.make_async_copy(gain_hbm, line, sem)
    fetch.start()
    me = row_index()
    page = lax.axis_index("page")
    band = blocks[0].shape[0]
    for step, block in zip(BLOCK_ORDER, blocks):
        at = pl.ds(pl.multiple_of((me ^ step) * band, band), band)
        held[at, :] = block[:, 3 * HPAIR :]
    resid_ref[...] = jnp.dot(select_ref[...], held[...], preferred_element_type=F32)
    main_ref[...] = jnp.zeros_like(main_ref)
    tail_ref[...] = jnp.zeros_like(tail_ref)
    core = me % 2
    size = own_ref.shape[0]
    half = pl.ds(pl.multiple_of(core * size, 16), size)
    cuts = ((0, own_ref[...]), (2, across_ref[...]), (3 - 2 * core, near_ref[half, :]))
    for step, cut in cuts:
        place_rows(weight_rows(cut), 2 * lax.rem(page + step, PAGES), main_ref, tail_ref)
    fetch.wait()
    whole = line[...].reshape(1, D)
    gain = jnp.zeros(gain_out.shape, F32)
    for pair in range(ROWS):
        parts = [whole[:, pair * WIDE : (pair + 1) * WIDE]]
        parts.append(whole[:, MAIN + pair * REST : MAIN + (pair + 1) * REST])
        gain = jnp.where(me == pair, jnp.concatenate(parts, axis=1), gain)
    gain_out[...] = gain


def last_kernel(swapped_ref, token_ref, main_ref, tail_ref):
    del token_ref
    size = swapped_ref.shape[0] // 2
    cut = swapped_ref[pl.ds(pl.multiple_of(row_index() % 2 * size, 16), size), :]
    tail_ref[...] = jnp.zeros_like(tail_ref)
    place_rows(weight_rows(cut), 0, main_ref, tail_ref)


def far_block():
    me = row_index()
    return pl.ds(pl.multiple_of((me // 2 ^ 3) * 2 * WIDE, 2 * WIDE), 2 * WIDE)


def collect_early(pieces, full):
    me = row_index()
    full[:, far_block()] = jnp.zeros((full.shape[0], 2 * WIDE), BF16)
    for step, piece in zip(PIECE_ORDER[:EARLY], pieces):
        full[:, pl.ds(pl.multiple_of((me ^ step) * WIDE, WIDE), WIDE)] = piece[...]


def collect_late(same, other):
    core = row_index() % 2
    left = jnp.where(core == 0, same[...], other[...])
    right = jnp.where(core == 0, other[...], same[...])
    return jnp.concatenate([left, right], axis=1)


def late_source():
    return lax.rem(lax.axis_index("page") + 1 + 2 * (row_index() % 2), PAGES)


def project_early_kernel(*rest):
    pieces = rest[:EARLY]
    main_ref, tail_ref, last_main_ref, last_tail_ref, resid_ref, out_ref, full = rest[EARLY:]
    collect_early(pieces, full)
    patches = resid_ref.shape[0]
    groups = patches // 4
    late = pl.ds(pl.multiple_of(late_source() * 2 * WIDE, 2 * WIDE), 2 * WIDE)
    base = jnp.dot(full[:patches], main_ref[...], preferred_element_type=F32) + resid_ref[...]
    base = base + jnp.dot(full[:patches, late], last_main_ref[...], preferred_element_type=F32)
    for corner in range(4):
        span = slice(corner * groups, (corner + 1) * groups)
        part = jnp.dot(full[patches:], tail_ref[corner], preferred_element_type=F32)
        part = part + jnp.dot(full[patches:, late], last_tail_ref[corner], preferred_element_type=F32)
        out_ref[span, :] = base[span] + part


def project_kernel(*rest):
    same, other, base_ref, main_ref, tail_ref, last_main_ref, last_tail_ref, gain_ref, out_ref = rest
    patches = base_ref.shape[0]
    groups = patches // 4
    block = far_block()
    is_last = late_source() == (row_index() // 2 ^ 3)
    full = collect_late(same, other)
    main = jnp.where(is_last, last_main_ref[...], main_ref[block, :])
    base = base_ref[...] + jnp.dot(full[:patches], main, preferred_element_type=F32)
    ones = jnp.ones((NOTES, HPAIR), BF16)
    contract = (((1,), (1,)), ((), ()))
    row = lax.broadcasted_iota(jnp.int32, (NOTES, groups), 0)
    notes = jnp.zeros((NOTES, groups), F32)
    ends = []
    for corner in range(4):
        span = slice(corner * groups, (corner + 1) * groups)
        tail = jnp.where(is_last, last_tail_ref[corner], tail_ref[corner, block, :])
        hidden = base[span] + jnp.dot(full[patches:], tail, preferred_element_type=F32)
        square = hidden * hidden
        high = square.astype(BF16)
        low = (square - high.astype(F32)).astype(BF16)
        total = lax.dot_general(ones, high, contract, preferred_element_type=F32)
        total = total + lax.dot_general(ones, low, contract, preferred_element_type=F32)
        coarse = total.astype(BF16).astype(F32)
        notes = jnp.where(row == corner, coarse, jnp.where(row == 4 + corner, total - coarse, notes))
        sent = hidden * gain_ref[...]
        out_ref[span, :] = sent[:, :WIDE].astype(BF16)
        ends.append(sent[:, WIDE:])
    out_ref[patches : patches + groups, :] = jnp.concatenate(ends, axis=1).astype(BF16)
    out_ref[patches + groups :, :] = notes.astype(BF16)


def tail_kernel(weight_ref, bias_hbm, token_ref, out_ref, bias_out, line, sem):
    del token_ref
    fetch = pltpu.make_async_copy(bias_hbm, line, sem)
    fetch.start()
    for pair in range(ROWS):
        cut = [corner * D + MAIN + pair * REST for corner in range(4)]
        out_ref[:, pair * WIDE : (pair + 1) * WIDE] = jnp.concatenate(
            [weight_ref[:, at : at + REST] for at in cut], axis=1
        )
    fetch.wait()
    units = bias_out.shape[0]
    bias_out[...] = jnp.broadcast_to(line[...].reshape(1, units), (8, units)).T[:, :1]


def add_pieces(sum_ref, before, weight_ref, tail_ref, pieces):
    groups = sum_ref.shape[2]
    patches = 4 * groups
    me = row_index()
    rows = jnp.concatenate([piece[: patches + groups] for _, piece in pieces], axis=1)
    spots = [pl.multiple_of((me ^ step) * WIDE, WIDE) for step, _ in pieces]
    ends = rows[patches:]
    tails = jnp.concatenate([tail_ref[:, pl.ds(spot, WIDE)] for spot in spots], axis=1)
    lane = lax.rem(lax.broadcasted_iota(jnp.int32, (1, rows.shape[1]), 1), WIDE)
    contract = (((1,), (1,)), ((), ()))
    for corner in range(4):
        columns = [weight_ref[:, pl.ds(pl.multiple_of(corner * D + spot, WIDE), WIDE)] for spot in spots]
        part = lax.dot_general(
            jnp.concatenate(columns, axis=1),
            rows[corner * groups : (corner + 1) * groups],
            contract,
            preferred_element_type=F32,
        )
        mine = jnp.where(lane // REST == corner, ends, jnp.zeros_like(ends))
        part = part + lax.dot_general(tails, mine, contract, preferred_element_type=F32)
        sum_ref[corner] = part if before is None else before[corner] + part
    return sum(piece[patches + groups :].astype(F32) for _, piece in pieces)


def merge_first_kernel(own, y, x, weight_ref, tail_ref, sum_ref, notes_ref):
    notes_ref[...] = add_pieces(sum_ref, None, weight_ref, tail_ref, [(0, own), (4, y), (2, x)])


def merge_second_kernel(own, y, x, before_ref, notes_before_ref, weight_ref, tail_ref, sum_ref, notes_ref):
    pieces = [(1, own), (5, y), (3, x)]
    notes_ref[...] = notes_before_ref[...] + add_pieces(sum_ref, before_ref, weight_ref, tail_ref, pieces)


def merge_kernel(far, near_far, before_ref, notes_ref, weight_ref, tail_ref, bias_ref, live_ref, out_ref, sum_ref):
    notes = notes_ref[...] + add_pieces(sum_ref, before_ref, weight_ref, tail_ref, [(6, far), (7, near_far)])
    scale = lax.rsqrt((notes[:4] + notes[4:8]) * (1.0 / D) + 1e-06)
    total = bias_ref[...]
    for corner in range(4):
        total = total + scale[corner : corner + 1] * sum_ref[corner]
    merged = 0.5 * total * (1.0 + lax.erf(total * math.sqrt(0.5)))
    out_ref[0] = jnp.where(live_ref[...] > 0.0, merged, 0.0).astype(BF16)


def kernel(body, name, out_shape, scratch=(), fetched=(), count=0, limit=24, flops=0, moved=0):
    specs = [pl.BlockSpec(memory_space=pltpu.VMEM) for _ in range(count)]
    for at in fetched:
        specs[at] = pl.BlockSpec(memory_space=pl.ANY)
    return pl.pallas_call(
        body,
        out_shape=out_shape,
        in_specs=specs,
        out_specs=jax.tree.map(lambda _: pl.BlockSpec(memory_space=pltpu.VMEM), out_shape),
        scratch_shapes=list(scratch),
        compiler_params=pltpu.CompilerParams(vmem_limit_bytes=limit * 1024 * 1024),
        cost_estimate=pl.CostEstimate(flops=flops, bytes_accessed=moved, transcendentals=0),
        name=name,
    )


def in_hbm(value):
    return pltpu.with_memory_space_constraint(value, pltpu.HBM)


def shape(*dims, dtype=BF16):
    return jax.ShapeDtypeStruct(dims, dtype)


def swap(value, step):
    return lax.ppermute(value, "row", [(row, row ^ step) for row in range(ROWS)])


def turn(value, low, high):
    pairs = [
        (page * ROWS + row, (page + (high if row % 2 else low)) % PAGES * ROWS + row)
        for page in range(PAGES)
        for row in range(ROWS)
    ]
    return lax.ppermute(value, ("page", "row"), pairs)


def after(value, *arrays):
    return lax.optimization_barrier((value, *arrays))[0]


def local_eight(qkv_rows, residual, out_weight, norm_gain, merge_weight, merge_bias, page_grid):
    band = qkv_rows.shape[1]
    patches = band * ROWS
    groups = patches // 4
    units = merge_weight.shape[0]
    depth = out_weight.shape[0]
    piece = patches + groups
    size = depth + depth // 4

    *sends, chip, own, grid = kernel(
        spread_kernel,
        "spread",
        [shape(band, 4 * HPAIR)] * ROWS
        + [shape(2 * size, WIDE), shape(size, WIDE), shape(8, WIDE, dtype=jnp.int32)],
        [
            pltpu.VMEM((band, 3 * D), BF16),
            pltpu.VMEM((band, D), BF16),
            pltpu.VMEM((depth, 2 * WIDE), BF16),
            pltpu.VMEM((depth, WIDE), BF16),
            pltpu.VMEM((ROWS, band, 4 * HPAIR), BF16),
            pltpu.SMEM(page_grid.shape, jnp.int32),
            pltpu.SemaphoreType.DMA((5,)),
        ],
        fetched=range(4),
        count=4,
        limit=24,
        moved=1 << 20,
    )(in_hbm(qkv_rows), in_hbm(residual), in_hbm(out_weight), in_hbm(page_grid))
    blocks = [sends[0]] + [swap(sends[step], step) for step in BLOCK_ORDER[1:]]
    select, dead, live = kernel(
        layout_kernel,
        "layout",
        [shape(patches, patches), shape(1, patches, dtype=F32), shape(1, groups, dtype=F32)],
        fetched=range(1, 1 + 3),
        count=1 + 3,
        moved=1 << 20,
    )(grid, *blocks[1:4])
    across = turn(after(own, *()), 2, 2)
    near = turn(after(chip, *()), 1, PAGES - 1)
    swapped = swap(near, 1)
    attn = kernel(
        attend_kernel,
        "attend",
        shape(piece, WIDE),
        [pltpu.VMEM((patches, HPAIR), BF16)] * 3,
        count=2 + ROWS,
        flops=20 * patches * patches * 4096,
        moved=1 << 20,
    )(select, dead, *blocks)
    resid, own_gain, main, tail = kernel(
        ready_kernel,
        "ready",
        [shape(patches, HPAIR, dtype=F32), shape(1, HPAIR, dtype=F32), shape(MAIN, HPAIR), shape(4, MAIN, HPAIR)],
        [pltpu.VMEM((patches, HPAIR), BF16), pltpu.VMEM((D,), F32), pltpu.SemaphoreType.DMA],
        fetched=(1, 2),
        count=3 + ROWS + 3,
        flops=10 * patches * patches * 4096,
        moved=4 << 20,
    )(select, in_hbm(norm_gain), attn, *blocks, own, across, near)
    last = kernel(
        last_kernel,
        "ready_last",
        [shape(2 * WIDE, HPAIR), shape(4, 2 * WIDE, HPAIR)],
        fetched=(1,),
        count=2,
        moved=4 << 20,
    )(swapped, main)
    x, y, far = [swap(attn, step) for step in (2, 4, 6)]
    pieces = [attn, x, y, swap(after(attn, main), 1), swap(x, 1), swap(after(y, last[0]), 1), far, swap(far, 1)]
    base = kernel(
        project_early_kernel,
        "project_early",
        shape(patches, HPAIR, dtype=F32),
        [pltpu.VMEM((piece, MAIN), BF16)],
        count=EARLY + 5,
        flops=4 * patches * MAIN * 4096,
        moved=4 << 20,
    )(*pieces[:EARLY], main, tail, *last, resid)
    hidden = kernel(
        project_kernel,
        "project",
        shape(piece + NOTES, WIDE),
        count=2 + 6,
        flops=patches * MAIN * 256,
        moved=4 << 20,
    )(*pieces[EARLY:], base, main, tail, *last, own_gain)
    ends, bias = kernel(
        tail_kernel,
        "merge_tail",
        [shape(units, MAIN), shape(units, 1, dtype=F32)],
        [pltpu.VMEM((units,), F32), pltpu.SemaphoreType.DMA],
        fetched=(1, 2),
        count=3,
        moved=4 << 20,
    )(merge_weight, in_hbm(merge_bias), hidden)
    sums = [shape(4, units, groups, dtype=F32), shape(NOTES, groups, dtype=F32)]
    y, x, far = [swap(hidden, step) for step in (4, 2, 6)]
    first = kernel(merge_first_kernel, "merge_first", sums, count=5, flops=1, moved=1)(
        hidden, y, x, merge_weight, ends
    )
    near = [swap(after(hidden, ends), 1), swap(y, 1), swap(x, 1)]
    second = kernel(merge_second_kernel, "merge_second", sums, count=7, flops=1, moved=1)(
        *near, *first, merge_weight, ends
    )
    return kernel(
        merge_kernel,
        "merge",
        shape(1, units, groups),
        [pltpu.VMEM((4, units, groups), F32)],
        count=8,
        flops=4 * units * groups * MAIN,
        moved=8 << 20,
    )(far, swap(after(far, first[0]), 1), *second, merge_weight, ends, bias, live)


def solution(mesh):
    in_specs = (
        P("page", "row", None),
        P("page", "row", None),
        P("page", None),
        P(),
        P("row", None),
        P("row"),
        P("page", None),
    )
    out_specs = P("page", "row", None)
    local = local_eight if mesh.shape["row"] == 8 and mesh.shape["page"] == 4 else local_any
    return jax.shard_map(local, mesh=mesh, in_specs=in_specs, out_specs=out_specs, check_vma=False)
```

```python
import functools
import math

import jax
import jax.numpy as jnp
from jax import lax
from jax.experimental import pallas as pl
from jax.experimental.pallas import tpu as pltpu
from jax.sharding import PartitionSpec as P

D = 1280
HEADS = 16
HDIM = 80


def local_any(qkv_rows, residual, out_weight, norm_gain, merge_weight, merge_bias, page_grid):
    row_count = lax.axis_size("row")
    q_split = max(1, row_count // HEADS)
    head_groups = row_count // q_split
    width = D // head_groups
    heads_per = width // HDIM
    band_len = qkv_rows.shape[1]
    part_len = band_len // q_split
    local_qkv = qkv_rows[0]
    queries = local_qkv[:, :D]
    key_vals = jnp.concatenate(
        [
            local_qkv[:, D : 2 * D].reshape(band_len, head_groups, width),
            local_qkv[:, 2 * D :].reshape(band_len, head_groups, width),
        ],
        axis=2,
    )
    q_send = (
        queries.reshape(q_split, part_len, head_groups, width)
        .transpose(2, 0, 1, 3)
        .reshape(row_count, part_len, width)
    )
    kv_send = jnp.broadcast_to(
        key_vals.transpose(1, 0, 2)[:, None], (head_groups, q_split, band_len, 2 * width)
    )
    kv_send = kv_send.reshape(row_count, band_len, 2 * width)
    q_recv, kv_recv = (
        lax.all_to_all(q_send, "row", split_axis=0, concat_axis=1, tiled=True),
        lax.all_to_all(kv_send, "row", split_axis=0, concat_axis=1, tiled=True),
    )
    kv_local = kv_recv[0]
    positions = jnp.arange(row_count * band_len, dtype=jnp.int32)
    valid_len = page_grid[0, 0] * page_grid[0, 1]
    key_valid = positions < valid_len
    key_total = kv_local.shape[0]
    key_heads = kv_local[:, :width].reshape(key_total, heads_per, HDIM)
    value_heads = kv_local[:, width:].reshape(key_total, heads_per, HDIM)
    query_total = row_count * part_len
    q_block = math.gcd(query_total, 512)
    q_blocks = q_recv[0].reshape(query_total // q_block, q_block, heads_per, HDIM)
    root_dim = math.sqrt(HDIM)

    def attend(q_span):
        scores = (
            jnp.einsum("qhd,khd->hqk", q_span, key_heads, preferred_element_type=jnp.float32)
            / root_dim
        )
        scores = jnp.where(key_valid[None, None, :], scores, -1e30)
        peak = jnp.max(scores, axis=2, keepdims=True)
        weights = jnp.exp(scores - peak)
        total = jnp.sum(weights, axis=2, keepdims=True)
        mixed = (
            jnp.einsum(
                "hqk,khd->hqd",
                weights.astype(jnp.bfloat16),
                value_heads,
                preferred_element_type=jnp.float32,
            )
            / total
        )
        return mixed.transpose(1, 0, 2).reshape(q_span.shape[0], width).astype(jnp.bfloat16)

    attn_heads = lax.map(attend, q_blocks).reshape(row_count, part_len, width)
    returned = lax.all_to_all(attn_heads, "row", split_axis=0, concat_axis=0, tiled=True)
    attn = (
        returned.reshape(head_groups, q_split, part_len, width)
        .transpose(1, 2, 0, 3)
        .reshape(band_len, D)
    )
    projected = jnp.dot(
        attn,
        lax.all_gather(out_weight, "page", axis=0, tiled=True),
        preferred_element_type=jnp.float32,
    )
    hidden = residual[0].astype(jnp.float32) + projected
    normed = (
        hidden * lax.rsqrt(jnp.mean(hidden * hidden, axis=1, keepdims=True) + 1e-06) * norm_gain
    ).astype(jnp.bfloat16)
    rows_n = page_grid[0, 0]
    cols_n = page_grid[0, 1]
    group_total = band_len * row_count // 4
    slots = jnp.arange(group_total, dtype=jnp.int32)
    half_cols = cols_n // 2
    live = slots < rows_n // 2 * half_cols
    first = jnp.where(live, 2 * (slots // half_cols) * cols_n + 2 * (slots % half_cols), 0)
    corners = [first, first + 1, first + cols_n, first + cols_n + 1]
    local_units = merge_weight.shape[0]
    page_all = lax.all_gather(normed, "row", axis=0, tiled=True)
    merged_sum = jnp.zeros((local_units, group_total), jnp.float32)
    for corner in range(4):
        picked = jnp.take(page_all, corners[corner], axis=0)
        merged_sum = merged_sum + jnp.einsum(
            "md,gd->mg",
            merge_weight[:, corner * D : (corner + 1) * D],
            picked,
            preferred_element_type=jnp.float32,
        )
    merged = jax.nn.gelu(merged_sum + merge_bias[:, None], approximate=False)
    merged = jnp.where(live[None, :], merged, 0.0).astype(jnp.bfloat16)
    return merged[None]


ROWS = 8
PAGES = 4
HPAIR = 2 * HDIM
WIDE = 128
REST = HPAIR - WIDE
MAIN = ROWS * WIDE
NOTES = 16
BLOCK_ORDER = (0, 4, 2, 6, 7, 3, 5, 1)
PIECE_ORDER = (0, 4, 2, 1, 5, 3, 6, 7)
ROOT = math.log2(math.e) / math.sqrt(HDIM)
BF16 = jnp.bfloat16
F32 = jnp.float32


def row_index():
    return lax.axis_index("row")


def pack_tail(wide):
    groups = wide.shape[0] // 4
    return jnp.concatenate([wide[at * groups : (at + 1) * groups] for at in range(4)], axis=1)


def spread_kernel(qkv_hbm, resid_hbm, weight_hbm, grid_hbm, *rest):
    outs = rest[:ROWS]
    chip_ref, slice_ref, grid_out, qkv, resid, main, tile, held, grid, sems = rest[ROWS:]
    me = row_index()
    depth = weight_hbm.shape[0]
    chip = pl.ds(pl.multiple_of(me // 2 * 2 * WIDE, 2 * WIDE), 2 * WIDE)
    ends = pl.ds(pl.multiple_of(MAIN + me // 4 * WIDE, WIDE), WIDE)
    copies = [
        pltpu.make_async_copy(qkv_hbm.at[0], qkv, sems.at[0]),
        pltpu.make_async_copy(resid_hbm.at[0], resid, sems.at[1]),
        pltpu.make_async_copy(weight_hbm.at[:, chip], main, sems.at[2]),
        pltpu.make_async_copy(weight_hbm.at[:, ends], tile, sems.at[3]),
        pltpu.make_async_copy(grid_hbm, grid, sems.at[4]),
    ]
    for copy in copies:
        copy.start()
    for copy in copies[2:]:
        copy.wait()
    low = me // 2 % 2 == 0
    size = depth + depth // 4
    for core in range(2):
        tail = jnp.where(low, tile[:, core * REST : (core + 1) * REST], tile[:, (core + 2) * REST : (core + 3) * REST])
        chip_ref[core * size : core * size + depth, :] = main[:, core * WIDE : (core + 1) * WIDE]
        chip_ref[core * size + depth : (core + 1) * size, :] = pack_tail(tail)
    slice_ref[...] = chip_ref[pl.ds(pl.multiple_of(me % 2 * size, 16), size), :]
    row = lax.broadcasted_iota(jnp.int32, grid_out.shape, 0)
    grid_out[...] = jnp.where(row == 0, grid[0, 0], grid[0, 1])
    for copy in copies[:2]:
        copy.wait()
    for dest in range(ROWS):
        at = dest * HPAIR
        parts = [qkv[:, part * D + at : part * D + at + HPAIR] for part in range(3)]
        parts.append(resid[:, dest * WIDE : (dest + 1) * WIDE])
        parts.append(resid[:, MAIN + dest * REST : MAIN + (dest + 1) * REST])
        held[dest] = jnp.concatenate(parts, axis=1)
    for step in range(ROWS):
        outs[step][...] = held[me ^ step]


def layout_kernel(grid_ref, *rest):
    select_ref, keys_ref, live_ref = rest[-3:]
    rows_n, cols_n = grid_ref[:1, :1], grid_ref[1:2, :1]
    patches = select_ref.shape[0]
    groups = patches // 4
    half = cols_n >> 1
    count = (rows_n >> 1) * half
    slots = lax.broadcasted_iota(jnp.int32, (groups, 1), 0)
    line = jnp.floor((slots.astype(F32) + 0.5) / half.astype(F32)).astype(jnp.int32)
    first = 2 * line * cols_n + 2 * (slots - line * half)
    at = lax.broadcasted_iota(jnp.int32, (groups, patches), 1)
    for corner in range(4):
        wanted = jnp.where(slots < count, first + (corner // 2) * cols_n + corner % 2, -1)
        select_ref[corner * groups : (corner + 1) * groups, :] = jnp.where(at == wanted, 1.0, 0.0).astype(BF16)
    key = lax.broadcasted_iota(jnp.int32, keys_ref.shape, 1)
    keys_ref[...] = jnp.where(key < rows_n * cols_n, 0.0, -1e30)
    slot = lax.broadcasted_iota(jnp.int32, live_ref.shape, 1)
    live_ref[...] = jnp.where(slot < count, 1.0, 0.0)


def attend_kernel(select_ref, dead_ref, *rest):
    blocks = rest[:ROWS]
    out_ref, q_all, k_all, v_all = rest[-4:]
    me = row_index()
    band = blocks[0].shape[0]
    patches = band * ROWS
    for step, block in zip(BLOCK_ORDER, blocks):
        at = pl.ds(pl.multiple_of((me ^ step) * band, band), band)
        q_all[at, :] = block[:, :HPAIR]
        k_all[at, :] = block[:, HPAIR : 2 * HPAIR]
        v_all[at, :] = block[:, 2 * HPAIR : 3 * HPAIR]
    queries = jnp.dot(select_ref[...], q_all[...], preferred_element_type=F32).astype(BF16)
    lane = lax.broadcasted_iota(jnp.int32, (1, HPAIR), 1)
    keys, values, dead = k_all[...], v_all[...], dead_ref[...]
    mixed = []
    for head in range(2):
        mine = (lane >= head * HDIM) & (lane < (head + 1) * HDIM)
        asked = jnp.where(mine, queries, jnp.zeros_like(queries))
        scores = lax.dot_general(asked, keys, (((1,), (1,)), ((), ())), preferred_element_type=F32) + dead
        weights = jnp.exp2((scores - jnp.max(scores, axis=1, keepdims=True)) * ROOT)
        total = jnp.sum(weights, axis=1, keepdims=True)
        mixed.append(jnp.dot(weights.astype(BF16), values, preferred_element_type=F32) / total)
    attn = jnp.where(lane < HDIM, mixed[0], mixed[1])
    out_ref[:patches, :] = attn[:, :WIDE].astype(BF16)
    out_ref[patches:, :] = pack_tail(attn[:, WIDE:]).astype(BF16)


def weight_rows(cut):
    depth = 2 * HPAIR
    packed = cut[depth:]
    tail = jnp.concatenate([packed[:, at * REST : (at + 1) * REST] for at in range(4)], axis=0)
    whole = jnp.concatenate([cut[:depth], tail], axis=1)
    return [whole[core * HPAIR : (core + 1) * HPAIR] for core in range(2)]


def place_rows(rows, base, main_ref, tail_ref):
    for core in range(2):
        pair = base + core
        main_ref[pl.ds(pl.multiple_of(pair * WIDE, WIDE), WIDE), :] = rows[core][:WIDE]
        for corner in range(4):
            spot = pl.multiple_of(pair * WIDE + corner * REST, REST)
            tail_ref[corner, pl.ds(spot, REST), :] = rows[core][WIDE:]


def ready_kernel(select_ref, gain_hbm, token_ref, *rest):
    del token_ref
    blocks = rest[:ROWS]
    own_ref, across_ref, near_ref = rest[ROWS : ROWS + 3]
    resid_ref, gain_out, main_ref, tail_ref, held, line, sem = rest[-7:]
    fetch = pltpu.make_async_copy(gain_hbm, line, sem)
    fetch.start()
    me = row_index()
    page = lax.axis_index("page")
    band = blocks[0].shape[0]
    for step, block in zip(BLOCK_ORDER, blocks):
        at = pl.ds(pl.multiple_of((me ^ step) * band, band), band)
        held[at, :] = block[:, 3 * HPAIR :]
    resid_ref[...] = jnp.dot(select_ref[...], held[...], preferred_element_type=F32)
    main_ref[...] = jnp.zeros_like(main_ref)
    tail_ref[...] = jnp.zeros_like(tail_ref)
    core = me % 2
    size = own_ref.shape[0]
    half = pl.ds(pl.multiple_of(core * size, 16), size)
    cuts = ((0, own_ref[...]), (2, across_ref[...]), (3 - 2 * core, near_ref[half, :]))
    for step, cut in cuts:
        place_rows(weight_rows(cut), 2 * lax.rem(page + step, PAGES), main_ref, tail_ref)
    fetch.wait()
    whole = line[...].reshape(1, D)
    gain = jnp.zeros(gain_out.shape, F32)
    for pair in range(ROWS):
        parts = [whole[:, pair * WIDE : (pair + 1) * WIDE]]
        parts.append(whole[:, MAIN + pair * REST : MAIN + (pair + 1) * REST])
        gain = jnp.where(me == pair, jnp.concatenate(parts, axis=1), gain)
    gain_out[...] = gain


def last_kernel(swapped_ref, token_ref, main_ref, tail_ref):
    del token_ref
    size = swapped_ref.shape[0] // 2
    cut = swapped_ref[pl.ds(pl.multiple_of(row_index() % 2 * size, 16), size), :]
    tail_ref[...] = jnp.zeros_like(tail_ref)
    place_rows(weight_rows(cut), 0, main_ref, tail_ref)


def far_block():
    me = row_index()
    return pl.ds(pl.multiple_of((me // 2 ^ 3) * 2 * WIDE, 2 * WIDE), 2 * WIDE)


def collect_late(same, other):
    core = row_index() % 2
    left = jnp.where(core == 0, same[...], other[...])
    right = jnp.where(core == 0, other[...], same[...])
    return jnp.concatenate([left, right], axis=1)


def late_source():
    return lax.rem(lax.axis_index("page") + 1 + 2 * (row_index() % 2), PAGES)


def add_features(steps, pieces, weights, before_ref, out_ref):
    main_ref, tail_ref, last_main_ref, last_tail_ref = weights
    me = row_index()
    patches = out_ref.shape[0]
    groups = patches // 4
    mains, tails = [], []
    for step in steps:
        pair = me ^ step
        columns = pl.ds(pl.multiple_of(pair * WIDE, WIDE), WIDE)
        late = pl.ds(pl.multiple_of(pair % 2 * WIDE, WIDE), WIDE)
        is_late = pair // 2 == late_source()
        mains.append(jnp.where(is_late, last_main_ref[late, :], main_ref[columns, :]))
        tails.append([jnp.where(is_late, last_tail_ref[at, late, :], tail_ref[at, columns, :]) for at in range(4)])
    rows = jnp.concatenate([piece[...] for piece in pieces], axis=1)
    base = before_ref[...] + jnp.dot(rows[:patches], jnp.concatenate(mains, axis=0), preferred_element_type=F32)
    for corner in range(4):
        span = slice(corner * groups, (corner + 1) * groups)
        tail = jnp.concatenate([tail[corner] for tail in tails], axis=0)
        out_ref[span, :] = base[span] + jnp.dot(rows[patches:], tail, preferred_element_type=F32)


def project_first_kernel(own, y, x, *rest):
    add_features((0, 4, 2), (own, y, x), rest[:4], *rest[4:])


def project_second_kernel(own, y, x, *rest):
    add_features((1, 5, 3), (own, y, x), rest[:4], *rest[4:])


def project_kernel(*rest):
    same, other, base_ref, main_ref, tail_ref, last_main_ref, last_tail_ref, gain_ref, out_ref = rest
    patches = base_ref.shape[0]
    groups = patches // 4
    block = far_block()
    is_last = late_source() == (row_index() // 2 ^ 3)
    full = collect_late(same, other)
    main = jnp.where(is_last, last_main_ref[...], main_ref[block, :])
    base = base_ref[...] + jnp.dot(full[:patches], main, preferred_element_type=F32)
    ones = jnp.ones((NOTES, HPAIR), BF16)
    contract = (((1,), (1,)), ((), ()))
    row = lax.broadcasted_iota(jnp.int32, (NOTES, groups), 0)
    notes = jnp.zeros((NOTES, groups), F32)
    ends = []
    for corner in range(4):
        span = slice(corner * groups, (corner + 1) * groups)
        tail = jnp.where(is_last, last_tail_ref[corner], tail_ref[corner, block, :])
        hidden = base[span] + jnp.dot(full[patches:], tail, preferred_element_type=F32)
        square = hidden * hidden
        high = square.astype(BF16)
        low = (square - high.astype(F32)).astype(BF16)
        total = lax.dot_general(ones, high, contract, preferred_element_type=F32)
        total = total + lax.dot_general(ones, low, contract, preferred_element_type=F32)
        coarse = total.astype(BF16).astype(F32)
        notes = jnp.where(row == corner, coarse, jnp.where(row == 4 + corner, total - coarse, notes))
        sent = hidden * gain_ref[...]
        out_ref[span, :] = sent[:, :WIDE].astype(BF16)
        ends.append(sent[:, WIDE:])
    out_ref[patches : patches + groups, :] = jnp.concatenate(ends, axis=1).astype(BF16)
    out_ref[patches + groups :, :] = notes.astype(BF16)


def tail_kernel(weight_ref, bias_hbm, token_ref, out_ref, bias_out, line, sem):
    del token_ref
    fetch = pltpu.make_async_copy(bias_hbm, line, sem)
    fetch.start()
    for pair in range(ROWS):
        cut = [corner * D + MAIN + pair * REST for corner in range(4)]
        out_ref[:, pair * WIDE : (pair + 1) * WIDE] = jnp.concatenate(
            [weight_ref[:, at : at + REST] for at in cut], axis=1
        )
    fetch.wait()
    units = bias_out.shape[0]
    bias_out[...] = jnp.broadcast_to(line[...].reshape(1, units), (8, units)).T[:, :1]


def merge_product(weight_ref, corner, groups, pieces):
    me = row_index()
    spots = [pl.multiple_of(corner * D + (me ^ step) * WIDE, WIDE) for step, _ in pieces]
    span = slice(corner * groups, (corner + 1) * groups)
    return lax.dot_general(
        jnp.concatenate([weight_ref[:, pl.ds(spot, WIDE)] for spot in spots], axis=1),
        jnp.concatenate([piece[span, :] for _, piece in pieces], axis=1),
        (((1,), (1,)), ((), ())),
        preferred_element_type=F32,
    )


def merge_first_kernel(own, y, x, weight_ref, sum_ref):
    for corner in range(4):
        sum_ref[corner] = merge_product(weight_ref, corner, sum_ref.shape[2], [(0, own), (4, y), (2, x)])


def merge_second_kernel(own, y, x, before_ref, weight_ref, sum_ref):
    for corner in range(4):
        part = merge_product(weight_ref, corner, sum_ref.shape[2], [(1, own), (5, y), (3, x)])
        sum_ref[corner] = before_ref[corner] + part


def merge_kernel(*rest):
    pieces = rest[:ROWS]
    before_ref, weight_ref, tail_ref, bias_ref, live_ref, out_ref, ends_ref = rest[ROWS:]
    me = row_index()
    groups = live_ref.shape[1]
    patches = 4 * groups
    contract = (((1,), (1,)), ((), ()))
    block = pl.multiple_of((me // 2 ^ 3) * 2 * WIDE, 2 * WIDE)
    rows = collect_late(pieces[6], pieces[7])
    parts = []
    for corner in range(4):
        parts.append(
            before_ref[corner]
            + lax.dot_general(
                weight_ref[:, pl.ds(pl.multiple_of(corner * D + block, 2 * WIDE), 2 * WIDE)],
                rows[corner * groups : (corner + 1) * groups],
                contract,
                preferred_element_type=F32,
            )
        )
    notes = jnp.zeros((NOTES, groups), F32)
    for step, piece in zip(PIECE_ORDER, pieces):
        notes = notes + piece[patches + groups :, :].astype(F32)
    scale = lax.rsqrt((notes[:4] + notes[4:8]) * (1.0 / D) + 1e-06)
    spread = jnp.concatenate([jnp.broadcast_to(scale[at : at + 1], (REST, groups)) for at in range(4)], axis=0).T
    for step, piece in zip(PIECE_ORDER, pieces):
        at = pl.ds(pl.multiple_of((me ^ step) * WIDE, WIDE), WIDE)
        ends_ref[:, at] = (piece[patches : patches + groups, :].astype(F32) * spread).astype(BF16)
    total = bias_ref[...] + lax.dot_general(tail_ref[...], ends_ref[...], contract, preferred_element_type=F32)
    for corner in range(4):
        total = total + scale[corner : corner + 1] * parts[corner]
    merged = 0.5 * total * (1.0 + lax.erf(total * math.sqrt(0.5)))
    out_ref[0] = jnp.where(live_ref[...] > 0.0, merged, 0.0).astype(BF16)


def kernel(body, name, out_shape, scratch=(), fetched=(), count=0, limit=24, flops=0, moved=0):
    specs = [pl.BlockSpec(memory_space=pltpu.VMEM) for _ in range(count)]
    for at in fetched:
        specs[at] = pl.BlockSpec(memory_space=pl.ANY)
    return pl.pallas_call(
        body,
        out_shape=out_shape,
        in_specs=specs,
        out_specs=jax.tree.map(lambda _: pl.BlockSpec(memory_space=pltpu.VMEM), out_shape),
        scratch_shapes=list(scratch),
        compiler_params=pltpu.CompilerParams(vmem_limit_bytes=limit * 1024 * 1024),
        cost_estimate=pl.CostEstimate(flops=flops, bytes_accessed=moved, transcendentals=0),
        name=name,
    )


def in_hbm(value):
    return pltpu.with_memory_space_constraint(value, pltpu.HBM)


def shape(*dims, dtype=BF16):
    return jax.ShapeDtypeStruct(dims, dtype)


def swap(value, step):
    return lax.ppermute(value, "row", [(row, row ^ step) for row in range(ROWS)])


def turn(value, low, high):
    pairs = [
        (page * ROWS + row, (page + (high if row % 2 else low)) % PAGES * ROWS + row)
        for page in range(PAGES)
        for row in range(ROWS)
    ]
    return lax.ppermute(value, ("page", "row"), pairs)


def after(value, *arrays):
    return lax.optimization_barrier((value, *arrays))[0]


def local_eight(qkv_rows, residual, out_weight, norm_gain, merge_weight, merge_bias, page_grid):
    band = qkv_rows.shape[1]
    patches = band * ROWS
    groups = patches // 4
    units = merge_weight.shape[0]
    depth = out_weight.shape[0]
    piece = patches + groups
    size = depth + depth // 4

    *sends, chip, own, grid = kernel(
        spread_kernel,
        "spread",
        [shape(band, 4 * HPAIR)] * ROWS
        + [shape(2 * size, WIDE), shape(size, WIDE), shape(8, WIDE, dtype=jnp.int32)],
        [
            pltpu.VMEM((band, 3 * D), BF16),
            pltpu.VMEM((band, D), BF16),
            pltpu.VMEM((depth, 2 * WIDE), BF16),
            pltpu.VMEM((depth, WIDE), BF16),
            pltpu.VMEM((ROWS, band, 4 * HPAIR), BF16),
            pltpu.SMEM(page_grid.shape, jnp.int32),
            pltpu.SemaphoreType.DMA((5,)),
        ],
        fetched=range(4),
        count=4,
        limit=24,
        moved=1 << 20,
    )(in_hbm(qkv_rows), in_hbm(residual), in_hbm(out_weight), in_hbm(page_grid))
    blocks = [sends[0]] + [swap(sends[step], step) for step in BLOCK_ORDER[1:]]
    select, dead, live = kernel(
        layout_kernel,
        "layout",
        [shape(patches, patches), shape(1, patches, dtype=F32), shape(1, groups, dtype=F32)],
        fetched=range(1, 1 + 3),
        count=1 + 3,
        moved=1 << 20,
    )(grid, *blocks[1:4])
    across = turn(after(own, *()), 2, 2)
    near = turn(after(chip, *()), 1, PAGES - 1)
    swapped = swap(near, 1)
    attn = kernel(
        attend_kernel,
        "attend",
        shape(piece, WIDE),
        [pltpu.VMEM((patches, HPAIR), BF16)] * 3,
        count=2 + ROWS,
        flops=20 * patches * patches * 4096,
        moved=1 << 20,
    )(select, dead, *blocks)
    resid, own_gain, main, tail = kernel(
        ready_kernel,
        "ready",
        [shape(patches, HPAIR, dtype=F32), shape(1, HPAIR, dtype=F32), shape(MAIN, HPAIR), shape(4, MAIN, HPAIR)],
        [pltpu.VMEM((patches, HPAIR), BF16), pltpu.VMEM((D,), F32), pltpu.SemaphoreType.DMA],
        fetched=(1, 2),
        count=3 + ROWS + 3,
        flops=10 * patches * patches * 4096,
        moved=4 << 20,
    )(select, in_hbm(norm_gain), attn, *blocks, own, across, near)
    last = kernel(
        last_kernel,
        "ready_last",
        [shape(2 * WIDE, HPAIR), shape(4, 2 * WIDE, HPAIR)],
        fetched=(1,),
        count=2,
        moved=4 << 20,
    )(swapped, main)
    y, x, far = [swap(attn, step) for step in (4, 2, 6)]
    weights = (main, tail, *last)
    rows = shape(patches, HPAIR, dtype=F32)
    first = kernel(project_first_kernel, "project_first", rows, count=8, flops=1, moved=1)(attn, y, x, *weights, resid)
    near = [swap(after(attn, main), 1), swap(after(y, last[0]), 1), swap(x, 1)]
    second = kernel(project_second_kernel, "project_second", rows, count=8, flops=1, moved=1)(*near, *weights, first)
    hidden = kernel(
        project_kernel,
        "project",
        shape(piece + NOTES, WIDE),
        count=2 + 6,
        flops=patches * MAIN * 256,
        moved=4 << 20,
    )(far, swap(after(far, first), 1), second, *weights, own_gain)
    ends, bias = kernel(
        tail_kernel,
        "merge_tail",
        [shape(units, MAIN), shape(units, 1, dtype=F32)],
        [pltpu.VMEM((units,), F32), pltpu.SemaphoreType.DMA],
        fetched=(1, 2),
        count=3,
        moved=4 << 20,
    )(merge_weight, in_hbm(merge_bias), hidden)
    sums = shape(4, units, groups, dtype=F32)
    y, x, far = [swap(hidden, step) for step in (4, 2, 6)]
    first = kernel(merge_first_kernel, "merge_first", sums, count=4, flops=1, moved=1)(hidden, y, x, merge_weight)
    near = [swap(after(hidden, ends), 1), swap(y, 1), swap(x, 1)]
    second = kernel(merge_second_kernel, "merge_second", sums, count=5, flops=1, moved=1)(*near, first, merge_weight)
    return kernel(
        merge_kernel,
        "merge",
        shape(1, units, groups),
        [pltpu.VMEM((groups, MAIN), BF16)],
        count=ROWS + 5,
        flops=4 * units * groups * MAIN,
        moved=8 << 20,
    )(hidden, y, x, *near, far, swap(after(far, first, *near), 1), second, merge_weight, ends, bias, live)


def solution(mesh):
    in_specs = (
        P("page", "row", None),
        P("page", "row", None),
        P("page", None),
        P(),
        P("row", None),
        P("row"),
        P("page", None),
    )
    out_specs = P("page", "row", None)
    local = local_eight if mesh.shape["row"] == 8 and mesh.shape["page"] == 4 else local_any
    return jax.shard_map(local, mesh=mesh, in_specs=in_specs, out_specs=out_specs, check_vma=False)
```

```python
import functools
import math

import jax
import jax.numpy as jnp
from jax import lax
from jax.experimental import pallas as pl
from jax.experimental.pallas import tpu as pltpu
from jax.sharding import PartitionSpec as P

D = 1280
HEADS = 16
HDIM = 80


def local_any(qkv_rows, residual, out_weight, norm_gain, merge_weight, merge_bias, page_grid):
    row_count = lax.axis_size("row")
    q_split = max(1, row_count // HEADS)
    head_groups = row_count // q_split
    width = D // head_groups
    heads_per = width // HDIM
    band_len = qkv_rows.shape[1]
    part_len = band_len // q_split
    local_qkv = qkv_rows[0]
    queries = local_qkv[:, :D]
    key_vals = jnp.concatenate(
        [
            local_qkv[:, D : 2 * D].reshape(band_len, head_groups, width),
            local_qkv[:, 2 * D :].reshape(band_len, head_groups, width),
        ],
        axis=2,
    )
    q_send = (
        queries.reshape(q_split, part_len, head_groups, width)
        .transpose(2, 0, 1, 3)
        .reshape(row_count, part_len, width)
    )
    kv_send = jnp.broadcast_to(
        key_vals.transpose(1, 0, 2)[:, None], (head_groups, q_split, band_len, 2 * width)
    )
    kv_send = kv_send.reshape(row_count, band_len, 2 * width)
    q_recv, kv_recv = (
        lax.all_to_all(q_send, "row", split_axis=0, concat_axis=1, tiled=True),
        lax.all_to_all(kv_send, "row", split_axis=0, concat_axis=1, tiled=True),
    )
    kv_local = kv_recv[0]
    positions = jnp.arange(row_count * band_len, dtype=jnp.int32)
    valid_len = page_grid[0, 0] * page_grid[0, 1]
    key_valid = positions < valid_len
    key_total = kv_local.shape[0]
    key_heads = kv_local[:, :width].reshape(key_total, heads_per, HDIM)
    value_heads = kv_local[:, width:].reshape(key_total, heads_per, HDIM)
    query_total = row_count * part_len
    q_block = math.gcd(query_total, 512)
    q_blocks = q_recv[0].reshape(query_total // q_block, q_block, heads_per, HDIM)
    root_dim = math.sqrt(HDIM)

    def attend(q_span):
        scores = (
            jnp.einsum("qhd,khd->hqk", q_span, key_heads, preferred_element_type=jnp.float32)
            / root_dim
        )
        scores = jnp.where(key_valid[None, None, :], scores, -1e30)
        peak = jnp.max(scores, axis=2, keepdims=True)
        weights = jnp.exp(scores - peak)
        total = jnp.sum(weights, axis=2, keepdims=True)
        mixed = (
            jnp.einsum(
                "hqk,khd->hqd",
                weights.astype(jnp.bfloat16),
                value_heads,
                preferred_element_type=jnp.float32,
            )
            / total
        )
        return mixed.transpose(1, 0, 2).reshape(q_span.shape[0], width).astype(jnp.bfloat16)

    attn_heads = lax.map(attend, q_blocks).reshape(row_count, part_len, width)
    returned = lax.all_to_all(attn_heads, "row", split_axis=0, concat_axis=0, tiled=True)
    attn = (
        returned.reshape(head_groups, q_split, part_len, width)
        .transpose(1, 2, 0, 3)
        .reshape(band_len, D)
    )
    projected = jnp.dot(
        attn,
        lax.all_gather(out_weight, "page", axis=0, tiled=True),
        preferred_element_type=jnp.float32,
    )
    hidden = residual[0].astype(jnp.float32) + projected
    normed = (
        hidden * lax.rsqrt(jnp.mean(hidden * hidden, axis=1, keepdims=True) + 1e-06) * norm_gain
    ).astype(jnp.bfloat16)
    rows_n = page_grid[0, 0]
    cols_n = page_grid[0, 1]
    group_total = band_len * row_count // 4
    slots = jnp.arange(group_total, dtype=jnp.int32)
    half_cols = cols_n // 2
    live = slots < rows_n // 2 * half_cols
    first = jnp.where(live, 2 * (slots // half_cols) * cols_n + 2 * (slots % half_cols), 0)
    corners = [first, first + 1, first + cols_n, first + cols_n + 1]
    local_units = merge_weight.shape[0]
    page_all = lax.all_gather(normed, "row", axis=0, tiled=True)
    merged_sum = jnp.zeros((local_units, group_total), jnp.float32)
    for corner in range(4):
        picked = jnp.take(page_all, corners[corner], axis=0)
        merged_sum = merged_sum + jnp.einsum(
            "md,gd->mg",
            merge_weight[:, corner * D : (corner + 1) * D],
            picked,
            preferred_element_type=jnp.float32,
        )
    merged = jax.nn.gelu(merged_sum + merge_bias[:, None], approximate=False)
    merged = jnp.where(live[None, :], merged, 0.0).astype(jnp.bfloat16)
    return merged[None]


ROWS = 8
PAGES = 4
HPAIR = 2 * HDIM
WIDE = 128
REST = HPAIR - WIDE
MAIN = ROWS * WIDE
NOTES = 16
BLOCK_ORDER = (0, 4, 2, 6, 7, 3, 5, 1)
PIECE_ORDER = (0, 4, 2, 1, 5, 3, 6, 7)
ROOT = math.log2(math.e) / math.sqrt(HDIM)
BF16 = jnp.bfloat16
F32 = jnp.float32


def row_index():
    return lax.axis_index("row")


def pack_tail(wide):
    groups = wide.shape[0] // 4
    return jnp.concatenate([wide[at * groups : (at + 1) * groups] for at in range(4)], axis=1)


def spread_kernel(qkv_hbm, resid_hbm, weight_hbm, grid_hbm, *rest):
    outs = rest[:ROWS]
    chip_ref, slice_ref, grid_out, qkv, resid, main, tile, held, grid, sems = rest[ROWS:]
    me = row_index()
    depth = weight_hbm.shape[0]
    chip = pl.ds(pl.multiple_of(me // 2 * 2 * WIDE, 2 * WIDE), 2 * WIDE)
    ends = pl.ds(pl.multiple_of(MAIN + me // 4 * WIDE, WIDE), WIDE)
    copies = [
        pltpu.make_async_copy(qkv_hbm.at[0], qkv, sems.at[0]),
        pltpu.make_async_copy(resid_hbm.at[0], resid, sems.at[1]),
        pltpu.make_async_copy(weight_hbm.at[:, chip], main, sems.at[2]),
        pltpu.make_async_copy(weight_hbm.at[:, ends], tile, sems.at[3]),
        pltpu.make_async_copy(grid_hbm, grid, sems.at[4]),
    ]
    for copy in copies:
        copy.start()
    for copy in copies[2:]:
        copy.wait()
    low = me // 2 % 2 == 0
    size = depth + depth // 4
    for core in range(2):
        tail = jnp.where(low, tile[:, core * REST : (core + 1) * REST], tile[:, (core + 2) * REST : (core + 3) * REST])
        chip_ref[core * size : core * size + depth, :] = main[:, core * WIDE : (core + 1) * WIDE]
        chip_ref[core * size + depth : (core + 1) * size, :] = pack_tail(tail)
    slice_ref[...] = chip_ref[pl.ds(pl.multiple_of(me % 2 * size, 16), size), :]
    row = lax.broadcasted_iota(jnp.int32, grid_out.shape, 0)
    grid_out[...] = jnp.where(row == 0, grid[0, 0], grid[0, 1])
    for copy in copies[:2]:
        copy.wait()
    for dest in range(ROWS):
        at = dest * HPAIR
        parts = [qkv[:, part * D + at : part * D + at + HPAIR] for part in range(3)]
        parts.append(resid[:, dest * WIDE : (dest + 1) * WIDE])
        parts.append(resid[:, MAIN + dest * REST : MAIN + (dest + 1) * REST])
        held[dest] = jnp.concatenate(parts, axis=1)
    for step in range(ROWS):
        outs[step][...] = held[me ^ step]


def layout_kernel(grid_ref, *rest):
    select_ref, keys_ref, live_ref = rest[-3:]
    rows_n, cols_n = grid_ref[:1, :1], grid_ref[1:2, :1]
    patches = select_ref.shape[0]
    groups = patches // 4
    half = cols_n >> 1
    count = (rows_n >> 1) * half
    slots = lax.broadcasted_iota(jnp.int32, (groups, 1), 0)
    line = jnp.floor((slots.astype(F32) + 0.5) / half.astype(F32)).astype(jnp.int32)
    first = 2 * line * cols_n + 2 * (slots - line * half)
    at = lax.broadcasted_iota(jnp.int32, (groups, patches), 1)
    for corner in range(4):
        wanted = jnp.where(slots < count, first + (corner // 2) * cols_n + corner % 2, -1)
        select_ref[corner * groups : (corner + 1) * groups, :] = jnp.where(at == wanted, 1.0, 0.0).astype(BF16)
    key = lax.broadcasted_iota(jnp.int32, keys_ref.shape, 1)
    keys_ref[...] = jnp.where(key < rows_n * cols_n, 0.0, -1e30)
    slot = lax.broadcasted_iota(jnp.int32, live_ref.shape, 1)
    live_ref[...] = jnp.where(slot < count, 1.0, 0.0)


def attend_kernel(select_ref, dead_ref, *rest):
    blocks = rest[:ROWS]
    out_ref, q_all, k_all, v_all = rest[-4:]
    me = row_index()
    band = blocks[0].shape[0]
    patches = band * ROWS
    for step, block in zip(BLOCK_ORDER, blocks):
        at = pl.ds(pl.multiple_of((me ^ step) * band, band), band)
        q_all[at, :] = block[:, :HPAIR]
        k_all[at, :] = block[:, HPAIR : 2 * HPAIR]
        v_all[at, :] = block[:, 2 * HPAIR : 3 * HPAIR]
    queries = jnp.dot(select_ref[...], q_all[...], preferred_element_type=F32).astype(BF16)
    lane = lax.broadcasted_iota(jnp.int32, (1, HPAIR), 1)
    keys, values, dead = k_all[...], v_all[...], dead_ref[...]
    mixed = []
    for head in range(2):
        mine = (lane >= head * HDIM) & (lane < (head + 1) * HDIM)
        asked = jnp.where(mine, queries, jnp.zeros_like(queries))
        scores = lax.dot_general(asked, keys, (((1,), (1,)), ((), ())), preferred_element_type=F32) + dead
        weights = jnp.exp2((scores - jnp.max(scores, axis=1, keepdims=True)) * ROOT)
        total = jnp.sum(weights, axis=1, keepdims=True)
        mixed.append(jnp.dot(weights.astype(BF16), values, preferred_element_type=F32) / total)
    attn = jnp.where(lane < HDIM, mixed[0], mixed[1])
    out_ref[:patches, :] = attn[:, :WIDE].astype(BF16)
    out_ref[patches:, :] = pack_tail(attn[:, WIDE:]).astype(BF16)


def weight_rows(cut):
    depth = 2 * HPAIR
    packed = cut[depth:]
    tail = jnp.concatenate([packed[:, at * REST : (at + 1) * REST] for at in range(4)], axis=0)
    whole = jnp.concatenate([cut[:depth], tail], axis=1)
    return [whole[core * HPAIR : (core + 1) * HPAIR] for core in range(2)]


def place_rows(rows, base, main_ref, tail_ref):
    for core in range(2):
        pair = base + core
        main_ref[pl.ds(pl.multiple_of(pair * WIDE, WIDE), WIDE), :] = rows[core][:WIDE]
        for corner in range(4):
            spot = pl.multiple_of(pair * WIDE + corner * REST, REST)
            tail_ref[corner, pl.ds(spot, REST), :] = rows[core][WIDE:]


def ready_kernel(select_ref, gain_hbm, token_ref, *rest):
    del token_ref
    blocks = rest[:ROWS]
    own_ref, near_ref = rest[ROWS : ROWS + 2]
    resid_ref, gain_out, main_ref, tail_ref, held, line, sem = rest[-7:]
    fetch = pltpu.make_async_copy(gain_hbm, line, sem)
    fetch.start()
    me = row_index()
    band = blocks[0].shape[0]
    for step, block in zip(BLOCK_ORDER, blocks):
        at = pl.ds(pl.multiple_of((me ^ step) * band, band), band)
        held[at, :] = block[:, 3 * HPAIR :]
    resid_ref[...] = jnp.dot(select_ref[...], held[...], preferred_element_type=F32)
    core = me % 2
    size = own_ref.shape[0]
    half = pl.ds(pl.multiple_of(core * size, 16), size)
    place_slices([(0, own_ref[...]), (3 - 2 * core, near_ref[half, :])], main_ref, tail_ref)
    fetch.wait()
    whole = line[...].reshape(1, D)
    gain = jnp.zeros(gain_out.shape, F32)
    for pair in range(ROWS):
        parts = [whole[:, pair * WIDE : (pair + 1) * WIDE]]
        parts.append(whole[:, MAIN + pair * REST : MAIN + (pair + 1) * REST])
        gain = jnp.where(me == pair, jnp.concatenate(parts, axis=1), gain)
    gain_out[...] = gain


def place_slices(cuts, main_ref, tail_ref):
    tail_ref[...] = jnp.zeros_like(tail_ref)
    for step, cut in cuts:
        place_rows(weight_rows(cut), 2 * lax.rem(lax.axis_index("page") + step, PAGES), main_ref, tail_ref)


def last_kernel(across_ref, swapped_ref, token_ref, main_ref, tail_ref):
    del token_ref
    core = row_index() % 2
    size = across_ref.shape[0]
    half = pl.ds(pl.multiple_of(core * size, 16), size)
    place_slices([(2, across_ref[...]), (1 + 2 * core, swapped_ref[half, :])], main_ref, tail_ref)


def far_block():
    me = row_index()
    return pl.ds(pl.multiple_of((me // 2 ^ 3) * 2 * WIDE, 2 * WIDE), 2 * WIDE)


def collect_late(same, other):
    core = row_index() % 2
    left = jnp.where(core == 0, same[...], other[...])
    right = jnp.where(core == 0, other[...], same[...])
    return jnp.concatenate([left, right], axis=1)


def came_last(block):
    page, core = lax.axis_index("page"), row_index() % 2
    return (block == lax.rem(page + 2, PAGES)) | (block == lax.rem(page + 1 + 2 * core, PAGES))


def add_features(steps, pieces, weights, before_ref, out_ref):
    main_ref, tail_ref, last_main_ref, last_tail_ref = weights
    me = row_index()
    patches = out_ref.shape[0]
    groups = patches // 4
    mains, tails = [], []
    for step in steps:
        pair = me ^ step
        columns = pl.ds(pl.multiple_of(pair * WIDE, WIDE), WIDE)
        is_last = came_last(pair // 2)
        mains.append(jnp.where(is_last, last_main_ref[columns, :], main_ref[columns, :]))
        tails.append([jnp.where(is_last, last_tail_ref[at, columns, :], tail_ref[at, columns, :]) for at in range(4)])
    rows = jnp.concatenate([piece[...] for piece in pieces], axis=1)
    base = before_ref[...] + jnp.dot(rows[:patches], jnp.concatenate(mains, axis=0), preferred_element_type=F32)
    for corner in range(4):
        span = slice(corner * groups, (corner + 1) * groups)
        tail = jnp.concatenate([tail[corner] for tail in tails], axis=0)
        out_ref[span, :] = base[span] + jnp.dot(rows[patches:], tail, preferred_element_type=F32)


def project_first_kernel(own, y, x, *rest):
    add_features((0, 4, 2), (own, y, x), rest[:4], *rest[4:])


def project_second_kernel(own, y, x, *rest):
    add_features((1, 5, 3), (own, y, x), rest[:4], *rest[4:])


def project_kernel(*rest):
    same, other, base_ref, main_ref, tail_ref, last_main_ref, last_tail_ref, gain_ref, out_ref = rest
    patches = base_ref.shape[0]
    groups = patches // 4
    block = far_block()
    is_last = came_last(row_index() // 2 ^ 3)
    full = collect_late(same, other)
    main = jnp.where(is_last, last_main_ref[block, :], main_ref[block, :])
    base = base_ref[...] + jnp.dot(full[:patches], main, preferred_element_type=F32)
    ones = jnp.ones((NOTES, HPAIR), BF16)
    contract = (((1,), (1,)), ((), ()))
    row = lax.broadcasted_iota(jnp.int32, (NOTES, groups), 0)
    notes = jnp.zeros((NOTES, groups), F32)
    ends = []
    for corner in range(4):
        span = slice(corner * groups, (corner + 1) * groups)
        tail = jnp.where(is_last, last_tail_ref[corner, block, :], tail_ref[corner, block, :])
        hidden = base[span] + jnp.dot(full[patches:], tail, preferred_element_type=F32)
        square = hidden * hidden
        high = square.astype(BF16)
        low = (square - high.astype(F32)).astype(BF16)
        total = lax.dot_general(ones, high, contract, preferred_element_type=F32)
        total = total + lax.dot_general(ones, low, contract, preferred_element_type=F32)
        coarse = total.astype(BF16).astype(F32)
        notes = jnp.where(row == corner, coarse, jnp.where(row == 4 + corner, total - coarse, notes))
        sent = hidden * gain_ref[...]
        out_ref[span, :] = sent[:, :WIDE].astype(BF16)
        ends.append(sent[:, WIDE:])
    out_ref[patches : patches + groups, :] = jnp.concatenate(ends, axis=1).astype(BF16)
    out_ref[patches + groups :, :] = notes.astype(BF16)


def tail_kernel(weight_ref, bias_hbm, token_ref, out_ref, bias_out, line, sem):
    del token_ref
    fetch = pltpu.make_async_copy(bias_hbm, line, sem)
    fetch.start()
    for pair in range(ROWS):
        cut = [corner * D + MAIN + pair * REST for corner in range(4)]
        out_ref[:, pair * WIDE : (pair + 1) * WIDE] = jnp.concatenate(
            [weight_ref[:, at : at + REST] for at in cut], axis=1
        )
    fetch.wait()
    units = bias_out.shape[0]
    bias_out[...] = jnp.broadcast_to(line[...].reshape(1, units), (8, units)).T[:, :1]


def merge_product(weight_ref, corner, groups, pieces):
    me = row_index()
    spots = [pl.multiple_of(corner * D + (me ^ step) * WIDE, WIDE) for step, _ in pieces]
    span = slice(corner * groups, (corner + 1) * groups)
    return lax.dot_general(
        jnp.concatenate([weight_ref[:, pl.ds(spot, WIDE)] for spot in spots], axis=1),
        jnp.concatenate([piece[span, :] for _, piece in pieces], axis=1),
        (((1,), (1,)), ((), ())),
        preferred_element_type=F32,
    )


def merge_first_kernel(own, y, x, weight_ref, sum_ref):
    for corner in range(4):
        sum_ref[corner] = merge_product(weight_ref, corner, sum_ref.shape[2], [(0, own), (4, y), (2, x)])


def merge_second_kernel(own, y, x, before_ref, weight_ref, sum_ref):
    for corner in range(4):
        part = merge_product(weight_ref, corner, sum_ref.shape[2], [(1, own), (5, y), (3, x)])
        sum_ref[corner] = before_ref[corner] + part


def merge_kernel(*rest):
    pieces = rest[:ROWS]
    before_ref, weight_ref, tail_ref, bias_ref, live_ref, out_ref, ends_ref = rest[ROWS:]
    me = row_index()
    groups = live_ref.shape[1]
    patches = 4 * groups
    contract = (((1,), (1,)), ((), ()))
    block = pl.multiple_of((me // 2 ^ 3) * 2 * WIDE, 2 * WIDE)
    rows = collect_late(pieces[6], pieces[7])
    parts = []
    for corner in range(4):
        parts.append(
            before_ref[corner]
            + lax.dot_general(
                weight_ref[:, pl.ds(pl.multiple_of(corner * D + block, 2 * WIDE), 2 * WIDE)],
                rows[corner * groups : (corner + 1) * groups],
                contract,
                preferred_element_type=F32,
            )
        )
    notes = jnp.zeros((NOTES, groups), F32)
    for step, piece in zip(PIECE_ORDER, pieces):
        notes = notes + piece[patches + groups :, :].astype(F32)
    scale = lax.rsqrt((notes[:4] + notes[4:8]) * (1.0 / D) + 1e-06)
    spread = jnp.concatenate([jnp.broadcast_to(scale[at : at + 1], (REST, groups)) for at in range(4)], axis=0).T
    for step, piece in zip(PIECE_ORDER, pieces):
        at = pl.ds(pl.multiple_of((me ^ step) * WIDE, WIDE), WIDE)
        ends_ref[:, at] = (piece[patches : patches + groups, :].astype(F32) * spread).astype(BF16)
    total = bias_ref[...] + lax.dot_general(tail_ref[...], ends_ref[...], contract, preferred_element_type=F32)
    for corner in range(4):
        total = total + scale[corner : corner + 1] * parts[corner]
    merged = 0.5 * total * (1.0 + lax.erf(total * math.sqrt(0.5)))
    out_ref[0] = jnp.where(live_ref[...] > 0.0, merged, 0.0).astype(BF16)


def kernel(body, name, out_shape, scratch=(), fetched=(), count=0, limit=24, flops=0, moved=0):
    specs = [pl.BlockSpec(memory_space=pltpu.VMEM) for _ in range(count)]
    for at in fetched:
        specs[at] = pl.BlockSpec(memory_space=pl.ANY)
    return pl.pallas_call(
        body,
        out_shape=out_shape,
        in_specs=specs,
        out_specs=jax.tree.map(lambda _: pl.BlockSpec(memory_space=pltpu.VMEM), out_shape),
        scratch_shapes=list(scratch),
        compiler_params=pltpu.CompilerParams(vmem_limit_bytes=limit * 1024 * 1024),
        cost_estimate=pl.CostEstimate(flops=flops, bytes_accessed=moved, transcendentals=0),
        name=name,
    )


def in_hbm(value):
    return pltpu.with_memory_space_constraint(value, pltpu.HBM)


def shape(*dims, dtype=BF16):
    return jax.ShapeDtypeStruct(dims, dtype)


def swap(value, step):
    return lax.ppermute(value, "row", [(row, row ^ step) for row in range(ROWS)])


def turn(value, low, high):
    pairs = [
        (page * ROWS + row, (page + (high if row % 2 else low)) % PAGES * ROWS + row)
        for page in range(PAGES)
        for row in range(ROWS)
    ]
    return lax.ppermute(value, ("page", "row"), pairs)


def after(value, *arrays):
    return lax.optimization_barrier((value, *arrays))[0]


def local_eight(qkv_rows, residual, out_weight, norm_gain, merge_weight, merge_bias, page_grid):
    band = qkv_rows.shape[1]
    patches = band * ROWS
    groups = patches // 4
    units = merge_weight.shape[0]
    depth = out_weight.shape[0]
    piece = patches + groups
    size = depth + depth // 4

    *sends, chip, own, grid = kernel(
        spread_kernel,
        "spread",
        [shape(band, 4 * HPAIR)] * ROWS
        + [shape(2 * size, WIDE), shape(size, WIDE), shape(8, WIDE, dtype=jnp.int32)],
        [
            pltpu.VMEM((band, 3 * D), BF16),
            pltpu.VMEM((band, D), BF16),
            pltpu.VMEM((depth, 2 * WIDE), BF16),
            pltpu.VMEM((depth, WIDE), BF16),
            pltpu.VMEM((ROWS, band, 4 * HPAIR), BF16),
            pltpu.SMEM(page_grid.shape, jnp.int32),
            pltpu.SemaphoreType.DMA((5,)),
        ],
        fetched=range(4),
        count=4,
        limit=24,
        moved=1 << 20,
    )(in_hbm(qkv_rows), in_hbm(residual), in_hbm(out_weight), in_hbm(page_grid))
    blocks = [sends[0]] + [swap(sends[step], step) for step in BLOCK_ORDER[1:]]
    select, dead, live = kernel(
        layout_kernel,
        "layout",
        [shape(patches, patches), shape(1, patches, dtype=F32), shape(1, groups, dtype=F32)],
        fetched=range(1, 1 + 3),
        count=1 + 3,
        moved=1 << 20,
    )(grid, *blocks[1:4])
    near = turn(after(chip, *()), 1, PAGES - 1)
    swapped = swap(near, 1)
    attn = kernel(
        attend_kernel,
        "attend",
        shape(piece, WIDE),
        [pltpu.VMEM((patches, HPAIR), BF16)] * 3,
        count=2 + ROWS,
        flops=20 * patches * patches * 4096,
        moved=1 << 20,
    )(select, dead, *blocks)
    across = turn(after(own, attn), 2, 2)
    resid, own_gain, main, tail = kernel(
        ready_kernel,
        "ready",
        [shape(patches, HPAIR, dtype=F32), shape(1, HPAIR, dtype=F32), shape(MAIN, HPAIR), shape(4, MAIN, HPAIR)],
        [pltpu.VMEM((patches, HPAIR), BF16), pltpu.VMEM((D,), F32), pltpu.SemaphoreType.DMA],
        fetched=(1, 2),
        count=3 + ROWS + 2,
        flops=10 * patches * patches * 4096,
        moved=4 << 20,
    )(select, in_hbm(norm_gain), attn, *blocks, own, near)
    last = kernel(
        last_kernel,
        "ready_last",
        [shape(MAIN, HPAIR), shape(4, MAIN, HPAIR)],
        fetched=(2,),
        count=3,
        flops=1,
        moved=1,
    )(across, swapped, main)
    y, x, far = [swap(attn, step) for step in (4, 2, 6)]
    weights = (main, tail, *last)
    rows = shape(patches, HPAIR, dtype=F32)
    first = kernel(project_first_kernel, "project_first", rows, count=8, flops=1, moved=1)(attn, y, x, *weights, resid)
    near = [swap(after(attn, last[0]), 1), swap(y, 1), swap(x, 1)]
    second = kernel(project_second_kernel, "project_second", rows, count=8, flops=1, moved=1)(*near, *weights, first)
    hidden = kernel(
        project_kernel,
        "project",
        shape(piece + NOTES, WIDE),
        count=2 + 6,
        flops=patches * MAIN * 256,
        moved=4 << 20,
    )(far, swap(far, 1), second, *weights, own_gain)
    ends, bias = kernel(
        tail_kernel,
        "merge_tail",
        [shape(units, MAIN), shape(units, 1, dtype=F32)],
        [pltpu.VMEM((units,), F32), pltpu.SemaphoreType.DMA],
        fetched=(1, 2),
        count=3,
        moved=4 << 20,
    )(merge_weight, in_hbm(merge_bias), hidden)
    sums = shape(4, units, groups, dtype=F32)
    y, x, far = [swap(hidden, step) for step in (4, 2, 6)]
    first = kernel(merge_first_kernel, "merge_first", sums, count=4, flops=1, moved=1)(hidden, y, x, merge_weight)
    near = [swap(after(hidden, ends), 1), swap(y, 1), swap(x, 1)]
    second = kernel(merge_second_kernel, "merge_second", sums, count=5, flops=1, moved=1)(*near, first, merge_weight)
    return kernel(
        merge_kernel,
        "merge",
        shape(1, units, groups),
        [pltpu.VMEM((groups, MAIN), BF16)],
        count=ROWS + 5,
        flops=4 * units * groups * MAIN,
        moved=8 << 20,
    )(hidden, y, x, *near, far, swap(after(far, first, *near), 1), second, merge_weight, ends, bias, live)


def solution(mesh):
    in_specs = (
        P("page", "row", None),
        P("page", "row", None),
        P("page", None),
        P(),
        P("row", None),
        P("row"),
        P("page", None),
    )
    out_specs = P("page", "row", None)
    local = local_eight if mesh.shape["row"] == 8 and mesh.shape["page"] == 4 else local_any
    return jax.shard_map(local, mesh=mesh, in_specs=in_specs, out_specs=out_specs, check_vma=False)
```

```python
import functools
import math

import jax
import jax.numpy as jnp
from jax import lax
from jax.experimental import pallas as pl
from jax.experimental.pallas import tpu as pltpu
from jax.sharding import PartitionSpec as P

D = 1280
HEADS = 16
HDIM = 80


def local_any(qkv_rows, residual, out_weight, norm_gain, merge_weight, merge_bias, page_grid):
    row_count = lax.axis_size("row")
    q_split = max(1, row_count // HEADS)
    head_groups = row_count // q_split
    width = D // head_groups
    heads_per = width // HDIM
    band_len = qkv_rows.shape[1]
    part_len = band_len // q_split
    local_qkv = qkv_rows[0]
    queries = local_qkv[:, :D]
    key_vals = jnp.concatenate(
        [
            local_qkv[:, D : 2 * D].reshape(band_len, head_groups, width),
            local_qkv[:, 2 * D :].reshape(band_len, head_groups, width),
        ],
        axis=2,
    )
    q_send = (
        queries.reshape(q_split, part_len, head_groups, width)
        .transpose(2, 0, 1, 3)
        .reshape(row_count, part_len, width)
    )
    kv_send = jnp.broadcast_to(
        key_vals.transpose(1, 0, 2)[:, None], (head_groups, q_split, band_len, 2 * width)
    )
    kv_send = kv_send.reshape(row_count, band_len, 2 * width)
    q_recv, kv_recv = (
        lax.all_to_all(q_send, "row", split_axis=0, concat_axis=1, tiled=True),
        lax.all_to_all(kv_send, "row", split_axis=0, concat_axis=1, tiled=True),
    )
    kv_local = kv_recv[0]
    positions = jnp.arange(row_count * band_len, dtype=jnp.int32)
    valid_len = page_grid[0, 0] * page_grid[0, 1]
    key_valid = positions < valid_len
    key_total = kv_local.shape[0]
    key_heads = kv_local[:, :width].reshape(key_total, heads_per, HDIM)
    value_heads = kv_local[:, width:].reshape(key_total, heads_per, HDIM)
    query_total = row_count * part_len
    q_block = math.gcd(query_total, 512)
    q_blocks = q_recv[0].reshape(query_total // q_block, q_block, heads_per, HDIM)
    root_dim = math.sqrt(HDIM)

    def attend(q_span):
        scores = (
            jnp.einsum("qhd,khd->hqk", q_span, key_heads, preferred_element_type=jnp.float32)
            / root_dim
        )
        scores = jnp.where(key_valid[None, None, :], scores, -1e30)
        peak = jnp.max(scores, axis=2, keepdims=True)
        weights = jnp.exp(scores - peak)
        total = jnp.sum(weights, axis=2, keepdims=True)
        mixed = (
            jnp.einsum(
                "hqk,khd->hqd",
                weights.astype(jnp.bfloat16),
                value_heads,
                preferred_element_type=jnp.float32,
            )
            / total
        )
        return mixed.transpose(1, 0, 2).reshape(q_span.shape[0], width).astype(jnp.bfloat16)

    attn_heads = lax.map(attend, q_blocks).reshape(row_count, part_len, width)
    returned = lax.all_to_all(attn_heads, "row", split_axis=0, concat_axis=0, tiled=True)
    attn = (
        returned.reshape(head_groups, q_split, part_len, width)
        .transpose(1, 2, 0, 3)
        .reshape(band_len, D)
    )
    projected = jnp.dot(
        attn,
        lax.all_gather(out_weight, "page", axis=0, tiled=True),
        preferred_element_type=jnp.float32,
    )
    hidden = residual[0].astype(jnp.float32) + projected
    normed = (
        hidden * lax.rsqrt(jnp.mean(hidden * hidden, axis=1, keepdims=True) + 1e-06) * norm_gain
    ).astype(jnp.bfloat16)
    rows_n = page_grid[0, 0]
    cols_n = page_grid[0, 1]
    group_total = band_len * row_count // 4
    slots = jnp.arange(group_total, dtype=jnp.int32)
    half_cols = cols_n // 2
    live = slots < rows_n // 2 * half_cols
    first = jnp.where(live, 2 * (slots // half_cols) * cols_n + 2 * (slots % half_cols), 0)
    corners = [first, first + 1, first + cols_n, first + cols_n + 1]
    local_units = merge_weight.shape[0]
    page_all = lax.all_gather(normed, "row", axis=0, tiled=True)
    merged_sum = jnp.zeros((local_units, group_total), jnp.float32)
    for corner in range(4):
        picked = jnp.take(page_all, corners[corner], axis=0)
        merged_sum = merged_sum + jnp.einsum(
            "md,gd->mg",
            merge_weight[:, corner * D : (corner + 1) * D],
            picked,
            preferred_element_type=jnp.float32,
        )
    merged = jax.nn.gelu(merged_sum + merge_bias[:, None], approximate=False)
    merged = jnp.where(live[None, :], merged, 0.0).astype(jnp.bfloat16)
    return merged[None]


ROWS = 8
PAGES = 4
HPAIR = 2 * HDIM
WIDE = 128
REST = HPAIR - WIDE
MAIN = ROWS * WIDE
NOTES = 16
RECEIVERS = ((0, 0), (4, 2), (2, 4), (6, 6), (7, 7), (3, 5), (5, 3), (1, 1))
SENDERS = ((0, 0), (4, 2), (2, 4), (6, 6), (7, 7), (5, 3), (3, 5), (1, 1))
OWNERS = ((0, 0), (4, 2), (2, 4), (1, 1), (3, 5), (5, 3), (6, 6), (7, 7))
ROOT = math.log2(math.e) / math.sqrt(HDIM)
BF16 = jnp.bfloat16
F32 = jnp.float32


def row_index():
    return lax.axis_index("row")


def steps(pairs):
    core = row_index() % 2
    return [even + (odd - even) * core for even, odd in pairs]


def pack_tail(wide):
    groups = wide.shape[0] // 4
    return jnp.concatenate([wide[at * groups : (at + 1) * groups] for at in range(4)], axis=1)


def spread_kernel(qkv_hbm, resid_hbm, weight_hbm, grid_hbm, *rest):
    outs = rest[:ROWS]
    chip_ref, slice_ref, grid_out, qkv, resid, main, tile, held, grid, sems = rest[ROWS:]
    me = row_index()
    depth = weight_hbm.shape[0]
    chip = pl.ds(pl.multiple_of(me // 2 * 2 * WIDE, 2 * WIDE), 2 * WIDE)
    ends = pl.ds(pl.multiple_of(MAIN + me // 4 * WIDE, WIDE), WIDE)
    copies = [
        pltpu.make_async_copy(qkv_hbm.at[0], qkv, sems.at[0]),
        pltpu.make_async_copy(resid_hbm.at[0], resid, sems.at[1]),
        pltpu.make_async_copy(weight_hbm.at[:, chip], main, sems.at[2]),
        pltpu.make_async_copy(weight_hbm.at[:, ends], tile, sems.at[3]),
        pltpu.make_async_copy(grid_hbm, grid, sems.at[4]),
    ]
    for copy in copies:
        copy.start()
    for copy in copies[2:]:
        copy.wait()
    low = me // 2 % 2 == 0
    size = depth + depth // 4
    for core in range(2):
        tail = jnp.where(low, tile[:, core * REST : (core + 1) * REST], tile[:, (core + 2) * REST : (core + 3) * REST])
        chip_ref[core * size : core * size + depth, :] = main[:, core * WIDE : (core + 1) * WIDE]
        chip_ref[core * size + depth : (core + 1) * size, :] = pack_tail(tail)
    slice_ref[...] = chip_ref[pl.ds(pl.multiple_of(me % 2 * size, 16), size), :]
    row = lax.broadcasted_iota(jnp.int32, grid_out.shape, 0)
    grid_out[...] = jnp.where(row == 0, grid[0, 0], grid[0, 1])
    for copy in copies[:2]:
        copy.wait()
    for dest in range(ROWS):
        at = dest * HPAIR
        parts = [qkv[:, part * D + at : part * D + at + HPAIR] for part in range(3)]
        parts.append(resid[:, dest * WIDE : (dest + 1) * WIDE])
        parts.append(resid[:, MAIN + dest * REST : MAIN + (dest + 1) * REST])
        held[dest] = jnp.concatenate(parts, axis=1)
    for step, out in zip(steps(RECEIVERS), outs):
        out[...] = held[me ^ step]


def layout_kernel(grid_ref, *rest):
    select_ref, keys_ref, live_ref = rest[-3:]
    rows_n, cols_n = grid_ref[:1, :1], grid_ref[1:2, :1]
    patches = select_ref.shape[0]
    groups = patches // 4
    half = cols_n >> 1
    count = (rows_n >> 1) * half
    slots = lax.broadcasted_iota(jnp.int32, (groups, 1), 0)
    line = jnp.floor((slots.astype(F32) + 0.5) / half.astype(F32)).astype(jnp.int32)
    first = 2 * line * cols_n + 2 * (slots - line * half)
    at = lax.broadcasted_iota(jnp.int32, (groups, patches), 1)
    for corner in range(4):
        wanted = jnp.where(slots < count, first + (corner // 2) * cols_n + corner % 2, -1)
        select_ref[corner * groups : (corner + 1) * groups, :] = jnp.where(at == wanted, 1.0, 0.0).astype(BF16)
    key = lax.broadcasted_iota(jnp.int32, keys_ref.shape, 1)
    keys_ref[...] = jnp.where(key < rows_n * cols_n, 0.0, -1e30)
    slot = lax.broadcasted_iota(jnp.int32, live_ref.shape, 1)
    live_ref[...] = jnp.where(slot < count, 1.0, 0.0)


def attend_kernel(select_ref, dead_ref, *rest):
    blocks = rest[:ROWS]
    out_ref, q_all, k_all, v_all = rest[-4:]
    me = row_index()
    band = blocks[0].shape[0]
    patches = band * ROWS
    for step, block in zip(steps(SENDERS), blocks):
        at = pl.ds(pl.multiple_of((me ^ step) * band, band), band)
        q_all[at, :] = block[:, :HPAIR]
        k_all[at, :] = block[:, HPAIR : 2 * HPAIR]
        v_all[at, :] = block[:, 2 * HPAIR : 3 * HPAIR]
    queries = jnp.dot(select_ref[...], q_all[...], preferred_element_type=F32).astype(BF16)
    lane = lax.broadcasted_iota(jnp.int32, (1, HPAIR), 1)
    keys, values, dead = k_all[...], v_all[...], dead_ref[...]
    mixed = []
    for head in range(2):
        mine = (lane >= head * HDIM) & (lane < (head + 1) * HDIM)
        asked = jnp.where(mine, queries, jnp.zeros_like(queries))
        scores = lax.dot_general(asked, keys, (((1,), (1,)), ((), ())), preferred_element_type=F32) + dead
        weights = jnp.exp2((scores - jnp.max(scores, axis=1, keepdims=True)) * ROOT)
        total = jnp.sum(weights, axis=1, keepdims=True)
        mixed.append(jnp.dot(weights.astype(BF16), values, preferred_element_type=F32) / total)
    attn = jnp.where(lane < HDIM, mixed[0], mixed[1])
    out_ref[:patches, :] = attn[:, :WIDE].astype(BF16)
    out_ref[patches:, :] = pack_tail(attn[:, WIDE:]).astype(BF16)


def weight_rows(cut):
    depth = 2 * HPAIR
    packed = cut[depth:]
    tail = jnp.concatenate([packed[:, at * REST : (at + 1) * REST] for at in range(4)], axis=0)
    whole = jnp.concatenate([cut[:depth], tail], axis=1)
    return [whole[core * HPAIR : (core + 1) * HPAIR] for core in range(2)]


def place_rows(rows, base, main_ref, tail_ref):
    for core in range(2):
        pair = base + core
        main_ref[pl.ds(pl.multiple_of(pair * WIDE, WIDE), WIDE), :] = rows[core][:WIDE]
        for corner in range(4):
            spot = pl.multiple_of(pair * WIDE + corner * REST, REST)
            tail_ref[corner, pl.ds(spot, REST), :] = rows[core][WIDE:]


def ready_kernel(select_ref, gain_hbm, token_ref, *rest):
    del token_ref
    blocks = rest[:ROWS]
    own_ref, near_ref = rest[ROWS : ROWS + 2]
    resid_ref, gain_out, main_ref, tail_ref, held, line, sem = rest[-7:]
    fetch = pltpu.make_async_copy(gain_hbm, line, sem)
    fetch.start()
    me = row_index()
    band = blocks[0].shape[0]
    for step, block in zip(steps(SENDERS), blocks):
        at = pl.ds(pl.multiple_of((me ^ step) * band, band), band)
        held[at, :] = block[:, 3 * HPAIR :]
    resid_ref[...] = jnp.dot(select_ref[...], held[...], preferred_element_type=F32)
    core = me % 2
    size = own_ref.shape[0]
    half = pl.ds(pl.multiple_of(core * size, 16), size)
    place_slices([(0, own_ref[...]), (3 - 2 * core, near_ref[half, :])], main_ref, tail_ref)
    fetch.wait()
    whole = line[...].reshape(1, D)
    gain = jnp.zeros(gain_out.shape, F32)
    for pair in range(ROWS):
        parts = [whole[:, pair * WIDE : (pair + 1) * WIDE]]
        parts.append(whole[:, MAIN + pair * REST : MAIN + (pair + 1) * REST])
        gain = jnp.where(me == pair, jnp.concatenate(parts, axis=1), gain)
    gain_out[...] = gain


def place_slices(cuts, main_ref, tail_ref):
    tail_ref[...] = jnp.zeros_like(tail_ref)
    for step, cut in cuts:
        place_rows(weight_rows(cut), 2 * lax.rem(lax.axis_index("page") + step, PAGES), main_ref, tail_ref)


def last_kernel(across_ref, swapped_ref, token_ref, main_ref, tail_ref):
    del token_ref
    core = row_index() % 2
    size = across_ref.shape[0]
    half = pl.ds(pl.multiple_of(core * size, 16), size)
    place_slices([(2, across_ref[...]), (1 + 2 * core, swapped_ref[half, :])], main_ref, tail_ref)


def far_block():
    me = row_index()
    return pl.ds(pl.multiple_of((me // 2 ^ 3) * 2 * WIDE, 2 * WIDE), 2 * WIDE)


def collect_late(same, other):
    core = row_index() % 2
    left = jnp.where(core == 0, same[...], other[...])
    right = jnp.where(core == 0, other[...], same[...])
    return jnp.concatenate([left, right], axis=1)


def came_last(block):
    page, core = lax.axis_index("page"), row_index() % 2
    return (block == lax.rem(page + 2, PAGES)) | (block == lax.rem(page + 1 + 2 * core, PAGES))


def add_features(owners, pieces, weights, before_ref, out_ref):
    main_ref, tail_ref, last_main_ref, last_tail_ref = weights
    me = row_index()
    patches = out_ref.shape[0]
    groups = patches // 4
    mains, tails = [], []
    for step in steps(owners):
        pair = me ^ step
        columns = pl.ds(pl.multiple_of(pair * WIDE, WIDE), WIDE)
        is_last = came_last(pair // 2)
        mains.append(jnp.where(is_last, last_main_ref[columns, :], main_ref[columns, :]))
        tails.append([jnp.where(is_last, last_tail_ref[at, columns, :], tail_ref[at, columns, :]) for at in range(4)])
    rows = jnp.concatenate([piece[...] for piece in pieces], axis=1)
    base = before_ref[...] + jnp.dot(rows[:patches], jnp.concatenate(mains, axis=0), preferred_element_type=F32)
    for corner in range(4):
        span = slice(corner * groups, (corner + 1) * groups)
        tail = jnp.concatenate([tail[corner] for tail in tails], axis=0)
        out_ref[span, :] = base[span] + jnp.dot(rows[patches:], tail, preferred_element_type=F32)


def project_first_kernel(*rest):
    add_features(OWNERS[:3], rest[:3], rest[3:7], *rest[7:])


def project_second_kernel(*rest):
    add_features(OWNERS[3:6], rest[:3], rest[3:7], *rest[7:])


def project_kernel(*rest):
    same, other, base_ref, main_ref, tail_ref, last_main_ref, last_tail_ref, gain_ref, out_ref = rest
    patches = base_ref.shape[0]
    groups = patches // 4
    block = far_block()
    is_last = came_last(row_index() // 2 ^ 3)
    full = collect_late(same, other)
    main = jnp.where(is_last, last_main_ref[block, :], main_ref[block, :])
    base = base_ref[...] + jnp.dot(full[:patches], main, preferred_element_type=F32)
    ones = jnp.ones((NOTES, HPAIR), BF16)
    contract = (((1,), (1,)), ((), ()))
    row = lax.broadcasted_iota(jnp.int32, (NOTES, groups), 0)
    notes = jnp.zeros((NOTES, groups), F32)
    ends = []
    for corner in range(4):
        span = slice(corner * groups, (corner + 1) * groups)
        tail = jnp.where(is_last, last_tail_ref[corner, block, :], tail_ref[corner, block, :])
        hidden = base[span] + jnp.dot(full[patches:], tail, preferred_element_type=F32)
        square = hidden * hidden
        high = square.astype(BF16)
        low = (square - high.astype(F32)).astype(BF16)
        total = lax.dot_general(ones, high, contract, preferred_element_type=F32)
        total = total + lax.dot_general(ones, low, contract, preferred_element_type=F32)
        coarse = total.astype(BF16).astype(F32)
        notes = jnp.where(row == corner, coarse, jnp.where(row == 4 + corner, total - coarse, notes))
        sent = hidden * gain_ref[...]
        out_ref[span, :] = sent[:, :WIDE].astype(BF16)
        ends.append(sent[:, WIDE:])
    out_ref[patches : patches + groups, :] = jnp.concatenate(ends, axis=1).astype(BF16)
    out_ref[patches + groups :, :] = notes.astype(BF16)


def tail_kernel(weight_ref, bias_hbm, token_ref, out_ref, bias_out, line, sem):
    del token_ref
    fetch = pltpu.make_async_copy(bias_hbm, line, sem)
    fetch.start()
    for pair in range(ROWS):
        cut = [corner * D + MAIN + pair * REST for corner in range(4)]
        out_ref[:, pair * WIDE : (pair + 1) * WIDE] = jnp.concatenate(
            [weight_ref[:, at : at + REST] for at in cut], axis=1
        )
    fetch.wait()
    units = bias_out.shape[0]
    bias_out[...] = jnp.broadcast_to(line[...].reshape(1, units), (8, units)).T[:, :1]


def merge_product(weight_ref, corner, groups, pieces):
    me = row_index()
    spots = [pl.multiple_of(corner * D + (me ^ step) * WIDE, WIDE) for step, _ in pieces]
    span = slice(corner * groups, (corner + 1) * groups)
    return lax.dot_general(
        jnp.concatenate([weight_ref[:, pl.ds(spot, WIDE)] for spot in spots], axis=1),
        jnp.concatenate([piece[span, :] for _, piece in pieces], axis=1),
        (((1,), (1,)), ((), ())),
        preferred_element_type=F32,
    )


def merge_first_kernel(*rest):
    pieces, (weight_ref, sum_ref) = list(zip(steps(OWNERS[:3]), rest[:3])), rest[3:]
    for corner in range(4):
        sum_ref[corner] = merge_product(weight_ref, corner, sum_ref.shape[2], pieces)


def merge_second_kernel(*rest):
    pieces, (before_ref, weight_ref, sum_ref) = list(zip(steps(OWNERS[3:6]), rest[:3])), rest[3:]
    for corner in range(4):
        sum_ref[corner] = before_ref[corner] + merge_product(weight_ref, corner, sum_ref.shape[2], pieces)


def merge_kernel(*rest):
    pieces = rest[:ROWS]
    before_ref, weight_ref, tail_ref, bias_ref, live_ref, out_ref, ends_ref = rest[ROWS:]
    me = row_index()
    groups = live_ref.shape[1]
    patches = 4 * groups
    contract = (((1,), (1,)), ((), ()))
    block = pl.multiple_of((me // 2 ^ 3) * 2 * WIDE, 2 * WIDE)
    rows = collect_late(pieces[6], pieces[7])
    parts = []
    for corner in range(4):
        parts.append(
            before_ref[corner]
            + lax.dot_general(
                weight_ref[:, pl.ds(pl.multiple_of(corner * D + block, 2 * WIDE), 2 * WIDE)],
                rows[corner * groups : (corner + 1) * groups],
                contract,
                preferred_element_type=F32,
            )
        )
    notes = jnp.zeros((NOTES, groups), F32)
    for step, piece in zip(steps(OWNERS), pieces):
        notes = notes + piece[patches + groups :, :].astype(F32)
    scale = lax.rsqrt((notes[:4] + notes[4:8]) * (1.0 / D) + 1e-06)
    spread = jnp.concatenate([jnp.broadcast_to(scale[at : at + 1], (REST, groups)) for at in range(4)], axis=0).T
    for step, piece in zip(steps(OWNERS), pieces):
        at = pl.ds(pl.multiple_of((me ^ step) * WIDE, WIDE), WIDE)
        ends_ref[:, at] = (piece[patches : patches + groups, :].astype(F32) * spread).astype(BF16)
    total = bias_ref[...] + lax.dot_general(tail_ref[...], ends_ref[...], contract, preferred_element_type=F32)
    for corner in range(4):
        total = total + scale[corner : corner + 1] * parts[corner]
    merged = 0.5 * total * (1.0 + lax.erf(total * math.sqrt(0.5)))
    out_ref[0] = jnp.where(live_ref[...] > 0.0, merged, 0.0).astype(BF16)


def kernel(body, name, out_shape, scratch=(), fetched=(), count=0, limit=24, flops=0, moved=0):
    specs = [pl.BlockSpec(memory_space=pltpu.VMEM) for _ in range(count)]
    for at in fetched:
        specs[at] = pl.BlockSpec(memory_space=pl.ANY)
    return pl.pallas_call(
        body,
        out_shape=out_shape,
        in_specs=specs,
        out_specs=jax.tree.map(lambda _: pl.BlockSpec(memory_space=pltpu.VMEM), out_shape),
        scratch_shapes=list(scratch),
        compiler_params=pltpu.CompilerParams(vmem_limit_bytes=limit * 1024 * 1024),
        cost_estimate=pl.CostEstimate(flops=flops, bytes_accessed=moved, transcendentals=0),
        name=name,
    )


def in_hbm(value):
    return pltpu.with_memory_space_constraint(value, pltpu.HBM)


def shape(*dims, dtype=BF16):
    return jax.ShapeDtypeStruct(dims, dtype)


def swap(value, even, odd=None):
    odd = even if odd is None else odd
    return lax.ppermute(value, "row", [(row, row ^ (odd if row % 2 else even)) for row in range(ROWS)])


def turn(value, low, high):
    pairs = [
        (page * ROWS + row, (page + (high if row % 2 else low)) % PAGES * ROWS + row)
        for page in range(PAGES)
        for row in range(ROWS)
    ]
    return lax.ppermute(value, ("page", "row"), pairs)


def after(value, *arrays):
    return lax.optimization_barrier((value, *arrays))[0]


def local_eight(qkv_rows, residual, out_weight, norm_gain, merge_weight, merge_bias, page_grid):
    band = qkv_rows.shape[1]
    patches = band * ROWS
    groups = patches // 4
    units = merge_weight.shape[0]
    depth = out_weight.shape[0]
    piece = patches + groups
    size = depth + depth // 4

    *sends, chip, own, grid = kernel(
        spread_kernel,
        "spread",
        [shape(band, 4 * HPAIR)] * ROWS
        + [shape(2 * size, WIDE), shape(size, WIDE), shape(8, WIDE, dtype=jnp.int32)],
        [
            pltpu.VMEM((band, 3 * D), BF16),
            pltpu.VMEM((band, D), BF16),
            pltpu.VMEM((depth, 2 * WIDE), BF16),
            pltpu.VMEM((depth, WIDE), BF16),
            pltpu.VMEM((ROWS, band, 4 * HPAIR), BF16),
            pltpu.SMEM(page_grid.shape, jnp.int32),
            pltpu.SemaphoreType.DMA((5,)),
        ],
        fetched=range(4),
        count=4,
        limit=24,
        moved=1 << 20,
    )(in_hbm(qkv_rows), in_hbm(residual), in_hbm(out_weight), in_hbm(page_grid))
    blocks = [sends[0]] + [swap(send, *pair) for send, pair in zip(sends[1:], RECEIVERS[1:])]
    select, dead, live = kernel(
        layout_kernel,
        "layout",
        [shape(patches, patches), shape(1, patches, dtype=F32), shape(1, groups, dtype=F32)],
        fetched=range(1, 1 + 3),
        count=1 + 3,
        moved=1 << 20,
    )(grid, *blocks[1:4])
    near = turn(after(chip, *()), 1, PAGES - 1)
    swapped = swap(near, 1)
    attn = kernel(
        attend_kernel,
        "attend",
        shape(piece, WIDE),
        [pltpu.VMEM((patches, HPAIR), BF16)] * 3,
        count=2 + ROWS,
        flops=20 * patches * patches * 4096,
        moved=1 << 20,
    )(select, dead, *blocks)
    across = turn(after(own, attn), 2, 2)
    resid, own_gain, main, tail = kernel(
        ready_kernel,
        "ready",
        [shape(patches, HPAIR, dtype=F32), shape(1, HPAIR, dtype=F32), shape(MAIN, HPAIR), shape(4, MAIN, HPAIR)],
        [pltpu.VMEM((patches, HPAIR), BF16), pltpu.VMEM((D,), F32), pltpu.SemaphoreType.DMA],
        fetched=(1, 2),
        count=3 + ROWS + 2,
        flops=10 * patches * patches * 4096,
        moved=4 << 20,
    )(select, in_hbm(norm_gain), attn, *blocks, own, near)
    last = kernel(
        last_kernel,
        "ready_last",
        [shape(MAIN, HPAIR), shape(4, MAIN, HPAIR)],
        fetched=(2,),
        count=3,
        flops=1,
        moved=1,
    )(across, swapped, main)
    one, two, far = swap(attn, 4, 2), swap(attn, 2, 4), swap(attn, 6)
    weights = (main, tail, *last)
    rows = shape(patches, HPAIR, dtype=F32)
    first = kernel(project_first_kernel, "project_first", rows, count=8, flops=1, moved=1)(attn, one, two, *weights, resid)
    near = [swap(after(attn, last[0]), 1), swap(one, 1), swap(two, 1)]
    second = kernel(project_second_kernel, "project_second", rows, count=8, flops=1, moved=1)(*near, *weights, first)
    hidden = kernel(
        project_kernel,
        "project",
        shape(piece + NOTES, WIDE),
        count=2 + 6,
        flops=patches * MAIN * 256,
        moved=4 << 20,
    )(far, swap(far, 1), second, *weights, own_gain)
    ends, bias = kernel(
        tail_kernel,
        "merge_tail",
        [shape(units, MAIN), shape(units, 1, dtype=F32)],
        [pltpu.VMEM((units,), F32), pltpu.SemaphoreType.DMA],
        fetched=(1, 2),
        count=3,
        moved=4 << 20,
    )(merge_weight, in_hbm(merge_bias), hidden)
    sums = shape(4, units, groups, dtype=F32)
    one, two, far = swap(hidden, 4, 2), swap(hidden, 2, 4), swap(hidden, 6)
    first = kernel(merge_first_kernel, "merge_first", sums, count=4, flops=1, moved=1)(hidden, one, two, merge_weight)
    near = [swap(after(hidden, ends), 1), swap(one, 1), swap(two, 1)]
    second = kernel(merge_second_kernel, "merge_second", sums, count=5, flops=1, moved=1)(*near, first, merge_weight)
    return kernel(
        merge_kernel,
        "merge",
        shape(1, units, groups),
        [pltpu.VMEM((groups, MAIN), BF16)],
        count=ROWS + 5,
        flops=4 * units * groups * MAIN,
        moved=8 << 20,
    )(hidden, one, two, *near, far, swap(after(far, first, *near), 1), second, merge_weight, ends, bias, live)


def solution(mesh):
    in_specs = (
        P("page", "row", None),
        P("page", "row", None),
        P("page", None),
        P(),
        P("row", None),
        P("row"),
        P("page", None),
    )
    out_specs = P("page", "row", None)
    local = local_eight if mesh.shape["row"] == 8 and mesh.shape["page"] == 4 else local_any
    return jax.shard_map(local, mesh=mesh, in_specs=in_specs, out_specs=out_specs, check_vma=False)
```

```python
import functools
import math

import jax
import jax.numpy as jnp
from jax import lax
from jax.experimental import pallas as pl
from jax.experimental.pallas import tpu as pltpu
from jax.sharding import PartitionSpec as P

D = 1280
HEADS = 16
HDIM = 80


def local_any(qkv_rows, residual, out_weight, norm_gain, merge_weight, merge_bias, page_grid):
    row_count = lax.axis_size("row")
    q_split = max(1, row_count // HEADS)
    head_groups = row_count // q_split
    width = D // head_groups
    heads_per = width // HDIM
    band_len = qkv_rows.shape[1]
    part_len = band_len // q_split
    local_qkv = qkv_rows[0]
    queries = local_qkv[:, :D]
    key_vals = jnp.concatenate(
        [
            local_qkv[:, D : 2 * D].reshape(band_len, head_groups, width),
            local_qkv[:, 2 * D :].reshape(band_len, head_groups, width),
        ],
        axis=2,
    )
    q_send = (
        queries.reshape(q_split, part_len, head_groups, width)
        .transpose(2, 0, 1, 3)
        .reshape(row_count, part_len, width)
    )
    kv_send = jnp.broadcast_to(
        key_vals.transpose(1, 0, 2)[:, None], (head_groups, q_split, band_len, 2 * width)
    )
    kv_send = kv_send.reshape(row_count, band_len, 2 * width)
    q_recv, kv_recv = (
        lax.all_to_all(q_send, "row", split_axis=0, concat_axis=1, tiled=True),
        lax.all_to_all(kv_send, "row", split_axis=0, concat_axis=1, tiled=True),
    )
    kv_local = kv_recv[0]
    positions = jnp.arange(row_count * band_len, dtype=jnp.int32)
    valid_len = page_grid[0, 0] * page_grid[0, 1]
    key_valid = positions < valid_len
    key_total = kv_local.shape[0]
    key_heads = kv_local[:, :width].reshape(key_total, heads_per, HDIM)
    value_heads = kv_local[:, width:].reshape(key_total, heads_per, HDIM)
    query_total = row_count * part_len
    q_block = math.gcd(query_total, 512)
    q_blocks = q_recv[0].reshape(query_total // q_block, q_block, heads_per, HDIM)
    root_dim = math.sqrt(HDIM)

    def attend(q_span):
        scores = (
            jnp.einsum("qhd,khd->hqk", q_span, key_heads, preferred_element_type=jnp.float32)
            / root_dim
        )
        scores = jnp.where(key_valid[None, None, :], scores, -1e30)
        peak = jnp.max(scores, axis=2, keepdims=True)
        weights = jnp.exp(scores - peak)
        total = jnp.sum(weights, axis=2, keepdims=True)
        mixed = (
            jnp.einsum(
                "hqk,khd->hqd",
                weights.astype(jnp.bfloat16),
                value_heads,
                preferred_element_type=jnp.float32,
            )
            / total
        )
        return mixed.transpose(1, 0, 2).reshape(q_span.shape[0], width).astype(jnp.bfloat16)

    attn_heads = lax.map(attend, q_blocks).reshape(row_count, part_len, width)
    returned = lax.all_to_all(attn_heads, "row", split_axis=0, concat_axis=0, tiled=True)
    attn = (
        returned.reshape(head_groups, q_split, part_len, width)
        .transpose(1, 2, 0, 3)
        .reshape(band_len, D)
    )
    projected = jnp.dot(
        attn,
        lax.all_gather(out_weight, "page", axis=0, tiled=True),
        preferred_element_type=jnp.float32,
    )
    hidden = residual[0].astype(jnp.float32) + projected
    normed = (
        hidden * lax.rsqrt(jnp.mean(hidden * hidden, axis=1, keepdims=True) + 1e-06) * norm_gain
    ).astype(jnp.bfloat16)
    rows_n = page_grid[0, 0]
    cols_n = page_grid[0, 1]
    group_total = band_len * row_count // 4
    slots = jnp.arange(group_total, dtype=jnp.int32)
    half_cols = cols_n // 2
    live = slots < rows_n // 2 * half_cols
    first = jnp.where(live, 2 * (slots // half_cols) * cols_n + 2 * (slots % half_cols), 0)
    corners = [first, first + 1, first + cols_n, first + cols_n + 1]
    local_units = merge_weight.shape[0]
    page_all = lax.all_gather(normed, "row", axis=0, tiled=True)
    merged_sum = jnp.zeros((local_units, group_total), jnp.float32)
    for corner in range(4):
        picked = jnp.take(page_all, corners[corner], axis=0)
        merged_sum = merged_sum + jnp.einsum(
            "md,gd->mg",
            merge_weight[:, corner * D : (corner + 1) * D],
            picked,
            preferred_element_type=jnp.float32,
        )
    merged = jax.nn.gelu(merged_sum + merge_bias[:, None], approximate=False)
    merged = jnp.where(live[None, :], merged, 0.0).astype(jnp.bfloat16)
    return merged[None]


ROWS = 8
PAGES = 4
HPAIR = 2 * HDIM
WIDE = 128
REST = HPAIR - WIDE
MAIN = ROWS * WIDE
NOTES = 16
RECEIVERS = ((0, 0), (6, 6), (7, 7), (4, 2), (2, 4), (3, 5), (5, 3), (1, 1))
SENDERS = ((0, 0), (6, 6), (7, 7), (4, 2), (2, 4), (5, 3), (3, 5), (1, 1))
OWNERS = (0, 4, 2, 1, 5, 3, 6, 7)
ROOT = math.log2(math.e) / math.sqrt(HDIM)
BF16 = jnp.bfloat16
F32 = jnp.float32


def row_index():
    return lax.axis_index("row")


def steps(pairs):
    core = row_index() % 2
    return [even + (odd - even) * core for even, odd in pairs]


def pack_tail(wide):
    groups = wide.shape[0] // 4
    return jnp.concatenate([wide[at * groups : (at + 1) * groups] for at in range(4)], axis=1)


def spread_kernel(qkv_hbm, resid_hbm, weight_hbm, grid_hbm, *rest):
    outs = rest[:ROWS]
    chip_ref, slice_ref, grid_out, qkv, resid, main, tile, held, grid, sems = rest[ROWS:]
    me = row_index()
    depth = weight_hbm.shape[0]
    chip = pl.ds(pl.multiple_of(me // 2 * 2 * WIDE, 2 * WIDE), 2 * WIDE)
    ends = pl.ds(pl.multiple_of(MAIN + me // 4 * WIDE, WIDE), WIDE)
    copies = [
        pltpu.make_async_copy(qkv_hbm.at[0], qkv, sems.at[0]),
        pltpu.make_async_copy(resid_hbm.at[0], resid, sems.at[1]),
        pltpu.make_async_copy(weight_hbm.at[:, chip], main, sems.at[2]),
        pltpu.make_async_copy(weight_hbm.at[:, ends], tile, sems.at[3]),
        pltpu.make_async_copy(grid_hbm, grid, sems.at[4]),
    ]
    for copy in copies:
        copy.start()
    for copy in copies[2:]:
        copy.wait()
    low = me // 2 % 2 == 0
    size = depth + depth // 4
    for core in range(2):
        tail = jnp.where(low, tile[:, core * REST : (core + 1) * REST], tile[:, (core + 2) * REST : (core + 3) * REST])
        chip_ref[core * size : core * size + depth, :] = main[:, core * WIDE : (core + 1) * WIDE]
        chip_ref[core * size + depth : (core + 1) * size, :] = pack_tail(tail)
    slice_ref[...] = chip_ref[pl.ds(pl.multiple_of(me % 2 * size, 16), size), :]
    row = lax.broadcasted_iota(jnp.int32, grid_out.shape, 0)
    grid_out[...] = jnp.where(row == 0, grid[0, 0], grid[0, 1])
    for copy in copies[:2]:
        copy.wait()
    for dest in range(ROWS):
        at = dest * HPAIR
        parts = [qkv[:, part * D + at : part * D + at + HPAIR] for part in range(3)]
        parts.append(resid[:, dest * WIDE : (dest + 1) * WIDE])
        parts.append(resid[:, MAIN + dest * REST : MAIN + (dest + 1) * REST])
        held[dest] = jnp.concatenate(parts, axis=1)
    for step, out in zip(steps(RECEIVERS), outs):
        out[...] = held[me ^ step]


def layout_kernel(grid_ref, *rest):
    select_ref, keys_ref, live_ref = rest[-3:]
    rows_n, cols_n = grid_ref[:1, :1], grid_ref[1:2, :1]
    patches = select_ref.shape[0]
    groups = patches // 4
    half = cols_n >> 1
    count = (rows_n >> 1) * half
    slots = lax.broadcasted_iota(jnp.int32, (groups, 1), 0)
    line = jnp.floor((slots.astype(F32) + 0.5) / half.astype(F32)).astype(jnp.int32)
    first = 2 * line * cols_n + 2 * (slots - line * half)
    at = lax.broadcasted_iota(jnp.int32, (groups, patches), 1)
    for corner in range(4):
        wanted = jnp.where(slots < count, first + (corner // 2) * cols_n + corner % 2, -1)
        select_ref[corner * groups : (corner + 1) * groups, :] = jnp.where(at == wanted, 1.0, 0.0).astype(BF16)
    key = lax.broadcasted_iota(jnp.int32, keys_ref.shape, 1)
    keys_ref[...] = jnp.where(key < rows_n * cols_n, 0.0, -1e30)
    slot = lax.broadcasted_iota(jnp.int32, live_ref.shape, 1)
    live_ref[...] = jnp.where(slot < count, 1.0, 0.0)


def attend_kernel(select_ref, dead_ref, *rest):
    blocks = rest[:ROWS]
    out_ref, q_all, k_all, v_all = rest[-4:]
    me = row_index()
    band = blocks[0].shape[0]
    patches = band * ROWS
    for step, block in zip(steps(SENDERS), blocks):
        at = pl.ds(pl.multiple_of((me ^ step) * band, band), band)
        q_all[at, :] = block[:, :HPAIR]
        k_all[at, :] = block[:, HPAIR : 2 * HPAIR]
        v_all[at, :] = block[:, 2 * HPAIR : 3 * HPAIR]
    queries = jnp.dot(select_ref[...], q_all[...], preferred_element_type=F32).astype(BF16)
    lane = lax.broadcasted_iota(jnp.int32, (1, HPAIR), 1)
    keys, values, dead = k_all[...], v_all[...], dead_ref[...]
    mixed = []
    for head in range(2):
        mine = (lane >= head * HDIM) & (lane < (head + 1) * HDIM)
        asked = jnp.where(mine, queries, jnp.zeros_like(queries))
        scores = lax.dot_general(asked, keys, (((1,), (1,)), ((), ())), preferred_element_type=F32) + dead
        weights = jnp.exp2((scores - jnp.max(scores, axis=1, keepdims=True)) * ROOT)
        total = jnp.sum(weights, axis=1, keepdims=True)
        mixed.append(jnp.dot(weights.astype(BF16), values, preferred_element_type=F32) / total)
    attn = jnp.where(lane < HDIM, mixed[0], mixed[1])
    out_ref[:patches, :] = attn[:, :WIDE].astype(BF16)
    out_ref[patches:, :] = pack_tail(attn[:, WIDE:]).astype(BF16)


def weight_rows(cut):
    depth = 2 * HPAIR
    packed = cut[depth:]
    tail = jnp.concatenate([packed[:, at * REST : (at + 1) * REST] for at in range(4)], axis=0)
    whole = jnp.concatenate([cut[:depth], tail], axis=1)
    return [whole[core * HPAIR : (core + 1) * HPAIR] for core in range(2)]


def place_rows(rows, base, main_ref, tail_ref):
    for core in range(2):
        pair = base + core
        main_ref[pl.ds(pl.multiple_of(pair * WIDE, WIDE), WIDE), :] = rows[core][:WIDE]
        for corner in range(4):
            spot = pl.multiple_of(pair * WIDE + corner * REST, REST)
            tail_ref[corner, pl.ds(spot, REST), :] = rows[core][WIDE:]


def ready_kernel(select_ref, gain_hbm, token_ref, *rest):
    del token_ref
    blocks = rest[:ROWS]
    own_ref, across_ref, near_ref = rest[ROWS : ROWS + 3]
    resid_ref, gain_out, main_ref, tail_ref, held, line, sem = rest[-7:]
    fetch = pltpu.make_async_copy(gain_hbm, line, sem)
    fetch.start()
    me = row_index()
    page = lax.axis_index("page")
    band = blocks[0].shape[0]
    for step, block in zip(steps(SENDERS), blocks):
        at = pl.ds(pl.multiple_of((me ^ step) * band, band), band)
        held[at, :] = block[:, 3 * HPAIR :]
    resid_ref[...] = jnp.dot(select_ref[...], held[...], preferred_element_type=F32)
    main_ref[...] = jnp.zeros_like(main_ref)
    tail_ref[...] = jnp.zeros_like(tail_ref)
    core = me % 2
    size = own_ref.shape[0]
    half = pl.ds(pl.multiple_of(core * size, 16), size)
    cuts = ((0, own_ref[...]), (2, across_ref[...]), (3 - 2 * core, near_ref[half, :]))
    for step, cut in cuts:
        place_rows(weight_rows(cut), 2 * lax.rem(page + step, PAGES), main_ref, tail_ref)
    fetch.wait()
    whole = line[...].reshape(1, D)
    gain = jnp.zeros(gain_out.shape, F32)
    for pair in range(ROWS):
        parts = [whole[:, pair * WIDE : (pair + 1) * WIDE]]
        parts.append(whole[:, MAIN + pair * REST : MAIN + (pair + 1) * REST])
        gain = jnp.where(me == pair, jnp.concatenate(parts, axis=1), gain)
    gain_out[...] = gain


def last_kernel(swapped_ref, token_ref, main_ref, tail_ref):
    del token_ref
    size = swapped_ref.shape[0] // 2
    cut = swapped_ref[pl.ds(pl.multiple_of(row_index() % 2 * size, 16), size), :]
    tail_ref[...] = jnp.zeros_like(tail_ref)
    place_rows(weight_rows(cut), 0, main_ref, tail_ref)


def far_block():
    me = row_index()
    return pl.ds(pl.multiple_of((me // 2 ^ 3) * 2 * WIDE, 2 * WIDE), 2 * WIDE)


def collect_late(same, other):
    core = row_index() % 2
    left = jnp.where(core == 0, same[...], other[...])
    right = jnp.where(core == 0, other[...], same[...])
    return jnp.concatenate([left, right], axis=1)


def late_source():
    return lax.rem(lax.axis_index("page") + 1 + 2 * (row_index() % 2), PAGES)


def add_features(owners, pieces, weights, before_ref, out_ref):
    main_ref, tail_ref, last_main_ref, last_tail_ref = weights
    me = row_index()
    patches = out_ref.shape[0]
    groups = patches // 4
    mains, tails = [], []
    for step in owners:
        pair = me ^ step
        columns = pl.ds(pl.multiple_of(pair * WIDE, WIDE), WIDE)
        late = pl.ds(pl.multiple_of(pair % 2 * WIDE, WIDE), WIDE)
        is_late = pair // 2 == late_source()
        mains.append(jnp.where(is_late, last_main_ref[late, :], main_ref[columns, :]))
        tails.append([jnp.where(is_late, last_tail_ref[at, late, :], tail_ref[at, columns, :]) for at in range(4)])
    rows = jnp.concatenate([piece[...] for piece in pieces], axis=1)
    base = before_ref[...] + jnp.dot(rows[:patches], jnp.concatenate(mains, axis=0), preferred_element_type=F32)
    for corner in range(4):
        span = slice(corner * groups, (corner + 1) * groups)
        tail = jnp.concatenate([tail[corner] for tail in tails], axis=0)
        out_ref[span, :] = base[span] + jnp.dot(rows[patches:], tail, preferred_element_type=F32)


def project_first_kernel(*rest):
    add_features(OWNERS[:3], rest[:3], rest[3:7], *rest[7:])


def project_second_kernel(*rest):
    add_features(OWNERS[3:6], rest[:3], rest[3:7], *rest[7:])


def project_kernel(*rest):
    same, other, base_ref, main_ref, tail_ref, last_main_ref, last_tail_ref, gain_ref, out_ref = rest
    patches = base_ref.shape[0]
    groups = patches // 4
    block = far_block()
    is_last = late_source() == (row_index() // 2 ^ 3)
    full = collect_late(same, other)
    main = jnp.where(is_last, last_main_ref[...], main_ref[block, :])
    base = base_ref[...] + jnp.dot(full[:patches], main, preferred_element_type=F32)
    ones = jnp.ones((NOTES, HPAIR), BF16)
    contract = (((1,), (1,)), ((), ()))
    row = lax.broadcasted_iota(jnp.int32, (NOTES, groups), 0)
    notes = jnp.zeros((NOTES, groups), F32)
    ends = []
    for corner in range(4):
        span = slice(corner * groups, (corner + 1) * groups)
        tail = jnp.where(is_last, last_tail_ref[corner], tail_ref[corner, block, :])
        hidden = base[span] + jnp.dot(full[patches:], tail, preferred_element_type=F32)
        square = hidden * hidden
        high = square.astype(BF16)
        low = (square - high.astype(F32)).astype(BF16)
        total = lax.dot_general(ones, high, contract, preferred_element_type=F32)
        total = total + lax.dot_general(ones, low, contract, preferred_element_type=F32)
        coarse = total.astype(BF16).astype(F32)
        notes = jnp.where(row == corner, coarse, jnp.where(row == 4 + corner, total - coarse, notes))
        sent = hidden * gain_ref[...]
        out_ref[span, :] = sent[:, :WIDE].astype(BF16)
        ends.append(sent[:, WIDE:])
    out_ref[patches : patches + groups, :] = jnp.concatenate(ends, axis=1).astype(BF16)
    out_ref[patches + groups :, :] = notes.astype(BF16)


def tail_kernel(weight_ref, bias_hbm, token_ref, out_ref, bias_out, line, sem):
    del token_ref
    fetch = pltpu.make_async_copy(bias_hbm, line, sem)
    fetch.start()
    for pair in range(ROWS):
        cut = [corner * D + MAIN + pair * REST for corner in range(4)]
        out_ref[:, pair * WIDE : (pair + 1) * WIDE] = jnp.concatenate(
            [weight_ref[:, at : at + REST] for at in cut], axis=1
        )
    fetch.wait()
    units = bias_out.shape[0]
    bias_out[...] = jnp.broadcast_to(line[...].reshape(1, units), (8, units)).T[:, :1]


def merge_product(weight_ref, corner, groups, pieces):
    me = row_index()
    spots = [pl.multiple_of(corner * D + (me ^ step) * WIDE, WIDE) for step, _ in pieces]
    span = slice(corner * groups, (corner + 1) * groups)
    return lax.dot_general(
        jnp.concatenate([weight_ref[:, pl.ds(spot, WIDE)] for spot in spots], axis=1),
        jnp.concatenate([piece[span, :] for _, piece in pieces], axis=1),
        (((1,), (1,)), ((), ())),
        preferred_element_type=F32,
    )


def merge_first_kernel(*rest):
    pieces, (weight_ref, sum_ref) = list(zip(OWNERS[:3], rest[:3])), rest[3:]
    for corner in range(4):
        sum_ref[corner] = merge_product(weight_ref, corner, sum_ref.shape[2], pieces)


def merge_second_kernel(*rest):
    pieces, (before_ref, weight_ref, sum_ref) = list(zip(OWNERS[3:6], rest[:3])), rest[3:]
    for corner in range(4):
        sum_ref[corner] = before_ref[corner] + merge_product(weight_ref, corner, sum_ref.shape[2], pieces)


def merge_kernel(*rest):
    pieces = rest[:ROWS]
    before_ref, weight_ref, tail_ref, bias_ref, live_ref, out_ref, ends_ref = rest[ROWS:]
    me = row_index()
    groups = live_ref.shape[1]
    patches = 4 * groups
    contract = (((1,), (1,)), ((), ()))
    block = pl.multiple_of((me // 2 ^ 3) * 2 * WIDE, 2 * WIDE)
    rows = collect_late(pieces[6], pieces[7])
    parts = []
    for corner in range(4):
        parts.append(
            before_ref[corner]
            + lax.dot_general(
                weight_ref[:, pl.ds(pl.multiple_of(corner * D + block, 2 * WIDE), 2 * WIDE)],
                rows[corner * groups : (corner + 1) * groups],
                contract,
                preferred_element_type=F32,
            )
        )
    notes = jnp.zeros((NOTES, groups), F32)
    for step, piece in zip(OWNERS, pieces):
        notes = notes + piece[patches + groups :, :].astype(F32)
    scale = lax.rsqrt((notes[:4] + notes[4:8]) * (1.0 / D) + 1e-06)
    spread = jnp.concatenate([jnp.broadcast_to(scale[at : at + 1], (REST, groups)) for at in range(4)], axis=0).T
    for step, piece in zip(OWNERS, pieces):
        at = pl.ds(pl.multiple_of((me ^ step) * WIDE, WIDE), WIDE)
        ends_ref[:, at] = (piece[patches : patches + groups, :].astype(F32) * spread).astype(BF16)
    total = bias_ref[...] + lax.dot_general(tail_ref[...], ends_ref[...], contract, preferred_element_type=F32)
    for corner in range(4):
        total = total + scale[corner : corner + 1] * parts[corner]
    merged = 0.5 * total * (1.0 + lax.erf(total * math.sqrt(0.5)))
    out_ref[0] = jnp.where(live_ref[...] > 0.0, merged, 0.0).astype(BF16)


def kernel(body, name, out_shape, scratch=(), fetched=(), count=0, limit=24, flops=0, moved=0):
    specs = [pl.BlockSpec(memory_space=pltpu.VMEM) for _ in range(count)]
    for at in fetched:
        specs[at] = pl.BlockSpec(memory_space=pl.ANY)
    return pl.pallas_call(
        body,
        out_shape=out_shape,
        in_specs=specs,
        out_specs=jax.tree.map(lambda _: pl.BlockSpec(memory_space=pltpu.VMEM), out_shape),
        scratch_shapes=list(scratch),
        compiler_params=pltpu.CompilerParams(vmem_limit_bytes=limit * 1024 * 1024),
        cost_estimate=pl.CostEstimate(flops=flops, bytes_accessed=moved, transcendentals=0),
        name=name,
    )


def in_hbm(value):
    return pltpu.with_memory_space_constraint(value, pltpu.HBM)


def shape(*dims, dtype=BF16):
    return jax.ShapeDtypeStruct(dims, dtype)


def swap(value, even, odd=None):
    odd = even if odd is None else odd
    return lax.ppermute(value, "row", [(row, row ^ (odd if row % 2 else even)) for row in range(ROWS)])


def turn(value, low, high):
    pairs = [
        (page * ROWS + row, (page + (high if row % 2 else low)) % PAGES * ROWS + row)
        for page in range(PAGES)
        for row in range(ROWS)
    ]
    return lax.ppermute(value, ("page", "row"), pairs)


def after(value, *arrays):
    return lax.optimization_barrier((value, *arrays))[0]


def local_eight(qkv_rows, residual, out_weight, norm_gain, merge_weight, merge_bias, page_grid):
    band = qkv_rows.shape[1]
    patches = band * ROWS
    groups = patches // 4
    units = merge_weight.shape[0]
    depth = out_weight.shape[0]
    piece = patches + groups
    size = depth + depth // 4

    *sends, chip, own, grid = kernel(
        spread_kernel,
        "spread",
        [shape(band, 4 * HPAIR)] * ROWS
        + [shape(2 * size, WIDE), shape(size, WIDE), shape(8, WIDE, dtype=jnp.int32)],
        [
            pltpu.VMEM((band, 3 * D), BF16),
            pltpu.VMEM((band, D), BF16),
            pltpu.VMEM((depth, 2 * WIDE), BF16),
            pltpu.VMEM((depth, WIDE), BF16),
            pltpu.VMEM((ROWS, band, 4 * HPAIR), BF16),
            pltpu.SMEM(page_grid.shape, jnp.int32),
            pltpu.SemaphoreType.DMA((5,)),
        ],
        fetched=range(4),
        count=4,
        limit=24,
        moved=1 << 20,
    )(in_hbm(qkv_rows), in_hbm(residual), in_hbm(out_weight), in_hbm(page_grid))
    blocks = [sends[0]] + [swap(send, *pair) for send, pair in zip(sends[1:], RECEIVERS[1:])]
    select, dead, live = kernel(
        layout_kernel,
        "layout",
        [shape(patches, patches), shape(1, patches, dtype=F32), shape(1, groups, dtype=F32)],
        fetched=range(1, 1 + 2),
        count=1 + 2,
        moved=1 << 20,
    )(grid, *blocks[1:3])
    across = turn(after(own, *()), 2, 2)
    near = turn(after(chip, *()), 1, PAGES - 1)
    swapped = swap(near, 1)
    attn = kernel(
        attend_kernel,
        "attend",
        shape(piece, WIDE),
        [pltpu.VMEM((patches, HPAIR), BF16)] * 3,
        count=2 + ROWS,
        flops=20 * patches * patches * 4096,
        moved=1 << 20,
    )(select, dead, *blocks)
    resid, own_gain, main, tail = kernel(
        ready_kernel,
        "ready",
        [shape(patches, HPAIR, dtype=F32), shape(1, HPAIR, dtype=F32), shape(MAIN, HPAIR), shape(4, MAIN, HPAIR)],
        [pltpu.VMEM((patches, HPAIR), BF16), pltpu.VMEM((D,), F32), pltpu.SemaphoreType.DMA],
        fetched=(1, 2),
        count=3 + ROWS + 3,
        flops=10 * patches * patches * 4096,
        moved=4 << 20,
    )(select, in_hbm(norm_gain), attn, *blocks, own, across, near)
    last = kernel(
        last_kernel,
        "ready_last",
        [shape(2 * WIDE, HPAIR), shape(4, 2 * WIDE, HPAIR)],
        fetched=(1,),
        count=2,
        moved=4 << 20,
    )(swapped, main)
    one, two, far = swap(attn, 4), swap(attn, 2), swap(attn, 6)
    weights = (main, tail, *last)
    rows = shape(patches, HPAIR, dtype=F32)
    first = kernel(project_first_kernel, "project_first", rows, count=8, flops=1, moved=1)(attn, one, two, *weights, resid)
    near = [swap(after(attn, main), 1), swap(after(one, last[0]), 1), swap(two, 1)]
    second = kernel(project_second_kernel, "project_second", rows, count=8, flops=1, moved=1)(*near, *weights, first)
    hidden = kernel(
        project_kernel,
        "project",
        shape(piece + NOTES, WIDE),
        count=2 + 6,
        flops=patches * MAIN * 256,
        moved=4 << 20,
    )(far, swap(after(far, first), 1), second, *weights, own_gain)
    ends, bias = kernel(
        tail_kernel,
        "merge_tail",
        [shape(units, MAIN), shape(units, 1, dtype=F32)],
        [pltpu.VMEM((units,), F32), pltpu.SemaphoreType.DMA],
        fetched=(1, 2),
        count=3,
        moved=4 << 20,
    )(merge_weight, in_hbm(merge_bias), hidden)
    sums = shape(4, units, groups, dtype=F32)
    one, two, far = swap(hidden, 4), swap(hidden, 2), swap(hidden, 6)
    first = kernel(merge_first_kernel, "merge_first", sums, count=4, flops=1, moved=1)(hidden, one, two, merge_weight)
    near = [swap(after(hidden, ends), 1), swap(one, 1), swap(two, 1)]
    second = kernel(merge_second_kernel, "merge_second", sums, count=5, flops=1, moved=1)(*near, first, merge_weight)
    return kernel(
        merge_kernel,
        "merge",
        shape(1, units, groups),
        [pltpu.VMEM((groups, MAIN), BF16)],
        count=ROWS + 5,
        flops=4 * units * groups * MAIN,
        moved=8 << 20,
    )(hidden, one, two, *near, far, swap(after(far, first, *near), 1), second, merge_weight, ends, bias, live)


def solution(mesh):
    in_specs = (
        P("page", "row", None),
        P("page", "row", None),
        P("page", None),
        P(),
        P("row", None),
        P("row"),
        P("page", None),
    )
    out_specs = P("page", "row", None)
    local = local_eight if mesh.shape["row"] == 8 and mesh.shape["page"] == 4 else local_any
    return jax.shard_map(local, mesh=mesh, in_specs=in_specs, out_specs=out_specs, check_vma=False)
```

```python
import functools
import math

import jax
import jax.numpy as jnp
from jax import lax
from jax.experimental import pallas as pl
from jax.experimental.pallas import tpu as pltpu
from jax.sharding import PartitionSpec as P

D = 1280
HEADS = 16
HDIM = 80


def local_any(qkv_rows, residual, out_weight, norm_gain, merge_weight, merge_bias, page_grid):
    row_count = lax.axis_size("row")
    q_split = max(1, row_count // HEADS)
    head_groups = row_count // q_split
    width = D // head_groups
    heads_per = width // HDIM
    band_len = qkv_rows.shape[1]
    part_len = band_len // q_split
    local_qkv = qkv_rows[0]
    queries = local_qkv[:, :D]
    key_vals = jnp.concatenate(
        [
            local_qkv[:, D : 2 * D].reshape(band_len, head_groups, width),
            local_qkv[:, 2 * D :].reshape(band_len, head_groups, width),
        ],
        axis=2,
    )
    q_send = (
        queries.reshape(q_split, part_len, head_groups, width)
        .transpose(2, 0, 1, 3)
        .reshape(row_count, part_len, width)
    )
    kv_send = jnp.broadcast_to(
        key_vals.transpose(1, 0, 2)[:, None], (head_groups, q_split, band_len, 2 * width)
    )
    kv_send = kv_send.reshape(row_count, band_len, 2 * width)
    q_recv, kv_recv = (
        lax.all_to_all(q_send, "row", split_axis=0, concat_axis=1, tiled=True),
        lax.all_to_all(kv_send, "row", split_axis=0, concat_axis=1, tiled=True),
    )
    kv_local = kv_recv[0]
    positions = jnp.arange(row_count * band_len, dtype=jnp.int32)
    valid_len = page_grid[0, 0] * page_grid[0, 1]
    key_valid = positions < valid_len
    key_total = kv_local.shape[0]
    key_heads = kv_local[:, :width].reshape(key_total, heads_per, HDIM)
    value_heads = kv_local[:, width:].reshape(key_total, heads_per, HDIM)
    query_total = row_count * part_len
    q_block = math.gcd(query_total, 512)
    q_blocks = q_recv[0].reshape(query_total // q_block, q_block, heads_per, HDIM)
    root_dim = math.sqrt(HDIM)

    def attend(q_span):
        scores = (
            jnp.einsum("qhd,khd->hqk", q_span, key_heads, preferred_element_type=jnp.float32)
            / root_dim
        )
        scores = jnp.where(key_valid[None, None, :], scores, -1e30)
        peak = jnp.max(scores, axis=2, keepdims=True)
        weights = jnp.exp(scores - peak)
        total = jnp.sum(weights, axis=2, keepdims=True)
        mixed = (
            jnp.einsum(
                "hqk,khd->hqd",
                weights.astype(jnp.bfloat16),
                value_heads,
                preferred_element_type=jnp.float32,
            )
            / total
        )
        return mixed.transpose(1, 0, 2).reshape(q_span.shape[0], width).astype(jnp.bfloat16)

    attn_heads = lax.map(attend, q_blocks).reshape(row_count, part_len, width)
    returned = lax.all_to_all(attn_heads, "row", split_axis=0, concat_axis=0, tiled=True)
    attn = (
        returned.reshape(head_groups, q_split, part_len, width)
        .transpose(1, 2, 0, 3)
        .reshape(band_len, D)
    )
    projected = jnp.dot(
        attn,
        lax.all_gather(out_weight, "page", axis=0, tiled=True),
        preferred_element_type=jnp.float32,
    )
    hidden = residual[0].astype(jnp.float32) + projected
    normed = (
        hidden * lax.rsqrt(jnp.mean(hidden * hidden, axis=1, keepdims=True) + 1e-06) * norm_gain
    ).astype(jnp.bfloat16)
    rows_n = page_grid[0, 0]
    cols_n = page_grid[0, 1]
    group_total = band_len * row_count // 4
    slots = jnp.arange(group_total, dtype=jnp.int32)
    half_cols = cols_n // 2
    live = slots < rows_n // 2 * half_cols
    first = jnp.where(live, 2 * (slots // half_cols) * cols_n + 2 * (slots % half_cols), 0)
    corners = [first, first + 1, first + cols_n, first + cols_n + 1]
    local_units = merge_weight.shape[0]
    page_all = lax.all_gather(normed, "row", axis=0, tiled=True)
    merged_sum = jnp.zeros((local_units, group_total), jnp.float32)
    for corner in range(4):
        picked = jnp.take(page_all, corners[corner], axis=0)
        merged_sum = merged_sum + jnp.einsum(
            "md,gd->mg",
            merge_weight[:, corner * D : (corner + 1) * D],
            picked,
            preferred_element_type=jnp.float32,
        )
    merged = jax.nn.gelu(merged_sum + merge_bias[:, None], approximate=False)
    merged = jnp.where(live[None, :], merged, 0.0).astype(jnp.bfloat16)
    return merged[None]


ROWS = 8
PAGES = 4
HPAIR = 2 * HDIM
WIDE = 128
REST = HPAIR - WIDE
MAIN = ROWS * WIDE
NOTES = 16
RECEIVERS = ((0, 0), (4, 2), (2, 4), (6, 6), (7, 7), (3, 5), (5, 3), (1, 1))
SENDERS = ((0, 0), (4, 2), (2, 4), (6, 6), (7, 7), (5, 3), (3, 5), (1, 1))
OWNERS = (0, 4, 2, 1, 5, 3, 6, 7)
ROOT = math.log2(math.e) / math.sqrt(HDIM)
BF16 = jnp.bfloat16
F32 = jnp.float32


def row_index():
    return lax.axis_index("row")


def steps(pairs):
    core = row_index() % 2
    return [even + (odd - even) * core for even, odd in pairs]


def pack_tail(wide):
    groups = wide.shape[0] // 4
    return jnp.concatenate([wide[at * groups : (at + 1) * groups] for at in range(4)], axis=1)


def spread_kernel(qkv_hbm, resid_hbm, grid_hbm, *rest):
    outs = rest[:ROWS]
    grid_out, qkv, resid, held, grid, sems = rest[ROWS:]
    me = row_index()
    copies = [
        pltpu.make_async_copy(grid_hbm, grid, sems.at[0]),
        pltpu.make_async_copy(resid_hbm.at[0], resid, sems.at[1]),
    ]
    part = qkv.shape[0] // 4
    for at in range(4):
        rows = pl.ds(at * part, part)
        copies.append(pltpu.make_async_copy(qkv_hbm.at[0, rows], qkv.at[rows], sems.at[2 + at]))
    for copy in reversed(copies):
        copy.start()
    for copy in copies:
        copy.wait()
    for dest in range(ROWS):
        at = dest * HPAIR
        parts = [qkv[:, part * D + at : part * D + at + HPAIR] for part in range(3)]
        parts.append(resid[:, dest * WIDE : (dest + 1) * WIDE])
        parts.append(resid[:, MAIN + dest * REST : MAIN + (dest + 1) * REST])
        held[dest] = jnp.concatenate(parts, axis=1)
    for step, out in zip(steps(RECEIVERS), outs):
        out[...] = held[me ^ step]
    row = lax.broadcasted_iota(jnp.int32, grid_out.shape, 0)
    grid_out[...] = jnp.where(row == 0, grid[0, 0], grid[0, 1])


def slice_kernel(weight_ref, *rest):
    chip_ref, slice_ref = rest[-2:]
    me = row_index()
    depth = weight_ref.shape[0]
    main = weight_ref[:, pl.ds(pl.multiple_of(me // 2 * 2 * WIDE, 2 * WIDE), 2 * WIDE)]
    tile = weight_ref[:, pl.ds(pl.multiple_of(MAIN + me // 4 * WIDE, WIDE), WIDE)]
    low = me // 2 % 2 == 0
    size = depth + depth // 4
    for core in range(2):
        tail = jnp.where(low, tile[:, core * REST : (core + 1) * REST], tile[:, (core + 2) * REST : (core + 3) * REST])
        chip_ref[core * size : core * size + depth, :] = main[:, core * WIDE : (core + 1) * WIDE]
        chip_ref[core * size + depth : (core + 1) * size, :] = pack_tail(tail)
    slice_ref[...] = chip_ref[pl.ds(pl.multiple_of(me % 2 * size, 16), size), :]


def layout_kernel(grid_ref, *rest):
    select_ref, keys_ref, live_ref = rest[-3:]
    rows_n, cols_n = grid_ref[:1, :1], grid_ref[1:2, :1]
    patches = select_ref.shape[0]
    groups = patches // 4
    half = cols_n >> 1
    count = (rows_n >> 1) * half
    slots = lax.broadcasted_iota(jnp.int32, (groups, 1), 0)
    line = jnp.floor((slots.astype(F32) + 0.5) / half.astype(F32)).astype(jnp.int32)
    first = 2 * line * cols_n + 2 * (slots - line * half)
    at = lax.broadcasted_iota(jnp.int32, (groups, patches), 1)
    for corner in range(4):
        wanted = jnp.where(slots < count, first + (corner // 2) * cols_n + corner % 2, -1)
        select_ref[corner * groups : (corner + 1) * groups, :] = jnp.where(at == wanted, 1.0, 0.0).astype(BF16)
    key = lax.broadcasted_iota(jnp.int32, keys_ref.shape, 1)
    keys_ref[...] = jnp.where(key < rows_n * cols_n, 0.0, -1e30)
    slot = lax.broadcasted_iota(jnp.int32, live_ref.shape, 1)
    live_ref[...] = jnp.where(slot < count, 1.0, 0.0)


def attend_kernel(select_ref, dead_ref, *rest):
    blocks = rest[:ROWS]
    out_ref, q_all, k_all, v_all = rest[-4:]
    me = row_index()
    band = blocks[0].shape[0]
    patches = band * ROWS
    for step, block in zip(steps(SENDERS), blocks):
        at = pl.ds(pl.multiple_of((me ^ step) * band, band), band)
        q_all[at, :] = block[:, :HPAIR]
        k_all[at, :] = block[:, HPAIR : 2 * HPAIR]
        v_all[at, :] = block[:, 2 * HPAIR : 3 * HPAIR]
    queries = jnp.dot(select_ref[...], q_all[...], preferred_element_type=F32).astype(BF16)
    lane = lax.broadcasted_iota(jnp.int32, (1, HPAIR), 1)
    keys, values, dead = k_all[...], v_all[...], dead_ref[...]
    mixed = []
    for head in range(2):
        mine = (lane >= head * HDIM) & (lane < (head + 1) * HDIM)
        asked = jnp.where(mine, queries, jnp.zeros_like(queries))
        scores = lax.dot_general(asked, keys, (((1,), (1,)), ((), ())), preferred_element_type=F32) + dead
        weights = jnp.exp2((scores - jnp.max(scores, axis=1, keepdims=True)) * ROOT)
        total = jnp.sum(weights, axis=1, keepdims=True)
        mixed.append(jnp.dot(weights.astype(BF16), values, preferred_element_type=F32) / total)
    attn = jnp.where(lane < HDIM, mixed[0], mixed[1])
    out_ref[:patches, :] = attn[:, :WIDE].astype(BF16)
    out_ref[patches:, :] = pack_tail(attn[:, WIDE:]).astype(BF16)


def weight_rows(cut):
    depth = 2 * HPAIR
    packed = cut[depth:]
    tail = jnp.concatenate([packed[:, at * REST : (at + 1) * REST] for at in range(4)], axis=0)
    whole = jnp.concatenate([cut[:depth], tail], axis=1)
    return [whole[core * HPAIR : (core + 1) * HPAIR] for core in range(2)]


def place_rows(rows, base, main_ref, tail_ref):
    for core in range(2):
        pair = base + core
        main_ref[pl.ds(pl.multiple_of(pair * WIDE, WIDE), WIDE), :] = rows[core][:WIDE]
        for corner in range(4):
            spot = pl.multiple_of(pair * WIDE + corner * REST, REST)
            tail_ref[corner, pl.ds(spot, REST), :] = rows[core][WIDE:]


def ready_kernel(select_ref, gain_hbm, token_ref, *rest):
    del token_ref
    blocks = rest[:ROWS]
    own_ref, near_ref = rest[ROWS : ROWS + 2]
    resid_ref, gain_out, main_ref, tail_ref, held, line, sem = rest[-7:]
    fetch = pltpu.make_async_copy(gain_hbm, line, sem)
    fetch.start()
    me = row_index()
    band = blocks[0].shape[0]
    for step, block in zip(steps(SENDERS), blocks):
        at = pl.ds(pl.multiple_of((me ^ step) * band, band), band)
        held[at, :] = block[:, 3 * HPAIR :]
    resid_ref[...] = jnp.dot(select_ref[...], held[...], preferred_element_type=F32)
    core = me % 2
    size = own_ref.shape[0]
    half = pl.ds(pl.multiple_of(core * size, 16), size)
    place_slices([(0, own_ref[...]), (3 - 2 * core, near_ref[half, :])], main_ref, tail_ref)
    fetch.wait()
    whole = line[...].reshape(1, D)
    gain = jnp.zeros(gain_out.shape, F32)
    for pair in range(ROWS):
        parts = [whole[:, pair * WIDE : (pair + 1) * WIDE]]
        parts.append(whole[:, MAIN + pair * REST : MAIN + (pair + 1) * REST])
        gain = jnp.where(me == pair, jnp.concatenate(parts, axis=1), gain)
    gain_out[...] = gain


def place_slices(cuts, main_ref, tail_ref):
    tail_ref[...] = jnp.zeros_like(tail_ref)
    for step, cut in cuts:
        place_rows(weight_rows(cut), 2 * lax.rem(lax.axis_index("page") + step, PAGES), main_ref, tail_ref)


def last_kernel(across_ref, swapped_ref, token_ref, main_ref, tail_ref):
    del token_ref
    core = row_index() % 2
    size = across_ref.shape[0]
    half = pl.ds(pl.multiple_of(core * size, 16), size)
    place_slices([(2, across_ref[...]), (1 + 2 * core, swapped_ref[half, :])], main_ref, tail_ref)


def far_block():
    me = row_index()
    return pl.ds(pl.multiple_of((me // 2 ^ 3) * 2 * WIDE, 2 * WIDE), 2 * WIDE)


def collect_late(same, other):
    core = row_index() % 2
    left = jnp.where(core == 0, same[...], other[...])
    right = jnp.where(core == 0, other[...], same[...])
    return jnp.concatenate([left, right], axis=1)


def came_last(block):
    page, core = lax.axis_index("page"), row_index() % 2
    return (block == lax.rem(page + 2, PAGES)) | (block == lax.rem(page + 1 + 2 * core, PAGES))


def add_features(owners, pieces, weights, before_ref, out_ref):
    main_ref, tail_ref, last_main_ref, last_tail_ref = weights
    me = row_index()
    patches = out_ref.shape[0]
    groups = patches // 4
    mains, tails = [], []
    for step in owners:
        pair = me ^ step
        columns = pl.ds(pl.multiple_of(pair * WIDE, WIDE), WIDE)
        is_last = came_last(pair // 2)
        mains.append(jnp.where(is_last, last_main_ref[columns, :], main_ref[columns, :]))
        tails.append([jnp.where(is_last, last_tail_ref[at, columns, :], tail_ref[at, columns, :]) for at in range(4)])
    rows = jnp.concatenate([piece[...] for piece in pieces], axis=1)
    base = before_ref[...] + jnp.dot(rows[:patches], jnp.concatenate(mains, axis=0), preferred_element_type=F32)
    for corner in range(4):
        span = slice(corner * groups, (corner + 1) * groups)
        tail = jnp.concatenate([tail[corner] for tail in tails], axis=0)
        out_ref[span, :] = base[span] + jnp.dot(rows[patches:], tail, preferred_element_type=F32)


def project_first_kernel(*rest):
    add_features(OWNERS[:3], rest[:3], rest[3:7], *rest[7:])


def project_second_kernel(*rest):
    add_features(OWNERS[3:6], rest[:3], rest[3:7], *rest[7:])


def project_kernel(*rest):
    same, other, base_ref, main_ref, tail_ref, last_main_ref, last_tail_ref, gain_ref, out_ref = rest
    patches = base_ref.shape[0]
    groups = patches // 4
    block = far_block()
    is_last = came_last(row_index() // 2 ^ 3)
    full = collect_late(same, other)
    main = jnp.where(is_last, last_main_ref[block, :], main_ref[block, :])
    base = base_ref[...] + jnp.dot(full[:patches], main, preferred_element_type=F32)
    ones = jnp.ones((NOTES, HPAIR), BF16)
    contract = (((1,), (1,)), ((), ()))
    row = lax.broadcasted_iota(jnp.int32, (NOTES, groups), 0)
    notes = jnp.zeros((NOTES, groups), F32)
    ends = []
    for corner in range(4):
        span = slice(corner * groups, (corner + 1) * groups)
        tail = jnp.where(is_last, last_tail_ref[corner, block, :], tail_ref[corner, block, :])
        hidden = base[span] + jnp.dot(full[patches:], tail, preferred_element_type=F32)
        square = hidden * hidden
        high = square.astype(BF16)
        low = (square - high.astype(F32)).astype(BF16)
        total = lax.dot_general(ones, high, contract, preferred_element_type=F32)
        total = total + lax.dot_general(ones, low, contract, preferred_element_type=F32)
        coarse = total.astype(BF16).astype(F32)
        notes = jnp.where(row == corner, coarse, jnp.where(row == 4 + corner, total - coarse, notes))
        sent = hidden * gain_ref[...]
        out_ref[span, :] = sent[:, :WIDE].astype(BF16)
        ends.append(sent[:, WIDE:])
    out_ref[patches : patches + groups, :] = jnp.concatenate(ends, axis=1).astype(BF16)
    out_ref[patches + groups :, :] = notes.astype(BF16)


def tail_kernel(weight_ref, bias_hbm, token_ref, out_ref, bias_out, line, sem):
    del token_ref
    fetch = pltpu.make_async_copy(bias_hbm, line, sem)
    fetch.start()
    for pair in range(ROWS):
        cut = [corner * D + MAIN + pair * REST for corner in range(4)]
        out_ref[:, pair * WIDE : (pair + 1) * WIDE] = jnp.concatenate(
            [weight_ref[:, at : at + REST] for at in cut], axis=1
        )
    fetch.wait()
    units = bias_out.shape[0]
    bias_out[...] = jnp.broadcast_to(line[...].reshape(1, units), (8, units)).T[:, :1]


def merge_product(weight_ref, corner, groups, pieces):
    me = row_index()
    spots = [pl.multiple_of(corner * D + (me ^ step) * WIDE, WIDE) for step, _ in pieces]
    span = slice(corner * groups, (corner + 1) * groups)
    return lax.dot_general(
        jnp.concatenate([weight_ref[:, pl.ds(spot, WIDE)] for spot in spots], axis=1),
        jnp.concatenate([piece[span, :] for _, piece in pieces], axis=1),
        (((1,), (1,)), ((), ())),
        preferred_element_type=F32,
    )


def merge_first_kernel(*rest):
    pieces, (weight_ref, sum_ref) = list(zip(OWNERS[:3], rest[:3])), rest[3:]
    for corner in range(4):
        sum_ref[corner] = merge_product(weight_ref, corner, sum_ref.shape[2], pieces)


def merge_second_kernel(*rest):
    pieces, (before_ref, weight_ref, sum_ref) = list(zip(OWNERS[3:6], rest[:3])), rest[3:]
    for corner in range(4):
        sum_ref[corner] = before_ref[corner] + merge_product(weight_ref, corner, sum_ref.shape[2], pieces)


def merge_kernel(*rest):
    pieces = rest[:ROWS]
    before_ref, weight_ref, tail_ref, bias_ref, live_ref, out_ref, ends_ref = rest[ROWS:]
    me = row_index()
    groups = live_ref.shape[1]
    patches = 4 * groups
    contract = (((1,), (1,)), ((), ()))
    block = pl.multiple_of((me // 2 ^ 3) * 2 * WIDE, 2 * WIDE)
    rows = collect_late(pieces[6], pieces[7])
    notes = jnp.zeros((NOTES, groups), F32)
    for step, piece in zip(OWNERS, pieces):
        notes = notes + piece[patches + groups :, :].astype(F32)
    scale = lax.rsqrt((notes[:4] + notes[4:8]) * (1.0 / D) + 1e-06)
    spread = jnp.concatenate([jnp.broadcast_to(scale[at : at + 1], (REST, groups)) for at in range(4)], axis=0).T
    for step, piece in zip(OWNERS, pieces):
        at = pl.ds(pl.multiple_of((me ^ step) * WIDE, WIDE), WIDE)
        ends_ref[:, at] = (piece[patches : patches + groups, :].astype(F32) * spread).astype(BF16)
    total = bias_ref[...] + lax.dot_general(tail_ref[...], ends_ref[...], contract, preferred_element_type=F32)
    for corner in range(4):
        part = before_ref[corner] + lax.dot_general(
            weight_ref[:, pl.ds(pl.multiple_of(corner * D + block, 2 * WIDE), 2 * WIDE)],
            rows[corner * groups : (corner + 1) * groups],
            contract,
            preferred_element_type=F32,
        )
        total = total + scale[corner : corner + 1] * part
    merged = 0.5 * total * (1.0 + lax.erf(total * math.sqrt(0.5)))
    out_ref[0] = jnp.where(live_ref[...] > 0.0, merged, 0.0).astype(BF16)


def kernel(body, name, out_shape, scratch=(), fetched=(), count=0, limit=24, flops=0, moved=0):
    specs = [pl.BlockSpec(memory_space=pltpu.VMEM) for _ in range(count)]
    for at in fetched:
        specs[at] = pl.BlockSpec(memory_space=pl.ANY)
    return pl.pallas_call(
        body,
        out_shape=out_shape,
        in_specs=specs,
        out_specs=jax.tree.map(lambda _: pl.BlockSpec(memory_space=pltpu.VMEM), out_shape),
        scratch_shapes=list(scratch),
        compiler_params=pltpu.CompilerParams(vmem_limit_bytes=limit * 1024 * 1024),
        cost_estimate=pl.CostEstimate(flops=flops, bytes_accessed=moved, transcendentals=0),
        name=name,
    )


def in_hbm(value):
    return pltpu.with_memory_space_constraint(value, pltpu.HBM)


def shape(*dims, dtype=BF16):
    return jax.ShapeDtypeStruct(dims, dtype)


def swap(value, even, odd=None):
    odd = even if odd is None else odd
    return lax.ppermute(value, "row", [(row, row ^ (odd if row % 2 else even)) for row in range(ROWS)])


def turn(value, low, high):
    pairs = [
        (page * ROWS + row, (page + (high if row % 2 else low)) % PAGES * ROWS + row)
        for page in range(PAGES)
        for row in range(ROWS)
    ]
    return lax.ppermute(value, ("page", "row"), pairs)


def after(value, *arrays):
    return lax.optimization_barrier((value, *arrays))[0]


def local_eight(qkv_rows, residual, out_weight, norm_gain, merge_weight, merge_bias, page_grid):
    band = qkv_rows.shape[1]
    patches = band * ROWS
    groups = patches // 4
    units = merge_weight.shape[0]
    depth = out_weight.shape[0]
    piece = patches + groups
    size = depth + depth // 4

    *sends, grid = kernel(
        spread_kernel,
        "spread",
        [shape(band, 4 * HPAIR)] * ROWS + [shape(8, WIDE, dtype=jnp.int32)],
        [
            pltpu.VMEM((band, 3 * D), BF16),
            pltpu.VMEM((band, D), BF16),
            pltpu.VMEM((ROWS, band, 4 * HPAIR), BF16),
            pltpu.SMEM(page_grid.shape, jnp.int32),
            pltpu.SemaphoreType.DMA((6,)),
        ],
        fetched=range(3),
        count=3,
        moved=1 << 20,
    )(in_hbm(qkv_rows), in_hbm(residual), in_hbm(page_grid))
    blocks = [sends[0]] + [swap(send, *pair) for send, pair in zip(sends[1:], RECEIVERS[1:])]
    select, dead, live = kernel(
        layout_kernel,
        "layout",
        [shape(patches, patches), shape(1, patches, dtype=F32), shape(1, groups, dtype=F32)],
        fetched=range(1, 1 + 3),
        count=1 + 3,
        moved=1 << 20,
    )(grid, *blocks[1:4])
    chip, own = kernel(
        slice_kernel,
        "out_weight_slices",
        [shape(2 * size, WIDE), shape(size, WIDE)],
        fetched=(1,),
        count=2,
        moved=1 << 20,
    )(out_weight, sends[0])
    near = turn(after(chip, *()), 1, PAGES - 1)
    swapped = swap(near, 1)
    attn = kernel(
        attend_kernel,
        "attend",
        shape(piece, WIDE),
        [pltpu.VMEM((patches, HPAIR), BF16)] * 3,
        count=2 + ROWS,
        flops=20 * patches * patches * 4096,
        moved=1 << 20,
    )(select, dead, *blocks)
    across = turn(after(own, attn), 2, 2)
    resid, own_gain, main, tail = kernel(
        ready_kernel,
        "ready",
        [shape(patches, HPAIR, dtype=F32), shape(1, HPAIR, dtype=F32), shape(MAIN, HPAIR), shape(4, MAIN, HPAIR)],
        [pltpu.VMEM((patches, HPAIR), BF16), pltpu.VMEM((D,), F32), pltpu.SemaphoreType.DMA],
        fetched=(1, 2),
        count=3 + ROWS + 2,
        flops=10 * patches * patches * 4096,
        moved=4 << 20,
    )(select, in_hbm(norm_gain), attn, *blocks, own, near)
    last = kernel(
        last_kernel,
        "ready_last",
        [shape(MAIN, HPAIR), shape(4, MAIN, HPAIR)],
        fetched=(2,),
        count=3,
        flops=1,
        moved=1,
    )(across, swapped, main)
    one, two, far = swap(attn, 4), swap(attn, 2), swap(attn, 6)
    weights = (main, tail, *last)
    rows = shape(patches, HPAIR, dtype=F32)
    first = kernel(project_first_kernel, "project_first", rows, count=8, flops=1, moved=1)(attn, one, two, *weights, resid)
    near = [swap(after(attn, last[0]), 1), swap(one, 1), swap(two, 1)]
    second = kernel(project_second_kernel, "project_second", rows, count=8, flops=1, moved=1)(*near, *weights, first)
    hidden = kernel(
        project_kernel,
        "project",
        shape(piece + NOTES, WIDE),
        count=2 + 6,
        flops=patches * MAIN * 256,
        moved=4 << 20,
    )(far, swap(far, 1), second, *weights, own_gain)
    ends, bias = kernel(
        tail_kernel,
        "merge_tail",
        [shape(units, MAIN), shape(units, 1, dtype=F32)],
        [pltpu.VMEM((units,), F32), pltpu.SemaphoreType.DMA],
        fetched=(1, 2),
        count=3,
        moved=4 << 20,
    )(merge_weight, in_hbm(merge_bias), hidden)
    sums = shape(4, units, groups, dtype=F32)
    one, two, far = swap(hidden, 4), swap(hidden, 2), swap(hidden, 6)
    first = kernel(merge_first_kernel, "merge_first", sums, count=4, flops=1, moved=1)(hidden, one, two, merge_weight)
    near = [swap(after(hidden, ends), 1), swap(one, 1), swap(two, 1)]
    second = kernel(merge_second_kernel, "merge_second", sums, count=5, flops=1, moved=1)(*near, first, merge_weight)
    return kernel(
        merge_kernel,
        "merge",
        shape(1, units, groups),
        [pltpu.VMEM((groups, MAIN), BF16)],
        count=ROWS + 5,
        flops=4 * units * groups * MAIN,
        moved=8 << 20,
    )(hidden, one, two, *near, far, swap(after(far, first, *near), 1), second, merge_weight, ends, bias, live)


def solution(mesh):
    in_specs = (
        P("page", "row", None),
        P("page", "row", None),
        P("page", None),
        P(),
        P("row", None),
        P("row"),
        P("page", None),
    )
    out_specs = P("page", "row", None)
    local = local_eight if mesh.shape["row"] == 8 and mesh.shape["page"] == 4 else local_any
    return jax.shard_map(local, mesh=mesh, in_specs=in_specs, out_specs=out_specs, check_vma=False)
```

```python
import functools
import math

import jax
import jax.numpy as jnp
from jax import lax
from jax.experimental import pallas as pl
from jax.experimental.pallas import tpu as pltpu
from jax.sharding import PartitionSpec as P

D = 1280
HEADS = 16
HDIM = 80


def local_any(qkv_rows, residual, out_weight, norm_gain, merge_weight, merge_bias, page_grid):
    row_count = lax.axis_size("row")
    q_split = max(1, row_count // HEADS)
    head_groups = row_count // q_split
    width = D // head_groups
    heads_per = width // HDIM
    band_len = qkv_rows.shape[1]
    part_len = band_len // q_split
    local_qkv = qkv_rows[0]
    queries = local_qkv[:, :D]
    key_vals = jnp.concatenate(
        [
            local_qkv[:, D : 2 * D].reshape(band_len, head_groups, width),
            local_qkv[:, 2 * D :].reshape(band_len, head_groups, width),
        ],
        axis=2,
    )
    q_send = (
        queries.reshape(q_split, part_len, head_groups, width)
        .transpose(2, 0, 1, 3)
        .reshape(row_count, part_len, width)
    )
    kv_send = jnp.broadcast_to(
        key_vals.transpose(1, 0, 2)[:, None], (head_groups, q_split, band_len, 2 * width)
    )
    kv_send = kv_send.reshape(row_count, band_len, 2 * width)
    q_recv, kv_recv = (
        lax.all_to_all(q_send, "row", split_axis=0, concat_axis=1, tiled=True),
        lax.all_to_all(kv_send, "row", split_axis=0, concat_axis=1, tiled=True),
    )
    kv_local = kv_recv[0]
    positions = jnp.arange(row_count * band_len, dtype=jnp.int32)
    valid_len = page_grid[0, 0] * page_grid[0, 1]
    key_valid = positions < valid_len
    key_total = kv_local.shape[0]
    key_heads = kv_local[:, :width].reshape(key_total, heads_per, HDIM)
    value_heads = kv_local[:, width:].reshape(key_total, heads_per, HDIM)
    query_total = row_count * part_len
    q_block = math.gcd(query_total, 512)
    q_blocks = q_recv[0].reshape(query_total // q_block, q_block, heads_per, HDIM)
    root_dim = math.sqrt(HDIM)

    def attend(q_span):
        scores = (
            jnp.einsum("qhd,khd->hqk", q_span, key_heads, preferred_element_type=jnp.float32)
            / root_dim
        )
        scores = jnp.where(key_valid[None, None, :], scores, -1e30)
        peak = jnp.max(scores, axis=2, keepdims=True)
        weights = jnp.exp(scores - peak)
        total = jnp.sum(weights, axis=2, keepdims=True)
        mixed = (
            jnp.einsum(
                "hqk,khd->hqd",
                weights.astype(jnp.bfloat16),
                value_heads,
                preferred_element_type=jnp.float32,
            )
            / total
        )
        return mixed.transpose(1, 0, 2).reshape(q_span.shape[0], width).astype(jnp.bfloat16)

    attn_heads = lax.map(attend, q_blocks).reshape(row_count, part_len, width)
    returned = lax.all_to_all(attn_heads, "row", split_axis=0, concat_axis=0, tiled=True)
    attn = (
        returned.reshape(head_groups, q_split, part_len, width)
        .transpose(1, 2, 0, 3)
        .reshape(band_len, D)
    )
    projected = jnp.dot(
        attn,
        lax.all_gather(out_weight, "page", axis=0, tiled=True),
        preferred_element_type=jnp.float32,
    )
    hidden = residual[0].astype(jnp.float32) + projected
    normed = (
        hidden * lax.rsqrt(jnp.mean(hidden * hidden, axis=1, keepdims=True) + 1e-06) * norm_gain
    ).astype(jnp.bfloat16)
    rows_n = page_grid[0, 0]
    cols_n = page_grid[0, 1]
    group_total = band_len * row_count // 4
    slots = jnp.arange(group_total, dtype=jnp.int32)
    half_cols = cols_n // 2
    live = slots < rows_n // 2 * half_cols
    first = jnp.where(live, 2 * (slots // half_cols) * cols_n + 2 * (slots % half_cols), 0)
    corners = [first, first + 1, first + cols_n, first + cols_n + 1]
    local_units = merge_weight.shape[0]
    page_all = lax.all_gather(normed, "row", axis=0, tiled=True)
    merged_sum = jnp.zeros((local_units, group_total), jnp.float32)
    for corner in range(4):
        picked = jnp.take(page_all, corners[corner], axis=0)
        merged_sum = merged_sum + jnp.einsum(
            "md,gd->mg",
            merge_weight[:, corner * D : (corner + 1) * D],
            picked,
            preferred_element_type=jnp.float32,
        )
    merged = jax.nn.gelu(merged_sum + merge_bias[:, None], approximate=False)
    merged = jnp.where(live[None, :], merged, 0.0).astype(jnp.bfloat16)
    return merged[None]


ROWS = 8
PAGES = 4
HPAIR = 2 * HDIM
WIDE = 128
REST = HPAIR - WIDE
MAIN = ROWS * WIDE
NOTES = 16
RECEIVERS = ((0, 0), (4, 2), (2, 4), (6, 6), (7, 7), (3, 5), (5, 3), (1, 1))
SENDERS = ((0, 0), (4, 2), (2, 4), (6, 6), (7, 7), (5, 3), (3, 5), (1, 1))
OWNERS = (0, 4, 2, 1, 5, 3, 6, 7)
ROOT = math.log2(math.e) / math.sqrt(HDIM)
BF16 = jnp.bfloat16
F32 = jnp.float32


def row_index():
    return lax.axis_index("row")


def steps(pairs):
    core = row_index() % 2
    return [even + (odd - even) * core for even, odd in pairs]


def pack_tail(wide):
    groups = wide.shape[0] // 4
    return jnp.concatenate([wide[at * groups : (at + 1) * groups] for at in range(4)], axis=1)


def spread_kernel(qkv_hbm, resid_hbm, grid_hbm, *rest):
    outs = rest[:ROWS]
    grid_out, qkv, resid, held, grid, sems = rest[ROWS:]
    me = row_index()
    copies = [
        pltpu.make_async_copy(grid_hbm, grid, sems.at[0]),
        pltpu.make_async_copy(resid_hbm.at[0], resid, sems.at[1]),
    ]
    part = qkv.shape[0] // 4
    for at in range(4):
        rows = pl.ds(at * part, part)
        copies.append(pltpu.make_async_copy(qkv_hbm.at[0, rows], qkv.at[rows], sems.at[2 + at]))
    for copy in reversed(copies):
        copy.start()
    for copy in copies:
        copy.wait()
    for dest in range(ROWS):
        at = dest * HPAIR
        parts = [qkv[:, part * D + at : part * D + at + HPAIR] for part in range(3)]
        parts.append(resid[:, dest * WIDE : (dest + 1) * WIDE])
        parts.append(resid[:, MAIN + dest * REST : MAIN + (dest + 1) * REST])
        held[dest] = jnp.concatenate(parts, axis=1)
    for step, out in zip(steps(RECEIVERS), outs):
        out[...] = held[me ^ step]
    row = lax.broadcasted_iota(jnp.int32, grid_out.shape, 0)
    grid_out[...] = jnp.where(row == 0, grid[0, 0], grid[0, 1])


def slice_kernel(weight_ref, *rest):
    chip_ref, slice_ref = rest[-2:]
    me = row_index()
    depth = weight_ref.shape[0]
    main = weight_ref[:, pl.ds(pl.multiple_of(me // 2 * 2 * WIDE, 2 * WIDE), 2 * WIDE)]
    tile = weight_ref[:, pl.ds(pl.multiple_of(MAIN + me // 4 * WIDE, WIDE), WIDE)]
    low = me // 2 % 2 == 0
    size = depth + depth // 4
    for core in range(2):
        tail = jnp.where(low, tile[:, core * REST : (core + 1) * REST], tile[:, (core + 2) * REST : (core + 3) * REST])
        chip_ref[core * size : core * size + depth, :] = main[:, core * WIDE : (core + 1) * WIDE]
        chip_ref[core * size + depth : (core + 1) * size, :] = pack_tail(tail)
    slice_ref[...] = chip_ref[pl.ds(pl.multiple_of(me % 2 * size, 16), size), :]


def layout_kernel(grid_ref, *rest):
    select_ref, keys_ref, live_ref = rest[-3:]
    rows_n, cols_n = grid_ref[:1, :1], grid_ref[1:2, :1]
    patches = select_ref.shape[0]
    groups = patches // 4
    half = cols_n >> 1
    count = (rows_n >> 1) * half
    slots = lax.broadcasted_iota(jnp.int32, (groups, 1), 0)
    line = jnp.floor((slots.astype(F32) + 0.5) / half.astype(F32)).astype(jnp.int32)
    first = 2 * line * cols_n + 2 * (slots - line * half)
    at = lax.broadcasted_iota(jnp.int32, (groups, patches), 1)
    for corner in range(4):
        wanted = jnp.where(slots < count, first + (corner // 2) * cols_n + corner % 2, -1)
        select_ref[corner * groups : (corner + 1) * groups, :] = jnp.where(at == wanted, 1.0, 0.0).astype(BF16)
    key = lax.broadcasted_iota(jnp.int32, keys_ref.shape, 1)
    keys_ref[...] = jnp.where(key < rows_n * cols_n, 0.0, -1e30)
    slot = lax.broadcasted_iota(jnp.int32, live_ref.shape, 1)
    live_ref[...] = jnp.where(slot < count, 1.0, 0.0)


def attend_kernel(select_ref, dead_ref, *rest):
    blocks = rest[:ROWS]
    out_ref, q_all, k_all, v_all = rest[-4:]
    me = row_index()
    band = blocks[0].shape[0]
    patches = band * ROWS
    for step, block in zip(steps(SENDERS), blocks):
        at = pl.ds(pl.multiple_of((me ^ step) * band, band), band)
        q_all[at, :] = block[:, :HPAIR]
        k_all[at, :] = block[:, HPAIR : 2 * HPAIR]
        v_all[at, :] = block[:, 2 * HPAIR : 3 * HPAIR]
    queries = jnp.dot(select_ref[...], q_all[...], preferred_element_type=F32).astype(BF16)
    lane = lax.broadcasted_iota(jnp.int32, (1, HPAIR), 1)
    keys, values, dead = k_all[...], v_all[...], dead_ref[...]
    mixed = []
    for head in range(2):
        mine = (lane >= head * HDIM) & (lane < (head + 1) * HDIM)
        asked = jnp.where(mine, queries, jnp.zeros_like(queries))
        scores = lax.dot_general(asked, keys, (((1,), (1,)), ((), ())), preferred_element_type=F32) + dead
        weights = jnp.exp2((scores - jnp.max(scores, axis=1, keepdims=True)) * ROOT)
        total = jnp.sum(weights, axis=1, keepdims=True)
        mixed.append(jnp.dot(weights.astype(BF16), values, preferred_element_type=F32) * (1.0 / total))
    attn = jnp.where(lane < HDIM, mixed[0], mixed[1])
    out_ref[:patches, :] = attn[:, :WIDE].astype(BF16)
    out_ref[patches:, :] = pack_tail(attn[:, WIDE:]).astype(BF16)


def weight_rows(cut):
    depth = 2 * HPAIR
    packed = cut[depth:]
    tail = jnp.concatenate([packed[:, at * REST : (at + 1) * REST] for at in range(4)], axis=0)
    whole = jnp.concatenate([cut[:depth], tail], axis=1)
    return [whole[core * HPAIR : (core + 1) * HPAIR] for core in range(2)]


def place_rows(rows, base, main_ref, tail_ref):
    for core in range(2):
        pair = base + core
        main_ref[pl.ds(pl.multiple_of(pair * WIDE, WIDE), WIDE), :] = rows[core][:WIDE]
        for corner in range(4):
            spot = pl.multiple_of(pair * WIDE + corner * REST, REST)
            tail_ref[corner, pl.ds(spot, REST), :] = rows[core][WIDE:]


def ready_kernel(select_ref, gain_hbm, token_ref, *rest):
    del token_ref
    blocks = rest[:ROWS]
    own_ref, near_ref = rest[ROWS : ROWS + 2]
    resid_ref, gain_out, main_ref, tail_ref, held, line, sem = rest[-7:]
    fetch = pltpu.make_async_copy(gain_hbm, line, sem)
    fetch.start()
    me = row_index()
    band = blocks[0].shape[0]
    for step, block in zip(steps(SENDERS), blocks):
        at = pl.ds(pl.multiple_of((me ^ step) * band, band), band)
        held[at, :] = block[:, 3 * HPAIR :]
    resid_ref[...] = jnp.dot(select_ref[...], held[...], preferred_element_type=F32)
    core = me % 2
    size = own_ref.shape[0]
    half = pl.ds(pl.multiple_of(core * size, 16), size)
    place_slices([(0, own_ref[...]), (3 - 2 * core, near_ref[half, :])], main_ref, tail_ref)
    fetch.wait()
    whole = line[...].reshape(1, D)
    gain = jnp.zeros(gain_out.shape, F32)
    for pair in range(ROWS):
        parts = [whole[:, pair * WIDE : (pair + 1) * WIDE]]
        parts.append(whole[:, MAIN + pair * REST : MAIN + (pair + 1) * REST])
        gain = jnp.where(me == pair, jnp.concatenate(parts, axis=1), gain)
    gain_out[...] = gain


def place_slices(cuts, main_ref, tail_ref):
    tail_ref[...] = jnp.zeros_like(tail_ref)
    for step, cut in cuts:
        place_rows(weight_rows(cut), 2 * lax.rem(lax.axis_index("page") + step, PAGES), main_ref, tail_ref)


def last_kernel(across_ref, swapped_ref, token_ref, main_ref, tail_ref):
    del token_ref
    core = row_index() % 2
    size = across_ref.shape[0]
    half = pl.ds(pl.multiple_of(core * size, 16), size)
    place_slices([(2, across_ref[...]), (1 + 2 * core, swapped_ref[half, :])], main_ref, tail_ref)


def far_block():
    me = row_index()
    return pl.ds(pl.multiple_of((me // 2 ^ 3) * 2 * WIDE, 2 * WIDE), 2 * WIDE)


def collect_late(same, other):
    core = row_index() % 2
    left = jnp.where(core == 0, same[...], other[...])
    right = jnp.where(core == 0, other[...], same[...])
    return jnp.concatenate([left, right], axis=1)


def came_last(block):
    page, core = lax.axis_index("page"), row_index() % 2
    return (block == lax.rem(page + 2, PAGES)) | (block == lax.rem(page + 1 + 2 * core, PAGES))


def add_features(owners, pieces, weights, before_ref, out_ref):
    main_ref, tail_ref, last_main_ref, last_tail_ref = weights
    me = row_index()
    patches = out_ref.shape[0]
    groups = patches // 4
    mains, tails = [], []
    for step in owners:
        pair = me ^ step
        columns = pl.ds(pl.multiple_of(pair * WIDE, WIDE), WIDE)
        is_last = came_last(pair // 2)
        mains.append(jnp.where(is_last, last_main_ref[columns, :], main_ref[columns, :]))
        tails.append([jnp.where(is_last, last_tail_ref[at, columns, :], tail_ref[at, columns, :]) for at in range(4)])
    rows = jnp.concatenate([piece[...] for piece in pieces], axis=1)
    base = before_ref[...] + jnp.dot(rows[:patches], jnp.concatenate(mains, axis=0), preferred_element_type=F32)
    for corner in range(4):
        span = slice(corner * groups, (corner + 1) * groups)
        tail = jnp.concatenate([tail[corner] for tail in tails], axis=0)
        out_ref[span, :] = base[span] + jnp.dot(rows[patches:], tail, preferred_element_type=F32)


def project_first_kernel(*rest):
    add_features(OWNERS[:3], rest[:3], rest[3:7], *rest[7:])


def project_second_kernel(*rest):
    add_features(OWNERS[3:6], rest[:3], rest[3:7], *rest[7:])


def project_kernel(*rest):
    same, other, base_ref, main_ref, tail_ref, last_main_ref, last_tail_ref, gain_ref, out_ref = rest
    patches = base_ref.shape[0]
    groups = patches // 4
    block = far_block()
    is_last = came_last(row_index() // 2 ^ 3)
    full = collect_late(same, other)
    main = jnp.where(is_last, last_main_ref[block, :], main_ref[block, :])
    base = base_ref[...] + jnp.dot(full[:patches], main, preferred_element_type=F32)
    ones = jnp.ones((NOTES, HPAIR), BF16)
    contract = (((1,), (1,)), ((), ()))
    row = lax.broadcasted_iota(jnp.int32, (NOTES, groups), 0)
    notes = jnp.zeros((NOTES, groups), F32)
    ends = []
    for corner in range(4):
        span = slice(corner * groups, (corner + 1) * groups)
        tail = jnp.where(is_last, last_tail_ref[corner, block, :], tail_ref[corner, block, :])
        hidden = base[span] + jnp.dot(full[patches:], tail, preferred_element_type=F32)
        square = hidden * hidden
        high = square.astype(BF16)
        low = (square - high.astype(F32)).astype(BF16)
        total = lax.dot_general(ones, high, contract, preferred_element_type=F32)
        total = total + lax.dot_general(ones, low, contract, preferred_element_type=F32)
        coarse = total.astype(BF16).astype(F32)
        notes = jnp.where(row == corner, coarse, jnp.where(row == 4 + corner, total - coarse, notes))
        sent = hidden * gain_ref[...]
        out_ref[span, :] = sent[:, :WIDE].astype(BF16)
        ends.append(sent[:, WIDE:])
    out_ref[patches : patches + groups, :] = jnp.concatenate(ends, axis=1).astype(BF16)
    out_ref[patches + groups :, :] = notes.astype(BF16)


def tail_kernel(weight_ref, bias_hbm, token_ref, out_ref, bias_out, line, sem):
    del token_ref
    fetch = pltpu.make_async_copy(bias_hbm, line, sem)
    fetch.start()
    for pair in range(ROWS):
        cut = [corner * D + MAIN + pair * REST for corner in range(4)]
        out_ref[:, pair * WIDE : (pair + 1) * WIDE] = jnp.concatenate(
            [weight_ref[:, at : at + REST] for at in cut], axis=1
        )
    fetch.wait()
    units = bias_out.shape[0]
    bias_out[...] = jnp.broadcast_to(line[...].reshape(1, units), (8, units)).T[:, :1]


def merge_product(weight_ref, corner, groups, pieces):
    me = row_index()
    spots = [pl.multiple_of(corner * D + (me ^ step) * WIDE, WIDE) for step, _ in pieces]
    span = slice(corner * groups, (corner + 1) * groups)
    return lax.dot_general(
        jnp.concatenate([weight_ref[:, pl.ds(spot, WIDE)] for spot in spots], axis=1),
        jnp.concatenate([piece[span, :] for _, piece in pieces], axis=1),
        (((1,), (1,)), ((), ())),
        preferred_element_type=F32,
    )


def tail_products(tail_ref, groups, pieces):
    me = row_index()
    columns = [tail_ref[:, pl.ds(pl.multiple_of((me ^ step) * WIDE, WIDE), WIDE)] for step, _ in pieces]
    tails = jnp.concatenate(columns, axis=1)
    ends = jnp.concatenate([piece[4 * groups : 5 * groups, :] for _, piece in pieces], axis=1)
    corner_of = lax.rem(lax.broadcasted_iota(jnp.int32, (1, ends.shape[1]), 1), WIDE) // REST
    return [
        lax.dot_general(
            tails,
            jnp.where(corner_of == corner, ends, jnp.zeros_like(ends)),
            (((1,), (1,)), ((), ())),
            preferred_element_type=F32,
        )
        for corner in range(4)
    ]


def merge_first_kernel(*rest):
    pieces, (weight_ref, tail_ref, sum_ref) = list(zip(OWNERS[:3], rest[:3])), rest[3:]
    groups = sum_ref.shape[2]
    for corner, tail in enumerate(tail_products(tail_ref, groups, pieces)):
        sum_ref[corner] = tail + merge_product(weight_ref, corner, groups, pieces)


def merge_second_kernel(*rest):
    pieces, (before_ref, weight_ref, tail_ref, sum_ref) = list(zip(OWNERS[3:6], rest[:3])), rest[3:]
    groups = sum_ref.shape[2]
    for corner, tail in enumerate(tail_products(tail_ref, groups, pieces)):
        sum_ref[corner] = before_ref[corner] + (tail + merge_product(weight_ref, corner, groups, pieces))


def merge_kernel(*rest):
    pieces = rest[:ROWS]
    before_ref, weight_ref, tail_ref, bias_ref, live_ref, out_ref = rest[ROWS:]
    me = row_index()
    groups = live_ref.shape[1]
    patches = 4 * groups
    contract = (((1,), (1,)), ((), ()))
    block = pl.multiple_of((me // 2 ^ 3) * 2 * WIDE, 2 * WIDE)
    rows = collect_late(pieces[6], pieces[7])
    notes = jnp.zeros((NOTES, groups), F32)
    for piece in pieces:
        notes = notes + piece[patches + groups :, :].astype(F32)
    scale = lax.rsqrt((notes[:4] + notes[4:8]) * (1.0 / D) + 1e-06)
    spread = jnp.concatenate([jnp.broadcast_to(scale[at : at + 1], (REST, groups)) for at in range(4)], axis=0).T
    ends = rows[patches : patches + groups].astype(F32) * jnp.concatenate([spread] * 2, axis=1)
    total = bias_ref[...] + lax.dot_general(
        tail_ref[:, pl.ds(block, 2 * WIDE)], ends.astype(BF16), contract, preferred_element_type=F32
    )
    for corner in range(4):
        part = before_ref[corner] + lax.dot_general(
            weight_ref[:, pl.ds(pl.multiple_of(corner * D + block, 2 * WIDE), 2 * WIDE)],
            rows[corner * groups : (corner + 1) * groups],
            contract,
            preferred_element_type=F32,
        )
        total = total + scale[corner : corner + 1] * part
    merged = 0.5 * total * (1.0 + lax.erf(total * math.sqrt(0.5)))
    out_ref[0] = jnp.where(live_ref[...] > 0.0, merged, 0.0).astype(BF16)


def kernel(body, name, out_shape, scratch=(), fetched=(), count=0, limit=24, flops=0, moved=0):
    specs = [pl.BlockSpec(memory_space=pltpu.VMEM) for _ in range(count)]
    for at in fetched:
        specs[at] = pl.BlockSpec(memory_space=pl.ANY)
    return pl.pallas_call(
        body,
        out_shape=out_shape,
        in_specs=specs,
        out_specs=jax.tree.map(lambda _: pl.BlockSpec(memory_space=pltpu.VMEM), out_shape),
        scratch_shapes=list(scratch),
        compiler_params=pltpu.CompilerParams(vmem_limit_bytes=limit * 1024 * 1024),
        cost_estimate=pl.CostEstimate(flops=flops, bytes_accessed=moved, transcendentals=0),
        name=name,
    )


def in_hbm(value):
    return pltpu.with_memory_space_constraint(value, pltpu.HBM)


def shape(*dims, dtype=BF16):
    return jax.ShapeDtypeStruct(dims, dtype)


def swap(value, even, odd=None):
    odd = even if odd is None else odd
    return lax.ppermute(value, "row", [(row, row ^ (odd if row % 2 else even)) for row in range(ROWS)])


def turn(value, low, high):
    pairs = [
        (page * ROWS + row, (page + (high if row % 2 else low)) % PAGES * ROWS + row)
        for page in range(PAGES)
        for row in range(ROWS)
    ]
    return lax.ppermute(value, ("page", "row"), pairs)


def after(value, *arrays):
    return lax.optimization_barrier((value, *arrays))[0]


def local_eight(qkv_rows, residual, out_weight, norm_gain, merge_weight, merge_bias, page_grid):
    band = qkv_rows.shape[1]
    patches = band * ROWS
    groups = patches // 4
    units = merge_weight.shape[0]
    depth = out_weight.shape[0]
    piece = patches + groups
    size = depth + depth // 4

    *sends, grid = kernel(
        spread_kernel,
        "spread",
        [shape(band, 4 * HPAIR)] * ROWS + [shape(8, WIDE, dtype=jnp.int32)],
        [
            pltpu.VMEM((band, 3 * D), BF16),
            pltpu.VMEM((band, D), BF16),
            pltpu.VMEM((ROWS, band, 4 * HPAIR), BF16),
            pltpu.SMEM(page_grid.shape, jnp.int32),
            pltpu.SemaphoreType.DMA((6,)),
        ],
        fetched=range(3),
        count=3,
        moved=1 << 20,
    )(in_hbm(qkv_rows), in_hbm(residual), in_hbm(page_grid))
    blocks = [sends[0]] + [swap(send, *pair) for send, pair in zip(sends[1:], RECEIVERS[1:])]
    select, dead, live = kernel(
        layout_kernel,
        "layout",
        [shape(patches, patches), shape(1, patches, dtype=F32), shape(1, groups, dtype=F32)],
        fetched=range(1, 1 + 3),
        count=1 + 3,
        moved=1 << 20,
    )(grid, *blocks[1:4])
    chip, own = kernel(
        slice_kernel,
        "out_weight_slices",
        [shape(2 * size, WIDE), shape(size, WIDE)],
        fetched=(1,),
        count=2,
        moved=1 << 20,
    )(out_weight, sends[0])
    near = turn(after(chip, *()), 1, PAGES - 1)
    swapped = swap(near, 1)
    attn = kernel(
        attend_kernel,
        "attend",
        shape(piece, WIDE),
        [pltpu.VMEM((patches, HPAIR), BF16)] * 3,
        count=2 + ROWS,
        flops=20 * patches * patches * 4096,
        moved=1 << 20,
    )(select, dead, *blocks)
    across = turn(after(own, attn), 2, 2)
    resid, own_gain, main, tail = kernel(
        ready_kernel,
        "ready",
        [shape(patches, HPAIR, dtype=F32), shape(1, HPAIR, dtype=F32), shape(MAIN, HPAIR), shape(4, MAIN, HPAIR)],
        [pltpu.VMEM((patches, HPAIR), BF16), pltpu.VMEM((D,), F32), pltpu.SemaphoreType.DMA],
        fetched=(1, 2),
        count=3 + ROWS + 2,
        flops=10 * patches * patches * 4096,
        moved=4 << 20,
    )(select, in_hbm(norm_gain), attn, *blocks, own, near)
    last = kernel(
        last_kernel,
        "ready_last",
        [shape(MAIN, HPAIR), shape(4, MAIN, HPAIR)],
        fetched=(2,),
        count=3,
        flops=1,
        moved=1,
    )(across, swapped, main)
    one, two, far = swap(attn, 4), swap(attn, 2), swap(attn, 6)
    weights = (main, tail, *last)
    rows = shape(patches, HPAIR, dtype=F32)
    first = kernel(project_first_kernel, "project_first", rows, count=8, flops=1, moved=1)(attn, one, two, *weights, resid)
    near = [swap(after(attn, last[0]), 1), swap(one, 1), swap(two, 1)]
    second = kernel(project_second_kernel, "project_second", rows, count=8, flops=1, moved=1)(*near, *weights, first)
    hidden = kernel(
        project_kernel,
        "project",
        shape(piece + NOTES, WIDE),
        count=2 + 6,
        flops=patches * MAIN * 256,
        moved=4 << 20,
    )(far, swap(far, 1), second, *weights, own_gain)
    ends, bias = kernel(
        tail_kernel,
        "merge_tail",
        [shape(units, MAIN), shape(units, 1, dtype=F32)],
        [pltpu.VMEM((units,), F32), pltpu.SemaphoreType.DMA],
        fetched=(1, 2),
        count=3,
        moved=4 << 20,
    )(merge_weight, in_hbm(merge_bias), hidden)
    sums = shape(4, units, groups, dtype=F32)
    one, two, far = swap(hidden, 4), swap(hidden, 2), swap(hidden, 6)
    first = kernel(merge_first_kernel, "merge_first", sums, count=5, flops=1, moved=1)(
        hidden, one, two, merge_weight, ends
    )
    near = [swap(after(hidden, ends), 1), swap(one, 1), swap(two, 1)]
    second = kernel(merge_second_kernel, "merge_second", sums, count=6, flops=1, moved=1)(
        *near, first, merge_weight, ends
    )
    return kernel(
        merge_kernel,
        "merge",
        shape(1, units, groups),
        count=ROWS + 5,
        flops=4 * units * groups * MAIN,
        moved=8 << 20,
    )(hidden, one, two, *near, far, swap(after(far, first, *near), 1), second, merge_weight, ends, bias, live)


def solution(mesh):
    in_specs = (
        P("page", "row", None),
        P("page", "row", None),
        P("page", None),
        P(),
        P("row", None),
        P("row"),
        P("page", None),
    )
    out_specs = P("page", "row", None)
    local = local_eight if mesh.shape["row"] == 8 and mesh.shape["page"] == 4 else local_any
    return jax.shard_map(local, mesh=mesh, in_specs=in_specs, out_specs=out_specs, check_vma=False)
```

```python
import functools
import math

import jax
import jax.numpy as jnp
from jax import lax
from jax.experimental import pallas as pl
from jax.experimental.pallas import tpu as pltpu
from jax.sharding import PartitionSpec as P

D = 1280
HEADS = 16
HDIM = 80


def local_any(qkv_rows, residual, out_weight, norm_gain, merge_weight, merge_bias, page_grid):
    row_count = lax.axis_size("row")
    q_split = max(1, row_count // HEADS)
    head_groups = row_count // q_split
    width = D // head_groups
    heads_per = width // HDIM
    band_len = qkv_rows.shape[1]
    part_len = band_len // q_split
    local_qkv = qkv_rows[0]
    queries = local_qkv[:, :D]
    key_vals = jnp.concatenate(
        [
            local_qkv[:, D : 2 * D].reshape(band_len, head_groups, width),
            local_qkv[:, 2 * D :].reshape(band_len, head_groups, width),
        ],
        axis=2,
    )
    q_send = (
        queries.reshape(q_split, part_len, head_groups, width)
        .transpose(2, 0, 1, 3)
        .reshape(row_count, part_len, width)
    )
    kv_send = jnp.broadcast_to(
        key_vals.transpose(1, 0, 2)[:, None], (head_groups, q_split, band_len, 2 * width)
    )
    kv_send = kv_send.reshape(row_count, band_len, 2 * width)
    q_recv, kv_recv = (
        lax.all_to_all(q_send, "row", split_axis=0, concat_axis=1, tiled=True),
        lax.all_to_all(kv_send, "row", split_axis=0, concat_axis=1, tiled=True),
    )
    kv_local = kv_recv[0]
    positions = jnp.arange(row_count * band_len, dtype=jnp.int32)
    valid_len = page_grid[0, 0] * page_grid[0, 1]
    key_valid = positions < valid_len
    key_total = kv_local.shape[0]
    key_heads = kv_local[:, :width].reshape(key_total, heads_per, HDIM)
    value_heads = kv_local[:, width:].reshape(key_total, heads_per, HDIM)
    query_total = row_count * part_len
    q_block = math.gcd(query_total, 512)
    q_blocks = q_recv[0].reshape(query_total // q_block, q_block, heads_per, HDIM)
    root_dim = math.sqrt(HDIM)

    def attend(q_span):
        scores = (
            jnp.einsum("qhd,khd->hqk", q_span, key_heads, preferred_element_type=jnp.float32)
            / root_dim
        )
        scores = jnp.where(key_valid[None, None, :], scores, -1e30)
        peak = jnp.max(scores, axis=2, keepdims=True)
        weights = jnp.exp(scores - peak)
        total = jnp.sum(weights, axis=2, keepdims=True)
        mixed = (
            jnp.einsum(
                "hqk,khd->hqd",
                weights.astype(jnp.bfloat16),
                value_heads,
                preferred_element_type=jnp.float32,
            )
            / total
        )
        return mixed.transpose(1, 0, 2).reshape(q_span.shape[0], width).astype(jnp.bfloat16)

    attn_heads = lax.map(attend, q_blocks).reshape(row_count, part_len, width)
    returned = lax.all_to_all(attn_heads, "row", split_axis=0, concat_axis=0, tiled=True)
    attn = (
        returned.reshape(head_groups, q_split, part_len, width)
        .transpose(1, 2, 0, 3)
        .reshape(band_len, D)
    )
    projected = jnp.dot(
        attn,
        lax.all_gather(out_weight, "page", axis=0, tiled=True),
        preferred_element_type=jnp.float32,
    )
    hidden = residual[0].astype(jnp.float32) + projected
    normed = (
        hidden * lax.rsqrt(jnp.mean(hidden * hidden, axis=1, keepdims=True) + 1e-06) * norm_gain
    ).astype(jnp.bfloat16)
    rows_n = page_grid[0, 0]
    cols_n = page_grid[0, 1]
    group_total = band_len * row_count // 4
    slots = jnp.arange(group_total, dtype=jnp.int32)
    half_cols = cols_n // 2
    live = slots < rows_n // 2 * half_cols
    first = jnp.where(live, 2 * (slots // half_cols) * cols_n + 2 * (slots % half_cols), 0)
    corners = [first, first + 1, first + cols_n, first + cols_n + 1]
    local_units = merge_weight.shape[0]
    page_all = lax.all_gather(normed, "row", axis=0, tiled=True)
    merged_sum = jnp.zeros((local_units, group_total), jnp.float32)
    for corner in range(4):
        picked = jnp.take(page_all, corners[corner], axis=0)
        merged_sum = merged_sum + jnp.einsum(
            "md,gd->mg",
            merge_weight[:, corner * D : (corner + 1) * D],
            picked,
            preferred_element_type=jnp.float32,
        )
    merged = jax.nn.gelu(merged_sum + merge_bias[:, None], approximate=False)
    merged = jnp.where(live[None, :], merged, 0.0).astype(jnp.bfloat16)
    return merged[None]


ROWS = 8
PAGES = 4
HPAIR = 2 * HDIM
WIDE = 128
REST = HPAIR - WIDE
MAIN = ROWS * WIDE
NOTES = 16
RECEIVERS = ((0, 0), (4, 2), (2, 4), (6, 6), (7, 7), (3, 5), (5, 3), (1, 1))
SENDERS = ((0, 0), (4, 2), (2, 4), (6, 6), (7, 7), (5, 3), (3, 5), (1, 1))
OWNERS = (0, 4, 2, 1, 5, 3, 6, 7)
ROOT = math.log2(math.e) / math.sqrt(HDIM)
BF16 = jnp.bfloat16
F32 = jnp.float32


def row_index():
    return lax.axis_index("row")


def steps(pairs):
    core = row_index() % 2
    return [even + (odd - even) * core for even, odd in pairs]


def pack_tail(wide):
    groups = wide.shape[0] // 4
    return jnp.concatenate([wide[at * groups : (at + 1) * groups] for at in range(4)], axis=1)


def spread_kernel(qkv_hbm, resid_hbm, grid_hbm, *rest):
    outs = rest[:ROWS]
    grid_out, qkv, resid, held, grid, sems = rest[ROWS:]
    me = row_index()
    copies = [
        pltpu.make_async_copy(grid_hbm, grid, sems.at[0]),
        pltpu.make_async_copy(resid_hbm.at[0], resid, sems.at[1]),
    ]
    part = qkv.shape[0] // 4
    for at in range(4):
        rows = pl.ds(at * part, part)
        copies.append(pltpu.make_async_copy(qkv_hbm.at[0, rows], qkv.at[rows], sems.at[2 + at]))
    for copy in reversed(copies):
        copy.start()
    for copy in copies:
        copy.wait()
    for dest in range(ROWS):
        at = dest * HPAIR
        parts = [qkv[:, part * D + at : part * D + at + HPAIR] for part in range(3)]
        parts.append(resid[:, dest * WIDE : (dest + 1) * WIDE])
        parts.append(resid[:, MAIN + dest * REST : MAIN + (dest + 1) * REST])
        held[dest] = jnp.concatenate(parts, axis=1)
    for step, out in zip(steps(RECEIVERS), outs):
        out[...] = held[me ^ step]
    row = lax.broadcasted_iota(jnp.int32, grid_out.shape, 0)
    grid_out[...] = jnp.where(row == 0, grid[0, 0], grid[0, 1])


def slice_kernel(weight_ref, *rest):
    chip_ref, slice_ref = rest[-2:]
    me = row_index()
    depth = weight_ref.shape[0]
    main = weight_ref[:, pl.ds(pl.multiple_of(me // 2 * 2 * WIDE, 2 * WIDE), 2 * WIDE)]
    tile = weight_ref[:, pl.ds(pl.multiple_of(MAIN + me // 4 * WIDE, WIDE), WIDE)]
    low = me // 2 % 2 == 0
    size = depth + depth // 4
    for core in range(2):
        tail = jnp.where(low, tile[:, core * REST : (core + 1) * REST], tile[:, (core + 2) * REST : (core + 3) * REST])
        chip_ref[core * size : core * size + depth, :] = main[:, core * WIDE : (core + 1) * WIDE]
        chip_ref[core * size + depth : (core + 1) * size, :] = pack_tail(tail)
    slice_ref[...] = chip_ref[pl.ds(pl.multiple_of(me % 2 * size, 16), size), :]


def layout_kernel(grid_ref, *rest):
    select_ref, keys_ref, live_ref = rest[-3:]
    rows_n, cols_n = grid_ref[:1, :1], grid_ref[1:2, :1]
    patches = select_ref.shape[0]
    groups = patches // 4
    half = cols_n >> 1
    count = (rows_n >> 1) * half
    slots = lax.broadcasted_iota(jnp.int32, (groups, 1), 0)
    line = jnp.floor((slots.astype(F32) + 0.5) / half.astype(F32)).astype(jnp.int32)
    first = 2 * line * cols_n + 2 * (slots - line * half)
    at = lax.broadcasted_iota(jnp.int32, (groups, patches), 1)
    for corner in range(4):
        wanted = jnp.where(slots < count, first + (corner // 2) * cols_n + corner % 2, -1)
        select_ref[corner * groups : (corner + 1) * groups, :] = jnp.where(at == wanted, 1.0, 0.0).astype(BF16)
    key = lax.broadcasted_iota(jnp.int32, keys_ref.shape, 1)
    keys_ref[...] = jnp.where(key < rows_n * cols_n, 0.0, -1e30)
    slot = lax.broadcasted_iota(jnp.int32, live_ref.shape, 1)
    live_ref[...] = jnp.where(slot < count, 1.0, 0.0)


def attend_kernel(select_ref, dead_ref, *rest):
    blocks = rest[:ROWS]
    out_ref, q_all, k_all, v_all = rest[-4:]
    me = row_index()
    band = blocks[0].shape[0]
    patches = band * ROWS
    for step, block in zip(steps(SENDERS), blocks):
        at = pl.ds(pl.multiple_of((me ^ step) * band, band), band)
        q_all[at, :] = block[:, :HPAIR]
        k_all[at, :] = block[:, HPAIR : 2 * HPAIR]
        v_all[at, :] = block[:, 2 * HPAIR : 3 * HPAIR]
    queries = jnp.dot(select_ref[...], q_all[...], preferred_element_type=F32).astype(BF16)
    lane = lax.broadcasted_iota(jnp.int32, (1, HPAIR), 1)
    keys, values, dead = k_all[...], v_all[...], dead_ref[...]
    mixed = []
    for head in range(2):
        mine = (lane >= head * HDIM) & (lane < (head + 1) * HDIM)
        asked = jnp.where(mine, queries, jnp.zeros_like(queries))
        scores = lax.dot_general(asked, keys, (((1,), (1,)), ((), ())), preferred_element_type=F32) + dead
        weights = jnp.exp2((scores - jnp.max(scores, axis=1, keepdims=True)) * ROOT)
        total = jnp.sum(weights, axis=1, keepdims=True)
        mixed.append(jnp.dot(weights.astype(BF16), values, preferred_element_type=F32) * (1.0 / total))
    attn = jnp.where(lane < HDIM, mixed[0], mixed[1])
    out_ref[:patches, :] = attn[:, :WIDE].astype(BF16)
    out_ref[patches:, :] = pack_tail(attn[:, WIDE:]).astype(BF16)


def weight_rows(cut):
    depth = 2 * HPAIR
    packed = cut[depth:]
    tail = jnp.concatenate([packed[:, at * REST : (at + 1) * REST] for at in range(4)], axis=0)
    whole = jnp.concatenate([cut[:depth], tail], axis=1)
    return [whole[core * HPAIR : (core + 1) * HPAIR] for core in range(2)]


def place_rows(rows, base, main_ref, tail_ref):
    for core in range(2):
        pair = base + core
        main_ref[pl.ds(pl.multiple_of(pair * WIDE, WIDE), WIDE), :] = rows[core][:WIDE]
        for corner in range(4):
            spot = pl.multiple_of(pair * WIDE + corner * REST, REST)
            tail_ref[corner, pl.ds(spot, REST), :] = rows[core][WIDE:]


def ready_kernel(select_ref, gain_hbm, token_ref, *rest):
    del token_ref
    blocks = rest[:ROWS]
    own_ref, near_ref = rest[ROWS : ROWS + 2]
    resid_ref, gain_out, main_ref, tail_ref, held, line, sem = rest[-7:]
    fetch = pltpu.make_async_copy(gain_hbm, line, sem)
    fetch.start()
    me = row_index()
    band = blocks[0].shape[0]
    for step, block in zip(steps(SENDERS), blocks):
        at = pl.ds(pl.multiple_of((me ^ step) * band, band), band)
        held[at, :] = block[:, 3 * HPAIR :]
    resid_ref[...] = jnp.dot(select_ref[...], held[...], preferred_element_type=F32)
    core = me % 2
    size = own_ref.shape[0]
    half = pl.ds(pl.multiple_of(core * size, 16), size)
    main_ref[...] = jnp.zeros_like(main_ref)
    tail_ref[...] = jnp.zeros_like(tail_ref)
    place_slices([(0, own_ref[...]), (3 - 2 * core, near_ref[half, :])], main_ref, tail_ref)
    fetch.wait()
    whole = line[...].reshape(1, D)
    gain = jnp.zeros(gain_out.shape, F32)
    for pair in range(ROWS):
        parts = [whole[:, pair * WIDE : (pair + 1) * WIDE]]
        parts.append(whole[:, MAIN + pair * REST : MAIN + (pair + 1) * REST])
        gain = jnp.where(me == pair, jnp.concatenate(parts, axis=1), gain)
    gain_out[...] = gain


def place_slices(cuts, main_ref, tail_ref):
    for step, cut in cuts:
        place_rows(weight_rows(cut), 2 * lax.rem(lax.axis_index("page") + step, PAGES), main_ref, tail_ref)


def last_kernel(across_ref, swapped_ref, main_before_ref, tail_before_ref, main_ref, tail_ref):
    main_ref[...] = main_before_ref[...]
    tail_ref[...] = tail_before_ref[...]
    core = row_index() % 2
    size = across_ref.shape[0]
    half = pl.ds(pl.multiple_of(core * size, 16), size)
    place_slices([(2, across_ref[...]), (1 + 2 * core, swapped_ref[half, :])], main_ref, tail_ref)


def far_block():
    me = row_index()
    return pl.ds(pl.multiple_of((me // 2 ^ 3) * 2 * WIDE, 2 * WIDE), 2 * WIDE)


def collect_late(same, other):
    core = row_index() % 2
    left = jnp.where(core == 0, same[...], other[...])
    right = jnp.where(core == 0, other[...], same[...])
    return jnp.concatenate([left, right], axis=1)


def add_features(owners, pieces, weights, before_ref, out_ref):
    main_ref, tail_ref = weights
    me = row_index()
    patches = out_ref.shape[0]
    groups = patches // 4
    mains, tails = [], []
    for step in owners:
        pair = me ^ step
        columns = pl.ds(pl.multiple_of(pair * WIDE, WIDE), WIDE)
        mains.append(main_ref[columns, :])
        tails.append([tail_ref[at, columns, :] for at in range(4)])
    rows = jnp.concatenate([piece[...] for piece in pieces], axis=1)
    base = before_ref[...] + jnp.dot(rows[:patches], jnp.concatenate(mains, axis=0), preferred_element_type=F32)
    for corner in range(4):
        span = slice(corner * groups, (corner + 1) * groups)
        tail = jnp.concatenate([tail[corner] for tail in tails], axis=0)
        out_ref[span, :] = base[span] + jnp.dot(rows[patches:], tail, preferred_element_type=F32)


def project_first_kernel(*rest):
    add_features(OWNERS[:3], rest[:3], rest[3:5], *rest[5:])


def project_second_kernel(*rest):
    add_features(OWNERS[3:6], rest[:3], rest[3:5], *rest[5:])


def project_kernel(*rest):
    same, other, base_ref, main_ref, tail_ref, gain_ref, out_ref = rest
    patches = base_ref.shape[0]
    groups = patches // 4
    block = far_block()
    full = collect_late(same, other)
    base = base_ref[...] + jnp.dot(full[:patches], main_ref[block, :], preferred_element_type=F32)
    hidden = []
    for corner in range(4):
        span = slice(corner * groups, (corner + 1) * groups)
        hidden.append(base[span] + jnp.dot(full[patches:], tail_ref[corner, block, :], preferred_element_type=F32))
    squares = jnp.concatenate([(rows * rows).astype(BF16) for rows in hidden], axis=0)
    sums = lax.dot_general(
        jnp.ones((NOTES, HPAIR), BF16), squares, (((1,), (1,)), ((), ())), preferred_element_type=F32
    )
    row = lax.broadcasted_iota(jnp.int32, (NOTES, groups), 0)
    notes = jnp.zeros((NOTES, groups), F32)
    ends = []
    for corner in range(4):
        total = sums[:, corner * groups : (corner + 1) * groups]
        coarse = total.astype(BF16).astype(F32)
        notes = jnp.where(row == corner, coarse, jnp.where(row == 4 + corner, total - coarse, notes))
        sent = hidden[corner] * gain_ref[...]
        out_ref[corner * groups : (corner + 1) * groups, :] = sent[:, :WIDE].astype(BF16)
        ends.append(sent[:, WIDE:])
    out_ref[patches : patches + groups, :] = jnp.concatenate(ends, axis=1).astype(BF16)
    out_ref[patches + groups :, :] = notes.astype(BF16)


def tail_kernel(weight_ref, bias_hbm, token_ref, out_ref, bias_out, line, sem):
    del token_ref
    fetch = pltpu.make_async_copy(bias_hbm, line, sem)
    fetch.start()
    for pair in range(ROWS):
        cut = [corner * D + MAIN + pair * REST for corner in range(4)]
        out_ref[:, pair * WIDE : (pair + 1) * WIDE] = jnp.concatenate(
            [weight_ref[:, at : at + REST] for at in cut], axis=1
        )
    fetch.wait()
    units = bias_out.shape[0]
    bias_out[...] = jnp.broadcast_to(line[...].reshape(1, units), (8, units)).T[:, :1]


def merge_product(weight_ref, corner, groups, pieces):
    me = row_index()
    spots = [pl.multiple_of(corner * D + (me ^ step) * WIDE, WIDE) for step, _ in pieces]
    span = slice(corner * groups, (corner + 1) * groups)
    return lax.dot_general(
        jnp.concatenate([weight_ref[:, pl.ds(spot, WIDE)] for spot in spots], axis=1),
        jnp.concatenate([piece[span, :] for _, piece in pieces], axis=1),
        (((1,), (1,)), ((), ())),
        preferred_element_type=F32,
    )


def tail_products(tail_ref, groups, pieces):
    me = row_index()
    columns = [tail_ref[:, pl.ds(pl.multiple_of((me ^ step) * WIDE, WIDE), WIDE)] for step, _ in pieces]
    tails = jnp.concatenate(columns, axis=1)
    ends = jnp.concatenate([piece[4 * groups : 5 * groups, :] for _, piece in pieces], axis=1)
    corner_of = lax.rem(lax.broadcasted_iota(jnp.int32, (1, ends.shape[1]), 1), WIDE) // REST
    return [
        lax.dot_general(
            tails,
            jnp.where(corner_of == corner, ends, jnp.zeros_like(ends)),
            (((1,), (1,)), ((), ())),
            preferred_element_type=F32,
        )
        for corner in range(4)
    ]


def merge_first_kernel(*rest):
    pieces, (weight_ref, tail_ref, sum_ref) = list(zip(OWNERS[:3], rest[:3])), rest[3:]
    groups = sum_ref.shape[2]
    for corner, tail in enumerate(tail_products(tail_ref, groups, pieces)):
        sum_ref[corner] = tail + merge_product(weight_ref, corner, groups, pieces)


def merge_second_kernel(*rest):
    pieces, (before_ref, weight_ref, tail_ref, sum_ref) = list(zip(OWNERS[3:6], rest[:3])), rest[3:]
    groups = sum_ref.shape[2]
    for corner, tail in enumerate(tail_products(tail_ref, groups, pieces)):
        sum_ref[corner] = before_ref[corner] + (tail + merge_product(weight_ref, corner, groups, pieces))


def merge_kernel(*rest):
    pieces = rest[:ROWS]
    before_ref, weight_ref, tail_ref, bias_ref, live_ref, out_ref = rest[ROWS:]
    me = row_index()
    groups = live_ref.shape[1]
    patches = 4 * groups
    contract = (((1,), (1,)), ((), ()))
    block = pl.multiple_of((me // 2 ^ 3) * 2 * WIDE, 2 * WIDE)
    rows = collect_late(pieces[6], pieces[7])
    notes = jnp.zeros((NOTES, groups), F32)
    for piece in pieces:
        notes = notes + piece[patches + groups :, :].astype(F32)
    scale = lax.rsqrt((notes[:4] + notes[4:8]) * (1.0 / D) + 1e-06)
    spread = jnp.concatenate([jnp.broadcast_to(scale[at : at + 1], (REST, groups)) for at in range(4)], axis=0).T
    ends = rows[patches : patches + groups].astype(F32) * jnp.concatenate([spread] * 2, axis=1)
    total = bias_ref[...] + lax.dot_general(
        tail_ref[:, pl.ds(block, 2 * WIDE)], ends.astype(BF16), contract, preferred_element_type=F32
    )
    for corner in range(4):
        part = before_ref[corner] + lax.dot_general(
            weight_ref[:, pl.ds(pl.multiple_of(corner * D + block, 2 * WIDE), 2 * WIDE)],
            rows[corner * groups : (corner + 1) * groups],
            contract,
            preferred_element_type=F32,
        )
        total = total + scale[corner : corner + 1] * part
    merged = 0.5 * total * (1.0 + lax.erf(total * math.sqrt(0.5)))
    out_ref[0] = jnp.where(live_ref[...] > 0.0, merged, 0.0).astype(BF16)


def kernel(body, name, out_shape, scratch=(), fetched=(), count=0, limit=24, flops=0, moved=0):
    specs = [pl.BlockSpec(memory_space=pltpu.VMEM) for _ in range(count)]
    for at in fetched:
        specs[at] = pl.BlockSpec(memory_space=pl.ANY)
    return pl.pallas_call(
        body,
        out_shape=out_shape,
        in_specs=specs,
        out_specs=jax.tree.map(lambda _: pl.BlockSpec(memory_space=pltpu.VMEM), out_shape),
        scratch_shapes=list(scratch),
        compiler_params=pltpu.CompilerParams(vmem_limit_bytes=limit * 1024 * 1024),
        cost_estimate=pl.CostEstimate(flops=flops, bytes_accessed=moved, transcendentals=0),
        name=name,
    )


def in_hbm(value):
    return pltpu.with_memory_space_constraint(value, pltpu.HBM)


def shape(*dims, dtype=BF16):
    return jax.ShapeDtypeStruct(dims, dtype)


def swap(value, even, odd=None):
    odd = even if odd is None else odd
    return lax.ppermute(value, "row", [(row, row ^ (odd if row % 2 else even)) for row in range(ROWS)])


def turn(value, low, high):
    pairs = [
        (page * ROWS + row, (page + (high if row % 2 else low)) % PAGES * ROWS + row)
        for page in range(PAGES)
        for row in range(ROWS)
    ]
    return lax.ppermute(value, ("page", "row"), pairs)


def after(value, *arrays):
    return lax.optimization_barrier((value, *arrays))[0]


def local_eight(qkv_rows, residual, out_weight, norm_gain, merge_weight, merge_bias, page_grid):
    band = qkv_rows.shape[1]
    patches = band * ROWS
    groups = patches // 4
    units = merge_weight.shape[0]
    depth = out_weight.shape[0]
    piece = patches + groups
    size = depth + depth // 4

    *sends, grid = kernel(
        spread_kernel,
        "spread",
        [shape(band, 4 * HPAIR)] * ROWS + [shape(8, WIDE, dtype=jnp.int32)],
        [
            pltpu.VMEM((band, 3 * D), BF16),
            pltpu.VMEM((band, D), BF16),
            pltpu.VMEM((ROWS, band, 4 * HPAIR), BF16),
            pltpu.SMEM(page_grid.shape, jnp.int32),
            pltpu.SemaphoreType.DMA((6,)),
        ],
        fetched=range(3),
        count=3,
        moved=1 << 20,
    )(in_hbm(qkv_rows), in_hbm(residual), in_hbm(page_grid))
    blocks = [sends[0]] + [swap(send, *pair) for send, pair in zip(sends[1:], RECEIVERS[1:])]
    select, dead, live = kernel(
        layout_kernel,
        "layout",
        [shape(patches, patches), shape(1, patches, dtype=F32), shape(1, groups, dtype=F32)],
        fetched=range(1, 1 + 3),
        count=1 + 3,
        moved=1 << 20,
    )(grid, *blocks[1:4])
    chip, own = kernel(
        slice_kernel,
        "out_weight_slices",
        [shape(2 * size, WIDE), shape(size, WIDE)],
        fetched=(1,),
        count=2,
        moved=1 << 20,
    )(out_weight, sends[0])
    near = turn(after(chip, *()), 1, PAGES - 1)
    swapped = swap(near, 1)
    attn = kernel(
        attend_kernel,
        "attend",
        shape(piece, WIDE),
        [pltpu.VMEM((patches, HPAIR), BF16)] * 3,
        count=2 + ROWS,
        flops=20 * patches * patches * 4096,
        moved=1 << 20,
    )(select, dead, *blocks)
    across = turn(after(own, attn), 2, 2)
    resid, own_gain, main, tail = kernel(
        ready_kernel,
        "ready",
        [shape(patches, HPAIR, dtype=F32), shape(1, HPAIR, dtype=F32), shape(MAIN, HPAIR), shape(4, MAIN, HPAIR)],
        [pltpu.VMEM((patches, HPAIR), BF16), pltpu.VMEM((D,), F32), pltpu.SemaphoreType.DMA],
        fetched=(1, 2),
        count=3 + ROWS + 2,
        flops=10 * patches * patches * 4096,
        moved=4 << 20,
    )(select, in_hbm(norm_gain), attn, *blocks, own, near)
    last = kernel(
        last_kernel,
        "ready_last",
        [shape(MAIN, HPAIR), shape(4, MAIN, HPAIR)],
        count=4,
        flops=1,
        moved=1,
    )(across, swapped, main, tail)
    one, two, far = swap(attn, 4), swap(attn, 2), swap(attn, 6)
    weights = tuple(last)
    rows = shape(patches, HPAIR, dtype=F32)
    first = kernel(project_first_kernel, "project_first", rows, count=6, flops=1, moved=1)(attn, one, two, *weights, resid)
    near = [swap(after(attn, last[0]), 1), swap(one, 1), swap(two, 1)]
    second = kernel(project_second_kernel, "project_second", rows, count=6, flops=1, moved=1)(*near, *weights, first)
    hidden = kernel(
        project_kernel,
        "project",
        shape(piece + NOTES, WIDE),
        count=2 + 4,
        flops=patches * MAIN * 256,
        moved=4 << 20,
    )(far, swap(far, 1), second, *weights, own_gain)
    ends, bias = kernel(
        tail_kernel,
        "merge_tail",
        [shape(units, MAIN), shape(units, 1, dtype=F32)],
        [pltpu.VMEM((units,), F32), pltpu.SemaphoreType.DMA],
        fetched=(1, 2),
        count=3,
        moved=4 << 20,
    )(merge_weight, in_hbm(merge_bias), hidden)
    sums = shape(4, units, groups, dtype=F32)
    one, two, far = swap(hidden, 4), swap(hidden, 2), swap(hidden, 6)
    first = kernel(merge_first_kernel, "merge_first", sums, count=5, flops=1, moved=1)(
        hidden, one, two, merge_weight, ends
    )
    near = [swap(after(hidden, ends), 1), swap(one, 1), swap(two, 1)]
    second = kernel(merge_second_kernel, "merge_second", sums, count=6, flops=1, moved=1)(
        *near, first, merge_weight, ends
    )
    return kernel(
        merge_kernel,
        "merge",
        shape(1, units, groups),
        count=ROWS + 5,
        flops=4 * units * groups * MAIN,
        moved=8 << 20,
    )(hidden, one, two, *near, far, swap(after(far, first, *near), 1), second, merge_weight, ends, bias, live)


def solution(mesh):
    in_specs = (
        P("page", "row", None),
        P("page", "row", None),
        P("page", None),
        P(),
        P("row", None),
        P("row"),
        P("page", None),
    )
    out_specs = P("page", "row", None)
    local = local_eight if mesh.shape["row"] == 8 and mesh.shape["page"] == 4 else local_any
    return jax.shard_map(local, mesh=mesh, in_specs=in_specs, out_specs=out_specs, check_vma=False)
```

```python
import functools
import math

import jax
import jax.numpy as jnp
from jax import lax
from jax.experimental import pallas as pl
from jax.experimental.pallas import tpu as pltpu
from jax.sharding import PartitionSpec as P

D = 1280
HEADS = 16
HDIM = 80


def local_any(qkv_rows, residual, out_weight, norm_gain, merge_weight, merge_bias, page_grid):
    row_count = lax.axis_size("row")
    q_split = max(1, row_count // HEADS)
    head_groups = row_count // q_split
    width = D // head_groups
    heads_per = width // HDIM
    band_len = qkv_rows.shape[1]
    part_len = band_len // q_split
    local_qkv = qkv_rows[0]
    queries = local_qkv[:, :D]
    key_vals = jnp.concatenate(
        [
            local_qkv[:, D : 2 * D].reshape(band_len, head_groups, width),
            local_qkv[:, 2 * D :].reshape(band_len, head_groups, width),
        ],
        axis=2,
    )
    q_send = (
        queries.reshape(q_split, part_len, head_groups, width)
        .transpose(2, 0, 1, 3)
        .reshape(row_count, part_len, width)
    )
    kv_send = jnp.broadcast_to(
        key_vals.transpose(1, 0, 2)[:, None], (head_groups, q_split, band_len, 2 * width)
    )
    kv_send = kv_send.reshape(row_count, band_len, 2 * width)
    q_recv, kv_recv = (
        lax.all_to_all(q_send, "row", split_axis=0, concat_axis=1, tiled=True),
        lax.all_to_all(kv_send, "row", split_axis=0, concat_axis=1, tiled=True),
    )
    kv_local = kv_recv[0]
    positions = jnp.arange(row_count * band_len, dtype=jnp.int32)
    valid_len = page_grid[0, 0] * page_grid[0, 1]
    key_valid = positions < valid_len
    key_total = kv_local.shape[0]
    key_heads = kv_local[:, :width].reshape(key_total, heads_per, HDIM)
    value_heads = kv_local[:, width:].reshape(key_total, heads_per, HDIM)
    query_total = row_count * part_len
    q_block = math.gcd(query_total, 512)
    q_blocks = q_recv[0].reshape(query_total // q_block, q_block, heads_per, HDIM)
    root_dim = math.sqrt(HDIM)

    def attend(q_span):
        scores = (
            jnp.einsum("qhd,khd->hqk", q_span, key_heads, preferred_element_type=jnp.float32)
            / root_dim
        )
        scores = jnp.where(key_valid[None, None, :], scores, -1e30)
        peak = jnp.max(scores, axis=2, keepdims=True)
        weights = jnp.exp(scores - peak)
        total = jnp.sum(weights, axis=2, keepdims=True)
        mixed = (
            jnp.einsum(
                "hqk,khd->hqd",
                weights.astype(jnp.bfloat16),
                value_heads,
                preferred_element_type=jnp.float32,
            )
            / total
        )
        return mixed.transpose(1, 0, 2).reshape(q_span.shape[0], width).astype(jnp.bfloat16)

    attn_heads = lax.map(attend, q_blocks).reshape(row_count, part_len, width)
    returned = lax.all_to_all(attn_heads, "row", split_axis=0, concat_axis=0, tiled=True)
    attn = (
        returned.reshape(head_groups, q_split, part_len, width)
        .transpose(1, 2, 0, 3)
        .reshape(band_len, D)
    )
    projected = jnp.dot(
        attn,
        lax.all_gather(out_weight, "page", axis=0, tiled=True),
        preferred_element_type=jnp.float32,
    )
    hidden = residual[0].astype(jnp.float32) + projected
    normed = (
        hidden * lax.rsqrt(jnp.mean(hidden * hidden, axis=1, keepdims=True) + 1e-06) * norm_gain
    ).astype(jnp.bfloat16)
    rows_n = page_grid[0, 0]
    cols_n = page_grid[0, 1]
    group_total = band_len * row_count // 4
    slots = jnp.arange(group_total, dtype=jnp.int32)
    half_cols = cols_n // 2
    live = slots < rows_n // 2 * half_cols
    first = jnp.where(live, 2 * (slots // half_cols) * cols_n + 2 * (slots % half_cols), 0)
    corners = [first, first + 1, first + cols_n, first + cols_n + 1]
    local_units = merge_weight.shape[0]
    page_all = lax.all_gather(normed, "row", axis=0, tiled=True)
    merged_sum = jnp.zeros((local_units, group_total), jnp.float32)
    for corner in range(4):
        picked = jnp.take(page_all, corners[corner], axis=0)
        merged_sum = merged_sum + jnp.einsum(
            "md,gd->mg",
            merge_weight[:, corner * D : (corner + 1) * D],
            picked,
            preferred_element_type=jnp.float32,
        )
    merged = jax.nn.gelu(merged_sum + merge_bias[:, None], approximate=False)
    merged = jnp.where(live[None, :], merged, 0.0).astype(jnp.bfloat16)
    return merged[None]


ROWS = 8
PAGES = 4
HPAIR = 2 * HDIM
WIDE = 128
REST = HPAIR - WIDE
MAIN = ROWS * WIDE
NOTES = 16
RECEIVERS = ((0, 0), (4, 2), (2, 4), (6, 6), (7, 7), (3, 5), (5, 3), (1, 1))
SENDERS = ((0, 0), (4, 2), (2, 4), (6, 6), (7, 7), (5, 3), (3, 5), (1, 1))
OWNERS = (0, 4, 2, 1, 5, 3, 6, 7)
ROOT = math.log2(math.e) / math.sqrt(HDIM)
BF16 = jnp.bfloat16
F32 = jnp.float32


def row_index():
    return lax.axis_index("row")


def steps(pairs):
    core = row_index() % 2
    return [even + (odd - even) * core for even, odd in pairs]


def pack_tail(wide):
    groups = wide.shape[0] // 4
    return jnp.concatenate([wide[at * groups : (at + 1) * groups] for at in range(4)], axis=1)


def spread_kernel(qkv_hbm, resid_hbm, grid_hbm, *rest):
    outs = rest[:ROWS]
    grid_out, qkv, resid, held, grid, sems = rest[ROWS:]
    me = row_index()
    copies = [
        pltpu.make_async_copy(grid_hbm, grid, sems.at[0]),
        pltpu.make_async_copy(resid_hbm.at[0], resid, sems.at[1]),
    ]
    part = qkv.shape[0] // 4
    for at in range(4):
        rows = pl.ds(at * part, part)
        copies.append(pltpu.make_async_copy(qkv_hbm.at[0, rows], qkv.at[rows], sems.at[2 + at]))
    for copy in reversed(copies):
        copy.start()
    for copy in copies:
        copy.wait()
    for dest in range(ROWS):
        at = dest * HPAIR
        parts = [qkv[:, part * D + at : part * D + at + HPAIR] for part in range(3)]
        parts.append(resid[:, dest * WIDE : (dest + 1) * WIDE])
        parts.append(resid[:, MAIN + dest * REST : MAIN + (dest + 1) * REST])
        held[dest] = jnp.concatenate(parts, axis=1)
    for step, out in zip(steps(RECEIVERS), outs):
        out[...] = held[me ^ step]
    row = lax.broadcasted_iota(jnp.int32, grid_out.shape, 0)
    grid_out[...] = jnp.where(row == 0, grid[0, 0], grid[0, 1])


def slice_kernel(weight_ref, *rest):
    chip_ref, slice_ref = rest[-2:]
    me = row_index()
    depth = weight_ref.shape[0]
    main = weight_ref[:, pl.ds(pl.multiple_of(me // 2 * 2 * WIDE, 2 * WIDE), 2 * WIDE)]
    tile = weight_ref[:, pl.ds(pl.multiple_of(MAIN + me // 4 * WIDE, WIDE), WIDE)]
    low = me // 2 % 2 == 0
    size = depth + depth // 4
    for core in range(2):
        tail = jnp.where(low, tile[:, core * REST : (core + 1) * REST], tile[:, (core + 2) * REST : (core + 3) * REST])
        chip_ref[core * size : core * size + depth, :] = main[:, core * WIDE : (core + 1) * WIDE]
        chip_ref[core * size + depth : (core + 1) * size, :] = pack_tail(tail)
    slice_ref[...] = chip_ref[pl.ds(pl.multiple_of(me % 2 * size, 16), size), :]


def layout_kernel(grid_ref, *rest):
    select_ref, keys_ref, live_ref = rest[-3:]
    rows_n, cols_n = grid_ref[:1, :1], grid_ref[1:2, :1]
    patches = select_ref.shape[0]
    groups = patches // 4
    half = cols_n >> 1
    count = (rows_n >> 1) * half
    slots = lax.broadcasted_iota(jnp.int32, (groups, 1), 0)
    line = jnp.floor((slots.astype(F32) + 0.5) / half.astype(F32)).astype(jnp.int32)
    first = 2 * line * cols_n + 2 * (slots - line * half)
    at = lax.broadcasted_iota(jnp.int32, (groups, patches), 1)
    for corner in range(4):
        wanted = jnp.where(slots < count, first + (corner // 2) * cols_n + corner % 2, -1)
        select_ref[corner * groups : (corner + 1) * groups, :] = jnp.where(at == wanted, 1.0, 0.0).astype(BF16)
    key = lax.broadcasted_iota(jnp.int32, keys_ref.shape, 1)
    keys_ref[...] = jnp.where(key < rows_n * cols_n, 0.0, -1e30)
    slot = lax.broadcasted_iota(jnp.int32, live_ref.shape, 1)
    live_ref[...] = jnp.where(slot < count, 1.0, 0.0)


def attend_kernel(select_ref, dead_ref, *rest):
    blocks = rest[:ROWS]
    out_ref, q_all, k_all, v_all = rest[-4:]
    me = row_index()
    band = blocks[0].shape[0]
    patches = band * ROWS
    for step, block in zip(steps(SENDERS), blocks):
        at = pl.ds(pl.multiple_of((me ^ step) * band, band), band)
        q_all[at, :] = block[:, :HPAIR]
        k_all[at, :] = block[:, HPAIR : 2 * HPAIR]
        v_all[at, :] = block[:, 2 * HPAIR : 3 * HPAIR]
    queries = jnp.dot(select_ref[...], q_all[...], preferred_element_type=F32).astype(BF16)
    lane = lax.broadcasted_iota(jnp.int32, (1, HPAIR), 1)
    keys, values, dead = k_all[...], v_all[...], dead_ref[...]
    mixed = []
    for head in range(2):
        mine = (lane >= head * HDIM) & (lane < (head + 1) * HDIM)
        asked = jnp.where(mine, queries, jnp.zeros_like(queries))
        scores = lax.dot_general(asked, keys, (((1,), (1,)), ((), ())), preferred_element_type=F32) + dead
        weights = jnp.exp2((scores - jnp.max(scores, axis=1, keepdims=True)) * ROOT)
        total = jnp.sum(weights, axis=1, keepdims=True)
        mixed.append(jnp.dot(weights.astype(BF16), values, preferred_element_type=F32) * (1.0 / total))
    attn = jnp.where(lane < HDIM, mixed[0], mixed[1])
    out_ref[:patches, :] = attn[:, :WIDE].astype(BF16)
    out_ref[patches:, :] = pack_tail(attn[:, WIDE:]).astype(BF16)


def weight_rows(cut):
    depth = 2 * HPAIR
    packed = cut[depth:]
    tail = jnp.concatenate([packed[:, at * REST : (at + 1) * REST] for at in range(4)], axis=0)
    whole = jnp.concatenate([cut[:depth], tail], axis=1)
    return [whole[core * HPAIR : (core + 1) * HPAIR] for core in range(2)]


def place_rows(rows, base, main_ref, tail_ref):
    for core in range(2):
        pair = base + core
        main_ref[pl.ds(pl.multiple_of(pair * WIDE, WIDE), WIDE), :] = rows[core][:WIDE]
        for corner in range(4):
            spot = pl.multiple_of(pair * WIDE + corner * REST, REST)
            tail_ref[corner, pl.ds(spot, REST), :] = rows[core][WIDE:]


def ready_kernel(select_ref, gain_hbm, token_ref, *rest):
    del token_ref
    blocks = rest[:ROWS]
    own_ref, near_ref = rest[ROWS : ROWS + 2]
    resid_ref, gain_out, main_ref, tail_ref, held, line, sem = rest[-7:]
    fetch = pltpu.make_async_copy(gain_hbm, line, sem)
    fetch.start()
    me = row_index()
    band = blocks[0].shape[0]
    for step, block in zip(steps(SENDERS), blocks):
        at = pl.ds(pl.multiple_of((me ^ step) * band, band), band)
        held[at, :] = block[:, 3 * HPAIR :]
    resid_ref[...] = jnp.dot(select_ref[...], held[...], preferred_element_type=F32)
    core = me % 2
    size = own_ref.shape[0]
    half = pl.ds(pl.multiple_of(core * size, 16), size)
    main_ref[...] = jnp.zeros_like(main_ref)
    tail_ref[...] = jnp.zeros_like(tail_ref)
    place_slices([(0, own_ref[...]), (3 - 2 * core, near_ref[half, :])], main_ref, tail_ref)
    fetch.wait()
    whole = line[...].reshape(1, D)
    gain = jnp.zeros(gain_out.shape, F32)
    for pair in range(ROWS):
        parts = [whole[:, pair * WIDE : (pair + 1) * WIDE]]
        parts.append(whole[:, MAIN + pair * REST : MAIN + (pair + 1) * REST])
        gain = jnp.where(me == pair, jnp.concatenate(parts, axis=1), gain)
    gain_out[...] = gain


def place_slices(cuts, main_ref, tail_ref):
    for step, cut in cuts:
        place_rows(weight_rows(cut), 2 * lax.rem(lax.axis_index("page") + step, PAGES), main_ref, tail_ref)


def last_kernel(across_ref, swapped_ref, main_before_ref, tail_before_ref, main_ref, tail_ref):
    main_ref[...] = main_before_ref[...]
    tail_ref[...] = tail_before_ref[...]
    core = row_index() % 2
    size = across_ref.shape[0]
    half = pl.ds(pl.multiple_of(core * size, 16), size)
    place_slices([(2, across_ref[...]), (1 + 2 * core, swapped_ref[half, :])], main_ref, tail_ref)


def far_block():
    me = row_index()
    return pl.ds(pl.multiple_of((me // 2 ^ 3) * 2 * WIDE, 2 * WIDE), 2 * WIDE)


def collect_late(same, other):
    core = row_index() % 2
    left = jnp.where(core == 0, same[...], other[...])
    right = jnp.where(core == 0, other[...], same[...])
    return jnp.concatenate([left, right], axis=1)


def add_features(owners, pieces, weights, before_ref, out_ref):
    main_ref, tail_ref = weights
    me = row_index()
    patches = out_ref.shape[0]
    groups = patches // 4
    mains, tails = [], []
    for step in owners:
        pair = me ^ step
        columns = pl.ds(pl.multiple_of(pair * WIDE, WIDE), WIDE)
        mains.append(main_ref[columns, :])
        tails.append([tail_ref[at, columns, :] for at in range(4)])
    rows = jnp.concatenate([piece[...] for piece in pieces], axis=1)
    base = before_ref[...] + jnp.dot(rows[:patches], jnp.concatenate(mains, axis=0), preferred_element_type=F32)
    for corner in range(4):
        span = slice(corner * groups, (corner + 1) * groups)
        tail = jnp.concatenate([tail[corner] for tail in tails], axis=0)
        out_ref[span, :] = base[span] + jnp.dot(rows[patches:], tail, preferred_element_type=F32)


def project_first_kernel(*rest):
    add_features(OWNERS[:3], rest[:3], rest[3:5], *rest[5:])


def project_second_kernel(*rest):
    add_features(OWNERS[3:6], rest[:3], rest[3:5], *rest[5:])


def project_kernel(*rest):
    same, other, base_ref, main_ref, tail_ref, gain_ref, out_ref = rest
    patches = base_ref.shape[0]
    groups = patches // 4
    block = far_block()
    full = collect_late(same, other)
    base = base_ref[...] + jnp.dot(full[:patches], main_ref[block, :], preferred_element_type=F32)
    hidden = []
    for corner in range(4):
        span = slice(corner * groups, (corner + 1) * groups)
        hidden.append(base[span] + jnp.dot(full[patches:], tail_ref[corner, block, :], preferred_element_type=F32))
    squares = jnp.concatenate([(rows * rows).astype(BF16) for rows in hidden], axis=0)
    sums = lax.dot_general(
        jnp.ones((NOTES, HPAIR), BF16), squares, (((1,), (1,)), ((), ())), preferred_element_type=F32
    )
    row = lax.broadcasted_iota(jnp.int32, (NOTES, groups), 0)
    notes = jnp.zeros((NOTES, groups), F32)
    ends = []
    for corner in range(4):
        total = sums[:, corner * groups : (corner + 1) * groups]
        coarse = total.astype(BF16).astype(F32)
        notes = jnp.where(row == corner, coarse, jnp.where(row == 4 + corner, total - coarse, notes))
        sent = hidden[corner] * gain_ref[...]
        out_ref[corner * groups : (corner + 1) * groups, :] = sent[:, :WIDE].astype(BF16)
        ends.append(sent[:, WIDE:])
    out_ref[patches : patches + groups, :] = jnp.concatenate(ends, axis=1).astype(BF16)
    out_ref[patches + groups :, :] = notes.astype(BF16)


def tail_kernel(weight_ref, bias_hbm, token_ref, out_ref, bias_out, line, sem):
    del token_ref
    fetch = pltpu.make_async_copy(bias_hbm, line, sem)
    fetch.start()
    for pair in range(ROWS):
        cut = [corner * D + MAIN + pair * REST for corner in range(4)]
        out_ref[:, pair * WIDE : (pair + 1) * WIDE] = jnp.concatenate(
            [weight_ref[:, at : at + REST] for at in cut], axis=1
        )
    fetch.wait()
    units = bias_out.shape[0]
    bias_out[...] = jnp.broadcast_to(line[...].reshape(1, units), (8, units)).T[:, :1]


def merge_product(weight_ref, corner, groups, pieces):
    me = row_index()
    spots = [pl.multiple_of(corner * D + (me ^ step) * WIDE, WIDE) for step, _ in pieces]
    span = slice(corner * groups, (corner + 1) * groups)
    return lax.dot_general(
        jnp.concatenate([weight_ref[:, pl.ds(spot, WIDE)] for spot in spots], axis=1),
        jnp.concatenate([piece[span, :] for _, piece in pieces], axis=1),
        (((1,), (1,)), ((), ())),
        preferred_element_type=F32,
    )


def tail_products(tail_ref, groups, pieces):
    me = row_index()
    columns = [tail_ref[:, pl.ds(pl.multiple_of((me ^ step) * WIDE, WIDE), WIDE)] for step, _ in pieces]
    tails = jnp.concatenate(columns, axis=1)
    ends = jnp.concatenate([piece[4 * groups : 5 * groups, :] for _, piece in pieces], axis=1)
    corner_of = lax.rem(lax.broadcasted_iota(jnp.int32, (1, ends.shape[1]), 1), WIDE) // REST
    return [
        lax.dot_general(
            tails,
            jnp.where(corner_of == corner, ends, jnp.zeros_like(ends)),
            (((1,), (1,)), ((), ())),
            preferred_element_type=F32,
        )
        for corner in range(4)
    ]


def merge_first_kernel(*rest):
    pieces, (weight_ref, tail_ref, sum_ref) = list(zip(OWNERS[:3], rest[:3])), rest[3:]
    groups = sum_ref.shape[2]
    for corner, tail in enumerate(tail_products(tail_ref, groups, pieces)):
        sum_ref[corner] = tail + merge_product(weight_ref, corner, groups, pieces)


def merge_second_kernel(*rest):
    pieces, (before_ref, weight_ref, tail_ref, sum_ref) = list(zip(OWNERS[3:6], rest[:3])), rest[3:]
    groups = sum_ref.shape[2]
    for corner, tail in enumerate(tail_products(tail_ref, groups, pieces)):
        sum_ref[corner] = before_ref[corner] + (tail + merge_product(weight_ref, corner, groups, pieces))


def merge_kernel(*rest):
    pieces = rest[:ROWS]
    before_ref, weight_ref, tail_ref, bias_ref, live_ref, out_hbm, held, sems = rest[ROWS:]
    me = row_index()
    groups = live_ref.shape[1]
    patches = 4 * groups
    contract = (((1,), (1,)), ((), ()))
    block = pl.multiple_of((me // 2 ^ 3) * 2 * WIDE, 2 * WIDE)
    rows = collect_late(pieces[6], pieces[7])
    notes = jnp.zeros((NOTES, groups), F32)
    for piece in pieces:
        notes = notes + piece[patches + groups :, :].astype(F32)
    scale = lax.rsqrt((notes[:4] + notes[4:8]) * (1.0 / D) + 1e-06)
    spread = jnp.concatenate([jnp.broadcast_to(scale[at : at + 1], (REST, groups)) for at in range(4)], axis=0).T
    ends = rows[patches : patches + groups].astype(F32) * jnp.concatenate([spread] * 2, axis=1)
    ends = ends.astype(BF16)
    half = held.shape[0] // 2
    copies = []
    for at in range(2):
        units = slice(at * half, (at + 1) * half)
        total = bias_ref[units, :] + lax.dot_general(
            tail_ref[units, pl.ds(block, 2 * WIDE)], ends, contract, preferred_element_type=F32
        )
        for corner in range(4):
            part = before_ref[corner, units] + lax.dot_general(
                weight_ref[units, pl.ds(pl.multiple_of(corner * D + block, 2 * WIDE), 2 * WIDE)],
                rows[corner * groups : (corner + 1) * groups],
                contract,
                preferred_element_type=F32,
            )
            total = total + scale[corner : corner + 1] * part
        merged = 0.5 * total * (1.0 + lax.erf(total * math.sqrt(0.5)))
        held[units, :] = jnp.where(live_ref[...] > 0.0, merged, 0.0).astype(BF16)
        copies.append(pltpu.make_async_copy(held.at[units], out_hbm.at[0, units], sems.at[at]))
        copies[at].start()
    for copy in copies:
        copy.wait()


def kernel(body, name, out_shape, scratch=(), fetched=(), count=0, limit=24, flops=0, moved=0, out=pltpu.VMEM):
    specs = [pl.BlockSpec(memory_space=pltpu.VMEM) for _ in range(count)]
    for at in fetched:
        specs[at] = pl.BlockSpec(memory_space=pl.ANY)
    return pl.pallas_call(
        body,
        out_shape=out_shape,
        in_specs=specs,
        out_specs=jax.tree.map(lambda _: pl.BlockSpec(memory_space=out), out_shape),
        scratch_shapes=list(scratch),
        compiler_params=pltpu.CompilerParams(vmem_limit_bytes=limit * 1024 * 1024),
        cost_estimate=pl.CostEstimate(flops=flops, bytes_accessed=moved, transcendentals=0),
        name=name,
    )


def in_hbm(value):
    return pltpu.with_memory_space_constraint(value, pltpu.HBM)


def shape(*dims, dtype=BF16):
    return jax.ShapeDtypeStruct(dims, dtype)


def swap(value, even, odd=None):
    odd = even if odd is None else odd
    return lax.ppermute(value, "row", [(row, row ^ (odd if row % 2 else even)) for row in range(ROWS)])


def turn(value, low, high):
    pairs = [
        (page * ROWS + row, (page + (high if row % 2 else low)) % PAGES * ROWS + row)
        for page in range(PAGES)
        for row in range(ROWS)
    ]
    return lax.ppermute(value, ("page", "row"), pairs)


def after(value, *arrays):
    return lax.optimization_barrier((value, *arrays))[0]


def local_eight(qkv_rows, residual, out_weight, norm_gain, merge_weight, merge_bias, page_grid):
    band = qkv_rows.shape[1]
    patches = band * ROWS
    groups = patches // 4
    units = merge_weight.shape[0]
    depth = out_weight.shape[0]
    piece = patches + groups
    size = depth + depth // 4

    *sends, grid = kernel(
        spread_kernel,
        "spread",
        [shape(band, 4 * HPAIR)] * ROWS + [shape(8, WIDE, dtype=jnp.int32)],
        [
            pltpu.VMEM((band, 3 * D), BF16),
            pltpu.VMEM((band, D), BF16),
            pltpu.VMEM((ROWS, band, 4 * HPAIR), BF16),
            pltpu.SMEM(page_grid.shape, jnp.int32),
            pltpu.SemaphoreType.DMA((6,)),
        ],
        fetched=range(3),
        count=3,
        moved=1 << 20,
    )(in_hbm(qkv_rows), in_hbm(residual), in_hbm(page_grid))
    blocks = [sends[0]] + [swap(send, *pair) for send, pair in zip(sends[1:], RECEIVERS[1:])]
    select, dead, live = kernel(
        layout_kernel,
        "layout",
        [shape(patches, patches), shape(1, patches, dtype=F32), shape(1, groups, dtype=F32)],
        fetched=range(1, 1 + 3),
        count=1 + 3,
        moved=1 << 20,
    )(grid, *blocks[1:4])
    chip, own = kernel(
        slice_kernel,
        "out_weight_slices",
        [shape(2 * size, WIDE), shape(size, WIDE)],
        fetched=(1,),
        count=2,
        moved=1 << 20,
    )(out_weight, sends[0])
    near = turn(after(chip, *()), 1, PAGES - 1)
    swapped = swap(near, 1)
    attn = kernel(
        attend_kernel,
        "attend",
        shape(piece, WIDE),
        [pltpu.VMEM((patches, HPAIR), BF16)] * 3,
        count=2 + ROWS,
        flops=20 * patches * patches * 4096,
        moved=1 << 20,
    )(select, dead, *blocks)
    across = turn(after(own, attn), 2, 2)
    resid, own_gain, main, tail = kernel(
        ready_kernel,
        "ready",
        [shape(patches, HPAIR, dtype=F32), shape(1, HPAIR, dtype=F32), shape(MAIN, HPAIR), shape(4, MAIN, HPAIR)],
        [pltpu.VMEM((patches, HPAIR), BF16), pltpu.VMEM((D,), F32), pltpu.SemaphoreType.DMA],
        fetched=(1, 2),
        count=3 + ROWS + 2,
        flops=10 * patches * patches * 4096,
        moved=4 << 20,
    )(select, in_hbm(norm_gain), attn, *blocks, own, near)
    last = kernel(
        last_kernel,
        "ready_last",
        [shape(MAIN, HPAIR), shape(4, MAIN, HPAIR)],
        count=4,
        flops=1,
        moved=1,
    )(across, swapped, main, tail)
    one, two, far = swap(attn, 4), swap(attn, 2), swap(attn, 6)
    weights = tuple(last)
    rows = shape(patches, HPAIR, dtype=F32)
    first = kernel(project_first_kernel, "project_first", rows, count=6, flops=1, moved=1)(attn, one, two, *weights, resid)
    near = [swap(after(attn, last[0]), 1), swap(one, 1), swap(two, 1)]
    second = kernel(project_second_kernel, "project_second", rows, count=6, flops=1, moved=1)(*near, *weights, first)
    hidden = kernel(
        project_kernel,
        "project",
        shape(piece + NOTES, WIDE),
        count=2 + 4,
        flops=patches * MAIN * 256,
        moved=4 << 20,
    )(far, swap(far, 1), second, *weights, own_gain)
    ends, bias = kernel(
        tail_kernel,
        "merge_tail",
        [shape(units, MAIN), shape(units, 1, dtype=F32)],
        [pltpu.VMEM((units,), F32), pltpu.SemaphoreType.DMA],
        fetched=(1, 2),
        count=3,
        moved=4 << 20,
    )(merge_weight, in_hbm(merge_bias), hidden)
    sums = shape(4, units, groups, dtype=F32)
    one, two, far = swap(hidden, 4), swap(hidden, 2), swap(hidden, 6)
    first = kernel(merge_first_kernel, "merge_first", sums, count=5, flops=1, moved=1)(
        hidden, one, two, merge_weight, ends
    )
    near = [swap(after(hidden, ends), 1), swap(one, 1), swap(two, 1)]
    second = kernel(merge_second_kernel, "merge_second", sums, count=6, flops=1, moved=1)(
        *near, first, merge_weight, ends
    )
    return kernel(
        merge_kernel,
        "merge",
        shape(1, units, groups),
        [pltpu.VMEM((units, groups), BF16), pltpu.SemaphoreType.DMA((2,))],
        out=pl.ANY,
        count=ROWS + 5,
        flops=4 * units * groups * MAIN,
        moved=8 << 20,
    )(hidden, one, two, *near, far, swap(after(far, first, *near), 1), second, merge_weight, ends, bias, live)


def solution(mesh):
    in_specs = (
        P("page", "row", None),
        P("page", "row", None),
        P("page", None),
        P(),
        P("row", None),
        P("row"),
        P("page", None),
    )
    out_specs = P("page", "row", None)
    local = local_eight if mesh.shape["row"] == 8 and mesh.shape["page"] == 4 else local_any
    return jax.shard_map(local, mesh=mesh, in_specs=in_specs, out_specs=out_specs, check_vma=False)
```

```python
import functools
import math

import jax
import jax.numpy as jnp
from jax import lax
from jax.experimental import pallas as pl
from jax.experimental.pallas import tpu as pltpu
from jax.sharding import PartitionSpec as P

D = 1280
HEADS = 16
HDIM = 80


def local_any(qkv_rows, residual, out_weight, norm_gain, merge_weight, merge_bias, page_grid):
    row_count = lax.axis_size("row")
    q_split = max(1, row_count // HEADS)
    head_groups = row_count // q_split
    width = D // head_groups
    heads_per = width // HDIM
    band_len = qkv_rows.shape[1]
    part_len = band_len // q_split
    local_qkv = qkv_rows[0]
    queries = local_qkv[:, :D]
    key_vals = jnp.concatenate(
        [
            local_qkv[:, D : 2 * D].reshape(band_len, head_groups, width),
            local_qkv[:, 2 * D :].reshape(band_len, head_groups, width),
        ],
        axis=2,
    )
    q_send = (
        queries.reshape(q_split, part_len, head_groups, width)
        .transpose(2, 0, 1, 3)
        .reshape(row_count, part_len, width)
    )
    kv_send = jnp.broadcast_to(
        key_vals.transpose(1, 0, 2)[:, None], (head_groups, q_split, band_len, 2 * width)
    )
    kv_send = kv_send.reshape(row_count, band_len, 2 * width)
    q_recv, kv_recv = (
        lax.all_to_all(q_send, "row", split_axis=0, concat_axis=1, tiled=True),
        lax.all_to_all(kv_send, "row", split_axis=0, concat_axis=1, tiled=True),
    )
    kv_local = kv_recv[0]
    positions = jnp.arange(row_count * band_len, dtype=jnp.int32)
    valid_len = page_grid[0, 0] * page_grid[0, 1]
    key_valid = positions < valid_len
    key_total = kv_local.shape[0]
    key_heads = kv_local[:, :width].reshape(key_total, heads_per, HDIM)
    value_heads = kv_local[:, width:].reshape(key_total, heads_per, HDIM)
    query_total = row_count * part_len
    q_block = math.gcd(query_total, 512)
    q_blocks = q_recv[0].reshape(query_total // q_block, q_block, heads_per, HDIM)
    root_dim = math.sqrt(HDIM)

    def attend(q_span):
        scores = (
            jnp.einsum("qhd,khd->hqk", q_span, key_heads, preferred_element_type=jnp.float32)
            / root_dim
        )
        scores = jnp.where(key_valid[None, None, :], scores, -1e30)
        peak = jnp.max(scores, axis=2, keepdims=True)
        weights = jnp.exp(scores - peak)
        total = jnp.sum(weights, axis=2, keepdims=True)
        mixed = (
            jnp.einsum(
                "hqk,khd->hqd",
                weights.astype(jnp.bfloat16),
                value_heads,
                preferred_element_type=jnp.float32,
            )
            / total
        )
        return mixed.transpose(1, 0, 2).reshape(q_span.shape[0], width).astype(jnp.bfloat16)

    attn_heads = lax.map(attend, q_blocks).reshape(row_count, part_len, width)
    returned = lax.all_to_all(attn_heads, "row", split_axis=0, concat_axis=0, tiled=True)
    attn = (
        returned.reshape(head_groups, q_split, part_len, width)
        .transpose(1, 2, 0, 3)
        .reshape(band_len, D)
    )
    projected = jnp.dot(
        attn,
        lax.all_gather(out_weight, "page", axis=0, tiled=True),
        preferred_element_type=jnp.float32,
    )
    hidden = residual[0].astype(jnp.float32) + projected
    normed = (
        hidden * lax.rsqrt(jnp.mean(hidden * hidden, axis=1, keepdims=True) + 1e-06) * norm_gain
    ).astype(jnp.bfloat16)
    rows_n = page_grid[0, 0]
    cols_n = page_grid[0, 1]
    group_total = band_len * row_count // 4
    slots = jnp.arange(group_total, dtype=jnp.int32)
    half_cols = cols_n // 2
    live = slots < rows_n // 2 * half_cols
    first = jnp.where(live, 2 * (slots // half_cols) * cols_n + 2 * (slots % half_cols), 0)
    corners = [first, first + 1, first + cols_n, first + cols_n + 1]
    local_units = merge_weight.shape[0]
    page_all = lax.all_gather(normed, "row", axis=0, tiled=True)
    merged_sum = jnp.zeros((local_units, group_total), jnp.float32)
    for corner in range(4):
        picked = jnp.take(page_all, corners[corner], axis=0)
        merged_sum = merged_sum + jnp.einsum(
            "md,gd->mg",
            merge_weight[:, corner * D : (corner + 1) * D],
            picked,
            preferred_element_type=jnp.float32,
        )
    merged = jax.nn.gelu(merged_sum + merge_bias[:, None], approximate=False)
    merged = jnp.where(live[None, :], merged, 0.0).astype(jnp.bfloat16)
    return merged[None]


ROWS = 8
PAGES = 4
HPAIR = 2 * HDIM
WIDE = 128
REST = HPAIR - WIDE
MAIN = ROWS * WIDE
NOTES = 16
RECEIVERS = ((0, 0), (6, 6), (7, 7), (4, 2), (2, 4), (3, 5), (5, 3), (1, 1))
SENDERS = ((0, 0), (6, 6), (7, 7), (4, 2), (2, 4), (5, 3), (3, 5), (1, 1))
OWNERS = (0, 4, 2, 1, 5, 3, 6, 7)
ROOT = math.log2(math.e) / math.sqrt(HDIM)
BF16 = jnp.bfloat16
F32 = jnp.float32


def row_index():
    return lax.axis_index("row")


def steps(pairs):
    core = row_index() % 2
    return [even + (odd - even) * core for even, odd in pairs]


def pack_tail(wide):
    groups = wide.shape[0] // 4
    return jnp.concatenate([wide[at * groups : (at + 1) * groups] for at in range(4)], axis=1)


def spread_kernel(qkv_hbm, resid_hbm, weight_hbm, grid_hbm, *rest):
    outs = rest[:ROWS]
    chip_ref, slice_ref, grid_out, qkv, resid, main, tile, held, grid, sems = rest[ROWS:]
    me = row_index()
    depth = weight_hbm.shape[0]
    chip = pl.ds(pl.multiple_of(me // 2 * 2 * WIDE, 2 * WIDE), 2 * WIDE)
    ends = pl.ds(pl.multiple_of(MAIN + me // 4 * WIDE, WIDE), WIDE)
    part = qkv.shape[0] // 4
    copies = []
    for at in range(4):
        rows = pl.ds(at * part, part)
        copies.append(pltpu.make_async_copy(qkv_hbm.at[0, rows], qkv.at[rows], sems.at[at]))
    copies.append(pltpu.make_async_copy(resid_hbm.at[0], resid, sems.at[4]))
    copies.append(pltpu.make_async_copy(weight_hbm.at[:, chip], main, sems.at[5]))
    copies.append(pltpu.make_async_copy(weight_hbm.at[:, ends], tile, sems.at[6]))
    copies.append(pltpu.make_async_copy(grid_hbm, grid, sems.at[7]))
    for copy in copies:
        copy.start()
    for copy in copies:
        copy.wait()
    for dest in range(ROWS):
        at = dest * HPAIR
        parts = [qkv[:, part * D + at : part * D + at + HPAIR] for part in range(3)]
        parts.append(resid[:, dest * WIDE : (dest + 1) * WIDE])
        parts.append(resid[:, MAIN + dest * REST : MAIN + (dest + 1) * REST])
        held[dest] = jnp.concatenate(parts, axis=1)
    for step, out in zip(steps(RECEIVERS), outs):
        out[...] = held[me ^ step]
    low = me // 2 % 2 == 0
    size = depth + depth // 4
    for core in range(2):
        tail = jnp.where(low, tile[:, core * REST : (core + 1) * REST], tile[:, (core + 2) * REST : (core + 3) * REST])
        chip_ref[core * size : core * size + depth, :] = main[:, core * WIDE : (core + 1) * WIDE]
        chip_ref[core * size + depth : (core + 1) * size, :] = pack_tail(tail)
    slice_ref[...] = chip_ref[pl.ds(pl.multiple_of(me % 2 * size, 16), size), :]
    row = lax.broadcasted_iota(jnp.int32, grid_out.shape, 0)
    grid_out[...] = jnp.where(row == 0, grid[0, 0], grid[0, 1])


def layout_kernel(grid_ref, *rest):
    select_ref, keys_ref, live_ref = rest[-3:]
    rows_n, cols_n = grid_ref[:1, :1], grid_ref[1:2, :1]
    patches = select_ref.shape[0]
    groups = patches // 4
    half = cols_n >> 1
    count = (rows_n >> 1) * half
    slots = lax.broadcasted_iota(jnp.int32, (groups, 1), 0)
    line = jnp.floor((slots.astype(F32) + 0.5) / half.astype(F32)).astype(jnp.int32)
    first = 2 * line * cols_n + 2 * (slots - line * half)
    at = lax.broadcasted_iota(jnp.int32, (groups, patches), 1)
    for corner in range(4):
        wanted = jnp.where(slots < count, first + (corner // 2) * cols_n + corner % 2, -1)
        select_ref[corner * groups : (corner + 1) * groups, :] = jnp.where(at == wanted, 1.0, 0.0).astype(BF16)
    key = lax.broadcasted_iota(jnp.int32, keys_ref.shape, 1)
    keys_ref[...] = jnp.where(key < rows_n * cols_n, 0.0, -1e30)
    slot = lax.broadcasted_iota(jnp.int32, live_ref.shape, 1)
    live_ref[...] = jnp.where(slot < count, 1.0, 0.0)


def attend_kernel(select_ref, dead_ref, *rest):
    blocks = rest[:ROWS]
    out_ref, q_all, k_all, v_all = rest[-4:]
    me = row_index()
    band = blocks[0].shape[0]
    patches = band * ROWS
    for step, block in zip(steps(SENDERS), blocks):
        at = pl.ds(pl.multiple_of((me ^ step) * band, band), band)
        q_all[at, :] = block[:, :HPAIR]
        k_all[at, :] = block[:, HPAIR : 2 * HPAIR]
        v_all[at, :] = block[:, 2 * HPAIR : 3 * HPAIR]
    queries = jnp.dot(select_ref[...], q_all[...], preferred_element_type=F32).astype(BF16)
    lane = lax.broadcasted_iota(jnp.int32, (1, HPAIR), 1)
    keys, values, dead = k_all[...], v_all[...], dead_ref[...]
    mixed = []
    for head in range(2):
        mine = (lane >= head * HDIM) & (lane < (head + 1) * HDIM)
        asked = jnp.where(mine, queries, jnp.zeros_like(queries))
        scores = lax.dot_general(asked, keys, (((1,), (1,)), ((), ())), preferred_element_type=F32) + dead
        weights = jnp.exp2((scores - jnp.max(scores, axis=1, keepdims=True)) * ROOT)
        total = jnp.sum(weights, axis=1, keepdims=True)
        mixed.append(jnp.dot(weights.astype(BF16), values, preferred_element_type=F32) * (1.0 / total))
    attn = jnp.where(lane < HDIM, mixed[0], mixed[1])
    out_ref[:patches, :] = attn[:, :WIDE].astype(BF16)
    out_ref[patches:, :] = pack_tail(attn[:, WIDE:]).astype(BF16)


def weight_rows(cut):
    depth = 2 * HPAIR
    packed = cut[depth:]
    tail = jnp.concatenate([packed[:, at * REST : (at + 1) * REST] for at in range(4)], axis=0)
    whole = jnp.concatenate([cut[:depth], tail], axis=1)
    return [whole[core * HPAIR : (core + 1) * HPAIR] for core in range(2)]


def place_rows(rows, base, main_ref, tail_ref):
    for core in range(2):
        pair = base + core
        main_ref[pl.ds(pl.multiple_of(pair * WIDE, WIDE), WIDE), :] = rows[core][:WIDE]
        for corner in range(4):
            spot = pl.multiple_of(pair * WIDE + corner * REST, REST)
            tail_ref[corner, pl.ds(spot, REST), :] = rows[core][WIDE:]


def ready_kernel(select_ref, gain_hbm, token_ref, *rest):
    del token_ref
    blocks = rest[:ROWS]
    own_ref, across_ref, near_ref = rest[ROWS : ROWS + 3]
    resid_ref, gain_out, main_ref, tail_ref, held, line, sem = rest[-7:]
    fetch = pltpu.make_async_copy(gain_hbm, line, sem)
    fetch.start()
    me = row_index()
    band = blocks[0].shape[0]
    for step, block in zip(steps(SENDERS), blocks):
        at = pl.ds(pl.multiple_of((me ^ step) * band, band), band)
        held[at, :] = block[:, 3 * HPAIR :]
    resid_ref[...] = jnp.dot(select_ref[...], held[...], preferred_element_type=F32)
    core = me % 2
    size = own_ref.shape[0]
    half = pl.ds(pl.multiple_of(core * size, 16), size)
    main_ref[...] = jnp.zeros_like(main_ref)
    tail_ref[...] = jnp.zeros_like(tail_ref)
    cuts = [(0, own_ref[...]), (2, across_ref[...]), (3 - 2 * core, near_ref[half, :])]
    place_slices(cuts, main_ref, tail_ref)
    fetch.wait()
    whole = line[...].reshape(1, D)
    gain = jnp.zeros(gain_out.shape, F32)
    for pair in range(ROWS):
        parts = [whole[:, pair * WIDE : (pair + 1) * WIDE]]
        parts.append(whole[:, MAIN + pair * REST : MAIN + (pair + 1) * REST])
        gain = jnp.where(me == pair, jnp.concatenate(parts, axis=1), gain)
    gain_out[...] = gain


def place_slices(cuts, main_ref, tail_ref):
    for step, cut in cuts:
        place_rows(weight_rows(cut), 2 * lax.rem(lax.axis_index("page") + step, PAGES), main_ref, tail_ref)


def last_kernel(swapped_ref, main_before_ref, tail_before_ref, main_ref, tail_ref):
    main_ref[...] = main_before_ref[...]
    tail_ref[...] = tail_before_ref[...]
    core = row_index() % 2
    size = swapped_ref.shape[0] // 2
    half = pl.ds(pl.multiple_of(core * size, 16), size)
    place_slices([(1 + 2 * core, swapped_ref[half, :])], main_ref, tail_ref)


def far_block():
    me = row_index()
    return pl.ds(pl.multiple_of((me // 2 ^ 3) * 2 * WIDE, 2 * WIDE), 2 * WIDE)


def collect_late(same, other):
    core = row_index() % 2
    left = jnp.where(core == 0, same[...], other[...])
    right = jnp.where(core == 0, other[...], same[...])
    return jnp.concatenate([left, right], axis=1)


def add_features(owners, pieces, weights, before_ref, out_ref):
    main_ref, tail_ref = weights
    me = row_index()
    patches = out_ref.shape[0]
    groups = patches // 4
    mains, tails = [], []
    for step in owners:
        pair = me ^ step
        columns = pl.ds(pl.multiple_of(pair * WIDE, WIDE), WIDE)
        mains.append(main_ref[columns, :])
        tails.append([tail_ref[at, columns, :] for at in range(4)])
    rows = jnp.concatenate([piece[...] for piece in pieces], axis=1)
    base = before_ref[...] + jnp.dot(rows[:patches], jnp.concatenate(mains, axis=0), preferred_element_type=F32)
    for corner in range(4):
        span = slice(corner * groups, (corner + 1) * groups)
        tail = jnp.concatenate([tail[corner] for tail in tails], axis=0)
        out_ref[span, :] = base[span] + jnp.dot(rows[patches:], tail, preferred_element_type=F32)


def project_first_kernel(*rest):
    add_features(OWNERS[:3], rest[:3], rest[3:5], *rest[5:])


def project_second_kernel(*rest):
    add_features(OWNERS[3:6], rest[:3], rest[3:5], *rest[5:])


def project_kernel(*rest):
    same, other, base_ref, main_ref, tail_ref, gain_ref, out_ref = rest
    patches = base_ref.shape[0]
    groups = patches // 4
    block = far_block()
    full = collect_late(same, other)
    base = base_ref[...] + jnp.dot(full[:patches], main_ref[block, :], preferred_element_type=F32)
    hidden = []
    for corner in range(4):
        span = slice(corner * groups, (corner + 1) * groups)
        hidden.append(base[span] + jnp.dot(full[patches:], tail_ref[corner, block, :], preferred_element_type=F32))
    squares = jnp.concatenate([(rows * rows).astype(BF16) for rows in hidden], axis=0)
    sums = lax.dot_general(
        jnp.ones((NOTES, HPAIR), BF16), squares, (((1,), (1,)), ((), ())), preferred_element_type=F32
    )
    row = lax.broadcasted_iota(jnp.int32, (NOTES, groups), 0)
    notes = jnp.zeros((NOTES, groups), F32)
    ends = []
    for corner in range(4):
        total = sums[:, corner * groups : (corner + 1) * groups]
        coarse = total.astype(BF16).astype(F32)
        notes = jnp.where(row == corner, coarse, jnp.where(row == 4 + corner, total - coarse, notes))
        sent = hidden[corner] * gain_ref[...]
        out_ref[corner * groups : (corner + 1) * groups, :] = sent[:, :WIDE].astype(BF16)
        ends.append(sent[:, WIDE:])
    out_ref[patches : patches + groups, :] = jnp.concatenate(ends, axis=1).astype(BF16)
    out_ref[patches + groups :, :] = notes.astype(BF16)


def tail_kernel(weight_ref, bias_hbm, token_ref, out_ref, bias_out, line, sem):
    del token_ref
    fetch = pltpu.make_async_copy(bias_hbm, line, sem)
    fetch.start()
    for pair in range(ROWS):
        cut = [corner * D + MAIN + pair * REST for corner in range(4)]
        out_ref[:, pair * WIDE : (pair + 1) * WIDE] = jnp.concatenate(
            [weight_ref[:, at : at + REST] for at in cut], axis=1
        )
    fetch.wait()
    units = bias_out.shape[0]
    bias_out[...] = jnp.broadcast_to(line[...].reshape(1, units), (8, units)).T[:, :1]


def merge_product(weight_ref, corner, groups, pieces):
    me = row_index()
    spots = [pl.multiple_of(corner * D + (me ^ step) * WIDE, WIDE) for step, _ in pieces]
    span = slice(corner * groups, (corner + 1) * groups)
    return lax.dot_general(
        jnp.concatenate([weight_ref[:, pl.ds(spot, WIDE)] for spot in spots], axis=1),
        jnp.concatenate([piece[span, :] for _, piece in pieces], axis=1),
        (((1,), (1,)), ((), ())),
        preferred_element_type=F32,
    )


def tail_products(tail_ref, groups, pieces):
    me = row_index()
    columns = [tail_ref[:, pl.ds(pl.multiple_of((me ^ step) * WIDE, WIDE), WIDE)] for step, _ in pieces]
    tails = jnp.concatenate(columns, axis=1)
    ends = jnp.concatenate([piece[4 * groups : 5 * groups, :] for _, piece in pieces], axis=1)
    corner_of = lax.rem(lax.broadcasted_iota(jnp.int32, (1, ends.shape[1]), 1), WIDE) // REST
    return [
        lax.dot_general(
            tails,
            jnp.where(corner_of == corner, ends, jnp.zeros_like(ends)),
            (((1,), (1,)), ((), ())),
            preferred_element_type=F32,
        )
        for corner in range(4)
    ]


def merge_first_kernel(*rest):
    pieces, (weight_ref, tail_ref, sum_ref) = list(zip(OWNERS[:3], rest[:3])), rest[3:]
    groups = sum_ref.shape[2]
    for corner, tail in enumerate(tail_products(tail_ref, groups, pieces)):
        sum_ref[corner] = tail + merge_product(weight_ref, corner, groups, pieces)


def merge_second_kernel(*rest):
    pieces, (before_ref, weight_ref, tail_ref, sum_ref) = list(zip(OWNERS[3:6], rest[:3])), rest[3:]
    groups = sum_ref.shape[2]
    for corner, tail in enumerate(tail_products(tail_ref, groups, pieces)):
        sum_ref[corner] = before_ref[corner] + (tail + merge_product(weight_ref, corner, groups, pieces))


def merge_kernel(*rest):
    pieces = rest[:ROWS]
    before_ref, weight_ref, tail_ref, bias_ref, live_ref, out_hbm, held, sems = rest[ROWS:]
    me = row_index()
    groups = live_ref.shape[1]
    patches = 4 * groups
    contract = (((1,), (1,)), ((), ()))
    block = pl.multiple_of((me // 2 ^ 3) * 2 * WIDE, 2 * WIDE)
    rows = collect_late(pieces[6], pieces[7])
    notes = jnp.zeros((NOTES, groups), F32)
    for piece in pieces:
        notes = notes + piece[patches + groups :, :].astype(F32)
    scale = lax.rsqrt((notes[:4] + notes[4:8]) * (1.0 / D) + 1e-06)
    spread = jnp.concatenate([jnp.broadcast_to(scale[at : at + 1], (REST, groups)) for at in range(4)], axis=0).T
    ends = rows[patches : patches + groups].astype(F32) * jnp.concatenate([spread] * 2, axis=1)
    ends = ends.astype(BF16)
    half = held.shape[0] // 2
    copies = []
    for at in range(2):
        units = slice(at * half, (at + 1) * half)
        total = bias_ref[units, :] + lax.dot_general(
            tail_ref[units, pl.ds(block, 2 * WIDE)], ends, contract, preferred_element_type=F32
        )
        for corner in range(4):
            part = before_ref[corner, units] + lax.dot_general(
                weight_ref[units, pl.ds(pl.multiple_of(corner * D + block, 2 * WIDE), 2 * WIDE)],
                rows[corner * groups : (corner + 1) * groups],
                contract,
                preferred_element_type=F32,
            )
            total = total + scale[corner : corner + 1] * part
        merged = 0.5 * total * (1.0 + lax.erf(total * math.sqrt(0.5)))
        held[units, :] = jnp.where(live_ref[...] > 0.0, merged, 0.0).astype(BF16)
        copies.append(pltpu.make_async_copy(held.at[units], out_hbm.at[0, units], sems.at[at]))
        copies[at].start()
    for copy in copies:
        copy.wait()


def kernel(body, name, out_shape, scratch=(), fetched=(), count=0, limit=24, flops=0, moved=0, out=pltpu.VMEM):
    specs = [pl.BlockSpec(memory_space=pltpu.VMEM) for _ in range(count)]
    for at in fetched:
        specs[at] = pl.BlockSpec(memory_space=pl.ANY)
    return pl.pallas_call(
        body,
        out_shape=out_shape,
        in_specs=specs,
        out_specs=jax.tree.map(lambda _: pl.BlockSpec(memory_space=out), out_shape),
        scratch_shapes=list(scratch),
        compiler_params=pltpu.CompilerParams(vmem_limit_bytes=limit * 1024 * 1024),
        cost_estimate=pl.CostEstimate(flops=flops, bytes_accessed=moved, transcendentals=0),
        name=name,
    )


def in_hbm(value):
    return pltpu.with_memory_space_constraint(value, pltpu.HBM)


def shape(*dims, dtype=BF16):
    return jax.ShapeDtypeStruct(dims, dtype)


def swap(value, even, odd=None):
    odd = even if odd is None else odd
    return lax.ppermute(value, "row", [(row, row ^ (odd if row % 2 else even)) for row in range(ROWS)])


def turn(value, low, high):
    pairs = [
        (page * ROWS + row, (page + (high if row % 2 else low)) % PAGES * ROWS + row)
        for page in range(PAGES)
        for row in range(ROWS)
    ]
    return lax.ppermute(value, ("page", "row"), pairs)


def after(value, *arrays):
    return lax.optimization_barrier((value, *arrays))[0]


def local_eight(qkv_rows, residual, out_weight, norm_gain, merge_weight, merge_bias, page_grid):
    band = qkv_rows.shape[1]
    patches = band * ROWS
    groups = patches // 4
    units = merge_weight.shape[0]
    depth = out_weight.shape[0]
    piece = patches + groups
    size = depth + depth // 4

    *sends, chip, own, grid = kernel(
        spread_kernel,
        "spread",
        [shape(band, 4 * HPAIR)] * ROWS
        + [shape(2 * size, WIDE), shape(size, WIDE), shape(8, WIDE, dtype=jnp.int32)],
        [
            pltpu.VMEM((band, 3 * D), BF16),
            pltpu.VMEM((band, D), BF16),
            pltpu.VMEM((depth, 2 * WIDE), BF16),
            pltpu.VMEM((depth, WIDE), BF16),
            pltpu.VMEM((ROWS, band, 4 * HPAIR), BF16),
            pltpu.SMEM(page_grid.shape, jnp.int32),
            pltpu.SemaphoreType.DMA((8,)),
        ],
        fetched=range(4),
        count=4,
        moved=1 << 20,
    )(in_hbm(qkv_rows), in_hbm(residual), in_hbm(out_weight), in_hbm(page_grid))
    blocks = [sends[0]] + [swap(send, *pair) for send, pair in zip(sends[1:], RECEIVERS[1:])]
    select, dead, live = kernel(
        layout_kernel,
        "layout",
        [shape(patches, patches), shape(1, patches, dtype=F32), shape(1, groups, dtype=F32)],
        fetched=range(1, 1 + 2),
        count=1 + 2,
        moved=1 << 20,
    )(grid, *blocks[1:3])
    near = turn(after(chip, *()), 1, PAGES - 1)
    swapped = swap(near, 1)
    attn = kernel(
        attend_kernel,
        "attend",
        shape(piece, WIDE),
        [pltpu.VMEM((patches, HPAIR), BF16)] * 3,
        count=2 + ROWS,
        flops=20 * patches * patches * 4096,
        moved=1 << 20,
    )(select, dead, *blocks)
    across = turn(own, 2, 2)
    resid, own_gain, main, tail = kernel(
        ready_kernel,
        "ready",
        [shape(patches, HPAIR, dtype=F32), shape(1, HPAIR, dtype=F32), shape(MAIN, HPAIR), shape(4, MAIN, HPAIR)],
        [pltpu.VMEM((patches, HPAIR), BF16), pltpu.VMEM((D,), F32), pltpu.SemaphoreType.DMA],
        fetched=(1, 2),
        count=3 + ROWS + 3,
        flops=10 * patches * patches * 4096,
        moved=4 << 20,
    )(select, in_hbm(norm_gain), attn, *blocks, own, across, near)
    one, two, far = swap(attn, 4), swap(attn, 2), swap(attn, 6)
    last = kernel(
        last_kernel,
        "ready_last",
        [shape(MAIN, HPAIR), shape(4, MAIN, HPAIR)],
        count=3,
        flops=1,
        moved=1,
    )(swapped, main, tail)
    near = [swap(after(attn, main), 1), swap(after(one, last[0]), 1), swap(two, 1)]
    weights = tuple(last)
    rows = shape(patches, HPAIR, dtype=F32)
    first = kernel(project_first_kernel, "project_first", rows, count=6, flops=1, moved=1)(attn, one, two, *weights, resid)
    second = kernel(project_second_kernel, "project_second", rows, count=6, flops=1, moved=1)(*near, *weights, first)
    hidden = kernel(
        project_kernel,
        "project",
        shape(piece + NOTES, WIDE),
        count=2 + 4,
        flops=patches * MAIN * 256,
        moved=4 << 20,
    )(far, swap(after(far, first), 1), second, *weights, own_gain)
    ends, bias = kernel(
        tail_kernel,
        "merge_tail",
        [shape(units, MAIN), shape(units, 1, dtype=F32)],
        [pltpu.VMEM((units,), F32), pltpu.SemaphoreType.DMA],
        fetched=(1, 2),
        count=3,
        moved=4 << 20,
    )(merge_weight, in_hbm(merge_bias), hidden)
    sums = shape(4, units, groups, dtype=F32)
    one, two, far = swap(hidden, 4), swap(hidden, 2), swap(hidden, 6)
    first = kernel(merge_first_kernel, "merge_first", sums, count=5, flops=1, moved=1)(
        hidden, one, two, merge_weight, ends
    )
    near = [swap(after(hidden, ends), 1), swap(one, 1), swap(two, 1)]
    second = kernel(merge_second_kernel, "merge_second", sums, count=6, flops=1, moved=1)(
        *near, first, merge_weight, ends
    )
    return kernel(
        merge_kernel,
        "merge",
        shape(1, units, groups),
        [pltpu.VMEM((units, groups), BF16), pltpu.SemaphoreType.DMA((2,))],
        out=pl.ANY,
        count=ROWS + 5,
        flops=4 * units * groups * MAIN,
        moved=8 << 20,
    )(hidden, one, two, *near, far, swap(after(far, first, *near), 1), second, merge_weight, ends, bias, live)


def solution(mesh):
    in_specs = (
        P("page", "row", None),
        P("page", "row", None),
        P("page", None),
        P(),
        P("row", None),
        P("row"),
        P("page", None),
    )
    out_specs = P("page", "row", None)
    local = local_eight if mesh.shape["row"] == 8 and mesh.shape["page"] == 4 else local_any
    return jax.shard_map(local, mesh=mesh, in_specs=in_specs, out_specs=out_specs, check_vma=False)
```

```python
import functools
import math

import jax
import jax.numpy as jnp
from jax import lax
from jax.experimental import pallas as pl
from jax.experimental.pallas import tpu as pltpu
from jax.sharding import PartitionSpec as P

D = 1280
HEADS = 16
HDIM = 80


def local_any(qkv_rows, residual, out_weight, norm_gain, merge_weight, merge_bias, page_grid):
    row_count = lax.axis_size("row")
    q_split = max(1, row_count // HEADS)
    head_groups = row_count // q_split
    width = D // head_groups
    heads_per = width // HDIM
    band_len = qkv_rows.shape[1]
    part_len = band_len // q_split
    local_qkv = qkv_rows[0]
    queries = local_qkv[:, :D]
    key_vals = jnp.concatenate(
        [
            local_qkv[:, D : 2 * D].reshape(band_len, head_groups, width),
            local_qkv[:, 2 * D :].reshape(band_len, head_groups, width),
        ],
        axis=2,
    )
    q_send = (
        queries.reshape(q_split, part_len, head_groups, width)
        .transpose(2, 0, 1, 3)
        .reshape(row_count, part_len, width)
    )
    kv_send = jnp.broadcast_to(
        key_vals.transpose(1, 0, 2)[:, None], (head_groups, q_split, band_len, 2 * width)
    )
    kv_send = kv_send.reshape(row_count, band_len, 2 * width)
    q_recv, kv_recv = (
        lax.all_to_all(q_send, "row", split_axis=0, concat_axis=1, tiled=True),
        lax.all_to_all(kv_send, "row", split_axis=0, concat_axis=1, tiled=True),
    )
    kv_local = kv_recv[0]
    positions = jnp.arange(row_count * band_len, dtype=jnp.int32)
    valid_len = page_grid[0, 0] * page_grid[0, 1]
    key_valid = positions < valid_len
    key_total = kv_local.shape[0]
    key_heads = kv_local[:, :width].reshape(key_total, heads_per, HDIM)
    value_heads = kv_local[:, width:].reshape(key_total, heads_per, HDIM)
    query_total = row_count * part_len
    q_block = math.gcd(query_total, 512)
    q_blocks = q_recv[0].reshape(query_total // q_block, q_block, heads_per, HDIM)
    root_dim = math.sqrt(HDIM)

    def attend(q_span):
        scores = (
            jnp.einsum("qhd,khd->hqk", q_span, key_heads, preferred_element_type=jnp.float32)
            / root_dim
        )
        scores = jnp.where(key_valid[None, None, :], scores, -1e30)
        peak = jnp.max(scores, axis=2, keepdims=True)
        weights = jnp.exp(scores - peak)
        total = jnp.sum(weights, axis=2, keepdims=True)
        mixed = (
            jnp.einsum(
                "hqk,khd->hqd",
                weights.astype(jnp.bfloat16),
                value_heads,
                preferred_element_type=jnp.float32,
            )
            / total
        )
        return mixed.transpose(1, 0, 2).reshape(q_span.shape[0], width).astype(jnp.bfloat16)

    attn_heads = lax.map(attend, q_blocks).reshape(row_count, part_len, width)
    returned = lax.all_to_all(attn_heads, "row", split_axis=0, concat_axis=0, tiled=True)
    attn = (
        returned.reshape(head_groups, q_split, part_len, width)
        .transpose(1, 2, 0, 3)
        .reshape(band_len, D)
    )
    projected = jnp.dot(
        attn,
        lax.all_gather(out_weight, "page", axis=0, tiled=True),
        preferred_element_type=jnp.float32,
    )
    hidden = residual[0].astype(jnp.float32) + projected
    normed = (
        hidden * lax.rsqrt(jnp.mean(hidden * hidden, axis=1, keepdims=True) + 1e-06) * norm_gain
    ).astype(jnp.bfloat16)
    rows_n = page_grid[0, 0]
    cols_n = page_grid[0, 1]
    group_total = band_len * row_count // 4
    slots = jnp.arange(group_total, dtype=jnp.int32)
    half_cols = cols_n // 2
    live = slots < rows_n // 2 * half_cols
    first = jnp.where(live, 2 * (slots // half_cols) * cols_n + 2 * (slots % half_cols), 0)
    corners = [first, first + 1, first + cols_n, first + cols_n + 1]
    local_units = merge_weight.shape[0]
    page_all = lax.all_gather(normed, "row", axis=0, tiled=True)
    merged_sum = jnp.zeros((local_units, group_total), jnp.float32)
    for corner in range(4):
        picked = jnp.take(page_all, corners[corner], axis=0)
        merged_sum = merged_sum + jnp.einsum(
            "md,gd->mg",
            merge_weight[:, corner * D : (corner + 1) * D],
            picked,
            preferred_element_type=jnp.float32,
        )
    merged = jax.nn.gelu(merged_sum + merge_bias[:, None], approximate=False)
    merged = jnp.where(live[None, :], merged, 0.0).astype(jnp.bfloat16)
    return merged[None]


ROWS = 8
PAGES = 4
HPAIR = 2 * HDIM
WIDE = 128
REST = HPAIR - WIDE
MAIN = ROWS * WIDE
NOTES = 16
RECEIVERS = ((0, 0), (4, 2), (2, 4), (6, 6), (7, 7), (3, 5), (5, 3), (1, 1))
SENDERS = ((0, 0), (4, 2), (2, 4), (6, 6), (7, 7), (5, 3), (3, 5), (1, 1))
OWNERS = (0, 4, 2, 1, 5, 3, 6, 7)
ROOT = math.log2(math.e) / math.sqrt(HDIM)
BF16 = jnp.bfloat16
F32 = jnp.float32


def row_index():
    return lax.axis_index("row")


def steps(pairs):
    core = row_index() % 2
    return [even + (odd - even) * core for even, odd in pairs]


def pack_tail(wide):
    groups = wide.shape[0] // 4
    return jnp.concatenate([wide[at * groups : (at + 1) * groups] for at in range(4)], axis=1)


def spread_kernel(qkv_hbm, resid_hbm, weight_hbm, grid_hbm, *rest):
    outs = rest[:ROWS]
    chip_ref, slice_ref, grid_out, qkv, resid, main, tile, held, grid, sems = rest[ROWS:]
    me = row_index()
    depth = weight_hbm.shape[0]
    chip = pl.ds(pl.multiple_of(me // 2 * 2 * WIDE, 2 * WIDE), 2 * WIDE)
    ends = pl.ds(pl.multiple_of(MAIN + me // 4 * WIDE, WIDE), WIDE)
    part = qkv.shape[0] // 4
    copies = []
    for at in range(4):
        rows = pl.ds(at * part, part)
        copies.append(pltpu.make_async_copy(qkv_hbm.at[0, rows], qkv.at[rows], sems.at[at]))
    copies.append(pltpu.make_async_copy(resid_hbm.at[0], resid, sems.at[4]))
    copies.append(pltpu.make_async_copy(weight_hbm.at[:, chip], main, sems.at[5]))
    copies.append(pltpu.make_async_copy(weight_hbm.at[:, ends], tile, sems.at[6]))
    copies.append(pltpu.make_async_copy(grid_hbm, grid, sems.at[7]))
    for copy in copies:
        copy.start()
    for copy in copies:
        copy.wait()
    for dest in range(ROWS):
        at = dest * HPAIR
        parts = [qkv[:, part * D + at : part * D + at + HPAIR] for part in range(3)]
        parts.append(resid[:, dest * WIDE : (dest + 1) * WIDE])
        parts.append(resid[:, MAIN + dest * REST : MAIN + (dest + 1) * REST])
        held[dest] = jnp.concatenate(parts, axis=1)
    for step, out in zip(steps(RECEIVERS), outs):
        out[...] = held[me ^ step]
    low = me // 2 % 2 == 0
    size = depth + depth // 4
    for core in range(2):
        tail = jnp.where(low, tile[:, core * REST : (core + 1) * REST], tile[:, (core + 2) * REST : (core + 3) * REST])
        chip_ref[core * size : core * size + depth, :] = main[:, core * WIDE : (core + 1) * WIDE]
        chip_ref[core * size + depth : (core + 1) * size, :] = pack_tail(tail)
    slice_ref[...] = chip_ref[pl.ds(pl.multiple_of(me % 2 * size, 16), size), :]
    row = lax.broadcasted_iota(jnp.int32, grid_out.shape, 0)
    grid_out[...] = jnp.where(row == 0, grid[0, 0], grid[0, 1])


def layout_kernel(grid_ref, *rest):
    select_ref, keys_ref, live_ref = rest[-3:]
    rows_n, cols_n = grid_ref[:1, :1], grid_ref[1:2, :1]
    patches = select_ref.shape[0]
    groups = patches // 4
    half = cols_n >> 1
    count = (rows_n >> 1) * half
    slots = lax.broadcasted_iota(jnp.int32, (groups, 1), 0)
    line = jnp.floor((slots.astype(F32) + 0.5) / half.astype(F32)).astype(jnp.int32)
    first = 2 * line * cols_n + 2 * (slots - line * half)
    at = lax.broadcasted_iota(jnp.int32, (groups, patches), 1)
    for corner in range(4):
        wanted = jnp.where(slots < count, first + (corner // 2) * cols_n + corner % 2, -1)
        select_ref[corner * groups : (corner + 1) * groups, :] = jnp.where(at == wanted, 1.0, 0.0).astype(BF16)
    key = lax.broadcasted_iota(jnp.int32, keys_ref.shape, 1)
    keys_ref[...] = jnp.where(key < rows_n * cols_n, 0.0, -1e30)
    slot = lax.broadcasted_iota(jnp.int32, live_ref.shape, 1)
    live_ref[...] = jnp.where(slot < count, 1.0, 0.0)


def attend_kernel(select_ref, dead_ref, *rest):
    blocks = rest[:ROWS]
    out_ref, q_all, k_all, v_all = rest[-4:]
    me = row_index()
    band = blocks[0].shape[0]
    patches = band * ROWS
    for step, block in zip(steps(SENDERS), blocks):
        at = pl.ds(pl.multiple_of((me ^ step) * band, band), band)
        q_all[at, :] = block[:, :HPAIR]
        k_all[at, :] = block[:, HPAIR : 2 * HPAIR]
        v_all[at, :] = block[:, 2 * HPAIR : 3 * HPAIR]
    queries = jnp.dot(select_ref[...], q_all[...], preferred_element_type=F32).astype(BF16)
    lane = lax.broadcasted_iota(jnp.int32, (1, HPAIR), 1)
    keys, values, dead = k_all[...], v_all[...], dead_ref[...]
    mixed = []
    for head in range(2):
        mine = (lane >= head * HDIM) & (lane < (head + 1) * HDIM)
        asked = jnp.where(mine, queries, jnp.zeros_like(queries))
        scores = lax.dot_general(asked, keys, (((1,), (1,)), ((), ())), preferred_element_type=F32) + dead
        weights = jnp.exp2((scores - jnp.max(scores, axis=1, keepdims=True)) * ROOT)
        total = jnp.sum(weights, axis=1, keepdims=True)
        mixed.append(jnp.dot(weights.astype(BF16), values, preferred_element_type=F32) * (1.0 / total))
    attn = jnp.where(lane < HDIM, mixed[0], mixed[1])
    out_ref[:patches, :] = attn[:, :WIDE].astype(BF16)
    out_ref[patches:, :] = pack_tail(attn[:, WIDE:]).astype(BF16)


def weight_rows(cut):
    depth = 2 * HPAIR
    packed = cut[depth:]
    tail = jnp.concatenate([packed[:, at * REST : (at + 1) * REST] for at in range(4)], axis=0)
    whole = jnp.concatenate([cut[:depth], tail], axis=1)
    return [whole[core * HPAIR : (core + 1) * HPAIR] for core in range(2)]


def place_rows(rows, base, main_ref, tail_ref):
    for core in range(2):
        pair = base + core
        main_ref[pl.ds(pl.multiple_of(pair * WIDE, WIDE), WIDE), :] = rows[core][:WIDE]
        for corner in range(4):
            spot = pl.multiple_of(pair * WIDE + corner * REST, REST)
            tail_ref[corner, pl.ds(spot, REST), :] = rows[core][WIDE:]


def ready_kernel(select_ref, gain_hbm, token_ref, *rest):
    del token_ref
    blocks = rest[:ROWS]
    own_ref, across_ref, near_ref = rest[ROWS : ROWS + 3]
    resid_ref, gain_out, main_ref, tail_ref, held, line, sem = rest[-7:]
    fetch = pltpu.make_async_copy(gain_hbm, line, sem)
    fetch.start()
    me = row_index()
    band = blocks[0].shape[0]
    for step, block in zip(steps(SENDERS), blocks):
        at = pl.ds(pl.multiple_of((me ^ step) * band, band), band)
        held[at, :] = block[:, 3 * HPAIR :]
    resid_ref[...] = jnp.dot(select_ref[...], held[...], preferred_element_type=F32)
    core = me % 2
    size = own_ref.shape[0]
    half = pl.ds(pl.multiple_of(core * size, 16), size)
    main_ref[...] = jnp.zeros_like(main_ref)
    tail_ref[...] = jnp.zeros_like(tail_ref)
    cuts = [(0, own_ref[...]), (2, across_ref[...]), (3 - 2 * core, near_ref[half, :])]
    place_slices(cuts, main_ref, tail_ref)
    fetch.wait()
    whole = line[...].reshape(1, D)
    gain = jnp.zeros(gain_out.shape, F32)
    for pair in range(ROWS):
        parts = [whole[:, pair * WIDE : (pair + 1) * WIDE]]
        parts.append(whole[:, MAIN + pair * REST : MAIN + (pair + 1) * REST])
        gain = jnp.where(me == pair, jnp.concatenate(parts, axis=1), gain)
    gain_out[...] = gain


def place_slices(cuts, main_ref, tail_ref):
    for step, cut in cuts:
        place_rows(weight_rows(cut), 2 * lax.rem(lax.axis_index("page") + step, PAGES), main_ref, tail_ref)


def last_kernel(swapped_ref, main_before_ref, tail_before_ref, main_ref, tail_ref):
    main_ref[...] = main_before_ref[...]
    tail_ref[...] = tail_before_ref[...]
    core = row_index() % 2
    size = swapped_ref.shape[0] // 2
    half = pl.ds(pl.multiple_of(core * size, 16), size)
    place_slices([(1 + 2 * core, swapped_ref[half, :])], main_ref, tail_ref)


def far_block():
    me = row_index()
    return pl.ds(pl.multiple_of((me // 2 ^ 3) * 2 * WIDE, 2 * WIDE), 2 * WIDE)


def collect_late(same, other):
    core = row_index() % 2
    left = jnp.where(core == 0, same[...], other[...])
    right = jnp.where(core == 0, other[...], same[...])
    return jnp.concatenate([left, right], axis=1)


def add_features(owners, pieces, weights, before_ref, out_ref):
    main_ref, tail_ref = weights
    me = row_index()
    patches = out_ref.shape[0]
    groups = patches // 4
    mains, tails = [], []
    for step in owners:
        pair = me ^ step
        columns = pl.ds(pl.multiple_of(pair * WIDE, WIDE), WIDE)
        mains.append(main_ref[columns, :])
        tails.append([tail_ref[at, columns, :] for at in range(4)])
    rows = jnp.concatenate([piece[...] for piece in pieces], axis=1)
    base = before_ref[...] + jnp.dot(rows[:patches], jnp.concatenate(mains, axis=0), preferred_element_type=F32)
    for corner in range(4):
        span = slice(corner * groups, (corner + 1) * groups)
        tail = jnp.concatenate([tail[corner] for tail in tails], axis=0)
        out_ref[span, :] = base[span] + jnp.dot(rows[patches:], tail, preferred_element_type=F32)


def project_first_kernel(*rest):
    add_features(OWNERS[:3], rest[:3], rest[3:5], *rest[5:])


def project_second_kernel(*rest):
    add_features(OWNERS[3:6], rest[:3], rest[3:5], *rest[5:])


def project_kernel(*rest):
    same, other, base_ref, main_ref, tail_ref, gain_ref, out_ref = rest
    patches = base_ref.shape[0]
    groups = patches // 4
    block = far_block()
    full = collect_late(same, other)
    base = base_ref[...] + jnp.dot(full[:patches], main_ref[block, :], preferred_element_type=F32)
    hidden = []
    for corner in range(4):
        span = slice(corner * groups, (corner + 1) * groups)
        hidden.append(base[span] + jnp.dot(full[patches:], tail_ref[corner, block, :], preferred_element_type=F32))
    squares = jnp.concatenate([(rows * rows).astype(BF16) for rows in hidden], axis=0)
    sums = lax.dot_general(
        jnp.ones((NOTES, HPAIR), BF16), squares, (((1,), (1,)), ((), ())), preferred_element_type=F32
    )
    row = lax.broadcasted_iota(jnp.int32, (NOTES, groups), 0)
    notes = jnp.zeros((NOTES, groups), F32)
    ends = []
    for corner in range(4):
        total = sums[:, corner * groups : (corner + 1) * groups]
        coarse = total.astype(BF16).astype(F32)
        notes = jnp.where(row == corner, coarse, jnp.where(row == 4 + corner, total - coarse, notes))
        sent = hidden[corner] * gain_ref[...]
        out_ref[corner * groups : (corner + 1) * groups, :] = sent[:, :WIDE].astype(BF16)
        ends.append(sent[:, WIDE:])
    out_ref[patches : patches + groups, :] = jnp.concatenate(ends, axis=1).astype(BF16)
    out_ref[patches + groups :, :] = notes.astype(BF16)


def tail_kernel(weight_ref, bias_hbm, token_ref, out_ref, bias_out, line, sem):
    del token_ref
    fetch = pltpu.make_async_copy(bias_hbm, line, sem)
    fetch.start()
    for pair in range(ROWS):
        cut = [corner * D + MAIN + pair * REST for corner in range(4)]
        out_ref[:, pair * WIDE : (pair + 1) * WIDE] = jnp.concatenate(
            [weight_ref[:, at : at + REST] for at in cut], axis=1
        )
    fetch.wait()
    units = bias_out.shape[0]
    bias_out[...] = jnp.broadcast_to(line[...].reshape(1, units), (8, units)).T[:, :1]


def merge_product(weight_ref, corner, groups, pieces):
    me = row_index()
    spots = [pl.multiple_of(corner * D + (me ^ step) * WIDE, WIDE) for step, _ in pieces]
    span = slice(corner * groups, (corner + 1) * groups)
    return lax.dot_general(
        jnp.concatenate([weight_ref[:, pl.ds(spot, WIDE)] for spot in spots], axis=1),
        jnp.concatenate([piece[span, :] for _, piece in pieces], axis=1),
        (((1,), (1,)), ((), ())),
        preferred_element_type=F32,
    )


def tail_products(tail_ref, groups, pieces):
    me = row_index()
    columns = [tail_ref[:, pl.ds(pl.multiple_of((me ^ step) * WIDE, WIDE), WIDE)] for step, _ in pieces]
    tails = jnp.concatenate(columns, axis=1)
    ends = jnp.concatenate([piece[4 * groups : 5 * groups, :] for _, piece in pieces], axis=1)
    corner_of = lax.rem(lax.broadcasted_iota(jnp.int32, (1, ends.shape[1]), 1), WIDE) // REST
    return [
        lax.dot_general(
            tails,
            jnp.where(corner_of == corner, ends, jnp.zeros_like(ends)),
            (((1,), (1,)), ((), ())),
            preferred_element_type=F32,
        )
        for corner in range(4)
    ]


def merge_first_kernel(*rest):
    pieces, (weight_ref, tail_ref, sum_ref) = list(zip(OWNERS[:3], rest[:3])), rest[3:]
    groups = sum_ref.shape[2]
    for corner, tail in enumerate(tail_products(tail_ref, groups, pieces)):
        sum_ref[corner] = tail + merge_product(weight_ref, corner, groups, pieces)


def merge_second_kernel(*rest):
    pieces, (before_ref, weight_ref, tail_ref, sum_ref) = list(zip(OWNERS[3:6], rest[:3])), rest[3:]
    groups = sum_ref.shape[2]
    for corner, tail in enumerate(tail_products(tail_ref, groups, pieces)):
        sum_ref[corner] = before_ref[corner] + (tail + merge_product(weight_ref, corner, groups, pieces))


def merge_kernel(*rest):
    pieces = rest[:ROWS]
    before_ref, weight_ref, tail_ref, bias_ref, live_ref, out_hbm, held, sems = rest[ROWS:]
    me = row_index()
    groups = live_ref.shape[1]
    patches = 4 * groups
    contract = (((1,), (1,)), ((), ()))
    block = pl.multiple_of((me // 2 ^ 3) * 2 * WIDE, 2 * WIDE)
    rows = collect_late(pieces[6], pieces[7])
    notes = jnp.zeros((NOTES, groups), F32)
    for piece in pieces:
        notes = notes + piece[patches + groups :, :].astype(F32)
    scale = lax.rsqrt((notes[:4] + notes[4:8]) * (1.0 / D) + 1e-06)
    spread = jnp.concatenate([jnp.broadcast_to(scale[at : at + 1], (REST, groups)) for at in range(4)], axis=0).T
    ends = rows[patches : patches + groups].astype(F32) * jnp.concatenate([spread] * 2, axis=1)
    ends = ends.astype(BF16)
    half = held.shape[0] // 2
    copies = []
    for at in range(2):
        units = slice(at * half, (at + 1) * half)
        total = bias_ref[units, :] + lax.dot_general(
            tail_ref[units, pl.ds(block, 2 * WIDE)], ends, contract, preferred_element_type=F32
        )
        for corner in range(4):
            part = before_ref[corner, units] + lax.dot_general(
                weight_ref[units, pl.ds(pl.multiple_of(corner * D + block, 2 * WIDE), 2 * WIDE)],
                rows[corner * groups : (corner + 1) * groups],
                contract,
                preferred_element_type=F32,
            )
            total = total + scale[corner : corner + 1] * part
        merged = 0.5 * total * (1.0 + lax.erf(total * math.sqrt(0.5)))
        held[units, :] = jnp.where(live_ref[...] > 0.0, merged, 0.0).astype(BF16)
        copies.append(pltpu.make_async_copy(held.at[units], out_hbm.at[0, units], sems.at[at]))
        copies[at].start()
    for copy in copies:
        copy.wait()


def kernel(body, name, out_shape, scratch=(), fetched=(), count=0, limit=24, flops=0, moved=0, out=pltpu.VMEM):
    specs = [pl.BlockSpec(memory_space=pltpu.VMEM) for _ in range(count)]
    for at in fetched:
        specs[at] = pl.BlockSpec(memory_space=pl.ANY)
    return pl.pallas_call(
        body,
        out_shape=out_shape,
        in_specs=specs,
        out_specs=jax.tree.map(lambda _: pl.BlockSpec(memory_space=out), out_shape),
        scratch_shapes=list(scratch),
        compiler_params=pltpu.CompilerParams(vmem_limit_bytes=limit * 1024 * 1024),
        cost_estimate=pl.CostEstimate(flops=flops, bytes_accessed=moved, transcendentals=0),
        name=name,
    )


def in_hbm(value):
    return pltpu.with_memory_space_constraint(value, pltpu.HBM)


def shape(*dims, dtype=BF16):
    return jax.ShapeDtypeStruct(dims, dtype)


def swap(value, even, odd=None):
    odd = even if odd is None else odd
    return lax.ppermute(value, "row", [(row, row ^ (odd if row % 2 else even)) for row in range(ROWS)])


def turn(value, low, high):
    pairs = [
        (page * ROWS + row, (page + (high if row % 2 else low)) % PAGES * ROWS + row)
        for page in range(PAGES)
        for row in range(ROWS)
    ]
    return lax.ppermute(value, ("page", "row"), pairs)


def after(value, *arrays):
    return lax.optimization_barrier((value, *arrays))[0]


def local_eight(qkv_rows, residual, out_weight, norm_gain, merge_weight, merge_bias, page_grid):
    band = qkv_rows.shape[1]
    patches = band * ROWS
    groups = patches // 4
    units = merge_weight.shape[0]
    depth = out_weight.shape[0]
    piece = patches + groups
    size = depth + depth // 4

    *sends, chip, own, grid = kernel(
        spread_kernel,
        "spread",
        [shape(band, 4 * HPAIR)] * ROWS
        + [shape(2 * size, WIDE), shape(size, WIDE), shape(8, WIDE, dtype=jnp.int32)],
        [
            pltpu.VMEM((band, 3 * D), BF16),
            pltpu.VMEM((band, D), BF16),
            pltpu.VMEM((depth, 2 * WIDE), BF16),
            pltpu.VMEM((depth, WIDE), BF16),
            pltpu.VMEM((ROWS, band, 4 * HPAIR), BF16),
            pltpu.SMEM(page_grid.shape, jnp.int32),
            pltpu.SemaphoreType.DMA((8,)),
        ],
        fetched=range(4),
        count=4,
        moved=1 << 20,
    )(in_hbm(qkv_rows), in_hbm(residual), in_hbm(out_weight), in_hbm(page_grid))
    blocks = [sends[0]] + [swap(send, *pair) for send, pair in zip(sends[1:], RECEIVERS[1:])]
    select, dead, live = kernel(
        layout_kernel,
        "layout",
        [shape(patches, patches), shape(1, patches, dtype=F32), shape(1, groups, dtype=F32)],
        fetched=range(1, 1 + 2),
        count=1 + 2,
        moved=1 << 20,
    )(grid, *blocks[1:3])
    near = turn(after(chip, *()), 1, PAGES - 1)
    swapped = swap(near, 1)
    attn = kernel(
        attend_kernel,
        "attend",
        shape(piece, WIDE),
        [pltpu.VMEM((patches, HPAIR), BF16)] * 3,
        count=2 + ROWS,
        flops=20 * patches * patches * 4096,
        moved=1 << 20,
    )(select, dead, *blocks)
    across = turn(own, 2, 2)
    resid, own_gain, main, tail = kernel(
        ready_kernel,
        "ready",
        [shape(patches, HPAIR, dtype=F32), shape(1, HPAIR, dtype=F32), shape(MAIN, HPAIR), shape(4, MAIN, HPAIR)],
        [pltpu.VMEM((patches, HPAIR), BF16), pltpu.VMEM((D,), F32), pltpu.SemaphoreType.DMA],
        fetched=(1, 2),
        count=3 + ROWS + 3,
        flops=10 * patches * patches * 4096,
        moved=4 << 20,
    )(select, in_hbm(norm_gain), attn, *blocks, own, across, near)
    one, two, far = swap(attn, 4), swap(attn, 2), swap(attn, 6)
    last = kernel(
        last_kernel,
        "ready_last",
        [shape(MAIN, HPAIR), shape(4, MAIN, HPAIR)],
        count=3,
        flops=1,
        moved=1,
    )(swapped, main, tail)
    near = [swap(after(attn, main), 1), swap(after(one, last[0]), 1), swap(two, 1)]
    weights = tuple(last)
    rows = shape(patches, HPAIR, dtype=F32)
    first = kernel(project_first_kernel, "project_first", rows, count=6, flops=1, moved=1)(attn, one, two, *weights, resid)
    second = kernel(project_second_kernel, "project_second", rows, count=6, flops=1, moved=1)(*near, *weights, first)
    hidden = kernel(
        project_kernel,
        "project",
        shape(piece + NOTES, WIDE),
        count=2 + 4,
        flops=patches * MAIN * 256,
        moved=4 << 20,
    )(far, swap(after(far, first), 1), second, *weights, own_gain)
    ends, bias = kernel(
        tail_kernel,
        "merge_tail",
        [shape(units, MAIN), shape(units, 1, dtype=F32)],
        [pltpu.VMEM((units,), F32), pltpu.SemaphoreType.DMA],
        fetched=(1, 2),
        count=3,
        moved=4 << 20,
    )(merge_weight, in_hbm(merge_bias), hidden)
    sums = shape(4, units, groups, dtype=F32)
    one, two, far = swap(hidden, 4), swap(hidden, 2), swap(hidden, 6)
    first = kernel(merge_first_kernel, "merge_first", sums, count=5, flops=1, moved=1)(
        hidden, one, two, merge_weight, ends
    )
    near = [swap(after(hidden, ends), 1), swap(one, 1), swap(two, 1)]
    second = kernel(merge_second_kernel, "merge_second", sums, count=6, flops=1, moved=1)(
        *near, first, merge_weight, ends
    )
    return kernel(
        merge_kernel,
        "merge",
        shape(1, units, groups),
        [pltpu.VMEM((units, groups), BF16), pltpu.SemaphoreType.DMA((2,))],
        out=pl.ANY,
        count=ROWS + 5,
        flops=4 * units * groups * MAIN,
        moved=8 << 20,
    )(hidden, one, two, *near, far, swap(after(far, first, *near), 1), second, merge_weight, ends, bias, live)


def solution(mesh):
    in_specs = (
        P("page", "row", None),
        P("page", "row", None),
        P("page", None),
        P(),
        P("row", None),
        P("row"),
        P("page", None),
    )
    out_specs = P("page", "row", None)
    local = local_eight if mesh.shape["row"] == 8 and mesh.shape["page"] == 4 else local_any
    return jax.shard_map(local, mesh=mesh, in_specs=in_specs, out_specs=out_specs, check_vma=False)
```

```python
import functools
import math

import jax
import jax.numpy as jnp
from jax import lax
from jax.experimental import pallas as pl
from jax.experimental.pallas import tpu as pltpu
from jax.sharding import PartitionSpec as P

D = 1280
HEADS = 16
HDIM = 80


def local_any(qkv_rows, residual, out_weight, norm_gain, merge_weight, merge_bias, page_grid):
    row_count = lax.axis_size("row")
    q_split = max(1, row_count // HEADS)
    head_groups = row_count // q_split
    width = D // head_groups
    heads_per = width // HDIM
    band_len = qkv_rows.shape[1]
    part_len = band_len // q_split
    local_qkv = qkv_rows[0]
    queries = local_qkv[:, :D]
    key_vals = jnp.concatenate(
        [
            local_qkv[:, D : 2 * D].reshape(band_len, head_groups, width),
            local_qkv[:, 2 * D :].reshape(band_len, head_groups, width),
        ],
        axis=2,
    )
    q_send = (
        queries.reshape(q_split, part_len, head_groups, width)
        .transpose(2, 0, 1, 3)
        .reshape(row_count, part_len, width)
    )
    kv_send = jnp.broadcast_to(
        key_vals.transpose(1, 0, 2)[:, None], (head_groups, q_split, band_len, 2 * width)
    )
    kv_send = kv_send.reshape(row_count, band_len, 2 * width)
    q_recv, kv_recv = (
        lax.all_to_all(q_send, "row", split_axis=0, concat_axis=1, tiled=True),
        lax.all_to_all(kv_send, "row", split_axis=0, concat_axis=1, tiled=True),
    )
    kv_local = kv_recv[0]
    positions = jnp.arange(row_count * band_len, dtype=jnp.int32)
    valid_len = page_grid[0, 0] * page_grid[0, 1]
    key_valid = positions < valid_len
    key_total = kv_local.shape[0]
    key_heads = kv_local[:, :width].reshape(key_total, heads_per, HDIM)
    value_heads = kv_local[:, width:].reshape(key_total, heads_per, HDIM)
    query_total = row_count * part_len
    q_block = math.gcd(query_total, 512)
    q_blocks = q_recv[0].reshape(query_total // q_block, q_block, heads_per, HDIM)
    root_dim = math.sqrt(HDIM)

    def attend(q_span):
        scores = (
            jnp.einsum("qhd,khd->hqk", q_span, key_heads, preferred_element_type=jnp.float32)
            / root_dim
        )
        scores = jnp.where(key_valid[None, None, :], scores, -1e30)
        peak = jnp.max(scores, axis=2, keepdims=True)
        weights = jnp.exp(scores - peak)
        total = jnp.sum(weights, axis=2, keepdims=True)
        mixed = (
            jnp.einsum(
                "hqk,khd->hqd",
                weights.astype(jnp.bfloat16),
                value_heads,
                preferred_element_type=jnp.float32,
            )
            / total
        )
        return mixed.transpose(1, 0, 2).reshape(q_span.shape[0], width).astype(jnp.bfloat16)

    attn_heads = lax.map(attend, q_blocks).reshape(row_count, part_len, width)
    returned = lax.all_to_all(attn_heads, "row", split_axis=0, concat_axis=0, tiled=True)
    attn = (
        returned.reshape(head_groups, q_split, part_len, width)
        .transpose(1, 2, 0, 3)
        .reshape(band_len, D)
    )
    projected = jnp.dot(
        attn,
        lax.all_gather(out_weight, "page", axis=0, tiled=True),
        preferred_element_type=jnp.float32,
    )
    hidden = residual[0].astype(jnp.float32) + projected
    normed = (
        hidden * lax.rsqrt(jnp.mean(hidden * hidden, axis=1, keepdims=True) + 1e-06) * norm_gain
    ).astype(jnp.bfloat16)
    rows_n = page_grid[0, 0]
    cols_n = page_grid[0, 1]
    group_total = band_len * row_count // 4
    slots = jnp.arange(group_total, dtype=jnp.int32)
    half_cols = cols_n // 2
    live = slots < rows_n // 2 * half_cols
    first = jnp.where(live, 2 * (slots // half_cols) * cols_n + 2 * (slots % half_cols), 0)
    corners = [first, first + 1, first + cols_n, first + cols_n + 1]
    local_units = merge_weight.shape[0]
    page_all = lax.all_gather(normed, "row", axis=0, tiled=True)
    merged_sum = jnp.zeros((local_units, group_total), jnp.float32)
    for corner in range(4):
        picked = jnp.take(page_all, corners[corner], axis=0)
        merged_sum = merged_sum + jnp.einsum(
            "md,gd->mg",
            merge_weight[:, corner * D : (corner + 1) * D],
            picked,
            preferred_element_type=jnp.float32,
        )
    merged = jax.nn.gelu(merged_sum + merge_bias[:, None], approximate=False)
    merged = jnp.where(live[None, :], merged, 0.0).astype(jnp.bfloat16)
    return merged[None]


ROWS = 8
PAGES = 4
HPAIR = 2 * HDIM
WIDE = 128
REST = HPAIR - WIDE
MAIN = ROWS * WIDE
NOTES = 16
RECEIVERS = ((0, 0), (4, 2), (2, 4), (6, 6), (7, 7), (3, 5), (5, 3), (1, 1))
SENDERS = ((0, 0), (4, 2), (2, 4), (6, 6), (7, 7), (5, 3), (3, 5), (1, 1))
OWNERS = (0, 4, 2, 1, 5, 3, 6, 7)
ROOT = math.log2(math.e) / math.sqrt(HDIM)
BF16 = jnp.bfloat16
F32 = jnp.float32


def row_index():
    return lax.axis_index("row")


def steps(pairs):
    core = row_index() % 2
    return [even + (odd - even) * core for even, odd in pairs]


def pack_tail(wide):
    groups = wide.shape[0] // 4
    return jnp.concatenate([wide[at * groups : (at + 1) * groups] for at in range(4)], axis=1)


def spread_kernel(qkv_hbm, resid_hbm, weight_hbm, grid_hbm, *rest):
    outs = rest[:ROWS]
    chip_ref, slice_ref, grid_out, qkv, resid, main, tile, held, grid, sems = rest[ROWS:]
    me = row_index()
    depth = weight_hbm.shape[0]
    chip = pl.ds(pl.multiple_of(me // 2 * 2 * WIDE, 2 * WIDE), 2 * WIDE)
    ends = pl.ds(pl.multiple_of(MAIN + me // 4 * WIDE, WIDE), WIDE)
    part = qkv.shape[0] // 4
    copies = []
    for at in range(4):
        rows = pl.ds(at * part, part)
        copies.append(pltpu.make_async_copy(qkv_hbm.at[0, rows], qkv.at[rows], sems.at[at]))
    copies.append(pltpu.make_async_copy(resid_hbm.at[0], resid, sems.at[4]))
    copies.append(pltpu.make_async_copy(weight_hbm.at[:, chip], main, sems.at[5]))
    copies.append(pltpu.make_async_copy(weight_hbm.at[:, ends], tile, sems.at[6]))
    copies.append(pltpu.make_async_copy(grid_hbm, grid, sems.at[7]))
    for copy in copies:
        copy.start()
    for copy in copies[:5]:
        copy.wait()
    for dest in range(ROWS):
        at = dest * HPAIR
        parts = [qkv[:, part * D + at : part * D + at + HPAIR] for part in range(3)]
        parts.append(resid[:, dest * WIDE : (dest + 1) * WIDE])
        parts.append(resid[:, MAIN + dest * REST : MAIN + (dest + 1) * REST])
        held[dest] = jnp.concatenate(parts, axis=1)
    for step, out in zip(steps(RECEIVERS), outs):
        out[...] = held[me ^ step]
    for copy in copies[5:]:
        copy.wait()
    low = me // 2 % 2 == 0
    size = depth + depth // 4
    for core in range(2):
        tail = jnp.where(low, tile[:, core * REST : (core + 1) * REST], tile[:, (core + 2) * REST : (core + 3) * REST])
        chip_ref[core * size : core * size + depth, :] = main[:, core * WIDE : (core + 1) * WIDE]
        chip_ref[core * size + depth : (core + 1) * size, :] = pack_tail(tail)
    slice_ref[...] = chip_ref[pl.ds(pl.multiple_of(me % 2 * size, 16), size), :]
    row = lax.broadcasted_iota(jnp.int32, grid_out.shape, 0)
    grid_out[...] = jnp.where(row == 0, grid[0, 0], grid[0, 1])


def layout_kernel(grid_ref, *rest):
    select_ref, keys_ref, live_ref = rest[-3:]
    rows_n, cols_n = grid_ref[:1, :1], grid_ref[1:2, :1]
    patches = select_ref.shape[0]
    groups = patches // 4
    half = cols_n >> 1
    count = (rows_n >> 1) * half
    slots = lax.broadcasted_iota(jnp.int32, (groups, 1), 0)
    line = jnp.floor((slots.astype(F32) + 0.5) / half.astype(F32)).astype(jnp.int32)
    first = 2 * line * cols_n + 2 * (slots - line * half)
    at = lax.broadcasted_iota(jnp.int32, (groups, patches), 1)
    for corner in range(4):
        wanted = jnp.where(slots < count, first + (corner // 2) * cols_n + corner % 2, -1)
        select_ref[corner * groups : (corner + 1) * groups, :] = jnp.where(at == wanted, 1.0, 0.0).astype(BF16)
    key = lax.broadcasted_iota(jnp.int32, keys_ref.shape, 1)
    keys_ref[...] = jnp.where(key < rows_n * cols_n, 0.0, -1e30)
    slot = lax.broadcasted_iota(jnp.int32, live_ref.shape, 1)
    live_ref[...] = jnp.where(slot < count, 1.0, 0.0)


def attend_kernel(select_ref, dead_ref, *rest):
    blocks = rest[:ROWS]
    out_ref, q_all, k_all, v_all = rest[-4:]
    me = row_index()
    band = blocks[0].shape[0]
    patches = band * ROWS
    for step, block in zip(steps(SENDERS), blocks):
        at = pl.ds(pl.multiple_of((me ^ step) * band, band), band)
        q_all[at, :] = block[:, :HPAIR]
        k_all[at, :] = block[:, HPAIR : 2 * HPAIR]
        v_all[at, :] = block[:, 2 * HPAIR : 3 * HPAIR]
    queries = jnp.dot(select_ref[...], q_all[...], preferred_element_type=F32).astype(BF16)
    lane = lax.broadcasted_iota(jnp.int32, (1, HPAIR), 1)
    keys, values, dead = k_all[...], v_all[...], dead_ref[...]
    mixed = []
    for head in range(2):
        mine = (lane >= head * HDIM) & (lane < (head + 1) * HDIM)
        asked = jnp.where(mine, queries, jnp.zeros_like(queries))
        scores = lax.dot_general(asked, keys, (((1,), (1,)), ((), ())), preferred_element_type=F32) + dead
        weights = jnp.exp2((scores - jnp.max(scores, axis=1, keepdims=True)) * ROOT)
        total = jnp.sum(weights, axis=1, keepdims=True)
        mixed.append(jnp.dot(weights.astype(BF16), values, preferred_element_type=F32) * (1.0 / total))
    attn = jnp.where(lane < HDIM, mixed[0], mixed[1])
    out_ref[:patches, :] = attn[:, :WIDE].astype(BF16)
    out_ref[patches:, :] = pack_tail(attn[:, WIDE:]).astype(BF16)


def weight_rows(cut):
    depth = 2 * HPAIR
    packed = cut[depth:]
    tail = jnp.concatenate([packed[:, at * REST : (at + 1) * REST] for at in range(4)], axis=0)
    whole = jnp.concatenate([cut[:depth], tail], axis=1)
    return [whole[core * HPAIR : (core + 1) * HPAIR] for core in range(2)]


def place_rows(rows, base, main_ref, tail_ref):
    for core in range(2):
        pair = base + core
        main_ref[pl.ds(pl.multiple_of(pair * WIDE, WIDE), WIDE), :] = rows[core][:WIDE]
        for corner in range(4):
            spot = pl.multiple_of(pair * WIDE + corner * REST, REST)
            tail_ref[corner, pl.ds(spot, REST), :] = rows[core][WIDE:]


def ready_kernel(select_ref, gain_hbm, token_ref, *rest):
    del token_ref
    blocks = rest[:ROWS]
    own_ref, across_ref, near_ref = rest[ROWS : ROWS + 3]
    resid_ref, gain_out, main_ref, tail_ref, held, line, sem = rest[-7:]
    fetch = pltpu.make_async_copy(gain_hbm, line, sem)
    fetch.start()
    me = row_index()
    band = blocks[0].shape[0]
    for step, block in zip(steps(SENDERS), blocks):
        at = pl.ds(pl.multiple_of((me ^ step) * band, band), band)
        held[at, :] = block[:, 3 * HPAIR :]
    resid_ref[...] = jnp.dot(select_ref[...], held[...], preferred_element_type=F32)
    core = me % 2
    size = own_ref.shape[0]
    half = pl.ds(pl.multiple_of(core * size, 16), size)
    main_ref[...] = jnp.zeros_like(main_ref)
    tail_ref[...] = jnp.zeros_like(tail_ref)
    cuts = [(0, own_ref[...]), (2, across_ref[...]), (3 - 2 * core, near_ref[half, :])]
    place_slices(cuts, main_ref, tail_ref)
    fetch.wait()
    whole = line[...].reshape(1, D)
    gain = jnp.zeros(gain_out.shape, F32)
    for pair in range(ROWS):
        parts = [whole[:, pair * WIDE : (pair + 1) * WIDE]]
        parts.append(whole[:, MAIN + pair * REST : MAIN + (pair + 1) * REST])
        gain = jnp.where(me == pair, jnp.concatenate(parts, axis=1), gain)
    gain_out[...] = gain


def place_slices(cuts, main_ref, tail_ref):
    for step, cut in cuts:
        place_rows(weight_rows(cut), 2 * lax.rem(lax.axis_index("page") + step, PAGES), main_ref, tail_ref)


def last_kernel(swapped_ref, main_before_ref, tail_before_ref, main_ref, tail_ref):
    main_ref[...] = main_before_ref[...]
    tail_ref[...] = tail_before_ref[...]
    core = row_index() % 2
    size = swapped_ref.shape[0] // 2
    half = pl.ds(pl.multiple_of(core * size, 16), size)
    place_slices([(1 + 2 * core, swapped_ref[half, :])], main_ref, tail_ref)


def far_block():
    me = row_index()
    return pl.ds(pl.multiple_of((me // 2 ^ 3) * 2 * WIDE, 2 * WIDE), 2 * WIDE)


def collect_late(same, other):
    core = row_index() % 2
    left = jnp.where(core == 0, same[...], other[...])
    right = jnp.where(core == 0, other[...], same[...])
    return jnp.concatenate([left, right], axis=1)


def add_features(owners, pieces, weights, before_ref, out_ref):
    main_ref, tail_ref = weights
    me = row_index()
    patches = out_ref.shape[0]
    groups = patches // 4
    mains, tails = [], []
    for step in owners:
        pair = me ^ step
        columns = pl.ds(pl.multiple_of(pair * WIDE, WIDE), WIDE)
        mains.append(main_ref[columns, :])
        tails.append([tail_ref[at, columns, :] for at in range(4)])
    rows = jnp.concatenate([piece[...] for piece in pieces], axis=1)
    base = before_ref[...] + jnp.dot(rows[:patches], jnp.concatenate(mains, axis=0), preferred_element_type=F32)
    for corner in range(4):
        span = slice(corner * groups, (corner + 1) * groups)
        tail = jnp.concatenate([tail[corner] for tail in tails], axis=0)
        out_ref[span, :] = base[span] + jnp.dot(rows[patches:], tail, preferred_element_type=F32)


def project_first_kernel(*rest):
    add_features(OWNERS[:3], rest[:3], rest[3:5], *rest[5:])


def project_second_kernel(*rest):
    add_features(OWNERS[3:6], rest[:3], rest[3:5], *rest[5:])


def project_kernel(*rest):
    same, other, base_ref, main_ref, tail_ref, gain_ref, out_ref = rest
    patches = base_ref.shape[0]
    groups = patches // 4
    block = far_block()
    full = collect_late(same, other)
    base = base_ref[...] + jnp.dot(full[:patches], main_ref[block, :], preferred_element_type=F32)
    hidden = []
    for corner in range(4):
        span = slice(corner * groups, (corner + 1) * groups)
        hidden.append(base[span] + jnp.dot(full[patches:], tail_ref[corner, block, :], preferred_element_type=F32))
    squares = jnp.concatenate([(rows * rows).astype(BF16) for rows in hidden], axis=0)
    sums = lax.dot_general(
        jnp.ones((NOTES, HPAIR), BF16), squares, (((1,), (1,)), ((), ())), preferred_element_type=F32
    )
    row = lax.broadcasted_iota(jnp.int32, (NOTES, groups), 0)
    notes = jnp.zeros((NOTES, groups), F32)
    ends = []
    for corner in range(4):
        total = sums[:, corner * groups : (corner + 1) * groups]
        coarse = total.astype(BF16).astype(F32)
        notes = jnp.where(row == corner, coarse, jnp.where(row == 4 + corner, total - coarse, notes))
        sent = hidden[corner] * gain_ref[...]
        out_ref[corner * groups : (corner + 1) * groups, :] = sent[:, :WIDE].astype(BF16)
        ends.append(sent[:, WIDE:])
    out_ref[patches : patches + groups, :] = jnp.concatenate(ends, axis=1).astype(BF16)
    out_ref[patches + groups :, :] = notes.astype(BF16)


def tail_kernel(weight_ref, bias_hbm, token_ref, out_ref, bias_out, line, sem):
    del token_ref
    fetch = pltpu.make_async_copy(bias_hbm, line, sem)
    fetch.start()
    for pair in range(ROWS):
        cut = [corner * D + MAIN + pair * REST for corner in range(4)]
        out_ref[:, pair * WIDE : (pair + 1) * WIDE] = jnp.concatenate(
            [weight_ref[:, at : at + REST] for at in cut], axis=1
        )
    fetch.wait()
    units = bias_out.shape[0]
    bias_out[...] = jnp.broadcast_to(line[...].reshape(1, units), (8, units)).T[:, :1]


def merge_product(weight_ref, corner, groups, pieces):
    me = row_index()
    spots = [pl.multiple_of(corner * D + (me ^ step) * WIDE, WIDE) for step, _ in pieces]
    span = slice(corner * groups, (corner + 1) * groups)
    return lax.dot_general(
        jnp.concatenate([weight_ref[:, pl.ds(spot, WIDE)] for spot in spots], axis=1),
        jnp.concatenate([piece[span, :] for _, piece in pieces], axis=1),
        (((1,), (1,)), ((), ())),
        preferred_element_type=F32,
    )


def tail_products(tail_ref, groups, pieces):
    me = row_index()
    columns = [tail_ref[:, pl.ds(pl.multiple_of((me ^ step) * WIDE, WIDE), WIDE)] for step, _ in pieces]
    tails = jnp.concatenate(columns, axis=1)
    ends = jnp.concatenate([piece[4 * groups : 5 * groups, :] for _, piece in pieces], axis=1)
    corner_of = lax.rem(lax.broadcasted_iota(jnp.int32, (1, ends.shape[1]), 1), WIDE) // REST
    return [
        lax.dot_general(
            tails,
            jnp.where(corner_of == corner, ends, jnp.zeros_like(ends)),
            (((1,), (1,)), ((), ())),
            preferred_element_type=F32,
        )
        for corner in range(4)
    ]


def merge_first_kernel(*rest):
    pieces, (weight_ref, tail_ref, sum_ref) = list(zip(OWNERS[:3], rest[:3])), rest[3:]
    groups = sum_ref.shape[2]
    for corner, tail in enumerate(tail_products(tail_ref, groups, pieces)):
        sum_ref[corner] = tail + merge_product(weight_ref, corner, groups, pieces)


def merge_second_kernel(*rest):
    pieces, (before_ref, weight_ref, tail_ref, sum_ref) = list(zip(OWNERS[3:6], rest[:3])), rest[3:]
    groups = sum_ref.shape[2]
    for corner, tail in enumerate(tail_products(tail_ref, groups, pieces)):
        sum_ref[corner] = before_ref[corner] + (tail + merge_product(weight_ref, corner, groups, pieces))


def merge_kernel(*rest):
    pieces = rest[:ROWS]
    before_ref, weight_ref, tail_ref, bias_ref, live_ref, out_hbm, held, sems = rest[ROWS:]
    me = row_index()
    groups = live_ref.shape[1]
    patches = 4 * groups
    contract = (((1,), (1,)), ((), ()))
    block = pl.multiple_of((me // 2 ^ 3) * 2 * WIDE, 2 * WIDE)
    rows = collect_late(pieces[6], pieces[7])
    notes = jnp.zeros((NOTES, groups), F32)
    for piece in pieces:
        notes = notes + piece[patches + groups :, :].astype(F32)
    scale = lax.rsqrt((notes[:4] + notes[4:8]) * (1.0 / D) + 1e-06)
    spread = jnp.concatenate([jnp.broadcast_to(scale[at : at + 1], (REST, groups)) for at in range(4)], axis=0).T
    ends = rows[patches : patches + groups].astype(F32) * jnp.concatenate([spread] * 2, axis=1)
    ends = ends.astype(BF16)
    half = held.shape[0] // 2
    copies = []
    for at in range(2):
        units = slice(at * half, (at + 1) * half)
        total = bias_ref[units, :] + lax.dot_general(
            tail_ref[units, pl.ds(block, 2 * WIDE)], ends, contract, preferred_element_type=F32
        )
        for corner in range(4):
            part = before_ref[corner, units] + lax.dot_general(
                weight_ref[units, pl.ds(pl.multiple_of(corner * D + block, 2 * WIDE), 2 * WIDE)],
                rows[corner * groups : (corner + 1) * groups],
                contract,
                preferred_element_type=F32,
            )
            total = total + scale[corner : corner + 1] * part
        merged = 0.5 * total * (1.0 + lax.erf(total * math.sqrt(0.5)))
        held[units, :] = jnp.where(live_ref[...] > 0.0, merged, 0.0).astype(BF16)
        copies.append(pltpu.make_async_copy(held.at[units], out_hbm.at[0, units], sems.at[at]))
        copies[at].start()
    for copy in copies:
        copy.wait()


def kernel(body, name, out_shape, scratch=(), fetched=(), count=0, limit=24, flops=0, moved=0, out=pltpu.VMEM):
    specs = [pl.BlockSpec(memory_space=pltpu.VMEM) for _ in range(count)]
    for at in fetched:
        specs[at] = pl.BlockSpec(memory_space=pl.ANY)
    return pl.pallas_call(
        body,
        out_shape=out_shape,
        in_specs=specs,
        out_specs=jax.tree.map(lambda _: pl.BlockSpec(memory_space=out), out_shape),
        scratch_shapes=list(scratch),
        compiler_params=pltpu.CompilerParams(vmem_limit_bytes=limit * 1024 * 1024),
        cost_estimate=pl.CostEstimate(flops=flops, bytes_accessed=moved, transcendentals=0),
        name=name,
    )


def in_hbm(value):
    return pltpu.with_memory_space_constraint(value, pltpu.HBM)


def shape(*dims, dtype=BF16):
    return jax.ShapeDtypeStruct(dims, dtype)


def swap(value, even, odd=None):
    odd = even if odd is None else odd
    return lax.ppermute(value, "row", [(row, row ^ (odd if row % 2 else even)) for row in range(ROWS)])


def turn(value, low, high):
    pairs = [
        (page * ROWS + row, (page + (high if row % 2 else low)) % PAGES * ROWS + row)
        for page in range(PAGES)
        for row in range(ROWS)
    ]
    return lax.ppermute(value, ("page", "row"), pairs)


def after(value, *arrays):
    return lax.optimization_barrier((value, *arrays))[0]


def local_eight(qkv_rows, residual, out_weight, norm_gain, merge_weight, merge_bias, page_grid):
    band = qkv_rows.shape[1]
    patches = band * ROWS
    groups = patches // 4
    units = merge_weight.shape[0]
    depth = out_weight.shape[0]
    piece = patches + groups
    size = depth + depth // 4

    *sends, chip, own, grid = kernel(
        spread_kernel,
        "spread",
        [shape(band, 4 * HPAIR)] * ROWS
        + [shape(2 * size, WIDE), shape(size, WIDE), shape(8, WIDE, dtype=jnp.int32)],
        [
            pltpu.VMEM((band, 3 * D), BF16),
            pltpu.VMEM((band, D), BF16),
            pltpu.VMEM((depth, 2 * WIDE), BF16),
            pltpu.VMEM((depth, WIDE), BF16),
            pltpu.VMEM((ROWS, band, 4 * HPAIR), BF16),
            pltpu.SMEM(page_grid.shape, jnp.int32),
            pltpu.SemaphoreType.DMA((8,)),
        ],
        fetched=range(4),
        count=4,
        moved=1 << 20,
    )(in_hbm(qkv_rows), in_hbm(residual), in_hbm(out_weight), in_hbm(page_grid))
    blocks = [sends[0]] + [swap(send, *pair) for send, pair in zip(sends[1:], RECEIVERS[1:])]
    select, dead, live = kernel(
        layout_kernel,
        "layout",
        [shape(patches, patches), shape(1, patches, dtype=F32), shape(1, groups, dtype=F32)],
        fetched=range(1, 1 + 2),
        count=1 + 2,
        moved=1 << 20,
    )(grid, *blocks[1:3])
    near = turn(after(chip, *()), 1, PAGES - 1)
    swapped = swap(near, 1)
    attn = kernel(
        attend_kernel,
        "attend",
        shape(piece, WIDE),
        [pltpu.VMEM((patches, HPAIR), BF16)] * 3,
        count=2 + ROWS,
        flops=20 * patches * patches * 4096,
        moved=1 << 20,
    )(select, dead, *blocks)
    across = turn(own, 2, 2)
    resid, own_gain, main, tail = kernel(
        ready_kernel,
        "ready",
        [shape(patches, HPAIR, dtype=F32), shape(1, HPAIR, dtype=F32), shape(MAIN, HPAIR), shape(4, MAIN, HPAIR)],
        [pltpu.VMEM((patches, HPAIR), BF16), pltpu.VMEM((D,), F32), pltpu.SemaphoreType.DMA],
        fetched=(1, 2),
        count=3 + ROWS + 3,
        flops=10 * patches * patches * 4096,
        moved=4 << 20,
    )(select, in_hbm(norm_gain), attn, *blocks, own, across, near)
    one, two, far = swap(attn, 4), swap(attn, 2), swap(attn, 6)
    last = kernel(
        last_kernel,
        "ready_last",
        [shape(MAIN, HPAIR), shape(4, MAIN, HPAIR)],
        count=3,
        flops=1,
        moved=1,
    )(swapped, main, tail)
    near = [swap(after(attn, main), 1), swap(after(one, last[0]), 1), swap(two, 1)]
    weights = tuple(last)
    rows = shape(patches, HPAIR, dtype=F32)
    first = kernel(project_first_kernel, "project_first", rows, count=6, flops=1, moved=1)(attn, one, two, *weights, resid)
    second = kernel(project_second_kernel, "project_second", rows, count=6, flops=1, moved=1)(*near, *weights, first)
    hidden = kernel(
        project_kernel,
        "project",
        shape(piece + NOTES, WIDE),
        count=2 + 4,
        flops=patches * MAIN * 256,
        moved=4 << 20,
    )(far, swap(after(far, first), 1), second, *weights, own_gain)
    ends, bias = kernel(
        tail_kernel,
        "merge_tail",
        [shape(units, MAIN), shape(units, 1, dtype=F32)],
        [pltpu.VMEM((units,), F32), pltpu.SemaphoreType.DMA],
        fetched=(1, 2),
        count=3,
        moved=4 << 20,
    )(merge_weight, in_hbm(merge_bias), hidden)
    sums = shape(4, units, groups, dtype=F32)
    one, two, far = swap(hidden, 4), swap(hidden, 2), swap(hidden, 6)
    first = kernel(merge_first_kernel, "merge_first", sums, count=5, flops=1, moved=1)(
        hidden, one, two, merge_weight, ends
    )
    near = [swap(after(hidden, ends), 1), swap(one, 1), swap(two, 1)]
    second = kernel(merge_second_kernel, "merge_second", sums, count=6, flops=1, moved=1)(
        *near, first, merge_weight, ends
    )
    return kernel(
        merge_kernel,
        "merge",
        shape(1, units, groups),
        [pltpu.VMEM((units, groups), BF16), pltpu.SemaphoreType.DMA((2,))],
        out=pl.ANY,
        count=ROWS + 5,
        flops=4 * units * groups * MAIN,
        moved=8 << 20,
    )(hidden, one, two, *near, far, swap(after(far, first, *near), 1), second, merge_weight, ends, bias, live)


def solution(mesh):
    in_specs = (
        P("page", "row", None),
        P("page", "row", None),
        P("page", None),
        P(),
        P("row", None),
        P("row"),
        P("page", None),
    )
    out_specs = P("page", "row", None)
    local = local_eight if mesh.shape["row"] == 8 and mesh.shape["page"] == 4 else local_any
    return jax.shard_map(local, mesh=mesh, in_specs=in_specs, out_specs=out_specs, check_vma=False)
```

```python
import functools
import math

import jax
import jax.numpy as jnp
from jax import lax
from jax.experimental import pallas as pl
from jax.experimental.pallas import tpu as pltpu
from jax.sharding import PartitionSpec as P

D = 1280
HEADS = 16
HDIM = 80


def local_any(qkv_rows, residual, out_weight, norm_gain, merge_weight, merge_bias, page_grid):
    row_count = lax.axis_size("row")
    q_split = max(1, row_count // HEADS)
    head_groups = row_count // q_split
    width = D // head_groups
    heads_per = width // HDIM
    band_len = qkv_rows.shape[1]
    part_len = band_len // q_split
    local_qkv = qkv_rows[0]
    queries = local_qkv[:, :D]
    key_vals = jnp.concatenate(
        [
            local_qkv[:, D : 2 * D].reshape(band_len, head_groups, width),
            local_qkv[:, 2 * D :].reshape(band_len, head_groups, width),
        ],
        axis=2,
    )
    q_send = (
        queries.reshape(q_split, part_len, head_groups, width)
        .transpose(2, 0, 1, 3)
        .reshape(row_count, part_len, width)
    )
    kv_send = jnp.broadcast_to(
        key_vals.transpose(1, 0, 2)[:, None], (head_groups, q_split, band_len, 2 * width)
    )
    kv_send = kv_send.reshape(row_count, band_len, 2 * width)
    q_recv, kv_recv = (
        lax.all_to_all(q_send, "row", split_axis=0, concat_axis=1, tiled=True),
        lax.all_to_all(kv_send, "row", split_axis=0, concat_axis=1, tiled=True),
    )
    kv_local = kv_recv[0]
    positions = jnp.arange(row_count * band_len, dtype=jnp.int32)
    valid_len = page_grid[0, 0] * page_grid[0, 1]
    key_valid = positions < valid_len
    key_total = kv_local.shape[0]
    key_heads = kv_local[:, :width].reshape(key_total, heads_per, HDIM)
    value_heads = kv_local[:, width:].reshape(key_total, heads_per, HDIM)
    query_total = row_count * part_len
    q_block = math.gcd(query_total, 512)
    q_blocks = q_recv[0].reshape(query_total // q_block, q_block, heads_per, HDIM)
    root_dim = math.sqrt(HDIM)

    def attend(q_span):
        scores = (
            jnp.einsum("qhd,khd->hqk", q_span, key_heads, preferred_element_type=jnp.float32)
            / root_dim
        )
        scores = jnp.where(key_valid[None, None, :], scores, -1e30)
        peak = jnp.max(scores, axis=2, keepdims=True)
        weights = jnp.exp(scores - peak)
        total = jnp.sum(weights, axis=2, keepdims=True)
        mixed = (
            jnp.einsum(
                "hqk,khd->hqd",
                weights.astype(jnp.bfloat16),
                value_heads,
                preferred_element_type=jnp.float32,
            )
            / total
        )
        return mixed.transpose(1, 0, 2).reshape(q_span.shape[0], width).astype(jnp.bfloat16)

    attn_heads = lax.map(attend, q_blocks).reshape(row_count, part_len, width)
    returned = lax.all_to_all(attn_heads, "row", split_axis=0, concat_axis=0, tiled=True)
    attn = (
        returned.reshape(head_groups, q_split, part_len, width)
        .transpose(1, 2, 0, 3)
        .reshape(band_len, D)
    )
    projected = jnp.dot(
        attn,
        lax.all_gather(out_weight, "page", axis=0, tiled=True),
        preferred_element_type=jnp.float32,
    )
    hidden = residual[0].astype(jnp.float32) + projected
    normed = (
        hidden * lax.rsqrt(jnp.mean(hidden * hidden, axis=1, keepdims=True) + 1e-06) * norm_gain
    ).astype(jnp.bfloat16)
    rows_n = page_grid[0, 0]
    cols_n = page_grid[0, 1]
    group_total = band_len * row_count // 4
    slots = jnp.arange(group_total, dtype=jnp.int32)
    half_cols = cols_n // 2
    live = slots < rows_n // 2 * half_cols
    first = jnp.where(live, 2 * (slots // half_cols) * cols_n + 2 * (slots % half_cols), 0)
    corners = [first, first + 1, first + cols_n, first + cols_n + 1]
    local_units = merge_weight.shape[0]
    page_all = lax.all_gather(normed, "row", axis=0, tiled=True)
    merged_sum = jnp.zeros((local_units, group_total), jnp.float32)
    for corner in range(4):
        picked = jnp.take(page_all, corners[corner], axis=0)
        merged_sum = merged_sum + jnp.einsum(
            "md,gd->mg",
            merge_weight[:, corner * D : (corner + 1) * D],
            picked,
            preferred_element_type=jnp.float32,
        )
    merged = jax.nn.gelu(merged_sum + merge_bias[:, None], approximate=False)
    merged = jnp.where(live[None, :], merged, 0.0).astype(jnp.bfloat16)
    return merged[None]


ROWS = 8
PAGES = 4
HPAIR = 2 * HDIM
WIDE = 128
REST = HPAIR - WIDE
MAIN = ROWS * WIDE
NOTES = 16
RECEIVERS = ((0, 0), (4, 2), (1, 1), (2, 4), (6, 6), (7, 7), (3, 5), (5, 3))
SENDERS = ((0, 0), (4, 2), (1, 1), (2, 4), (6, 6), (7, 7), (5, 3), (3, 5))
OWNERS = (0, 4, 2, 1, 5, 3, 6, 7)
ROOT = math.log2(math.e) / math.sqrt(HDIM)
BF16 = jnp.bfloat16
F32 = jnp.float32


def row_index():
    return lax.axis_index("row")


def steps(pairs):
    core = row_index() % 2
    return [even + (odd - even) * core for even, odd in pairs]


def pack_tail(wide):
    groups = wide.shape[0] // 4
    return jnp.concatenate([wide[at * groups : (at + 1) * groups] for at in range(4)], axis=1)


def spread_kernel(qkv_hbm, resid_hbm, weight_hbm, grid_hbm, *rest):
    outs = rest[:ROWS]
    chip_ref, slice_ref, grid_out, qkv, resid, main, tile, held, grid, sems = rest[ROWS:]
    me = row_index()
    depth = weight_hbm.shape[0]
    chip = pl.ds(pl.multiple_of(me // 2 * 2 * WIDE, 2 * WIDE), 2 * WIDE)
    ends = pl.ds(pl.multiple_of(MAIN + me // 4 * WIDE, WIDE), WIDE)
    part = qkv.shape[0] // 4
    copies = []
    for at in range(4):
        rows = pl.ds(at * part, part)
        copies.append(pltpu.make_async_copy(qkv_hbm.at[0, rows], qkv.at[rows], sems.at[at]))
    copies.append(pltpu.make_async_copy(resid_hbm.at[0], resid, sems.at[4]))
    copies.append(pltpu.make_async_copy(weight_hbm.at[:, chip], main, sems.at[5]))
    copies.append(pltpu.make_async_copy(weight_hbm.at[:, ends], tile, sems.at[6]))
    copies.append(pltpu.make_async_copy(grid_hbm, grid, sems.at[7]))
    for copy in copies:
        copy.start()
    for copy in copies:
        copy.wait()
    for dest in range(ROWS):
        at = dest * HPAIR
        parts = [qkv[:, part * D + at : part * D + at + HPAIR] for part in range(3)]
        parts.append(resid[:, dest * WIDE : (dest + 1) * WIDE])
        parts.append(resid[:, MAIN + dest * REST : MAIN + (dest + 1) * REST])
        held[dest] = jnp.concatenate(parts, axis=1)
    for step, out in zip(steps(RECEIVERS), outs):
        out[...] = held[me ^ step]
    low = me // 2 % 2 == 0
    size = depth + depth // 4
    for core in range(2):
        tail = jnp.where(low, tile[:, core * REST : (core + 1) * REST], tile[:, (core + 2) * REST : (core + 3) * REST])
        chip_ref[core * size : core * size + depth, :] = main[:, core * WIDE : (core + 1) * WIDE]
        chip_ref[core * size + depth : (core + 1) * size, :] = pack_tail(tail)
    slice_ref[...] = chip_ref[pl.ds(pl.multiple_of(me % 2 * size, 16), size), :]
    row = lax.broadcasted_iota(jnp.int32, grid_out.shape, 0)
    grid_out[...] = jnp.where(row == 0, grid[0, 0], grid[0, 1])


def layout_kernel(grid_ref, *rest):
    select_ref, keys_ref, live_ref = rest[-3:]
    rows_n, cols_n = grid_ref[:1, :1], grid_ref[1:2, :1]
    patches = select_ref.shape[0]
    groups = patches // 4
    half = cols_n >> 1
    count = (rows_n >> 1) * half
    slots = lax.broadcasted_iota(jnp.int32, (groups, 1), 0)
    line = jnp.floor((slots.astype(F32) + 0.5) / half.astype(F32)).astype(jnp.int32)
    first = 2 * line * cols_n + 2 * (slots - line * half)
    at = lax.broadcasted_iota(jnp.int32, (groups, patches), 1)
    for corner in range(4):
        wanted = jnp.where(slots < count, first + (corner // 2) * cols_n + corner % 2, -1)
        select_ref[corner * groups : (corner + 1) * groups, :] = jnp.where(at == wanted, 1.0, 0.0).astype(BF16)
    key = lax.broadcasted_iota(jnp.int32, keys_ref.shape, 1)
    keys_ref[...] = jnp.where(key < rows_n * cols_n, 0.0, -1e30)
    slot = lax.broadcasted_iota(jnp.int32, live_ref.shape, 1)
    live_ref[...] = jnp.where(slot < count, 1.0, 0.0)


def attend_kernel(select_ref, dead_ref, *rest):
    blocks = rest[:ROWS]
    out_ref, q_all, k_all, v_all = rest[-4:]
    me = row_index()
    band = blocks[0].shape[0]
    patches = band * ROWS
    for step, block in zip(steps(SENDERS), blocks):
        at = pl.ds(pl.multiple_of((me ^ step) * band, band), band)
        q_all[at, :] = block[:, :HPAIR]
        k_all[at, :] = block[:, HPAIR : 2 * HPAIR]
        v_all[at, :] = block[:, 2 * HPAIR : 3 * HPAIR]
    queries = jnp.dot(select_ref[...], q_all[...], preferred_element_type=F32).astype(BF16)
    lane = lax.broadcasted_iota(jnp.int32, (1, HPAIR), 1)
    keys, values, dead = k_all[...], v_all[...], dead_ref[...]
    mixed = []
    for head in range(2):
        mine = (lane >= head * HDIM) & (lane < (head + 1) * HDIM)
        asked = jnp.where(mine, queries, jnp.zeros_like(queries))
        scores = lax.dot_general(asked, keys, (((1,), (1,)), ((), ())), preferred_element_type=F32) + dead
        weights = jnp.exp2((scores - jnp.max(scores, axis=1, keepdims=True)) * ROOT)
        total = jnp.sum(weights, axis=1, keepdims=True)
        mixed.append(jnp.dot(weights.astype(BF16), values, preferred_element_type=F32) * (1.0 / total))
    attn = jnp.where(lane < HDIM, mixed[0], mixed[1])
    out_ref[:patches, :] = attn[:, :WIDE].astype(BF16)
    out_ref[patches:, :] = pack_tail(attn[:, WIDE:]).astype(BF16)


def weight_rows(cut):
    depth = 2 * HPAIR
    packed = cut[depth:]
    tail = jnp.concatenate([packed[:, at * REST : (at + 1) * REST] for at in range(4)], axis=0)
    whole = jnp.concatenate([cut[:depth], tail], axis=1)
    return [whole[core * HPAIR : (core + 1) * HPAIR] for core in range(2)]


def place_rows(rows, base, main_ref, tail_ref):
    for core in range(2):
        pair = base + core
        main_ref[pl.ds(pl.multiple_of(pair * WIDE, WIDE), WIDE), :] = rows[core][:WIDE]
        for corner in range(4):
            spot = pl.multiple_of(pair * WIDE + corner * REST, REST)
            tail_ref[corner, pl.ds(spot, REST), :] = rows[core][WIDE:]


def ready_kernel(select_ref, gain_hbm, token_ref, *rest):
    del token_ref
    blocks = rest[:ROWS]
    own_ref, across_ref, near_ref = rest[ROWS : ROWS + 3]
    resid_ref, gain_out, main_ref, tail_ref, held, line, sem = rest[-7:]
    fetch = pltpu.make_async_copy(gain_hbm, line, sem)
    fetch.start()
    me = row_index()
    band = blocks[0].shape[0]
    for step, block in zip(steps(SENDERS), blocks):
        at = pl.ds(pl.multiple_of((me ^ step) * band, band), band)
        held[at, :] = block[:, 3 * HPAIR :]
    resid_ref[...] = jnp.dot(select_ref[...], held[...], preferred_element_type=F32)
    core = me % 2
    size = own_ref.shape[0]
    half = pl.ds(pl.multiple_of(core * size, 16), size)
    main_ref[...] = jnp.zeros_like(main_ref)
    tail_ref[...] = jnp.zeros_like(tail_ref)
    cuts = [(0, own_ref[...]), (2, across_ref[...]), (3 - 2 * core, near_ref[half, :])]
    place_slices(cuts, main_ref, tail_ref)
    fetch.wait()
    whole = line[...].reshape(1, D)
    gain = jnp.zeros(gain_out.shape, F32)
    for pair in range(ROWS):
        parts = [whole[:, pair * WIDE : (pair + 1) * WIDE]]
        parts.append(whole[:, MAIN + pair * REST : MAIN + (pair + 1) * REST])
        gain = jnp.where(me == pair, jnp.concatenate(parts, axis=1), gain)
    gain_out[...] = gain


def place_slices(cuts, main_ref, tail_ref):
    for step, cut in cuts:
        place_rows(weight_rows(cut), 2 * lax.rem(lax.axis_index("page") + step, PAGES), main_ref, tail_ref)


def last_kernel(swapped_ref, main_before_ref, tail_before_ref, main_ref, tail_ref):
    main_ref[...] = main_before_ref[...]
    tail_ref[...] = tail_before_ref[...]
    core = row_index() % 2
    size = swapped_ref.shape[0] // 2
    half = pl.ds(pl.multiple_of(core * size, 16), size)
    place_slices([(1 + 2 * core, swapped_ref[half, :])], main_ref, tail_ref)


def far_block():
    me = row_index()
    return pl.ds(pl.multiple_of((me // 2 ^ 3) * 2 * WIDE, 2 * WIDE), 2 * WIDE)


def collect_late(same, other):
    core = row_index() % 2
    left = jnp.where(core == 0, same[...], other[...])
    right = jnp.where(core == 0, other[...], same[...])
    return jnp.concatenate([left, right], axis=1)


def add_features(owners, pieces, weights, before_ref, out_ref):
    main_ref, tail_ref = weights
    me = row_index()
    patches = out_ref.shape[0]
    groups = patches // 4
    mains, tails = [], []
    for step in owners:
        pair = me ^ step
        columns = pl.ds(pl.multiple_of(pair * WIDE, WIDE), WIDE)
        mains.append(main_ref[columns, :])
        tails.append([tail_ref[at, columns, :] for at in range(4)])
    rows = jnp.concatenate([piece[...] for piece in pieces], axis=1)
    base = before_ref[...] + jnp.dot(rows[:patches], jnp.concatenate(mains, axis=0), preferred_element_type=F32)
    for corner in range(4):
        span = slice(corner * groups, (corner + 1) * groups)
        tail = jnp.concatenate([tail[corner] for tail in tails], axis=0)
        out_ref[span, :] = base[span] + jnp.dot(rows[patches:], tail, preferred_element_type=F32)


def project_first_kernel(*rest):
    add_features(OWNERS[:3], rest[:3], rest[3:5], *rest[5:])


def project_second_kernel(*rest):
    add_features(OWNERS[3:6], rest[:3], rest[3:5], *rest[5:])


def project_kernel(*rest):
    same, other, base_ref, main_ref, tail_ref, gain_ref, out_ref = rest
    patches = base_ref.shape[0]
    groups = patches // 4
    block = far_block()
    full = collect_late(same, other)
    base = base_ref[...] + jnp.dot(full[:patches], main_ref[block, :], preferred_element_type=F32)
    hidden = []
    for corner in range(4):
        span = slice(corner * groups, (corner + 1) * groups)
        hidden.append(base[span] + jnp.dot(full[patches:], tail_ref[corner, block, :], preferred_element_type=F32))
    squares = jnp.concatenate([(rows * rows).astype(BF16) for rows in hidden], axis=0)
    sums = lax.dot_general(
        jnp.ones((NOTES, HPAIR), BF16), squares, (((1,), (1,)), ((), ())), preferred_element_type=F32
    )
    row = lax.broadcasted_iota(jnp.int32, (NOTES, groups), 0)
    notes = jnp.zeros((NOTES, groups), F32)
    ends = []
    for corner in range(4):
        total = sums[:, corner * groups : (corner + 1) * groups]
        coarse = total.astype(BF16).astype(F32)
        notes = jnp.where(row == corner, coarse, jnp.where(row == 4 + corner, total - coarse, notes))
        sent = hidden[corner] * gain_ref[...]
        out_ref[corner * groups : (corner + 1) * groups, :] = sent[:, :WIDE].astype(BF16)
        ends.append(sent[:, WIDE:])
    out_ref[patches : patches + groups, :] = jnp.concatenate(ends, axis=1).astype(BF16)
    out_ref[patches + groups :, :] = notes.astype(BF16)


def tail_kernel(weight_ref, bias_hbm, token_ref, out_ref, bias_out, line, sem):
    del token_ref
    fetch = pltpu.make_async_copy(bias_hbm, line, sem)
    fetch.start()
    for pair in range(ROWS):
        cut = [corner * D + MAIN + pair * REST for corner in range(4)]
        out_ref[:, pair * WIDE : (pair + 1) * WIDE] = jnp.concatenate(
            [weight_ref[:, at : at + REST] for at in cut], axis=1
        )
    fetch.wait()
    units = bias_out.shape[0]
    bias_out[...] = jnp.broadcast_to(line[...].reshape(1, units), (8, units)).T[:, :1]


def merge_product(weight_ref, corner, groups, pieces):
    me = row_index()
    spots = [pl.multiple_of(corner * D + (me ^ step) * WIDE, WIDE) for step, _ in pieces]
    span = slice(corner * groups, (corner + 1) * groups)
    return lax.dot_general(
        jnp.concatenate([weight_ref[:, pl.ds(spot, WIDE)] for spot in spots], axis=1),
        jnp.concatenate([piece[span, :] for _, piece in pieces], axis=1),
        (((1,), (1,)), ((), ())),
        preferred_element_type=F32,
    )


def tail_products(tail_ref, groups, pieces):
    me = row_index()
    columns = [tail_ref[:, pl.ds(pl.multiple_of((me ^ step) * WIDE, WIDE), WIDE)] for step, _ in pieces]
    tails = jnp.concatenate(columns, axis=1)
    ends = jnp.concatenate([piece[4 * groups : 5 * groups, :] for _, piece in pieces], axis=1)
    corner_of = lax.rem(lax.broadcasted_iota(jnp.int32, (1, ends.shape[1]), 1), WIDE) // REST
    return [
        lax.dot_general(
            tails,
            jnp.where(corner_of == corner, ends, jnp.zeros_like(ends)),
            (((1,), (1,)), ((), ())),
            preferred_element_type=F32,
        )
        for corner in range(4)
    ]


def merge_first_kernel(*rest):
    pieces, (weight_ref, tail_ref, sum_ref) = list(zip(OWNERS[:3], rest[:3])), rest[3:]
    groups = sum_ref.shape[2]
    for corner, tail in enumerate(tail_products(tail_ref, groups, pieces)):
        sum_ref[corner] = tail + merge_product(weight_ref, corner, groups, pieces)


def merge_second_kernel(*rest):
    pieces, (before_ref, weight_ref, tail_ref, sum_ref) = list(zip(OWNERS[3:6], rest[:3])), rest[3:]
    groups = sum_ref.shape[2]
    for corner, tail in enumerate(tail_products(tail_ref, groups, pieces)):
        sum_ref[corner] = before_ref[corner] + (tail + merge_product(weight_ref, corner, groups, pieces))


def merge_kernel(*rest):
    pieces = rest[:ROWS]
    before_ref, weight_ref, tail_ref, bias_ref, live_ref, out_hbm, held, sems = rest[ROWS:]
    me = row_index()
    groups = live_ref.shape[1]
    patches = 4 * groups
    contract = (((1,), (1,)), ((), ()))
    block = pl.multiple_of((me // 2 ^ 3) * 2 * WIDE, 2 * WIDE)
    rows = collect_late(pieces[6], pieces[7])
    notes = jnp.zeros((NOTES, groups), F32)
    for piece in pieces:
        notes = notes + piece[patches + groups :, :].astype(F32)
    scale = lax.rsqrt((notes[:4] + notes[4:8]) * (1.0 / D) + 1e-06)
    spread = jnp.concatenate([jnp.broadcast_to(scale[at : at + 1], (REST, groups)) for at in range(4)], axis=0).T
    ends = rows[patches : patches + groups].astype(F32) * jnp.concatenate([spread] * 2, axis=1)
    ends = ends.astype(BF16)
    half = held.shape[0] // 2
    copies = []
    for at in range(2):
        units = slice(at * half, (at + 1) * half)
        total = bias_ref[units, :] + lax.dot_general(
            tail_ref[units, pl.ds(block, 2 * WIDE)], ends, contract, preferred_element_type=F32
        )
        for corner in range(4):
            part = before_ref[corner, units] + lax.dot_general(
                weight_ref[units, pl.ds(pl.multiple_of(corner * D + block, 2 * WIDE), 2 * WIDE)],
                rows[corner * groups : (corner + 1) * groups],
                contract,
                preferred_element_type=F32,
            )
            total = total + scale[corner : corner + 1] * part
        merged = 0.5 * total * (1.0 + lax.erf(total * math.sqrt(0.5)))
        held[units, :] = jnp.where(live_ref[...] > 0.0, merged, 0.0).astype(BF16)
        copies.append(pltpu.make_async_copy(held.at[units], out_hbm.at[0, units], sems.at[at]))
        copies[at].start()
    for copy in copies:
        copy.wait()


def kernel(body, name, out_shape, scratch=(), fetched=(), count=0, limit=24, flops=0, moved=0, out=pltpu.VMEM):
    specs = [pl.BlockSpec(memory_space=pltpu.VMEM) for _ in range(count)]
    for at in fetched:
        specs[at] = pl.BlockSpec(memory_space=pl.ANY)
    return pl.pallas_call(
        body,
        out_shape=out_shape,
        in_specs=specs,
        out_specs=jax.tree.map(lambda _: pl.BlockSpec(memory_space=out), out_shape),
        scratch_shapes=list(scratch),
        compiler_params=pltpu.CompilerParams(vmem_limit_bytes=limit * 1024 * 1024),
        cost_estimate=pl.CostEstimate(flops=flops, bytes_accessed=moved, transcendentals=0),
        name=name,
    )


def in_hbm(value):
    return pltpu.with_memory_space_constraint(value, pltpu.HBM)


def shape(*dims, dtype=BF16):
    return jax.ShapeDtypeStruct(dims, dtype)


def swap(value, even, odd=None):
    odd = even if odd is None else odd
    return lax.ppermute(value, "row", [(row, row ^ (odd if row % 2 else even)) for row in range(ROWS)])


def turn(value, low, high):
    pairs = [
        (page * ROWS + row, (page + (high if row % 2 else low)) % PAGES * ROWS + row)
        for page in range(PAGES)
        for row in range(ROWS)
    ]
    return lax.ppermute(value, ("page", "row"), pairs)


def after(value, *arrays):
    return lax.optimization_barrier((value, *arrays))[0]


def local_eight(qkv_rows, residual, out_weight, norm_gain, merge_weight, merge_bias, page_grid):
    band = qkv_rows.shape[1]
    patches = band * ROWS
    groups = patches // 4
    units = merge_weight.shape[0]
    depth = out_weight.shape[0]
    piece = patches + groups
    size = depth + depth // 4

    *sends, chip, own, grid = kernel(
        spread_kernel,
        "spread",
        [shape(band, 4 * HPAIR)] * ROWS
        + [shape(2 * size, WIDE), shape(size, WIDE), shape(8, WIDE, dtype=jnp.int32)],
        [
            pltpu.VMEM((band, 3 * D), BF16),
            pltpu.VMEM((band, D), BF16),
            pltpu.VMEM((depth, 2 * WIDE), BF16),
            pltpu.VMEM((depth, WIDE), BF16),
            pltpu.VMEM((ROWS, band, 4 * HPAIR), BF16),
            pltpu.SMEM(page_grid.shape, jnp.int32),
            pltpu.SemaphoreType.DMA((8,)),
        ],
        fetched=range(4),
        count=4,
        moved=1 << 20,
    )(in_hbm(qkv_rows), in_hbm(residual), in_hbm(out_weight), in_hbm(page_grid))
    blocks = [sends[0]] + [swap(send, *pair) for send, pair in zip(sends[1:], RECEIVERS[1:])]
    select, dead, live = kernel(
        layout_kernel,
        "layout",
        [shape(patches, patches), shape(1, patches, dtype=F32), shape(1, groups, dtype=F32)],
        fetched=range(1, 1 + 2),
        count=1 + 2,
        moved=1 << 20,
    )(grid, *blocks[1:3])
    near = turn(after(chip, *()), 1, PAGES - 1)
    swapped = swap(near, 1)
    attn = kernel(
        attend_kernel,
        "attend",
        shape(piece, WIDE),
        [pltpu.VMEM((patches, HPAIR), BF16)] * 3,
        count=2 + ROWS,
        flops=20 * patches * patches * 4096,
        moved=1 << 20,
    )(select, dead, *blocks)
    across = turn(own, 2, 2)
    resid, own_gain, main, tail = kernel(
        ready_kernel,
        "ready",
        [shape(patches, HPAIR, dtype=F32), shape(1, HPAIR, dtype=F32), shape(MAIN, HPAIR), shape(4, MAIN, HPAIR)],
        [pltpu.VMEM((patches, HPAIR), BF16), pltpu.VMEM((D,), F32), pltpu.SemaphoreType.DMA],
        fetched=(1, 2),
        count=3 + ROWS + 3,
        flops=10 * patches * patches * 4096,
        moved=4 << 20,
    )(select, in_hbm(norm_gain), attn, *blocks, own, across, near)
    one, two, far = swap(attn, 4), swap(attn, 2), swap(attn, 6)
    last = kernel(
        last_kernel,
        "ready_last",
        [shape(MAIN, HPAIR), shape(4, MAIN, HPAIR)],
        count=3,
        flops=1,
        moved=1,
    )(swapped, main, tail)
    near = [swap(after(attn, main), 1), swap(after(one, last[0]), 1), swap(two, 1)]
    weights = tuple(last)
    rows = shape(patches, HPAIR, dtype=F32)
    first = kernel(project_first_kernel, "project_first", rows, count=6, flops=1, moved=1)(attn, one, two, *weights, resid)
    second = kernel(project_second_kernel, "project_second", rows, count=6, flops=1, moved=1)(*near, *weights, first)
    hidden = kernel(
        project_kernel,
        "project",
        shape(piece + NOTES, WIDE),
        count=2 + 4,
        flops=patches * MAIN * 256,
        moved=4 << 20,
    )(far, swap(after(far, first), 1), second, *weights, own_gain)
    ends, bias = kernel(
        tail_kernel,
        "merge_tail",
        [shape(units, MAIN), shape(units, 1, dtype=F32)],
        [pltpu.VMEM((units,), F32), pltpu.SemaphoreType.DMA],
        fetched=(1, 2),
        count=3,
        moved=4 << 20,
    )(merge_weight, in_hbm(merge_bias), hidden)
    sums = shape(4, units, groups, dtype=F32)
    one, two, far = swap(hidden, 4), swap(hidden, 2), swap(hidden, 6)
    first = kernel(merge_first_kernel, "merge_first", sums, count=5, flops=1, moved=1)(
        hidden, one, two, merge_weight, ends
    )
    near = [swap(after(hidden, ends), 1), swap(one, 1), swap(two, 1)]
    second = kernel(merge_second_kernel, "merge_second", sums, count=6, flops=1, moved=1)(
        *near, first, merge_weight, ends
    )
    return kernel(
        merge_kernel,
        "merge",
        shape(1, units, groups),
        [pltpu.VMEM((units, groups), BF16), pltpu.SemaphoreType.DMA((2,))],
        out=pl.ANY,
        count=ROWS + 5,
        flops=4 * units * groups * MAIN,
        moved=8 << 20,
    )(hidden, one, two, *near, far, swap(after(far, first, *near), 1), second, merge_weight, ends, bias, live)


def solution(mesh):
    in_specs = (
        P("page", "row", None),
        P("page", "row", None),
        P("page", None),
        P(),
        P("row", None),
        P("row"),
        P("page", None),
    )
    out_specs = P("page", "row", None)
    local = local_eight if mesh.shape["row"] == 8 and mesh.shape["page"] == 4 else local_any
    return jax.shard_map(local, mesh=mesh, in_specs=in_specs, out_specs=out_specs, check_vma=False)
```

```python
import functools
import math

import jax
import jax.numpy as jnp
from jax import lax
from jax.experimental import pallas as pl
from jax.experimental.pallas import tpu as pltpu
from jax.sharding import PartitionSpec as P

D = 1280
HEADS = 16
HDIM = 80


def local_any(qkv_rows, residual, out_weight, norm_gain, merge_weight, merge_bias, page_grid):
    row_count = lax.axis_size("row")
    q_split = max(1, row_count // HEADS)
    head_groups = row_count // q_split
    width = D // head_groups
    heads_per = width // HDIM
    band_len = qkv_rows.shape[1]
    part_len = band_len // q_split
    local_qkv = qkv_rows[0]
    queries = local_qkv[:, :D]
    key_vals = jnp.concatenate(
        [
            local_qkv[:, D : 2 * D].reshape(band_len, head_groups, width),
            local_qkv[:, 2 * D :].reshape(band_len, head_groups, width),
        ],
        axis=2,
    )
    q_send = (
        queries.reshape(q_split, part_len, head_groups, width)
        .transpose(2, 0, 1, 3)
        .reshape(row_count, part_len, width)
    )
    kv_send = jnp.broadcast_to(
        key_vals.transpose(1, 0, 2)[:, None], (head_groups, q_split, band_len, 2 * width)
    )
    kv_send = kv_send.reshape(row_count, band_len, 2 * width)
    q_recv, kv_recv = (
        lax.all_to_all(q_send, "row", split_axis=0, concat_axis=1, tiled=True),
        lax.all_to_all(kv_send, "row", split_axis=0, concat_axis=1, tiled=True),
    )
    kv_local = kv_recv[0]
    positions = jnp.arange(row_count * band_len, dtype=jnp.int32)
    valid_len = page_grid[0, 0] * page_grid[0, 1]
    key_valid = positions < valid_len
    key_total = kv_local.shape[0]
    key_heads = kv_local[:, :width].reshape(key_total, heads_per, HDIM)
    value_heads = kv_local[:, width:].reshape(key_total, heads_per, HDIM)
    query_total = row_count * part_len
    q_block = math.gcd(query_total, 512)
    q_blocks = q_recv[0].reshape(query_total // q_block, q_block, heads_per, HDIM)
    root_dim = math.sqrt(HDIM)

    def attend(q_span):
        scores = (
            jnp.einsum("qhd,khd->hqk", q_span, key_heads, preferred_element_type=jnp.float32)
            / root_dim
        )
        scores = jnp.where(key_valid[None, None, :], scores, -1e30)
        peak = jnp.max(scores, axis=2, keepdims=True)
        weights = jnp.exp(scores - peak)
        total = jnp.sum(weights, axis=2, keepdims=True)
        mixed = (
            jnp.einsum(
                "hqk,khd->hqd",
                weights.astype(jnp.bfloat16),
                value_heads,
                preferred_element_type=jnp.float32,
            )
            / total
        )
        return mixed.transpose(1, 0, 2).reshape(q_span.shape[0], width).astype(jnp.bfloat16)

    attn_heads = lax.map(attend, q_blocks).reshape(row_count, part_len, width)
    returned = lax.all_to_all(attn_heads, "row", split_axis=0, concat_axis=0, tiled=True)
    attn = (
        returned.reshape(head_groups, q_split, part_len, width)
        .transpose(1, 2, 0, 3)
        .reshape(band_len, D)
    )
    projected = jnp.dot(
        attn,
        lax.all_gather(out_weight, "page", axis=0, tiled=True),
        preferred_element_type=jnp.float32,
    )
    hidden = residual[0].astype(jnp.float32) + projected
    normed = (
        hidden * lax.rsqrt(jnp.mean(hidden * hidden, axis=1, keepdims=True) + 1e-06) * norm_gain
    ).astype(jnp.bfloat16)
    rows_n = page_grid[0, 0]
    cols_n = page_grid[0, 1]
    group_total = band_len * row_count // 4
    slots = jnp.arange(group_total, dtype=jnp.int32)
    half_cols = cols_n // 2
    live = slots < rows_n // 2 * half_cols
    first = jnp.where(live, 2 * (slots // half_cols) * cols_n + 2 * (slots % half_cols), 0)
    corners = [first, first + 1, first + cols_n, first + cols_n + 1]
    local_units = merge_weight.shape[0]
    page_all = lax.all_gather(normed, "row", axis=0, tiled=True)
    merged_sum = jnp.zeros((local_units, group_total), jnp.float32)
    for corner in range(4):
        picked = jnp.take(page_all, corners[corner], axis=0)
        merged_sum = merged_sum + jnp.einsum(
            "md,gd->mg",
            merge_weight[:, corner * D : (corner + 1) * D],
            picked,
            preferred_element_type=jnp.float32,
        )
    merged = jax.nn.gelu(merged_sum + merge_bias[:, None], approximate=False)
    merged = jnp.where(live[None, :], merged, 0.0).astype(jnp.bfloat16)
    return merged[None]


ROWS = 8
PAGES = 4
HPAIR = 2 * HDIM
WIDE = 128
REST = HPAIR - WIDE
MAIN = ROWS * WIDE
NOTES = 16
RECEIVERS = ((0, 0), (4, 2), (2, 4), (1, 1), (6, 6), (7, 7), (3, 5), (5, 3))
SENDERS = ((0, 0), (4, 2), (2, 4), (1, 1), (6, 6), (7, 7), (5, 3), (3, 5))
OWNERS = (0, 4, 2, 1, 5, 3, 6, 7)
ROOT = math.log2(math.e) / math.sqrt(HDIM)
BF16 = jnp.bfloat16
F32 = jnp.float32


def row_index():
    return lax.axis_index("row")


def steps(pairs):
    core = row_index() % 2
    return [even + (odd - even) * core for even, odd in pairs]


def pack_tail(wide):
    groups = wide.shape[0] // 4
    return jnp.concatenate([wide[at * groups : (at + 1) * groups] for at in range(4)], axis=1)


def spread_kernel(qkv_hbm, resid_hbm, weight_hbm, grid_hbm, *rest):
    outs = rest[:ROWS]
    chip_ref, slice_ref, grid_out, qkv, resid, main, tile, held, grid, sems = rest[ROWS:]
    me = row_index()
    depth = weight_hbm.shape[0]
    chip = pl.ds(pl.multiple_of(me // 2 * 2 * WIDE, 2 * WIDE), 2 * WIDE)
    ends = pl.ds(pl.multiple_of(MAIN + me // 4 * WIDE, WIDE), WIDE)
    part = qkv.shape[0] // 4
    copies = []
    for at in range(4):
        rows = pl.ds(at * part, part)
        copies.append(pltpu.make_async_copy(qkv_hbm.at[0, rows], qkv.at[rows], sems.at[at]))
    copies.append(pltpu.make_async_copy(resid_hbm.at[0], resid, sems.at[4]))
    copies.append(pltpu.make_async_copy(weight_hbm.at[:, chip], main, sems.at[5]))
    copies.append(pltpu.make_async_copy(weight_hbm.at[:, ends], tile, sems.at[6]))
    copies.append(pltpu.make_async_copy(grid_hbm, grid, sems.at[7]))
    for copy in copies:
        copy.start()
    for copy in copies:
        copy.wait()
    for dest in range(ROWS):
        at = dest * HPAIR
        parts = [qkv[:, part * D + at : part * D + at + HPAIR] for part in range(3)]
        parts.append(resid[:, dest * WIDE : (dest + 1) * WIDE])
        parts.append(resid[:, MAIN + dest * REST : MAIN + (dest + 1) * REST])
        held[dest] = jnp.concatenate(parts, axis=1)
    for step, out in zip(steps(RECEIVERS), outs):
        out[...] = held[me ^ step]
    low = me // 2 % 2 == 0
    size = depth + depth // 4
    for core in range(2):
        tail = jnp.where(low, tile[:, core * REST : (core + 1) * REST], tile[:, (core + 2) * REST : (core + 3) * REST])
        chip_ref[core * size : core * size + depth, :] = main[:, core * WIDE : (core + 1) * WIDE]
        chip_ref[core * size + depth : (core + 1) * size, :] = pack_tail(tail)
    slice_ref[...] = chip_ref[pl.ds(pl.multiple_of(me % 2 * size, 16), size), :]
    row = lax.broadcasted_iota(jnp.int32, grid_out.shape, 0)
    grid_out[...] = jnp.where(row == 0, grid[0, 0], grid[0, 1])


def layout_kernel(grid_ref, *rest):
    select_ref, keys_ref, live_ref = rest[-3:]
    rows_n, cols_n = grid_ref[:1, :1], grid_ref[1:2, :1]
    patches = select_ref.shape[0]
    groups = patches // 4
    half = cols_n >> 1
    count = (rows_n >> 1) * half
    slots = lax.broadcasted_iota(jnp.int32, (groups, 1), 0)
    line = jnp.floor((slots.astype(F32) + 0.5) / half.astype(F32)).astype(jnp.int32)
    first = 2 * line * cols_n + 2 * (slots - line * half)
    at = lax.broadcasted_iota(jnp.int32, (groups, patches), 1)
    for corner in range(4):
        wanted = jnp.where(slots < count, first + (corner // 2) * cols_n + corner % 2, -1)
        select_ref[corner * groups : (corner + 1) * groups, :] = jnp.where(at == wanted, 1.0, 0.0).astype(BF16)
    key = lax.broadcasted_iota(jnp.int32, keys_ref.shape, 1)
    keys_ref[...] = jnp.where(key < rows_n * cols_n, 0.0, -1e30)
    slot = lax.broadcasted_iota(jnp.int32, live_ref.shape, 1)
    live_ref[...] = jnp.where(slot < count, 1.0, 0.0)


def attend_kernel(select_ref, dead_ref, *rest):
    blocks = rest[:ROWS]
    out_ref, q_all, k_all, v_all = rest[-4:]
    me = row_index()
    band = blocks[0].shape[0]
    patches = band * ROWS
    for step, block in zip(steps(SENDERS), blocks):
        at = pl.ds(pl.multiple_of((me ^ step) * band, band), band)
        q_all[at, :] = block[:, :HPAIR]
        k_all[at, :] = block[:, HPAIR : 2 * HPAIR]
        v_all[at, :] = block[:, 2 * HPAIR : 3 * HPAIR]
    queries = jnp.dot(select_ref[...], q_all[...], preferred_element_type=F32).astype(BF16)
    lane = lax.broadcasted_iota(jnp.int32, (1, HPAIR), 1)
    keys, values, dead = k_all[...], v_all[...], dead_ref[...]
    mixed = []
    for head in range(2):
        mine = (lane >= head * HDIM) & (lane < (head + 1) * HDIM)
        asked = jnp.where(mine, queries, jnp.zeros_like(queries))
        scores = lax.dot_general(asked, keys, (((1,), (1,)), ((), ())), preferred_element_type=F32) + dead
        weights = jnp.exp2((scores - jnp.max(scores, axis=1, keepdims=True)) * ROOT)
        total = jnp.sum(weights, axis=1, keepdims=True)
        mixed.append(jnp.dot(weights.astype(BF16), values, preferred_element_type=F32) * (1.0 / total))
    attn = jnp.where(lane < HDIM, mixed[0], mixed[1])
    out_ref[:patches, :] = attn[:, :WIDE].astype(BF16)
    out_ref[patches:, :] = pack_tail(attn[:, WIDE:]).astype(BF16)


def weight_rows(cut):
    depth = 2 * HPAIR
    packed = cut[depth:]
    tail = jnp.concatenate([packed[:, at * REST : (at + 1) * REST] for at in range(4)], axis=0)
    whole = jnp.concatenate([cut[:depth], tail], axis=1)
    return [whole[core * HPAIR : (core + 1) * HPAIR] for core in range(2)]


def place_rows(rows, base, main_ref, tail_ref):
    for core in range(2):
        pair = base + core
        main_ref[pl.ds(pl.multiple_of(pair * WIDE, WIDE), WIDE), :] = rows[core][:WIDE]
        for corner in range(4):
            spot = pl.multiple_of(pair * WIDE + corner * REST, REST)
            tail_ref[corner, pl.ds(spot, REST), :] = rows[core][WIDE:]


def ready_kernel(select_ref, gain_hbm, token_ref, *rest):
    del token_ref
    blocks = rest[:ROWS]
    own_ref, across_ref, near_ref = rest[ROWS : ROWS + 3]
    resid_ref, gain_out, main_ref, tail_ref, held, line, sem = rest[-7:]
    fetch = pltpu.make_async_copy(gain_hbm, line, sem)
    fetch.start()
    me = row_index()
    band = blocks[0].shape[0]
    for step, block in zip(steps(SENDERS), blocks):
        at = pl.ds(pl.multiple_of((me ^ step) * band, band), band)
        held[at, :] = block[:, 3 * HPAIR :]
    resid_ref[...] = jnp.dot(select_ref[...], held[...], preferred_element_type=F32)
    core = me % 2
    size = own_ref.shape[0]
    half = pl.ds(pl.multiple_of(core * size, 16), size)
    main_ref[...] = jnp.zeros_like(main_ref)
    tail_ref[...] = jnp.zeros_like(tail_ref)
    cuts = [(0, own_ref[...]), (2, across_ref[...]), (3 - 2 * core, near_ref[half, :])]
    place_slices(cuts, main_ref, tail_ref)
    fetch.wait()
    whole = line[...].reshape(1, D)
    gain = jnp.zeros(gain_out.shape, F32)
    for pair in range(ROWS):
        parts = [whole[:, pair * WIDE : (pair + 1) * WIDE]]
        parts.append(whole[:, MAIN + pair * REST : MAIN + (pair + 1) * REST])
        gain = jnp.where(me == pair, jnp.concatenate(parts, axis=1), gain)
    gain_out[...] = gain


def place_slices(cuts, main_ref, tail_ref):
    for step, cut in cuts:
        place_rows(weight_rows(cut), 2 * lax.rem(lax.axis_index("page") + step, PAGES), main_ref, tail_ref)


def last_kernel(swapped_ref, main_before_ref, tail_before_ref, main_ref, tail_ref):
    main_ref[...] = main_before_ref[...]
    tail_ref[...] = tail_before_ref[...]
    core = row_index() % 2
    size = swapped_ref.shape[0] // 2
    half = pl.ds(pl.multiple_of(core * size, 16), size)
    place_slices([(1 + 2 * core, swapped_ref[half, :])], main_ref, tail_ref)


def far_block():
    me = row_index()
    return pl.ds(pl.multiple_of((me // 2 ^ 3) * 2 * WIDE, 2 * WIDE), 2 * WIDE)


def collect_late(same, other):
    core = row_index() % 2
    left = jnp.where(core == 0, same[...], other[...])
    right = jnp.where(core == 0, other[...], same[...])
    return jnp.concatenate([left, right], axis=1)


def add_features(owners, pieces, weights, before_ref, out_ref):
    main_ref, tail_ref = weights
    me = row_index()
    patches = out_ref.shape[0]
    groups = patches // 4
    mains, tails = [], []
    for step in owners:
        pair = me ^ step
        columns = pl.ds(pl.multiple_of(pair * WIDE, WIDE), WIDE)
        mains.append(main_ref[columns, :])
        tails.append([tail_ref[at, columns, :] for at in range(4)])
    rows = jnp.concatenate([piece[...] for piece in pieces], axis=1)
    base = before_ref[...] + jnp.dot(rows[:patches], jnp.concatenate(mains, axis=0), preferred_element_type=F32)
    for corner in range(4):
        span = slice(corner * groups, (corner + 1) * groups)
        tail = jnp.concatenate([tail[corner] for tail in tails], axis=0)
        out_ref[span, :] = base[span] + jnp.dot(rows[patches:], tail, preferred_element_type=F32)


def project_first_kernel(*rest):
    add_features(OWNERS[:3], rest[:3], rest[3:5], *rest[5:])


def project_second_kernel(*rest):
    add_features(OWNERS[3:6], rest[:3], rest[3:5], *rest[5:])


def project_kernel(*rest):
    same, other, base_ref, main_ref, tail_ref, gain_ref, out_ref = rest
    patches = base_ref.shape[0]
    groups = patches // 4
    block = far_block()
    full = collect_late(same, other)
    base = base_ref[...] + jnp.dot(full[:patches], main_ref[block, :], preferred_element_type=F32)
    hidden = []
    for corner in range(4):
        span = slice(corner * groups, (corner + 1) * groups)
        hidden.append(base[span] + jnp.dot(full[patches:], tail_ref[corner, block, :], preferred_element_type=F32))
    squares = jnp.concatenate([(rows * rows).astype(BF16) for rows in hidden], axis=0)
    sums = lax.dot_general(
        jnp.ones((NOTES, HPAIR), BF16), squares, (((1,), (1,)), ((), ())), preferred_element_type=F32
    )
    row = lax.broadcasted_iota(jnp.int32, (NOTES, groups), 0)
    notes = jnp.zeros((NOTES, groups), F32)
    ends = []
    for corner in range(4):
        total = sums[:, corner * groups : (corner + 1) * groups]
        coarse = total.astype(BF16).astype(F32)
        notes = jnp.where(row == corner, coarse, jnp.where(row == 4 + corner, total - coarse, notes))
        sent = hidden[corner] * gain_ref[...]
        out_ref[corner * groups : (corner + 1) * groups, :] = sent[:, :WIDE].astype(BF16)
        ends.append(sent[:, WIDE:])
    out_ref[patches : patches + groups, :] = jnp.concatenate(ends, axis=1).astype(BF16)
    out_ref[patches + groups :, :] = notes.astype(BF16)


def tail_kernel(weight_ref, bias_hbm, token_ref, out_ref, bias_out, line, sem):
    del token_ref
    fetch = pltpu.make_async_copy(bias_hbm, line, sem)
    fetch.start()
    for pair in range(ROWS):
        cut = [corner * D + MAIN + pair * REST for corner in range(4)]
        out_ref[:, pair * WIDE : (pair + 1) * WIDE] = jnp.concatenate(
            [weight_ref[:, at : at + REST] for at in cut], axis=1
        )
    fetch.wait()
    units = bias_out.shape[0]
    bias_out[...] = jnp.broadcast_to(line[...].reshape(1, units), (8, units)).T[:, :1]


def merge_product(weight_ref, corner, groups, pieces):
    me = row_index()
    spots = [pl.multiple_of(corner * D + (me ^ step) * WIDE, WIDE) for step, _ in pieces]
    span = slice(corner * groups, (corner + 1) * groups)
    return lax.dot_general(
        jnp.concatenate([weight_ref[:, pl.ds(spot, WIDE)] for spot in spots], axis=1),
        jnp.concatenate([piece[span, :] for _, piece in pieces], axis=1),
        (((1,), (1,)), ((), ())),
        preferred_element_type=F32,
    )


def tail_products(tail_ref, groups, pieces):
    me = row_index()
    columns = [tail_ref[:, pl.ds(pl.multiple_of((me ^ step) * WIDE, WIDE), WIDE)] for step, _ in pieces]
    tails = jnp.concatenate(columns, axis=1)
    ends = jnp.concatenate([piece[4 * groups : 5 * groups, :] for _, piece in pieces], axis=1)
    corner_of = lax.rem(lax.broadcasted_iota(jnp.int32, (1, ends.shape[1]), 1), WIDE) // REST
    return [
        lax.dot_general(
            tails,
            jnp.where(corner_of == corner, ends, jnp.zeros_like(ends)),
            (((1,), (1,)), ((), ())),
            preferred_element_type=F32,
        )
        for corner in range(4)
    ]


def merge_first_kernel(*rest):
    pieces, (weight_ref, tail_ref, sum_ref) = list(zip(OWNERS[:3], rest[:3])), rest[3:]
    groups = sum_ref.shape[2]
    for corner, tail in enumerate(tail_products(tail_ref, groups, pieces)):
        sum_ref[corner] = tail + merge_product(weight_ref, corner, groups, pieces)


def merge_second_kernel(*rest):
    pieces, (before_ref, weight_ref, tail_ref, sum_ref) = list(zip(OWNERS[3:6], rest[:3])), rest[3:]
    groups = sum_ref.shape[2]
    for corner, tail in enumerate(tail_products(tail_ref, groups, pieces)):
        sum_ref[corner] = before_ref[corner] + (tail + merge_product(weight_ref, corner, groups, pieces))


def merge_kernel(*rest):
    pieces = rest[:ROWS]
    before_ref, weight_ref, tail_ref, bias_ref, live_ref, out_hbm, held, sems = rest[ROWS:]
    me = row_index()
    groups = live_ref.shape[1]
    patches = 4 * groups
    contract = (((1,), (1,)), ((), ()))
    block = pl.multiple_of((me // 2 ^ 3) * 2 * WIDE, 2 * WIDE)
    rows = collect_late(pieces[6], pieces[7])
    notes = jnp.zeros((NOTES, groups), F32)
    for piece in pieces:
        notes = notes + piece[patches + groups :, :].astype(F32)
    scale = lax.rsqrt((notes[:4] + notes[4:8]) * (1.0 / D) + 1e-06)
    spread = jnp.concatenate([jnp.broadcast_to(scale[at : at + 1], (REST, groups)) for at in range(4)], axis=0).T
    ends = rows[patches : patches + groups].astype(F32) * jnp.concatenate([spread] * 2, axis=1)
    ends = ends.astype(BF16)
    half = held.shape[0] // 2
    copies = []
    for at in range(2):
        units = slice(at * half, (at + 1) * half)
        total = bias_ref[units, :] + lax.dot_general(
            tail_ref[units, pl.ds(block, 2 * WIDE)], ends, contract, preferred_element_type=F32
        )
        for corner in range(4):
            part = before_ref[corner, units] + lax.dot_general(
                weight_ref[units, pl.ds(pl.multiple_of(corner * D + block, 2 * WIDE), 2 * WIDE)],
                rows[corner * groups : (corner + 1) * groups],
                contract,
                preferred_element_type=F32,
            )
            total = total + scale[corner : corner + 1] * part
        merged = 0.5 * total * (1.0 + lax.erf(total * math.sqrt(0.5)))
        held[units, :] = jnp.where(live_ref[...] > 0.0, merged, 0.0).astype(BF16)
        copies.append(pltpu.make_async_copy(held.at[units], out_hbm.at[0, units], sems.at[at]))
        copies[at].start()
    for copy in copies:
        copy.wait()


def kernel(body, name, out_shape, scratch=(), fetched=(), count=0, limit=24, flops=0, moved=0, out=pltpu.VMEM):
    specs = [pl.BlockSpec(memory_space=pltpu.VMEM) for _ in range(count)]
    for at in fetched:
        specs[at] = pl.BlockSpec(memory_space=pl.ANY)
    return pl.pallas_call(
        body,
        out_shape=out_shape,
        in_specs=specs,
        out_specs=jax.tree.map(lambda _: pl.BlockSpec(memory_space=out), out_shape),
        scratch_shapes=list(scratch),
        compiler_params=pltpu.CompilerParams(vmem_limit_bytes=limit * 1024 * 1024),
        cost_estimate=pl.CostEstimate(flops=flops, bytes_accessed=moved, transcendentals=0),
        name=name,
    )


def in_hbm(value):
    return pltpu.with_memory_space_constraint(value, pltpu.HBM)


def shape(*dims, dtype=BF16):
    return jax.ShapeDtypeStruct(dims, dtype)


def swap(value, even, odd=None):
    odd = even if odd is None else odd
    return lax.ppermute(value, "row", [(row, row ^ (odd if row % 2 else even)) for row in range(ROWS)])


def turn(value, low, high):
    pairs = [
        (page * ROWS + row, (page + (high if row % 2 else low)) % PAGES * ROWS + row)
        for page in range(PAGES)
        for row in range(ROWS)
    ]
    return lax.ppermute(value, ("page", "row"), pairs)


def after(value, *arrays):
    return lax.optimization_barrier((value, *arrays))[0]


def local_eight(qkv_rows, residual, out_weight, norm_gain, merge_weight, merge_bias, page_grid):
    band = qkv_rows.shape[1]
    patches = band * ROWS
    groups = patches // 4
    units = merge_weight.shape[0]
    depth = out_weight.shape[0]
    piece = patches + groups
    size = depth + depth // 4

    *sends, chip, own, grid = kernel(
        spread_kernel,
        "spread",
        [shape(band, 4 * HPAIR)] * ROWS
        + [shape(2 * size, WIDE), shape(size, WIDE), shape(8, WIDE, dtype=jnp.int32)],
        [
            pltpu.VMEM((band, 3 * D), BF16),
            pltpu.VMEM((band, D), BF16),
            pltpu.VMEM((depth, 2 * WIDE), BF16),
            pltpu.VMEM((depth, WIDE), BF16),
            pltpu.VMEM((ROWS, band, 4 * HPAIR), BF16),
            pltpu.SMEM(page_grid.shape, jnp.int32),
            pltpu.SemaphoreType.DMA((8,)),
        ],
        fetched=range(4),
        count=4,
        moved=1 << 20,
    )(in_hbm(qkv_rows), in_hbm(residual), in_hbm(out_weight), in_hbm(page_grid))
    blocks = [sends[0]] + [swap(send, *pair) for send, pair in zip(sends[1:], RECEIVERS[1:])]
    select, dead, live = kernel(
        layout_kernel,
        "layout",
        [shape(patches, patches), shape(1, patches, dtype=F32), shape(1, groups, dtype=F32)],
        fetched=range(1, 1 + 2),
        count=1 + 2,
        moved=1 << 20,
    )(grid, *blocks[1:3])
    near = turn(after(chip, *()), 1, PAGES - 1)
    swapped = swap(near, 1)
    attn = kernel(
        attend_kernel,
        "attend",
        shape(piece, WIDE),
        [pltpu.VMEM((patches, HPAIR), BF16)] * 3,
        count=2 + ROWS,
        flops=20 * patches * patches * 4096,
        moved=1 << 20,
    )(select, dead, *blocks)
    across = turn(own, 2, 2)
    resid, own_gain, main, tail = kernel(
        ready_kernel,
        "ready",
        [shape(patches, HPAIR, dtype=F32), shape(1, HPAIR, dtype=F32), shape(MAIN, HPAIR), shape(4, MAIN, HPAIR)],
        [pltpu.VMEM((patches, HPAIR), BF16), pltpu.VMEM((D,), F32), pltpu.SemaphoreType.DMA],
        fetched=(1, 2),
        count=3 + ROWS + 3,
        flops=10 * patches * patches * 4096,
        moved=4 << 20,
    )(select, in_hbm(norm_gain), attn, *blocks, own, across, near)
    one, two, far = swap(attn, 4), swap(attn, 2), swap(attn, 6)
    last = kernel(
        last_kernel,
        "ready_last",
        [shape(MAIN, HPAIR), shape(4, MAIN, HPAIR)],
        count=3,
        flops=1,
        moved=1,
    )(swapped, main, tail)
    near = [swap(after(attn, main), 1), swap(after(one, last[0]), 1), swap(two, 1)]
    weights = tuple(last)
    rows = shape(patches, HPAIR, dtype=F32)
    first = kernel(project_first_kernel, "project_first", rows, count=6, flops=1, moved=1)(attn, one, two, *weights, resid)
    second = kernel(project_second_kernel, "project_second", rows, count=6, flops=1, moved=1)(*near, *weights, first)
    hidden = kernel(
        project_kernel,
        "project",
        shape(piece + NOTES, WIDE),
        count=2 + 4,
        flops=patches * MAIN * 256,
        moved=4 << 20,
    )(far, swap(after(far, first), 1), second, *weights, own_gain)
    ends, bias = kernel(
        tail_kernel,
        "merge_tail",
        [shape(units, MAIN), shape(units, 1, dtype=F32)],
        [pltpu.VMEM((units,), F32), pltpu.SemaphoreType.DMA],
        fetched=(1, 2),
        count=3,
        moved=4 << 20,
    )(merge_weight, in_hbm(merge_bias), hidden)
    sums = shape(4, units, groups, dtype=F32)
    one, two, far = swap(hidden, 4), swap(hidden, 2), swap(hidden, 6)
    first = kernel(merge_first_kernel, "merge_first", sums, count=5, flops=1, moved=1)(
        hidden, one, two, merge_weight, ends
    )
    near = [swap(after(hidden, ends), 1), swap(one, 1), swap(two, 1)]
    second = kernel(merge_second_kernel, "merge_second", sums, count=6, flops=1, moved=1)(
        *near, first, merge_weight, ends
    )
    return kernel(
        merge_kernel,
        "merge",
        shape(1, units, groups),
        [pltpu.VMEM((units, groups), BF16), pltpu.SemaphoreType.DMA((2,))],
        out=pl.ANY,
        count=ROWS + 5,
        flops=4 * units * groups * MAIN,
        moved=8 << 20,
    )(hidden, one, two, *near, far, swap(after(far, first, *near), 1), second, merge_weight, ends, bias, live)


def solution(mesh):
    in_specs = (
        P("page", "row", None),
        P("page", "row", None),
        P("page", None),
        P(),
        P("row", None),
        P("row"),
        P("page", None),
    )
    out_specs = P("page", "row", None)
    local = local_eight if mesh.shape["row"] == 8 and mesh.shape["page"] == 4 else local_any
    return jax.shard_map(local, mesh=mesh, in_specs=in_specs, out_specs=out_specs, check_vma=False)
```

```python
import functools
import math

import jax
import jax.numpy as jnp
from jax import lax
from jax.experimental import pallas as pl
from jax.experimental.pallas import tpu as pltpu
from jax.sharding import PartitionSpec as P

D = 1280
HEADS = 16
HDIM = 80


def local_any(qkv_rows, residual, out_weight, norm_gain, merge_weight, merge_bias, page_grid):
    row_count = lax.axis_size("row")
    q_split = max(1, row_count // HEADS)
    head_groups = row_count // q_split
    width = D // head_groups
    heads_per = width // HDIM
    band_len = qkv_rows.shape[1]
    part_len = band_len // q_split
    local_qkv = qkv_rows[0]
    queries = local_qkv[:, :D]
    key_vals = jnp.concatenate(
        [
            local_qkv[:, D : 2 * D].reshape(band_len, head_groups, width),
            local_qkv[:, 2 * D :].reshape(band_len, head_groups, width),
        ],
        axis=2,
    )
    q_send = (
        queries.reshape(q_split, part_len, head_groups, width)
        .transpose(2, 0, 1, 3)
        .reshape(row_count, part_len, width)
    )
    kv_send = jnp.broadcast_to(
        key_vals.transpose(1, 0, 2)[:, None], (head_groups, q_split, band_len, 2 * width)
    )
    kv_send = kv_send.reshape(row_count, band_len, 2 * width)
    q_recv, kv_recv = (
        lax.all_to_all(q_send, "row", split_axis=0, concat_axis=1, tiled=True),
        lax.all_to_all(kv_send, "row", split_axis=0, concat_axis=1, tiled=True),
    )
    kv_local = kv_recv[0]
    positions = jnp.arange(row_count * band_len, dtype=jnp.int32)
    valid_len = page_grid[0, 0] * page_grid[0, 1]
    key_valid = positions < valid_len
    key_total = kv_local.shape[0]
    key_heads = kv_local[:, :width].reshape(key_total, heads_per, HDIM)
    value_heads = kv_local[:, width:].reshape(key_total, heads_per, HDIM)
    query_total = row_count * part_len
    q_block = math.gcd(query_total, 512)
    q_blocks = q_recv[0].reshape(query_total // q_block, q_block, heads_per, HDIM)
    root_dim = math.sqrt(HDIM)

    def attend(q_span):
        scores = (
            jnp.einsum("qhd,khd->hqk", q_span, key_heads, preferred_element_type=jnp.float32)
            / root_dim
        )
        scores = jnp.where(key_valid[None, None, :], scores, -1e30)
        peak = jnp.max(scores, axis=2, keepdims=True)
        weights = jnp.exp(scores - peak)
        total = jnp.sum(weights, axis=2, keepdims=True)
        mixed = (
            jnp.einsum(
                "hqk,khd->hqd",
                weights.astype(jnp.bfloat16),
                value_heads,
                preferred_element_type=jnp.float32,
            )
            / total
        )
        return mixed.transpose(1, 0, 2).reshape(q_span.shape[0], width).astype(jnp.bfloat16)

    attn_heads = lax.map(attend, q_blocks).reshape(row_count, part_len, width)
    returned = lax.all_to_all(attn_heads, "row", split_axis=0, concat_axis=0, tiled=True)
    attn = (
        returned.reshape(head_groups, q_split, part_len, width)
        .transpose(1, 2, 0, 3)
        .reshape(band_len, D)
    )
    projected = jnp.dot(
        attn,
        lax.all_gather(out_weight, "page", axis=0, tiled=True),
        preferred_element_type=jnp.float32,
    )
    hidden = residual[0].astype(jnp.float32) + projected
    normed = (
        hidden * lax.rsqrt(jnp.mean(hidden * hidden, axis=1, keepdims=True) + 1e-06) * norm_gain
    ).astype(jnp.bfloat16)
    rows_n = page_grid[0, 0]
    cols_n = page_grid[0, 1]
    group_total = band_len * row_count // 4
    slots = jnp.arange(group_total, dtype=jnp.int32)
    half_cols = cols_n // 2
    live = slots < rows_n // 2 * half_cols
    first = jnp.where(live, 2 * (slots // half_cols) * cols_n + 2 * (slots % half_cols), 0)
    corners = [first, first + 1, first + cols_n, first + cols_n + 1]
    local_units = merge_weight.shape[0]
    page_all = lax.all_gather(normed, "row", axis=0, tiled=True)
    merged_sum = jnp.zeros((local_units, group_total), jnp.float32)
    for corner in range(4):
        picked = jnp.take(page_all, corners[corner], axis=0)
        merged_sum = merged_sum + jnp.einsum(
            "md,gd->mg",
            merge_weight[:, corner * D : (corner + 1) * D],
            picked,
            preferred_element_type=jnp.float32,
        )
    merged = jax.nn.gelu(merged_sum + merge_bias[:, None], approximate=False)
    merged = jnp.where(live[None, :], merged, 0.0).astype(jnp.bfloat16)
    return merged[None]


ROWS = 8
PAGES = 4
HPAIR = 2 * HDIM
WIDE = 128
REST = HPAIR - WIDE
MAIN = ROWS * WIDE
NOTES = 16
RECEIVERS = ((0, 0), (1, 1), (4, 2), (2, 4), (6, 6), (7, 7), (3, 5), (5, 3))
SENDERS = ((0, 0), (1, 1), (4, 2), (2, 4), (6, 6), (7, 7), (5, 3), (3, 5))
OWNERS = (0, 4, 2, 1, 5, 3, 6, 7)
ROOT = math.log2(math.e) / math.sqrt(HDIM)
BF16 = jnp.bfloat16
F32 = jnp.float32


def row_index():
    return lax.axis_index("row")


def steps(pairs):
    core = row_index() % 2
    return [even + (odd - even) * core for even, odd in pairs]


def pack_tail(wide):
    groups = wide.shape[0] // 4
    return jnp.concatenate([wide[at * groups : (at + 1) * groups] for at in range(4)], axis=1)


def spread_kernel(qkv_hbm, resid_hbm, weight_hbm, grid_hbm, *rest):
    outs = rest[:ROWS]
    chip_ref, slice_ref, grid_out, qkv, resid, main, tile, held, grid, sems = rest[ROWS:]
    me = row_index()
    depth = weight_hbm.shape[0]
    chip = pl.ds(pl.multiple_of(me // 2 * 2 * WIDE, 2 * WIDE), 2 * WIDE)
    ends = pl.ds(pl.multiple_of(MAIN + me // 4 * WIDE, WIDE), WIDE)
    part = qkv.shape[0] // 4
    copies = []
    for at in range(4):
        rows = pl.ds(at * part, part)
        copies.append(pltpu.make_async_copy(qkv_hbm.at[0, rows], qkv.at[rows], sems.at[at]))
    copies.append(pltpu.make_async_copy(resid_hbm.at[0], resid, sems.at[4]))
    copies.append(pltpu.make_async_copy(weight_hbm.at[:, chip], main, sems.at[5]))
    copies.append(pltpu.make_async_copy(weight_hbm.at[:, ends], tile, sems.at[6]))
    copies.append(pltpu.make_async_copy(grid_hbm, grid, sems.at[7]))
    for copy in copies:
        copy.start()
    for copy in copies:
        copy.wait()
    for dest in range(ROWS):
        at = dest * HPAIR
        parts = [qkv[:, part * D + at : part * D + at + HPAIR] for part in range(3)]
        parts.append(resid[:, dest * WIDE : (dest + 1) * WIDE])
        parts.append(resid[:, MAIN + dest * REST : MAIN + (dest + 1) * REST])
        held[dest] = jnp.concatenate(parts, axis=1)
    for step, out in zip(steps(RECEIVERS), outs):
        out[...] = held[me ^ step]
    low = me // 2 % 2 == 0
    size = depth + depth // 4
    for core in range(2):
        tail = jnp.where(low, tile[:, core * REST : (core + 1) * REST], tile[:, (core + 2) * REST : (core + 3) * REST])
        chip_ref[core * size : core * size + depth, :] = main[:, core * WIDE : (core + 1) * WIDE]
        chip_ref[core * size + depth : (core + 1) * size, :] = pack_tail(tail)
    slice_ref[...] = chip_ref[pl.ds(pl.multiple_of(me % 2 * size, 16), size), :]
    row = lax.broadcasted_iota(jnp.int32, grid_out.shape, 0)
    grid_out[...] = jnp.where(row == 0, grid[0, 0], grid[0, 1])


def layout_kernel(grid_ref, *rest):
    select_ref, keys_ref, live_ref = rest[-3:]
    rows_n, cols_n = grid_ref[:1, :1], grid_ref[1:2, :1]
    patches = select_ref.shape[0]
    groups = patches // 4
    half = cols_n >> 1
    count = (rows_n >> 1) * half
    slots = lax.broadcasted_iota(jnp.int32, (groups, 1), 0)
    line = jnp.floor((slots.astype(F32) + 0.5) / half.astype(F32)).astype(jnp.int32)
    first = 2 * line * cols_n + 2 * (slots - line * half)
    at = lax.broadcasted_iota(jnp.int32, (groups, patches), 1)
    for corner in range(4):
        wanted = jnp.where(slots < count, first + (corner // 2) * cols_n + corner % 2, -1)
        select_ref[corner * groups : (corner + 1) * groups, :] = jnp.where(at == wanted, 1.0, 0.0).astype(BF16)
    key = lax.broadcasted_iota(jnp.int32, keys_ref.shape, 1)
    keys_ref[...] = jnp.where(key < rows_n * cols_n, 0.0, -1e30)
    slot = lax.broadcasted_iota(jnp.int32, live_ref.shape, 1)
    live_ref[...] = jnp.where(slot < count, 1.0, 0.0)


def attend_kernel(select_ref, dead_ref, *rest):
    blocks = rest[:ROWS]
    out_ref, q_all, k_all, v_all = rest[-4:]
    me = row_index()
    band = blocks[0].shape[0]
    patches = band * ROWS
    for step, block in zip(steps(SENDERS), blocks):
        at = pl.ds(pl.multiple_of((me ^ step) * band, band), band)
        q_all[at, :] = block[:, :HPAIR]
        k_all[at, :] = block[:, HPAIR : 2 * HPAIR]
        v_all[at, :] = block[:, 2 * HPAIR : 3 * HPAIR]
    queries = jnp.dot(select_ref[...], q_all[...], preferred_element_type=F32).astype(BF16)
    lane = lax.broadcasted_iota(jnp.int32, (1, HPAIR), 1)
    keys, values, dead = k_all[...], v_all[...], dead_ref[...]
    mixed = []
    for head in range(2):
        mine = (lane >= head * HDIM) & (lane < (head + 1) * HDIM)
        asked = jnp.where(mine, queries, jnp.zeros_like(queries))
        scores = lax.dot_general(asked, keys, (((1,), (1,)), ((), ())), preferred_element_type=F32) + dead
        weights = jnp.exp2((scores - jnp.max(scores, axis=1, keepdims=True)) * ROOT)
        total = jnp.sum(weights, axis=1, keepdims=True)
        mixed.append(jnp.dot(weights.astype(BF16), values, preferred_element_type=F32) * (1.0 / total))
    attn = jnp.where(lane < HDIM, mixed[0], mixed[1])
    out_ref[:patches, :] = attn[:, :WIDE].astype(BF16)
    out_ref[patches:, :] = pack_tail(attn[:, WIDE:]).astype(BF16)


def weight_rows(cut):
    depth = 2 * HPAIR
    packed = cut[depth:]
    tail = jnp.concatenate([packed[:, at * REST : (at + 1) * REST] for at in range(4)], axis=0)
    whole = jnp.concatenate([cut[:depth], tail], axis=1)
    return [whole[core * HPAIR : (core + 1) * HPAIR] for core in range(2)]


def place_rows(rows, base, main_ref, tail_ref):
    for core in range(2):
        pair = base + core
        main_ref[pl.ds(pl.multiple_of(pair * WIDE, WIDE), WIDE), :] = rows[core][:WIDE]
        for corner in range(4):
            spot = pl.multiple_of(pair * WIDE + corner * REST, REST)
            tail_ref[corner, pl.ds(spot, REST), :] = rows[core][WIDE:]


def ready_kernel(select_ref, gain_hbm, token_ref, *rest):
    del token_ref
    blocks = rest[:ROWS]
    own_ref, across_ref, near_ref = rest[ROWS : ROWS + 3]
    resid_ref, gain_out, main_ref, tail_ref, held, line, sem = rest[-7:]
    fetch = pltpu.make_async_copy(gain_hbm, line, sem)
    fetch.start()
    me = row_index()
    band = blocks[0].shape[0]
    for step, block in zip(steps(SENDERS), blocks):
        at = pl.ds(pl.multiple_of((me ^ step) * band, band), band)
        held[at, :] = block[:, 3 * HPAIR :]
    resid_ref[...] = jnp.dot(select_ref[...], held[...], preferred_element_type=F32)
    core = me % 2
    size = own_ref.shape[0]
    half = pl.ds(pl.multiple_of(core * size, 16), size)
    main_ref[...] = jnp.zeros_like(main_ref)
    tail_ref[...] = jnp.zeros_like(tail_ref)
    cuts = [(0, own_ref[...]), (2, across_ref[...]), (3 - 2 * core, near_ref[half, :])]
    place_slices(cuts, main_ref, tail_ref)
    fetch.wait()
    whole = line[...].reshape(1, D)
    gain = jnp.zeros(gain_out.shape, F32)
    for pair in range(ROWS):
        parts = [whole[:, pair * WIDE : (pair + 1) * WIDE]]
        parts.append(whole[:, MAIN + pair * REST : MAIN + (pair + 1) * REST])
        gain = jnp.where(me == pair, jnp.concatenate(parts, axis=1), gain)
    gain_out[...] = gain


def place_slices(cuts, main_ref, tail_ref):
    for step, cut in cuts:
        place_rows(weight_rows(cut), 2 * lax.rem(lax.axis_index("page") + step, PAGES), main_ref, tail_ref)


def last_kernel(swapped_ref, main_before_ref, tail_before_ref, main_ref, tail_ref):
    main_ref[...] = main_before_ref[...]
    tail_ref[...] = tail_before_ref[...]
    core = row_index() % 2
    size = swapped_ref.shape[0] // 2
    half = pl.ds(pl.multiple_of(core * size, 16), size)
    place_slices([(1 + 2 * core, swapped_ref[half, :])], main_ref, tail_ref)


def far_block():
    me = row_index()
    return pl.ds(pl.multiple_of((me // 2 ^ 3) * 2 * WIDE, 2 * WIDE), 2 * WIDE)


def collect_late(same, other):
    core = row_index() % 2
    left = jnp.where(core == 0, same[...], other[...])
    right = jnp.where(core == 0, other[...], same[...])
    return jnp.concatenate([left, right], axis=1)


def add_features(owners, pieces, weights, before_ref, out_ref):
    main_ref, tail_ref = weights
    me = row_index()
    patches = out_ref.shape[0]
    groups = patches // 4
    mains, tails = [], []
    for step in owners:
        pair = me ^ step
        columns = pl.ds(pl.multiple_of(pair * WIDE, WIDE), WIDE)
        mains.append(main_ref[columns, :])
        tails.append([tail_ref[at, columns, :] for at in range(4)])
    rows = jnp.concatenate([piece[...] for piece in pieces], axis=1)
    base = before_ref[...] + jnp.dot(rows[:patches], jnp.concatenate(mains, axis=0), preferred_element_type=F32)
    for corner in range(4):
        span = slice(corner * groups, (corner + 1) * groups)
        tail = jnp.concatenate([tail[corner] for tail in tails], axis=0)
        out_ref[span, :] = base[span] + jnp.dot(rows[patches:], tail, preferred_element_type=F32)


def project_first_kernel(*rest):
    add_features(OWNERS[:3], rest[:3], rest[3:5], *rest[5:])


def project_second_kernel(*rest):
    add_features(OWNERS[3:6], rest[:3], rest[3:5], *rest[5:])


def project_kernel(*rest):
    same, other, base_ref, main_ref, tail_ref, gain_ref, out_ref = rest
    patches = base_ref.shape[0]
    groups = patches // 4
    block = far_block()
    full = collect_late(same, other)
    base = base_ref[...] + jnp.dot(full[:patches], main_ref[block, :], preferred_element_type=F32)
    hidden = []
    for corner in range(4):
        span = slice(corner * groups, (corner + 1) * groups)
        hidden.append(base[span] + jnp.dot(full[patches:], tail_ref[corner, block, :], preferred_element_type=F32))
    squares = jnp.concatenate([(rows * rows).astype(BF16) for rows in hidden], axis=0)
    sums = lax.dot_general(
        jnp.ones((NOTES, HPAIR), BF16), squares, (((1,), (1,)), ((), ())), preferred_element_type=F32
    )
    row = lax.broadcasted_iota(jnp.int32, (NOTES, groups), 0)
    notes = jnp.zeros((NOTES, groups), F32)
    ends = []
    for corner in range(4):
        total = sums[:, corner * groups : (corner + 1) * groups]
        coarse = total.astype(BF16).astype(F32)
        notes = jnp.where(row == corner, coarse, jnp.where(row == 4 + corner, total - coarse, notes))
        sent = hidden[corner] * gain_ref[...]
        out_ref[corner * groups : (corner + 1) * groups, :] = sent[:, :WIDE].astype(BF16)
        ends.append(sent[:, WIDE:])
    out_ref[patches : patches + groups, :] = jnp.concatenate(ends, axis=1).astype(BF16)
    out_ref[patches + groups :, :] = notes.astype(BF16)


def tail_kernel(weight_ref, bias_hbm, token_ref, out_ref, bias_out, line, sem):
    del token_ref
    fetch = pltpu.make_async_copy(bias_hbm, line, sem)
    fetch.start()
    for pair in range(ROWS):
        cut = [corner * D + MAIN + pair * REST for corner in range(4)]
        out_ref[:, pair * WIDE : (pair + 1) * WIDE] = jnp.concatenate(
            [weight_ref[:, at : at + REST] for at in cut], axis=1
        )
    fetch.wait()
    units = bias_out.shape[0]
    bias_out[...] = jnp.broadcast_to(line[...].reshape(1, units), (8, units)).T[:, :1]


def merge_product(weight_ref, corner, groups, pieces):
    me = row_index()
    spots = [pl.multiple_of(corner * D + (me ^ step) * WIDE, WIDE) for step, _ in pieces]
    span = slice(corner * groups, (corner + 1) * groups)
    return lax.dot_general(
        jnp.concatenate([weight_ref[:, pl.ds(spot, WIDE)] for spot in spots], axis=1),
        jnp.concatenate([piece[span, :] for _, piece in pieces], axis=1),
        (((1,), (1,)), ((), ())),
        preferred_element_type=F32,
    )


def tail_products(tail_ref, groups, pieces):
    me = row_index()
    columns = [tail_ref[:, pl.ds(pl.multiple_of((me ^ step) * WIDE, WIDE), WIDE)] for step, _ in pieces]
    tails = jnp.concatenate(columns, axis=1)
    ends = jnp.concatenate([piece[4 * groups : 5 * groups, :] for _, piece in pieces], axis=1)
    corner_of = lax.rem(lax.broadcasted_iota(jnp.int32, (1, ends.shape[1]), 1), WIDE) // REST
    return [
        lax.dot_general(
            tails,
            jnp.where(corner_of == corner, ends, jnp.zeros_like(ends)),
            (((1,), (1,)), ((), ())),
            preferred_element_type=F32,
        )
        for corner in range(4)
    ]


def merge_first_kernel(*rest):
    pieces, (weight_ref, tail_ref, sum_ref) = list(zip(OWNERS[:3], rest[:3])), rest[3:]
    groups = sum_ref.shape[2]
    for corner, tail in enumerate(tail_products(tail_ref, groups, pieces)):
        sum_ref[corner] = tail + merge_product(weight_ref, corner, groups, pieces)


def merge_second_kernel(*rest):
    pieces, (before_ref, weight_ref, tail_ref, sum_ref) = list(zip(OWNERS[3:6], rest[:3])), rest[3:]
    groups = sum_ref.shape[2]
    for corner, tail in enumerate(tail_products(tail_ref, groups, pieces)):
        sum_ref[corner] = before_ref[corner] + (tail + merge_product(weight_ref, corner, groups, pieces))


def merge_kernel(*rest):
    pieces = rest[:ROWS]
    before_ref, weight_ref, tail_ref, bias_ref, live_ref, out_hbm, held, sems = rest[ROWS:]
    me = row_index()
    groups = live_ref.shape[1]
    patches = 4 * groups
    contract = (((1,), (1,)), ((), ()))
    block = pl.multiple_of((me // 2 ^ 3) * 2 * WIDE, 2 * WIDE)
    rows = collect_late(pieces[6], pieces[7])
    notes = jnp.zeros((NOTES, groups), F32)
    for piece in pieces:
        notes = notes + piece[patches + groups :, :].astype(F32)
    scale = lax.rsqrt((notes[:4] + notes[4:8]) * (1.0 / D) + 1e-06)
    spread = jnp.concatenate([jnp.broadcast_to(scale[at : at + 1], (REST, groups)) for at in range(4)], axis=0).T
    ends = rows[patches : patches + groups].astype(F32) * jnp.concatenate([spread] * 2, axis=1)
    ends = ends.astype(BF16)
    half = held.shape[0] // 2
    copies = []
    for at in range(2):
        units = slice(at * half, (at + 1) * half)
        total = bias_ref[units, :] + lax.dot_general(
            tail_ref[units, pl.ds(block, 2 * WIDE)], ends, contract, preferred_element_type=F32
        )
        for corner in range(4):
            part = before_ref[corner, units] + lax.dot_general(
                weight_ref[units, pl.ds(pl.multiple_of(corner * D + block, 2 * WIDE), 2 * WIDE)],
                rows[corner * groups : (corner + 1) * groups],
                contract,
                preferred_element_type=F32,
            )
            total = total + scale[corner : corner + 1] * part
        merged = 0.5 * total * (1.0 + lax.erf(total * math.sqrt(0.5)))
        held[units, :] = jnp.where(live_ref[...] > 0.0, merged, 0.0).astype(BF16)
        copies.append(pltpu.make_async_copy(held.at[units], out_hbm.at[0, units], sems.at[at]))
        copies[at].start()
    for copy in copies:
        copy.wait()


def kernel(body, name, out_shape, scratch=(), fetched=(), count=0, limit=24, flops=0, moved=0, out=pltpu.VMEM):
    specs = [pl.BlockSpec(memory_space=pltpu.VMEM) for _ in range(count)]
    for at in fetched:
        specs[at] = pl.BlockSpec(memory_space=pl.ANY)
    return pl.pallas_call(
        body,
        out_shape=out_shape,
        in_specs=specs,
        out_specs=jax.tree.map(lambda _: pl.BlockSpec(memory_space=out), out_shape),
        scratch_shapes=list(scratch),
        compiler_params=pltpu.CompilerParams(vmem_limit_bytes=limit * 1024 * 1024),
        cost_estimate=pl.CostEstimate(flops=flops, bytes_accessed=moved, transcendentals=0),
        name=name,
    )


def in_hbm(value):
    return pltpu.with_memory_space_constraint(value, pltpu.HBM)


def shape(*dims, dtype=BF16):
    return jax.ShapeDtypeStruct(dims, dtype)


def swap(value, even, odd=None):
    odd = even if odd is None else odd
    return lax.ppermute(value, "row", [(row, row ^ (odd if row % 2 else even)) for row in range(ROWS)])


def turn(value, low, high):
    pairs = [
        (page * ROWS + row, (page + (high if row % 2 else low)) % PAGES * ROWS + row)
        for page in range(PAGES)
        for row in range(ROWS)
    ]
    return lax.ppermute(value, ("page", "row"), pairs)


def after(value, *arrays):
    return lax.optimization_barrier((value, *arrays))[0]


def local_eight(qkv_rows, residual, out_weight, norm_gain, merge_weight, merge_bias, page_grid):
    band = qkv_rows.shape[1]
    patches = band * ROWS
    groups = patches // 4
    units = merge_weight.shape[0]
    depth = out_weight.shape[0]
    piece = patches + groups
    size = depth + depth // 4

    *sends, chip, own, grid = kernel(
        spread_kernel,
        "spread",
        [shape(band, 4 * HPAIR)] * ROWS
        + [shape(2 * size, WIDE), shape(size, WIDE), shape(8, WIDE, dtype=jnp.int32)],
        [
            pltpu.VMEM((band, 3 * D), BF16),
            pltpu.VMEM((band, D), BF16),
            pltpu.VMEM((depth, 2 * WIDE), BF16),
            pltpu.VMEM((depth, WIDE), BF16),
            pltpu.VMEM((ROWS, band, 4 * HPAIR), BF16),
            pltpu.SMEM(page_grid.shape, jnp.int32),
            pltpu.SemaphoreType.DMA((8,)),
        ],
        fetched=range(4),
        count=4,
        moved=1 << 20,
    )(in_hbm(qkv_rows), in_hbm(residual), in_hbm(out_weight), in_hbm(page_grid))
    blocks = [sends[0]] + [swap(send, *pair) for send, pair in zip(sends[1:], RECEIVERS[1:])]
    select, dead, live = kernel(
        layout_kernel,
        "layout",
        [shape(patches, patches), shape(1, patches, dtype=F32), shape(1, groups, dtype=F32)],
        fetched=range(1, 1 + 2),
        count=1 + 2,
        moved=1 << 20,
    )(grid, *blocks[1:3])
    near = turn(after(chip, *()), 1, PAGES - 1)
    swapped = swap(near, 1)
    attn = kernel(
        attend_kernel,
        "attend",
        shape(piece, WIDE),
        [pltpu.VMEM((patches, HPAIR), BF16)] * 3,
        count=2 + ROWS,
        flops=20 * patches * patches * 4096,
        moved=1 << 20,
    )(select, dead, *blocks)
    across = turn(own, 2, 2)
    resid, own_gain, main, tail = kernel(
        ready_kernel,
        "ready",
        [shape(patches, HPAIR, dtype=F32), shape(1, HPAIR, dtype=F32), shape(MAIN, HPAIR), shape(4, MAIN, HPAIR)],
        [pltpu.VMEM((patches, HPAIR), BF16), pltpu.VMEM((D,), F32), pltpu.SemaphoreType.DMA],
        fetched=(1, 2),
        count=3 + ROWS + 3,
        flops=10 * patches * patches * 4096,
        moved=4 << 20,
    )(select, in_hbm(norm_gain), attn, *blocks, own, across, near)
    one, two, far = swap(attn, 4), swap(attn, 2), swap(attn, 6)
    last = kernel(
        last_kernel,
        "ready_last",
        [shape(MAIN, HPAIR), shape(4, MAIN, HPAIR)],
        count=3,
        flops=1,
        moved=1,
    )(swapped, main, tail)
    near = [swap(after(attn, main), 1), swap(after(one, last[0]), 1), swap(two, 1)]
    weights = tuple(last)
    rows = shape(patches, HPAIR, dtype=F32)
    first = kernel(project_first_kernel, "project_first", rows, count=6, flops=1, moved=1)(attn, one, two, *weights, resid)
    second = kernel(project_second_kernel, "project_second", rows, count=6, flops=1, moved=1)(*near, *weights, first)
    hidden = kernel(
        project_kernel,
        "project",
        shape(piece + NOTES, WIDE),
        count=2 + 4,
        flops=patches * MAIN * 256,
        moved=4 << 20,
    )(far, swap(after(far, first), 1), second, *weights, own_gain)
    ends, bias = kernel(
        tail_kernel,
        "merge_tail",
        [shape(units, MAIN), shape(units, 1, dtype=F32)],
        [pltpu.VMEM((units,), F32), pltpu.SemaphoreType.DMA],
        fetched=(1, 2),
        count=3,
        moved=4 << 20,
    )(merge_weight, in_hbm(merge_bias), hidden)
    sums = shape(4, units, groups, dtype=F32)
    one, two, far = swap(hidden, 4), swap(hidden, 2), swap(hidden, 6)
    first = kernel(merge_first_kernel, "merge_first", sums, count=5, flops=1, moved=1)(
        hidden, one, two, merge_weight, ends
    )
    near = [swap(after(hidden, ends), 1), swap(one, 1), swap(two, 1)]
    second = kernel(merge_second_kernel, "merge_second", sums, count=6, flops=1, moved=1)(
        *near, first, merge_weight, ends
    )
    return kernel(
        merge_kernel,
        "merge",
        shape(1, units, groups),
        [pltpu.VMEM((units, groups), BF16), pltpu.SemaphoreType.DMA((2,))],
        out=pl.ANY,
        count=ROWS + 5,
        flops=4 * units * groups * MAIN,
        moved=8 << 20,
    )(hidden, one, two, *near, far, swap(after(far, first, *near), 1), second, merge_weight, ends, bias, live)


def solution(mesh):
    in_specs = (
        P("page", "row", None),
        P("page", "row", None),
        P("page", None),
        P(),
        P("row", None),
        P("row"),
        P("page", None),
    )
    out_specs = P("page", "row", None)
    local = local_eight if mesh.shape["row"] == 8 and mesh.shape["page"] == 4 else local_any
    return jax.shard_map(local, mesh=mesh, in_specs=in_specs, out_specs=out_specs, check_vma=False)
```

```python
import functools
import math

import jax
import jax.numpy as jnp
from jax import lax
from jax.experimental import pallas as pl
from jax.experimental.pallas import tpu as pltpu
from jax.sharding import PartitionSpec as P

D = 1280
HEADS = 16
HDIM = 80


def local_any(qkv_rows, residual, out_weight, norm_gain, merge_weight, merge_bias, page_grid):
    row_count = lax.axis_size("row")
    q_split = max(1, row_count // HEADS)
    head_groups = row_count // q_split
    width = D // head_groups
    heads_per = width // HDIM
    band_len = qkv_rows.shape[1]
    part_len = band_len // q_split
    local_qkv = qkv_rows[0]
    queries = local_qkv[:, :D]
    key_vals = jnp.concatenate(
        [
            local_qkv[:, D : 2 * D].reshape(band_len, head_groups, width),
            local_qkv[:, 2 * D :].reshape(band_len, head_groups, width),
        ],
        axis=2,
    )
    q_send = (
        queries.reshape(q_split, part_len, head_groups, width)
        .transpose(2, 0, 1, 3)
        .reshape(row_count, part_len, width)
    )
    kv_send = jnp.broadcast_to(
        key_vals.transpose(1, 0, 2)[:, None], (head_groups, q_split, band_len, 2 * width)
    )
    kv_send = kv_send.reshape(row_count, band_len, 2 * width)
    q_recv, kv_recv = (
        lax.all_to_all(q_send, "row", split_axis=0, concat_axis=1, tiled=True),
        lax.all_to_all(kv_send, "row", split_axis=0, concat_axis=1, tiled=True),
    )
    kv_local = kv_recv[0]
    positions = jnp.arange(row_count * band_len, dtype=jnp.int32)
    valid_len = page_grid[0, 0] * page_grid[0, 1]
    key_valid = positions < valid_len
    key_total = kv_local.shape[0]
    key_heads = kv_local[:, :width].reshape(key_total, heads_per, HDIM)
    value_heads = kv_local[:, width:].reshape(key_total, heads_per, HDIM)
    query_total = row_count * part_len
    q_block = math.gcd(query_total, 512)
    q_blocks = q_recv[0].reshape(query_total // q_block, q_block, heads_per, HDIM)
    root_dim = math.sqrt(HDIM)

    def attend(q_span):
        scores = (
            jnp.einsum("qhd,khd->hqk", q_span, key_heads, preferred_element_type=jnp.float32)
            / root_dim
        )
        scores = jnp.where(key_valid[None, None, :], scores, -1e30)
        peak = jnp.max(scores, axis=2, keepdims=True)
        weights = jnp.exp(scores - peak)
        total = jnp.sum(weights, axis=2, keepdims=True)
        mixed = (
            jnp.einsum(
                "hqk,khd->hqd",
                weights.astype(jnp.bfloat16),
                value_heads,
                preferred_element_type=jnp.float32,
            )
            / total
        )
        return mixed.transpose(1, 0, 2).reshape(q_span.shape[0], width).astype(jnp.bfloat16)

    attn_heads = lax.map(attend, q_blocks).reshape(row_count, part_len, width)
    returned = lax.all_to_all(attn_heads, "row", split_axis=0, concat_axis=0, tiled=True)
    attn = (
        returned.reshape(head_groups, q_split, part_len, width)
        .transpose(1, 2, 0, 3)
        .reshape(band_len, D)
    )
    projected = jnp.dot(
        attn,
        lax.all_gather(out_weight, "page", axis=0, tiled=True),
        preferred_element_type=jnp.float32,
    )
    hidden = residual[0].astype(jnp.float32) + projected
    normed = (
        hidden * lax.rsqrt(jnp.mean(hidden * hidden, axis=1, keepdims=True) + 1e-06) * norm_gain
    ).astype(jnp.bfloat16)
    rows_n = page_grid[0, 0]
    cols_n = page_grid[0, 1]
    group_total = band_len * row_count // 4
    slots = jnp.arange(group_total, dtype=jnp.int32)
    half_cols = cols_n // 2
    live = slots < rows_n // 2 * half_cols
    first = jnp.where(live, 2 * (slots // half_cols) * cols_n + 2 * (slots % half_cols), 0)
    corners = [first, first + 1, first + cols_n, first + cols_n + 1]
    local_units = merge_weight.shape[0]
    page_all = lax.all_gather(normed, "row", axis=0, tiled=True)
    merged_sum = jnp.zeros((local_units, group_total), jnp.float32)
    for corner in range(4):
        picked = jnp.take(page_all, corners[corner], axis=0)
        merged_sum = merged_sum + jnp.einsum(
            "md,gd->mg",
            merge_weight[:, corner * D : (corner + 1) * D],
            picked,
            preferred_element_type=jnp.float32,
        )
    merged = jax.nn.gelu(merged_sum + merge_bias[:, None], approximate=False)
    merged = jnp.where(live[None, :], merged, 0.0).astype(jnp.bfloat16)
    return merged[None]


ROWS = 8
PAGES = 4
HPAIR = 2 * HDIM
WIDE = 128
REST = HPAIR - WIDE
MAIN = ROWS * WIDE
NOTES = 16
RECEIVERS = ((0, 0), (1, 1), (4, 2), (6, 6), (2, 4), (7, 7), (3, 5), (5, 3))
SENDERS = ((0, 0), (1, 1), (4, 2), (6, 6), (2, 4), (7, 7), (5, 3), (3, 5))
OWNERS = (0, 4, 2, 1, 5, 3, 6, 7)
ROOT = math.log2(math.e) / math.sqrt(HDIM)
BF16 = jnp.bfloat16
F32 = jnp.float32


def row_index():
    return lax.axis_index("row")


def steps(pairs):
    core = row_index() % 2
    return [even + (odd - even) * core for even, odd in pairs]


def pack_tail(wide):
    groups = wide.shape[0] // 4
    return jnp.concatenate([wide[at * groups : (at + 1) * groups] for at in range(4)], axis=1)


def spread_kernel(qkv_hbm, resid_hbm, weight_hbm, grid_hbm, *rest):
    outs = rest[:ROWS]
    chip_ref, slice_ref, grid_out, qkv, resid, main, tile, held, grid, sems = rest[ROWS:]
    me = row_index()
    depth = weight_hbm.shape[0]
    chip = pl.ds(pl.multiple_of(me // 2 * 2 * WIDE, 2 * WIDE), 2 * WIDE)
    ends = pl.ds(pl.multiple_of(MAIN + me // 4 * WIDE, WIDE), WIDE)
    part = qkv.shape[0] // 4
    copies = []
    for at in range(4):
        rows = pl.ds(at * part, part)
        copies.append(pltpu.make_async_copy(qkv_hbm.at[0, rows], qkv.at[rows], sems.at[at]))
    copies.append(pltpu.make_async_copy(resid_hbm.at[0], resid, sems.at[4]))
    copies.append(pltpu.make_async_copy(weight_hbm.at[:, chip], main, sems.at[5]))
    copies.append(pltpu.make_async_copy(weight_hbm.at[:, ends], tile, sems.at[6]))
    copies.append(pltpu.make_async_copy(grid_hbm, grid, sems.at[7]))
    for copy in copies:
        copy.start()
    for copy in copies:
        copy.wait()
    for dest in range(ROWS):
        at = dest * HPAIR
        parts = [qkv[:, part * D + at : part * D + at + HPAIR] for part in range(3)]
        parts.append(resid[:, dest * WIDE : (dest + 1) * WIDE])
        parts.append(resid[:, MAIN + dest * REST : MAIN + (dest + 1) * REST])
        held[dest] = jnp.concatenate(parts, axis=1)
    for step, out in zip(steps(RECEIVERS), outs):
        out[...] = held[me ^ step]
    low = me // 2 % 2 == 0
    size = depth + depth // 4
    for core in range(2):
        tail = jnp.where(low, tile[:, core * REST : (core + 1) * REST], tile[:, (core + 2) * REST : (core + 3) * REST])
        chip_ref[core * size : core * size + depth, :] = main[:, core * WIDE : (core + 1) * WIDE]
        chip_ref[core * size + depth : (core + 1) * size, :] = pack_tail(tail)
    slice_ref[...] = chip_ref[pl.ds(pl.multiple_of(me % 2 * size, 16), size), :]
    row = lax.broadcasted_iota(jnp.int32, grid_out.shape, 0)
    grid_out[...] = jnp.where(row == 0, grid[0, 0], grid[0, 1])


def layout_kernel(grid_ref, *rest):
    select_ref, keys_ref, live_ref = rest[-3:]
    rows_n, cols_n = grid_ref[:1, :1], grid_ref[1:2, :1]
    patches = select_ref.shape[0]
    groups = patches // 4
    half = cols_n >> 1
    count = (rows_n >> 1) * half
    slots = lax.broadcasted_iota(jnp.int32, (groups, 1), 0)
    line = jnp.floor((slots.astype(F32) + 0.5) / half.astype(F32)).astype(jnp.int32)
    first = 2 * line * cols_n + 2 * (slots - line * half)
    at = lax.broadcasted_iota(jnp.int32, (groups, patches), 1)
    for corner in range(4):
        wanted = jnp.where(slots < count, first + (corner // 2) * cols_n + corner % 2, -1)
        select_ref[corner * groups : (corner + 1) * groups, :] = jnp.where(at == wanted, 1.0, 0.0).astype(BF16)
    key = lax.broadcasted_iota(jnp.int32, keys_ref.shape, 1)
    keys_ref[...] = jnp.where(key < rows_n * cols_n, 0.0, -1e30)
    slot = lax.broadcasted_iota(jnp.int32, live_ref.shape, 1)
    live_ref[...] = jnp.where(slot < count, 1.0, 0.0)


def attend_kernel(select_ref, dead_ref, *rest):
    blocks = rest[:ROWS]
    out_ref, q_all, k_all, v_all = rest[-4:]
    me = row_index()
    band = blocks[0].shape[0]
    patches = band * ROWS
    for step, block in zip(steps(SENDERS), blocks):
        at = pl.ds(pl.multiple_of((me ^ step) * band, band), band)
        q_all[at, :] = block[:, :HPAIR]
        k_all[at, :] = block[:, HPAIR : 2 * HPAIR]
        v_all[at, :] = block[:, 2 * HPAIR : 3 * HPAIR]
    queries = jnp.dot(select_ref[...], q_all[...], preferred_element_type=F32).astype(BF16)
    lane = lax.broadcasted_iota(jnp.int32, (1, HPAIR), 1)
    keys, values, dead = k_all[...], v_all[...], dead_ref[...]
    mixed = []
    for head in range(2):
        mine = (lane >= head * HDIM) & (lane < (head + 1) * HDIM)
        asked = jnp.where(mine, queries, jnp.zeros_like(queries))
        scores = lax.dot_general(asked, keys, (((1,), (1,)), ((), ())), preferred_element_type=F32) + dead
        weights = jnp.exp2((scores - jnp.max(scores, axis=1, keepdims=True)) * ROOT)
        total = jnp.sum(weights, axis=1, keepdims=True)
        mixed.append(jnp.dot(weights.astype(BF16), values, preferred_element_type=F32) * (1.0 / total))
    attn = jnp.where(lane < HDIM, mixed[0], mixed[1])
    out_ref[:patches, :] = attn[:, :WIDE].astype(BF16)
    out_ref[patches:, :] = pack_tail(attn[:, WIDE:]).astype(BF16)


def weight_rows(cut):
    depth = 2 * HPAIR
    packed = cut[depth:]
    tail = jnp.concatenate([packed[:, at * REST : (at + 1) * REST] for at in range(4)], axis=0)
    whole = jnp.concatenate([cut[:depth], tail], axis=1)
    return [whole[core * HPAIR : (core + 1) * HPAIR] for core in range(2)]


def place_rows(rows, base, main_ref, tail_ref):
    for core in range(2):
        pair = base + core
        main_ref[pl.ds(pl.multiple_of(pair * WIDE, WIDE), WIDE), :] = rows[core][:WIDE]
        for corner in range(4):
            spot = pl.multiple_of(pair * WIDE + corner * REST, REST)
            tail_ref[corner, pl.ds(spot, REST), :] = rows[core][WIDE:]


def ready_kernel(select_ref, gain_hbm, token_ref, *rest):
    del token_ref
    blocks = rest[:ROWS]
    own_ref, across_ref, near_ref = rest[ROWS : ROWS + 3]
    resid_ref, gain_out, main_ref, tail_ref, held, line, sem = rest[-7:]
    fetch = pltpu.make_async_copy(gain_hbm, line, sem)
    fetch.start()
    me = row_index()
    band = blocks[0].shape[0]
    for step, block in zip(steps(SENDERS), blocks):
        at = pl.ds(pl.multiple_of((me ^ step) * band, band), band)
        held[at, :] = block[:, 3 * HPAIR :]
    resid_ref[...] = jnp.dot(select_ref[...], held[...], preferred_element_type=F32)
    core = me % 2
    size = own_ref.shape[0]
    half = pl.ds(pl.multiple_of(core * size, 16), size)
    main_ref[...] = jnp.zeros_like(main_ref)
    tail_ref[...] = jnp.zeros_like(tail_ref)
    cuts = [(0, own_ref[...]), (2, across_ref[...]), (3 - 2 * core, near_ref[half, :])]
    place_slices(cuts, main_ref, tail_ref)
    fetch.wait()
    whole = line[...].reshape(1, D)
    gain = jnp.zeros(gain_out.shape, F32)
    for pair in range(ROWS):
        parts = [whole[:, pair * WIDE : (pair + 1) * WIDE]]
        parts.append(whole[:, MAIN + pair * REST : MAIN + (pair + 1) * REST])
        gain = jnp.where(me == pair, jnp.concatenate(parts, axis=1), gain)
    gain_out[...] = gain


def place_slices(cuts, main_ref, tail_ref):
    for step, cut in cuts:
        place_rows(weight_rows(cut), 2 * lax.rem(lax.axis_index("page") + step, PAGES), main_ref, tail_ref)


def last_kernel(swapped_ref, main_before_ref, tail_before_ref, main_ref, tail_ref):
    main_ref[...] = main_before_ref[...]
    tail_ref[...] = tail_before_ref[...]
    core = row_index() % 2
    size = swapped_ref.shape[0] // 2
    half = pl.ds(pl.multiple_of(core * size, 16), size)
    place_slices([(1 + 2 * core, swapped_ref[half, :])], main_ref, tail_ref)


def far_block():
    me = row_index()
    return pl.ds(pl.multiple_of((me // 2 ^ 3) * 2 * WIDE, 2 * WIDE), 2 * WIDE)


def collect_late(same, other):
    core = row_index() % 2
    left = jnp.where(core == 0, same[...], other[...])
    right = jnp.where(core == 0, other[...], same[...])
    return jnp.concatenate([left, right], axis=1)


def add_features(owners, pieces, weights, before_ref, out_ref):
    main_ref, tail_ref = weights
    me = row_index()
    patches = out_ref.shape[0]
    groups = patches // 4
    mains, tails = [], []
    for step in owners:
        pair = me ^ step
        columns = pl.ds(pl.multiple_of(pair * WIDE, WIDE), WIDE)
        mains.append(main_ref[columns, :])
        tails.append([tail_ref[at, columns, :] for at in range(4)])
    rows = jnp.concatenate([piece[...] for piece in pieces], axis=1)
    base = before_ref[...] + jnp.dot(rows[:patches], jnp.concatenate(mains, axis=0), preferred_element_type=F32)
    for corner in range(4):
        span = slice(corner * groups, (corner + 1) * groups)
        tail = jnp.concatenate([tail[corner] for tail in tails], axis=0)
        out_ref[span, :] = base[span] + jnp.dot(rows[patches:], tail, preferred_element_type=F32)


def project_first_kernel(*rest):
    add_features(OWNERS[:3], rest[:3], rest[3:5], *rest[5:])


def project_second_kernel(*rest):
    add_features(OWNERS[3:6], rest[:3], rest[3:5], *rest[5:])


def project_kernel(*rest):
    same, other, base_ref, main_ref, tail_ref, gain_ref, out_ref = rest
    patches = base_ref.shape[0]
    groups = patches // 4
    block = far_block()
    full = collect_late(same, other)
    base = base_ref[...] + jnp.dot(full[:patches], main_ref[block, :], preferred_element_type=F32)
    hidden = []
    for corner in range(4):
        span = slice(corner * groups, (corner + 1) * groups)
        hidden.append(base[span] + jnp.dot(full[patches:], tail_ref[corner, block, :], preferred_element_type=F32))
    squares = jnp.concatenate([(rows * rows).astype(BF16) for rows in hidden], axis=0)
    sums = lax.dot_general(
        jnp.ones((NOTES, HPAIR), BF16), squares, (((1,), (1,)), ((), ())), preferred_element_type=F32
    )
    row = lax.broadcasted_iota(jnp.int32, (NOTES, groups), 0)
    notes = jnp.zeros((NOTES, groups), F32)
    ends = []
    for corner in range(4):
        total = sums[:, corner * groups : (corner + 1) * groups]
        coarse = total.astype(BF16).astype(F32)
        notes = jnp.where(row == corner, coarse, jnp.where(row == 4 + corner, total - coarse, notes))
        sent = hidden[corner] * gain_ref[...]
        out_ref[corner * groups : (corner + 1) * groups, :] = sent[:, :WIDE].astype(BF16)
        ends.append(sent[:, WIDE:])
    out_ref[patches : patches + groups, :] = jnp.concatenate(ends, axis=1).astype(BF16)
    out_ref[patches + groups :, :] = notes.astype(BF16)


def tail_kernel(weight_ref, bias_hbm, token_ref, out_ref, bias_out, line, sem):
    del token_ref
    fetch = pltpu.make_async_copy(bias_hbm, line, sem)
    fetch.start()
    for pair in range(ROWS):
        cut = [corner * D + MAIN + pair * REST for corner in range(4)]
        out_ref[:, pair * WIDE : (pair + 1) * WIDE] = jnp.concatenate(
            [weight_ref[:, at : at + REST] for at in cut], axis=1
        )
    fetch.wait()
    units = bias_out.shape[0]
    bias_out[...] = jnp.broadcast_to(line[...].reshape(1, units), (8, units)).T[:, :1]


def merge_product(weight_ref, corner, groups, pieces):
    me = row_index()
    spots = [pl.multiple_of(corner * D + (me ^ step) * WIDE, WIDE) for step, _ in pieces]
    span = slice(corner * groups, (corner + 1) * groups)
    return lax.dot_general(
        jnp.concatenate([weight_ref[:, pl.ds(spot, WIDE)] for spot in spots], axis=1),
        jnp.concatenate([piece[span, :] for _, piece in pieces], axis=1),
        (((1,), (1,)), ((), ())),
        preferred_element_type=F32,
    )


def tail_products(tail_ref, groups, pieces):
    me = row_index()
    columns = [tail_ref[:, pl.ds(pl.multiple_of((me ^ step) * WIDE, WIDE), WIDE)] for step, _ in pieces]
    tails = jnp.concatenate(columns, axis=1)
    ends = jnp.concatenate([piece[4 * groups : 5 * groups, :] for _, piece in pieces], axis=1)
    corner_of = lax.rem(lax.broadcasted_iota(jnp.int32, (1, ends.shape[1]), 1), WIDE) // REST
    return [
        lax.dot_general(
            tails,
            jnp.where(corner_of == corner, ends, jnp.zeros_like(ends)),
            (((1,), (1,)), ((), ())),
            preferred_element_type=F32,
        )
        for corner in range(4)
    ]


def merge_first_kernel(*rest):
    pieces, (weight_ref, tail_ref, sum_ref) = list(zip(OWNERS[:3], rest[:3])), rest[3:]
    groups = sum_ref.shape[2]
    for corner, tail in enumerate(tail_products(tail_ref, groups, pieces)):
        sum_ref[corner] = tail + merge_product(weight_ref, corner, groups, pieces)


def merge_second_kernel(*rest):
    pieces, (before_ref, weight_ref, tail_ref, sum_ref) = list(zip(OWNERS[3:6], rest[:3])), rest[3:]
    groups = sum_ref.shape[2]
    for corner, tail in enumerate(tail_products(tail_ref, groups, pieces)):
        sum_ref[corner] = before_ref[corner] + (tail + merge_product(weight_ref, corner, groups, pieces))


def merge_kernel(*rest):
    pieces = rest[:ROWS]
    before_ref, weight_ref, tail_ref, bias_ref, live_ref, out_hbm, held, sems = rest[ROWS:]
    me = row_index()
    groups = live_ref.shape[1]
    patches = 4 * groups
    contract = (((1,), (1,)), ((), ()))
    block = pl.multiple_of((me // 2 ^ 3) * 2 * WIDE, 2 * WIDE)
    rows = collect_late(pieces[6], pieces[7])
    notes = jnp.zeros((NOTES, groups), F32)
    for piece in pieces:
        notes = notes + piece[patches + groups :, :].astype(F32)
    scale = lax.rsqrt((notes[:4] + notes[4:8]) * (1.0 / D) + 1e-06)
    spread = jnp.concatenate([jnp.broadcast_to(scale[at : at + 1], (REST, groups)) for at in range(4)], axis=0).T
    ends = rows[patches : patches + groups].astype(F32) * jnp.concatenate([spread] * 2, axis=1)
    ends = ends.astype(BF16)
    half = held.shape[0] // 2
    copies = []
    for at in range(2):
        units = slice(at * half, (at + 1) * half)
        total = bias_ref[units, :] + lax.dot_general(
            tail_ref[units, pl.ds(block, 2 * WIDE)], ends, contract, preferred_element_type=F32
        )
        for corner in range(4):
            part = before_ref[corner, units] + lax.dot_general(
                weight_ref[units, pl.ds(pl.multiple_of(corner * D + block, 2 * WIDE), 2 * WIDE)],
                rows[corner * groups : (corner + 1) * groups],
                contract,
                preferred_element_type=F32,
            )
            total = total + scale[corner : corner + 1] * part
        merged = 0.5 * total * (1.0 + lax.erf(total * math.sqrt(0.5)))
        held[units, :] = jnp.where(live_ref[...] > 0.0, merged, 0.0).astype(BF16)
        copies.append(pltpu.make_async_copy(held.at[units], out_hbm.at[0, units], sems.at[at]))
        copies[at].start()
    for copy in copies:
        copy.wait()


def kernel(body, name, out_shape, scratch=(), fetched=(), count=0, limit=24, flops=0, moved=0, out=pltpu.VMEM):
    specs = [pl.BlockSpec(memory_space=pltpu.VMEM) for _ in range(count)]
    for at in fetched:
        specs[at] = pl.BlockSpec(memory_space=pl.ANY)
    return pl.pallas_call(
        body,
        out_shape=out_shape,
        in_specs=specs,
        out_specs=jax.tree.map(lambda _: pl.BlockSpec(memory_space=out), out_shape),
        scratch_shapes=list(scratch),
        compiler_params=pltpu.CompilerParams(vmem_limit_bytes=limit * 1024 * 1024),
        cost_estimate=pl.CostEstimate(flops=flops, bytes_accessed=moved, transcendentals=0),
        name=name,
    )


def in_hbm(value):
    return pltpu.with_memory_space_constraint(value, pltpu.HBM)


def shape(*dims, dtype=BF16):
    return jax.ShapeDtypeStruct(dims, dtype)


def swap(value, even, odd=None):
    odd = even if odd is None else odd
    return lax.ppermute(value, "row", [(row, row ^ (odd if row % 2 else even)) for row in range(ROWS)])


def turn(value, low, high):
    pairs = [
        (page * ROWS + row, (page + (high if row % 2 else low)) % PAGES * ROWS + row)
        for page in range(PAGES)
        for row in range(ROWS)
    ]
    return lax.ppermute(value, ("page", "row"), pairs)


def after(value, *arrays):
    return lax.optimization_barrier((value, *arrays))[0]


def local_eight(qkv_rows, residual, out_weight, norm_gain, merge_weight, merge_bias, page_grid):
    band = qkv_rows.shape[1]
    patches = band * ROWS
    groups = patches // 4
    units = merge_weight.shape[0]
    depth = out_weight.shape[0]
    piece = patches + groups
    size = depth + depth // 4

    *sends, chip, own, grid = kernel(
        spread_kernel,
        "spread",
        [shape(band, 4 * HPAIR)] * ROWS
        + [shape(2 * size, WIDE), shape(size, WIDE), shape(8, WIDE, dtype=jnp.int32)],
        [
            pltpu.VMEM((band, 3 * D), BF16),
            pltpu.VMEM((band, D), BF16),
            pltpu.VMEM((depth, 2 * WIDE), BF16),
            pltpu.VMEM((depth, WIDE), BF16),
            pltpu.VMEM((ROWS, band, 4 * HPAIR), BF16),
            pltpu.SMEM(page_grid.shape, jnp.int32),
            pltpu.SemaphoreType.DMA((8,)),
        ],
        fetched=range(4),
        count=4,
        moved=1 << 20,
    )(in_hbm(qkv_rows), in_hbm(residual), in_hbm(out_weight), in_hbm(page_grid))
    blocks = [sends[0]] + [swap(send, *pair) for send, pair in zip(sends[1:], RECEIVERS[1:])]
    select, dead, live = kernel(
        layout_kernel,
        "layout",
        [shape(patches, patches), shape(1, patches, dtype=F32), shape(1, groups, dtype=F32)],
        fetched=range(1, 1 + 2),
        count=1 + 2,
        moved=1 << 20,
    )(grid, *blocks[1:3])
    near = turn(after(chip, *()), 1, PAGES - 1)
    swapped = swap(near, 1)
    attn = kernel(
        attend_kernel,
        "attend",
        shape(piece, WIDE),
        [pltpu.VMEM((patches, HPAIR), BF16)] * 3,
        count=2 + ROWS,
        flops=20 * patches * patches * 4096,
        moved=1 << 20,
    )(select, dead, *blocks)
    across = turn(own, 2, 2)
    resid, own_gain, main, tail = kernel(
        ready_kernel,
        "ready",
        [shape(patches, HPAIR, dtype=F32), shape(1, HPAIR, dtype=F32), shape(MAIN, HPAIR), shape(4, MAIN, HPAIR)],
        [pltpu.VMEM((patches, HPAIR), BF16), pltpu.VMEM((D,), F32), pltpu.SemaphoreType.DMA],
        fetched=(1, 2),
        count=3 + ROWS + 3,
        flops=10 * patches * patches * 4096,
        moved=4 << 20,
    )(select, in_hbm(norm_gain), attn, *blocks, own, across, near)
    one, two, far = swap(attn, 4), swap(attn, 2), swap(attn, 6)
    last = kernel(
        last_kernel,
        "ready_last",
        [shape(MAIN, HPAIR), shape(4, MAIN, HPAIR)],
        count=3,
        flops=1,
        moved=1,
    )(swapped, main, tail)
    near = [swap(after(attn, main), 1), swap(after(one, last[0]), 1), swap(two, 1)]
    weights = tuple(last)
    rows = shape(patches, HPAIR, dtype=F32)
    first = kernel(project_first_kernel, "project_first", rows, count=6, flops=1, moved=1)(attn, one, two, *weights, resid)
    second = kernel(project_second_kernel, "project_second", rows, count=6, flops=1, moved=1)(*near, *weights, first)
    hidden = kernel(
        project_kernel,
        "project",
        shape(piece + NOTES, WIDE),
        count=2 + 4,
        flops=patches * MAIN * 256,
        moved=4 << 20,
    )(far, swap(after(far, first), 1), second, *weights, own_gain)
    ends, bias = kernel(
        tail_kernel,
        "merge_tail",
        [shape(units, MAIN), shape(units, 1, dtype=F32)],
        [pltpu.VMEM((units,), F32), pltpu.SemaphoreType.DMA],
        fetched=(1, 2),
        count=3,
        moved=4 << 20,
    )(merge_weight, in_hbm(merge_bias), hidden)
    sums = shape(4, units, groups, dtype=F32)
    one, two, far = swap(hidden, 4), swap(hidden, 2), swap(hidden, 6)
    first = kernel(merge_first_kernel, "merge_first", sums, count=5, flops=1, moved=1)(
        hidden, one, two, merge_weight, ends
    )
    near = [swap(after(hidden, ends), 1), swap(one, 1), swap(two, 1)]
    second = kernel(merge_second_kernel, "merge_second", sums, count=6, flops=1, moved=1)(
        *near, first, merge_weight, ends
    )
    return kernel(
        merge_kernel,
        "merge",
        shape(1, units, groups),
        [pltpu.VMEM((units, groups), BF16), pltpu.SemaphoreType.DMA((2,))],
        out=pl.ANY,
        count=ROWS + 5,
        flops=4 * units * groups * MAIN,
        moved=8 << 20,
    )(hidden, one, two, *near, far, swap(after(far, first, *near), 1), second, merge_weight, ends, bias, live)


def solution(mesh):
    in_specs = (
        P("page", "row", None),
        P("page", "row", None),
        P("page", None),
        P(),
        P("row", None),
        P("row"),
        P("page", None),
    )
    out_specs = P("page", "row", None)
    local = local_eight if mesh.shape["row"] == 8 and mesh.shape["page"] == 4 else local_any
    return jax.shard_map(local, mesh=mesh, in_specs=in_specs, out_specs=out_specs, check_vma=False)
```
